32 devices in a mesh: seq: 8 (over z, x), head: 4 (over y, core).
Axes of the slice: x: 2, y: 2, z: 4, core: 2. Of those that a mesh axis runs over, the one named last changes fastest.
Arguments:
- tokens: bfloat16 [4096, 4, 768], P(('seq', 'head')), may hold values from -6 to 6
- w_qkv: bfloat16 [768, 12, 3, 64], P(None, 'head'), may hold values from -0.21875 to 0.21875
- bias_qv: float32 [12, 2, 64], P('head'), may hold values from -1.8 to 1.8
- w_out: bfloat16 [12, 64, 768], P('head'), may hold values from -0.625 to 0.625
- bias_out: float32 [768], replicated, may hold values from -1.8 to 1.8
- gain_one: float32 [768], replicated, may hold values from 0.5 to 1.5
- bias_one: float32 [768], replicated, may hold values from -1.8 to 1.8
- up_weight: bfloat16 [768, 3072], P(None, 'head'), may hold values from -0.21875 to 0.21875
- up_bias_vector: bfloat16 [3072], P('head'), may hold values from -1.796875 to 1.796875
- down_weight: bfloat16 [3072, 768], P('head'), may hold values from -0.109375 to 0.109375
- down_bias_vector: float32 [768], replicated, may hold values from -1.8 to 1.8
- gain_two: float32 [768], replicated, may hold values from 0.5 to 1.5
- bias_two: float32 [768], replicated, may hold values from -1.8 to 1.8
- d_out: bfloat16 [4096, 4, 768], P(('seq', 'head')), may hold values from -6 to 6
- key_mask: int32 [4, 4096], replicated, may hold values from 0 to 1, as said below
- rand_idx: int32 [4, 64, 12, 3], replicated, may hold values from 1 to 62, as said below
Outputs:
- block_out: bfloat16 [4096, 4, 768], P(('seq', 'head'))
- d_tokens: bfloat16 [4096, 4, 768], P(('seq', 'head'))
- grad_w_qkv: float32 [768, 12, 3, 64], P(None, 'head')
- grad_bias_qv: float32 [12, 2, 64], P('head')
- grad_w_out: float32 [12, 64, 768], P('head')
- grad_bias_out: float32 [768], replicated
- grad_gain_one: float32 [768], replicated
- grad_bias_one: float32 [768], replicated
- grad_w_in: float32 [768, 3072], P(None, 'head')
- grad_bias_in: float32 [3072], P('head')
- grad_w_back: float32 [3072, 768], P('head')
- grad_bias_back: float32 [768], replicated
- grad_gain_two: float32 [768], replicated
- grad_bias_two: float32 [768], replicated
The draws below stay inside these ranges and needn't reach their ends.
Inputs may be any that keep to these rules, and one draw needn't show every extreme that they name: key_mask[s, 0] is 1 for every sequence s. rand_idx[s, j, h] holds three different blocks, none of them 0, 63, j - 1, j or j + 1.
All inputs are finite; a program needn't handle non-finite values.
Results may differ from the reference program's by a relative error of at most 0.015.
Values may be sent and summed in bfloat16 or wider, within the bound.
No kernel may reach another device: no remote copies, remote signals or barrier semaphores. Data moves between devices by JAX's collectives and lax.ppermute only.
A program may use at most 320 MiB of HBM per device.

```python
import jax
import jax.numpy as jnp
from jax import lax

D = 768
HEADS = 12
HDIM = 64
FF = 3072
BLOCK = 64
LEN = 4096
SEQS = 4
NB = 64


def draw_key_mask(key, part):
    key = jax.random.fold_in(key, 11)
    rate_key = jax.random.fold_in(key, 1)
    roll_key = jax.random.fold_in(key, 2)
    rates = jax.random.randint(rate_key, (SEQS, 1), 5, 26)
    rolls = jax.random.randint(roll_key, (SEQS, LEN), 0, 100)
    keep_bits = (rolls >= rates).astype(jnp.int32)
    first_pos = (jnp.arange(LEN) == 0)[None, :]
    return jnp.where(first_pos, 1, keep_bits).astype(jnp.int32)


def draw_rand_idx(key, part):
    key = jax.random.fold_in(key, 23)
    raw_scores = jax.random.randint(key, (SEQS, NB, HEADS, NB), 0, 1 << 20)
    blocks = jnp.arange(NB).astype(jnp.int32)
    rows_ids = jnp.arange(NB).astype(jnp.int32)[:, None]
    banned = (blocks[None, :] == 0) | (blocks[None, :] == NB - 1) | (jnp.abs(blocks[None, :] - rows_ids) <= 1)
    distinct = raw_scores * NB + blocks
    distinct = jnp.where(banned[None, :, None, :], -1 - blocks, distinct)
    picked = lax.top_k(distinct, 3)[1]
    return picked.astype(jnp.int32)


def steps_of(key, shape, split, low, top_value):
    level = 1.0
    for dim, blocks in split:
        draws = jax.random.uniform(jax.random.fold_in(jax.random.fold_in(key, 6), dim), (blocks,), jnp.float32, low / len(split), top_value / len(split))
        level = level * jnp.repeat(jnp.exp(draws), shape[dim] // blocks).reshape((-1,) + (1,) * (len(shape) - 1 - dim))
    return level


def gaussian(own_key, dims, scale, most, shards=(), held_as=jnp.bfloat16):
    factor_of = steps_of(own_key, dims, shards, -0.22, 0.18) if shards else 1.0
    values = jax.random.normal(own_key, dims, jnp.float32) * scale * factor_of
    return jnp.minimum(jnp.maximum(values, -most), most).astype(held_as)


def setup_inputs(seed: int = 0) -> dict:
    arg_keys = jax.random.split(jax.random.key(seed), 17)
    return {
        "tokens": gaussian(arg_keys[0], (LEN, SEQS, D), 1.0, 6.0, ((0, 32),)),
        "w_qkv": gaussian(arg_keys[1], (D, HEADS, 3, HDIM), D ** -0.5, 0.21875, ((1, 4),)),
        "bias_qv": gaussian(arg_keys[2], (HEADS, 2, HDIM), 0.3, 1.8, ((0, 4),), jnp.float32),
        "w_out": gaussian(arg_keys[3], (HEADS, HDIM, D), (D // 8) ** -0.5, 0.625, ((0, 4),)),
        "bias_out": gaussian(arg_keys[4], (D,), 0.3, 1.8, (), jnp.float32),
        "gain_one": jnp.clip(1.0 + 0.1 * jax.random.normal(arg_keys[5], (D,), jnp.float32), 0.5, 1.5),
        "bias_one": gaussian(arg_keys[6], (D,), 0.3, 1.8, (), jnp.float32),
        "up_weight": gaussian(arg_keys[7], (D, FF), D ** -0.5, 0.21875, ((1, 4),)),
        "up_bias_vector": gaussian(arg_keys[8], (FF,), 0.3, 1.796875, ((0, 4),)),
        "down_weight": gaussian(arg_keys[9], (FF, D), FF ** -0.5, 0.109375, ((0, 4),)),
        "down_bias_vector": gaussian(arg_keys[10], (D,), 0.3, 1.8, (), jnp.float32),
        "gain_two": jnp.clip(1.0 + 0.1 * jax.random.normal(arg_keys[11], (D,), jnp.float32), 0.5, 1.5),
        "bias_two": gaussian(arg_keys[12], (D,), 0.3, 1.8, (), jnp.float32),
        "d_out": gaussian(arg_keys[13], (LEN, SEQS, D), 1.0, 6.0, ((0, 32),)),
        "key_mask": draw_key_mask(jax.random.fold_in(arg_keys[16], 71), 0),
        "rand_idx": draw_rand_idx(jax.random.fold_in(arg_keys[16], 71), 0),
    }


NORM_EPS = 1e-12
MASK_FILL = -1000000000.0
MATMUL_ACCURACY = lax.Precision.HIGHEST

@jax.custom_vjp
def reduced_cast(v):
    return lax.optimization_barrier(v.astype(jnp.bfloat16)).astype(jnp.float32)

@jax.custom_vjp
def reduced_cast_backward(v):
    return v

def low_keep(v):
    return (reduced_cast(v), None)

def low_pass(kept, grad):
    return (grad,)

def back_keep(v):
    return (v, None)

def back_low(kept, grad):
    return (reduced_cast(grad),)
reduced_cast.defvjp(low_keep, low_pass)
reduced_cast_backward.defvjp(back_keep, back_low)

def layer_norm(resid, gain, shift):
    row_mean = lax.optimization_barrier(jnp.mean(resid, axis=-1, keepdims=True))
    centred = resid - row_mean
    variance = lax.optimization_barrier(jnp.mean(centred * centred, axis=-1, keepdims=True))
    return centred * lax.rsqrt(variance + NORM_EPS) * gain + shift

def sequence_attention(queries, keys_seq, values_seq, key_valid, chosen):
    score_scale = HDIM ** (-0.5)
    blocks = jnp.arange(NB).astype(jnp.int32)
    window = blocks[:, None] + jnp.arange(-1, 2).astype(jnp.int32)[None, :]
    window_ok = (window >= 1) & (window <= NB - 2)
    fixed_ids = jnp.concatenate([jnp.clip(window, 0, NB - 1).astype(jnp.int32), jnp.broadcast_to(jnp.array([0, NB - 1], jnp.int32), (NB, 2))], axis=1)
    fixed_ok = jnp.concatenate([window_ok, jnp.ones((NB, 2), bool)], axis=1)
    block_table = jnp.concatenate([jnp.broadcast_to(fixed_ids[:, None, :], (NB, HEADS, 5)).astype(jnp.int32), chosen.astype(jnp.int32)], axis=2)
    table_ok = jnp.concatenate([jnp.broadcast_to(fixed_ok[:, None, :], (NB, HEADS, 5)), jnp.ones((NB, HEADS, 3), bool)], axis=2)
    key_blocks = keys_seq.reshape(NB, BLOCK, HEADS, HDIM)
    value_blocks = values_seq.reshape(NB, BLOCK, HEADS, HDIM)
    head_index = jnp.arange(HEADS).astype(jnp.int32)[None, :, None]
    key_pick = key_blocks[block_table, :, head_index, :].reshape(NB, HEADS, 8 * BLOCK, HDIM)
    value_pick = value_blocks[block_table, :, head_index, :].reshape(NB, HEADS, 8 * BLOCK, HDIM)
    valid_pick = (key_valid.reshape(NB, BLOCK)[block_table] & table_ok[..., None]).reshape(NB, HEADS, 8 * BLOCK)
    query_blocks = queries.reshape(NB, BLOCK, HEADS, HDIM)
    scores = jnp.einsum('jqhd,jhkd->jhqk', query_blocks, key_pick, precision=MATMUL_ACCURACY) * score_scale
    scores = reduced_cast_backward(jnp.where(valid_pick[:, :, None, :], scores, MASK_FILL))
    attn_prob = reduced_cast(jax.nn.softmax(scores, axis=-1))
    sparse = jnp.einsum('jhqk,jhkd->jqhd', attn_prob, value_pick, precision=MATMUL_ACCURACY)
    edge_queries = query_blocks[jnp.array([0, NB - 1], jnp.int32)]
    edge_scores = jnp.einsum('gqhd,lhd->ghql', edge_queries, keys_seq, precision=MATMUL_ACCURACY) * score_scale
    edge_scores = reduced_cast_backward(jnp.where(key_valid[None, None, None, :], edge_scores, MASK_FILL))
    edge_prob = reduced_cast(jax.nn.softmax(edge_scores, axis=-1))
    edge_out = jnp.einsum('ghql,lhd->gqhd', edge_prob, values_seq, precision=MATMUL_ACCURACY)
    sparse = sparse.at[0].set(edge_out[0]).at[NB - 1].set(edge_out[1])
    return sparse.reshape(LEN, HEADS, HDIM)

def attend_one(packed):
    projected, key_valid, chosen = packed
    return sequence_attention(projected[:, :, 0], projected[:, :, 1], projected[:, :, 2], key_valid, chosen)

def forward(tokens, w_qkv, bias_qv, w_out, bias_out, gain_one, bias_one, up_weight, up_bias_vector, down_weight, down_bias_vector, gain_two, bias_two, key_valid, rand_idx):
    bias_full = jnp.stack([bias_qv[:, 0], jnp.zeros_like(bias_qv[:, 0]), bias_qv[:, 1]], axis=1)
    projected = jnp.einsum('lsd,dhce->lshce', tokens, w_qkv, precision=MATMUL_ACCURACY) + bias_full
    projected = reduced_cast_backward(reduced_cast(projected))
    per_seq = jnp.transpose(projected, (1, 0, 2, 3, 4))
    attn = lax.map(jax.checkpoint(attend_one), (per_seq, key_valid, rand_idx))
    attn = reduced_cast_backward(reduced_cast(jnp.transpose(attn, (1, 0, 2, 3))))
    branch = reduced_cast_backward(jnp.einsum('lshe,hed->lsd', attn, w_out, precision=MATMUL_ACCURACY) + bias_out)
    first_residual_output = layer_norm(tokens + branch, gain_one, bias_one)
    preactivation_values = reduced_cast_backward(jnp.einsum('ony,yx->onx', reduced_cast(first_residual_output), up_weight, precision=MATMUL_ACCURACY) + up_bias_vector)
    hidden_activation = reduced_cast(jax.nn.gelu(preactivation_values, approximate=True))
    feedforward_output = reduced_cast_backward(jnp.einsum('trh,hz->trz', hidden_activation, down_weight, precision=MATMUL_ACCURACY) + down_bias_vector)
    return layer_norm(first_residual_output + feedforward_output, gain_two, bias_two)

def reference(tokens, w_qkv, bias_qv, w_out, bias_out, gain_one, bias_one, up_weight, up_bias_vector, down_weight, down_bias_vector, gain_two, bias_two, d_out, key_mask, rand_idx):
    key_valid = key_mask == 1

    def wrapped(*params):
        return forward(*params, key_valid, rand_idx)
    primals = tuple((arr.astype(jnp.float32) for arr in (tokens, w_qkv, bias_qv, w_out, bias_out, gain_one, bias_one, up_weight, up_bias_vector, down_weight, down_bias_vector, gain_two, bias_two)))
    result, pullback = jax.vjp(wrapped, *primals)
    grads = pullback(d_out.astype(jnp.float32))
    return (result.astype(jnp.bfloat16), grads[0].astype(jnp.bfloat16), grads[1], grads[2], grads[3], grads[4], grads[5], grads[6], grads[7], grads[8], grads[9], grads[10], grads[11], grads[12])
```

```python
import functools

import jax
import jax.numpy as jnp
import numpy as np
from jax import lax
from jax.experimental import pallas as pl
from jax.experimental.pallas import tpu as pltpu
from jax.sharding import Mesh
from jax.sharding import PartitionSpec as P

BLOCK = 64
PICKS = 8
CHUNK = 512
NORM_EPS = 1e-12
MASK_FILL = -1000000000.0

f32 = jnp.float32
bf16 = jnp.bfloat16

PLANE = ("part", "hy", "hc")
HEAD = ("hy", "hc")
SEQ = ("sq", "part")


def norm_fwd(resid, gain, shift):
    row_mean = jnp.mean(resid, axis=-1, keepdims=True)
    centred = resid - row_mean
    inv_std = lax.rsqrt(jnp.mean(centred * centred, axis=-1, keepdims=True) + NORM_EPS)
    normed = centred * inv_std
    return (normed * gain + shift, normed, inv_std)


def norm_back(upstream, normed, inv_std, gain):
    d_normed = upstream * gain
    d_resid = inv_std * (
        d_normed
        - jnp.mean(d_normed, axis=-1, keepdims=True)
        - normed * jnp.mean(d_normed * normed, axis=-1, keepdims=True)
    )
    return (d_resid, jnp.sum(upstream * normed, axis=0), jnp.sum(upstream, axis=0))


def tanh_gelu(values):
    return jax.nn.gelu(values, approximate=True)


def gelu_back(preactivation_values, upstream):
    return jax.vjp(tanh_gelu, preactivation_values)[1](upstream)[0]


def dot_nt(a, b):
    return lax.dot_general(a, b, (((1,), (1,)), ((), ())), preferred_element_type=f32)


def dot_nn(a, b):
    return lax.dot_general(a, b, (((1,), (0,)), ((), ())), preferred_element_type=f32)


def dot_tn(a, b):
    return lax.dot_general(a, b, (((0,), (0,)), ((), ())), preferred_element_type=f32)


def gathered(kv_ref, table_ref, base, cols):
    return jnp.concatenate(
        [
            kv_ref[pl.ds(pl.multiple_of(table_ref[base + u] * BLOCK, BLOCK), BLOCK), cols]
            for u in range(PICKS)
        ],
        axis=0,
    )


def lane_pick(values, lane):
    lanes = lax.broadcasted_iota(jnp.int32, values.shape, 1)
    return jnp.sum(jnp.where(lanes == lane, values, 0.0), axis=1, keepdims=True)


def attn_fwd_kernel(heads, hd, table_ref, edge_ref, q_ref, kv_ref, bias_ref, mask_ref, o_ref, lse_ref, s_ref):
    wide = 2 * hd
    blocks = q_ref.shape[0] // BLOCK
    chunks = kv_ref.shape[0] // CHUNK
    lanes = lax.broadcasted_iota(jnp.int32, (BLOCK, 128), 1)

    def one(jl, carry):
        rows = pl.ds(pl.multiple_of(jl * BLOCK, BLOCK), BLOCK)
        outs = []
        lse_tile = jnp.zeros((BLOCK, 128), f32)
        for h in range(heads):
            cols = slice(h * wide, (h + 1) * wide)
            kvg = gathered(kv_ref, table_ref, (jl * heads + h) * PICKS, cols)
            s = dot_nt(q_ref[rows, cols], kvg) + bias_ref[jl, h : h + 1, :]
            top = jnp.max(s, axis=1, keepdims=True)
            p = jnp.exp(s - top)
            total = jnp.sum(p, axis=1, keepdims=True)
            low = (p * (1.0 / total)).astype(bf16)
            outs.append(dot_nn(low, kvg)[:, hd:])
            lse_tile = jnp.where(lanes == h, top + jnp.log(total), lse_tile)
        o_ref[rows, :] = jnp.concatenate(outs, axis=1).astype(bf16)
        lse_ref[rows, :] = lse_tile
        return carry

    lax.fori_loop(0, blocks, one, 0)

    def edge(jl):
        rows = slice(jl * BLOCK, (jl + 1) * BLOCK)
        outs = []
        lse_tile = jnp.zeros((BLOCK, 128), f32)
        for h in range(heads):
            cols = slice(h * wide, (h + 1) * wide)
            q = q_ref[rows, cols]

            def score(c, top):
                part = pl.ds(pl.multiple_of(c * CHUNK, CHUNK), CHUNK)
                s = dot_nt(q, kv_ref[part, cols]) + mask_ref[:, part]
                s_ref[:, part] = s
                return jnp.maximum(top, jnp.max(s, axis=1, keepdims=True))

            top = lax.fori_loop(0, chunks, score, jnp.full((BLOCK, 1), -3e38, f32))

            def add(c, total):
                part = pl.ds(pl.multiple_of(c * CHUNK, CHUNK), CHUNK)
                return total + jnp.sum(jnp.exp(s_ref[:, part] - top), axis=1, keepdims=True)

            total = lax.fori_loop(0, chunks, add, jnp.zeros((BLOCK, 1), f32))
            inv = 1.0 / total

            def out(c, acc):
                part = pl.ds(pl.multiple_of(c * CHUNK, CHUNK), CHUNK)
                low = (jnp.exp(s_ref[:, part] - top) * inv).astype(bf16)
                return acc + dot_nn(low, kv_ref[part, cols])

            acc = lax.fori_loop(0, chunks, out, jnp.zeros((BLOCK, wide), f32))
            outs.append(acc[:, hd:])
            lse_tile = jnp.where(lanes == h, top + jnp.log(total), lse_tile)
        o_ref[rows, :] = jnp.concatenate(outs, axis=1).astype(bf16)
        lse_ref[rows, :] = lse_tile

    @pl.when(edge_ref[0] == 1)
    def _():
        edge(0)

    @pl.when(edge_ref[1] == 1)
    def _():
        edge(blocks - 1)


def attn_bwd_kernel(
    heads, hd, scale, table_ref, edge_ref, qd_ref, kv_ref, bias_ref, mask_ref, lse_ref, dq_ref, dkv_ref, acc_ref, p_ref, dp_ref
):
    wide = 2 * hd
    blocks = qd_ref.shape[0] // BLOCK
    chunks = kv_ref.shape[0] // CHUNK
    left = lax.broadcasted_iota(jnp.int32, (BLOCK, wide), 1) < hd
    nil = jnp.zeros((BLOCK, wide), bf16)

    def clear(c, carry):
        part = pl.ds(pl.multiple_of(c * CHUNK, CHUNK), CHUNK)
        acc_ref[part, :] = jnp.zeros((CHUNK, heads * wide), f32)
        return carry

    lax.fori_loop(0, chunks, clear, 0)

    def stacked(qd):
        return jnp.concatenate([jnp.where(left, qd, nil), jnp.where(left, nil, qd)], axis=0)

    def one(jl, carry):
        rows = pl.ds(pl.multiple_of(jl * BLOCK, BLOCK), BLOCK)
        lse_tile = lse_ref[rows, :]
        outs = []
        for h in range(heads):
            cols = slice(h * wide, (h + 1) * wide)
            base = (jl * heads + h) * PICKS
            kvg = gathered(kv_ref, table_ref, base, cols)
            both = stacked(qd_ref[rows, cols])
            prod = dot_nt(both, kvg)
            p = jnp.exp(prod[:BLOCK] + bias_ref[jl, h : h + 1, :] - lane_pick(lse_tile, h))
            dp = prod[BLOCK:]
            dot_row = jnp.sum(p * dp, axis=1, keepdims=True)
            ds = (p * (dp - dot_row)).astype(bf16)
            outs.append(dot_nn(ds, kvg)[:, :hd])
            dkv = dot_tn(jnp.concatenate([ds, p.astype(bf16)], axis=0), both)
            for u in range(PICKS):
                place = pl.ds(pl.multiple_of(table_ref[base + u] * BLOCK, BLOCK), BLOCK)
                acc_ref[place, cols] += dkv[u * BLOCK : (u + 1) * BLOCK]
        dq_ref[rows, :] = (jnp.concatenate(outs, axis=1) * scale).astype(bf16)
        return carry

    lax.fori_loop(edge_ref[0], blocks - edge_ref[1], one, 0)

    def edge(jl):
        rows = slice(jl * BLOCK, (jl + 1) * BLOCK)
        lse_tile = lse_ref[rows, :]
        outs = []
        for h in range(heads):
            cols = slice(h * wide, (h + 1) * wide)
            both = stacked(qd_ref[rows, cols])
            lse = lane_pick(lse_tile, h)

            def first(c, total):
                part = pl.ds(pl.multiple_of(c * CHUNK, CHUNK), CHUNK)
                prod = dot_nt(both, kv_ref[part, cols])
                p = jnp.exp(prod[:BLOCK] + mask_ref[:, part] - lse)
                dp = prod[BLOCK:]
                p_ref[:, part] = p
                dp_ref[:, part] = dp
                return total + jnp.sum(p * dp, axis=1, keepdims=True)

            dot_row = lax.fori_loop(0, chunks, first, jnp.zeros((BLOCK, 1), f32))

            def second(c, dq):
                part = pl.ds(pl.multiple_of(c * CHUNK, CHUNK), CHUNK)
                p = p_ref[:, part]
                ds = (p * (dp_ref[:, part] - dot_row)).astype(bf16)
                acc_ref[part, cols] += dot_tn(jnp.concatenate([ds, p.astype(bf16)], axis=0), both)
                return dq + dot_nn(ds, kv_ref[part, cols])

            dq = lax.fori_loop(0, chunks, second, jnp.zeros((BLOCK, wide), f32))
            outs.append(dq[:, :hd])
        dq_ref[rows, :] = (jnp.concatenate(outs, axis=1) * scale).astype(bf16)

    @pl.when(edge_ref[0] == 1)
    def _():
        edge(0)

    @pl.when(edge_ref[1] == 1)
    def _():
        edge(blocks - 1)

    def put(c, carry):
        part = pl.ds(pl.multiple_of(c * CHUNK, CHUNK), CHUNK)
        dkv_ref[part, :] = acc_ref[part, :].astype(bf16)
        return carry

    lax.fori_loop(0, chunks, put, 0)


SMEM_SPEC = pl.BlockSpec(memory_space=pltpu.SMEM)
VMEM_SPEC = pl.BlockSpec(memory_space=pltpu.VMEM)
VMEM_LIMIT = 48 * 1024 * 1024


def attn_forward(heads, hd, table, edges, q, kv, bias, mask):
    rows, keys = q.shape[0], kv.shape[0]
    return pl.pallas_call(
        functools.partial(attn_fwd_kernel, heads, hd),
        out_shape=(
            jax.ShapeDtypeStruct((rows, heads * hd), bf16),
            jax.ShapeDtypeStruct((rows, 128), f32),
        ),
        in_specs=[SMEM_SPEC] * 2 + [VMEM_SPEC] * 4,
        out_specs=(VMEM_SPEC, VMEM_SPEC),
        scratch_shapes=[pltpu.VMEM((BLOCK, keys), f32)],
        compiler_params=pltpu.CompilerParams(vmem_limit_bytes=VMEM_LIMIT),
        cost_estimate=pl.CostEstimate(
            flops=4 * rows * heads * CHUNK * 2 * hd, bytes_accessed=8 << 20, transcendentals=rows * heads * CHUNK
        ),
        name="attn_forward",
    )(table, edges, q, kv, bias, mask)


def attn_backward(heads, hd, scale, table, edges, qd, kv, bias, mask, lse):
    rows, keys = qd.shape[0], kv.shape[0]
    return pl.pallas_call(
        functools.partial(attn_bwd_kernel, heads, hd, scale),
        out_shape=(
            jax.ShapeDtypeStruct((rows, heads * hd), bf16),
            jax.ShapeDtypeStruct((keys, heads * 2 * hd), bf16),
        ),
        in_specs=[SMEM_SPEC] * 2 + [VMEM_SPEC] * 5,
        out_specs=(VMEM_SPEC, VMEM_SPEC),
        scratch_shapes=[
            pltpu.VMEM((keys, heads * 2 * hd), f32),
            pltpu.VMEM((BLOCK, keys), f32),
            pltpu.VMEM((BLOCK, keys), f32),
        ],
        compiler_params=pltpu.CompilerParams(vmem_limit_bytes=VMEM_LIMIT),
        cost_estimate=pl.CostEstimate(
            flops=10 * rows * heads * CHUNK * 2 * hd, bytes_accessed=12 << 20, transcendentals=rows * heads * CHUNK
        ),
        name="attn_backward",
    )(table, edges, qd, kv, bias, mask, lse)


def per_device(
    tokens,
    w_qkv,
    bias_qv,
    w_out,
    bias_out,
    gain_one,
    bias_one,
    up_weight,
    up_bias_vector,
    down_weight,
    down_bias_vector,
    gain_two,
    bias_two,
    d_out,
    key_mask,
    rand_idx,
):
    sq = lax.axis_index("sq")
    part = lax.axis_index("part")
    head = lax.axis_index(HEAD)
    parts = lax.axis_size("part")
    groups = lax.axis_size(HEAD)
    span, seqs, width = tokens.shape
    heads, hd = w_qkv.shape[1], w_qkv.shape[3]
    scale = hd ** (-0.5)
    length = key_mask.shape[1]
    blocks_all = length // BLOCK
    per_chunk = groups * span // BLOCK
    mine = seqs * per_chunk

    tok = lax.all_to_all(jnp.transpose(tokens, (1, 0, 2)), "sq", 0, 0, tiled=True)
    x_all = lax.all_gather(tok, PLANE, axis=0, tiled=False)
    d_res = lax.all_to_all(jnp.transpose(d_out, (1, 0, 2)), "sq", 0, 0, tiled=True)

    w_out_full = lax.all_gather(w_out.reshape(heads * hd, width), HEAD, axis=0, tiled=False)
    up_full = lax.all_gather(up_weight, HEAD, axis=0, tiled=False)
    down_full = lax.all_gather(down_weight, HEAD, axis=0, tiled=False)
    up_bias_full = lax.all_gather(up_bias_vector.astype(f32), HEAD, axis=0, tiled=False)

    chunk_ids = jnp.arange(seqs) * parts + part
    block_ids = (chunk_ids[:, None] * per_chunk + jnp.arange(per_chunk)[None, :]).reshape(mine)
    rand_seq = lax.dynamic_index_in_dim(rand_idx, sq, 0, keepdims=False)
    rand_head = lax.dynamic_slice_in_dim(rand_seq, head * heads, heads, 1)
    chosen = jnp.take(rand_head, block_ids, axis=0)
    window = block_ids[:, None] + jnp.arange(-1, 2)[None, :]
    window_ok = (window >= 1) & (window <= blocks_all - 2)
    fixed_ids = jnp.concatenate(
        [
            jnp.clip(window, 0, blocks_all - 1),
            jnp.broadcast_to(jnp.array([0, blocks_all - 1], jnp.int32), (mine, 2)),
        ],
        axis=1,
    )
    fixed_ok = jnp.concatenate([window_ok, jnp.ones((mine, 2), bool)], axis=1)
    table = jnp.concatenate(
        [jnp.broadcast_to(fixed_ids[:, None, :], (mine, heads, 5)), chosen], axis=2
    )
    table_ok = jnp.concatenate(
        [
            jnp.broadcast_to(fixed_ok[:, None, :], (mine, heads, 5)),
            jnp.ones((mine, heads, PICKS - 5), bool),
        ],
        axis=2,
    )
    mask_seq = lax.dynamic_index_in_dim(key_mask, sq, 0, keepdims=False)
    mask_blocks = (mask_seq == 1).reshape(blocks_all, BLOCK).astype(bf16)
    onehot = (table[..., None] == jnp.arange(blocks_all)).astype(bf16) * table_ok[..., None].astype(bf16)
    allowed = jnp.einsum("jhub,bk->jhuk", onehot, mask_blocks, preferred_element_type=f32)
    bias_rows = ((1.0 - allowed) * MASK_FILL).reshape(mine, heads, PICKS * BLOCK)
    mask_row = jnp.where(mask_seq == 1, 0.0, MASK_FILL).astype(f32).reshape(1, length)
    edges = jnp.stack([part == 0, part == parts - 1]).astype(jnp.int32)
    table = table.reshape(-1).astype(jnp.int32)

    w_kv = w_qkv[:, :, 1:].reshape(width, heads * 2 * hd)
    bias_kv = jnp.stack([jnp.zeros((heads, hd), f32), bias_qv[:, 1]], axis=1).reshape(heads * 2 * hd)
    w_q = w_qkv[:, :, 0].reshape(width, heads * hd)
    bias_q = bias_qv[:, 0].reshape(heads * hd)
    x_rows = x_all.reshape(parts, groups, seqs, span, width)
    x_mine = lax.dynamic_index_in_dim(x_rows, part, 0, keepdims=False)
    kv_rows = (jnp.einsum("pgzsd,dc->pgzsc", x_rows, w_kv, preferred_element_type=f32) + bias_kv).astype(bf16)
    kv = jnp.transpose(kv_rows, (2, 0, 1, 3, 4)).reshape(length, heads * 2 * hd)
    q_rows = (jnp.einsum("gzsd,dc->gzsc", x_mine, w_q, preferred_element_type=f32) + bias_q).astype(bf16)
    q_low = jnp.transpose(q_rows, (1, 0, 2, 3)).reshape(mine * BLOCK, heads, hd) * bf16(scale)
    q_pad = jnp.concatenate([q_low, jnp.zeros_like(q_low)], axis=-1).reshape(mine * BLOCK, heads * 2 * hd)

    attn_mine, lse = attn_forward(heads, hd, table, edges, q_pad, kv, bias_rows, mask_row)
    attn_send = jnp.transpose(attn_mine.reshape(seqs, groups, span, heads * hd), (1, 0, 2, 3))
    attn = lax.all_to_all(attn_send, HEAD, 0, 0, tiled=True).reshape(groups, seqs * span, heads * hd)

    rows = seqs * span
    tok_rows = tok.reshape(rows, width)
    branch = jnp.einsum("grc,gcd->rd", attn, w_out_full, preferred_element_type=f32) + bias_out
    y_one, normed_one, inv_one = norm_fwd(tok_rows.astype(f32) + branch, gain_one, bias_one)
    y_low = y_one.astype(bf16)
    pre = jnp.einsum("rd,gdf->grf", y_low, up_full, preferred_element_type=f32) + up_bias_full[:, None, :]
    hidden = tanh_gelu(pre).astype(bf16)
    ffn = jnp.einsum("grf,gfd->rd", hidden, down_full, preferred_element_type=f32) + down_bias_vector
    result, normed_two, inv_two = norm_fwd(y_one + ffn, gain_two, bias_two)
    result = lax.all_to_all(result.astype(bf16).reshape(seqs, span, width), "sq", 0, 0, tiled=True)
    d_two, grad_gain_two, grad_bias_two = norm_back(
        d_res.reshape(rows, width).astype(f32), normed_two, inv_two, gain_two
    )
    d_ffn = d_two.astype(bf16)
    grad_bias_back = jnp.sum(d_ffn.astype(f32), axis=0)
    d_hidden = jnp.einsum("rd,gfd->grf", d_ffn, down_full, preferred_element_type=f32)
    d_pre = gelu_back(pre, d_hidden).astype(bf16)
    d_y_ffn = jnp.einsum("grf,gdf->rd", d_pre, up_full, preferred_element_type=f32)
    grad_w_in = jnp.einsum("rd,grf->gdf", y_low, d_pre, preferred_element_type=f32).astype(bf16)
    grad_bias_in = jnp.sum(d_pre.astype(f32), axis=1)
    grad_w_back = jnp.einsum("grf,rd->gfd", hidden, d_ffn, preferred_element_type=f32).astype(bf16)
    d_one, grad_gain_one, grad_bias_one = norm_back(d_two + d_y_ffn, normed_one, inv_one, gain_one)
    d_branch = d_one.astype(bf16)
    grad_bias_out = jnp.sum(d_branch.astype(f32), axis=0)
    d_attn = jnp.einsum("rd,gcd->grc", d_branch, w_out_full, preferred_element_type=f32).astype(bf16)
    grad_w_out = jnp.einsum("grc,rd->gcd", attn, d_branch, preferred_element_type=f32).astype(bf16)

    d_attn_mine = lax.all_to_all(d_attn.reshape(groups, seqs, span, heads * hd), HEAD, 0, 0, tiled=True)
    d_attn_nat = jnp.transpose(d_attn_mine, (1, 0, 2, 3)).reshape(mine * BLOCK, heads, hd)
    qd = jnp.concatenate([q_low, d_attn_nat], axis=-1).reshape(mine * BLOCK, heads * 2 * hd)

    wide_part = jnp.concatenate([grad_w_in, grad_w_back, grad_w_out], axis=1)
    wide_sum = lax.psum_scatter(wide_part, HEAD, scatter_dimension=0, tiled=True)[0]
    wide_sum = lax.psum(wide_sum, SEQ)

    dq, dkv = attn_backward(heads, hd, scale, table, edges, qd, kv, bias_rows, mask_row, lse)
    dkv_rows = jnp.transpose(
        dkv.reshape(seqs, parts, groups, span, heads * 2 * hd), (1, 2, 0, 3, 4)
    )
    dq_rows = jnp.transpose(dq.reshape(seqs, groups, span, heads * hd), (1, 0, 2, 3))
    dq_all = lax.dynamic_update_index_in_dim(
        jnp.zeros((parts, groups, seqs, span, heads * hd), bf16), dq_rows, part, 0
    )
    d_x = jnp.einsum("pgzsc,dc->pgzsd", dkv_rows, w_kv, preferred_element_type=f32) + jnp.einsum(
        "pgzsc,dc->pgzsd", dq_all, w_q, preferred_element_type=f32
    )
    d_x = lax.psum_scatter(
        d_x.astype(bf16).reshape(parts * groups, seqs, span, width), PLANE, scatter_dimension=0, tiled=True
    )
    d_tok = (d_one + d_x.reshape(rows, width).astype(f32)).astype(bf16)
    d_tok = lax.all_to_all(d_tok.reshape(seqs, span, width), "sq", 0, 0, tiled=True)

    grad_kv = jnp.einsum("pgzsd,pgzsc->dc", x_rows, dkv_rows, preferred_element_type=f32)
    grad_q = jnp.einsum("gzsd,gzsc->dc", x_mine, dq_rows, preferred_element_type=f32)
    grad_w_qkv = jnp.concatenate(
        [grad_q.reshape(width, heads, 1, hd), grad_kv.reshape(width, heads, 2, hd)], axis=2
    )
    bias_q_sum = jnp.sum(dq_rows.astype(f32), axis=(0, 1, 2)).reshape(heads, 1, hd)
    bias_v_sum = jnp.sum(dkv_rows.astype(f32), axis=(0, 1, 2, 3)).reshape(heads, 2, hd)[:, 1:]
    grad_bias_qv = jnp.concatenate([bias_q_sum, bias_v_sum], axis=1)
    grad_w_qkv = lax.psum(grad_w_qkv.astype(bf16), SEQ).astype(f32)

    small = jnp.stack(
        [grad_bias_out, grad_gain_one, grad_bias_one, grad_bias_back, grad_gain_two, grad_bias_two]
    )
    all_bias_in = grad_bias_in
    bias_qv_all = lax.dynamic_update_index_in_dim(
        jnp.zeros((groups, heads * 2 * hd), f32), grad_bias_qv.reshape(-1), head, 0
    )
    packed = jnp.concatenate([small.reshape(-1), all_bias_in.reshape(-1), bias_qv_all.reshape(-1)])
    packed = lax.psum(packed, ("sq", "part", "hy", "hc"))
    n_small = 6 * width
    small = packed[:n_small].reshape(6, width)
    n_in = n_small + all_bias_in.size
    hidden_dev = up_weight.shape[1]
    grad_bias_in = lax.dynamic_slice_in_dim(packed[n_small:n_in], head * hidden_dev, hidden_dev, 0)
    grad_bias_qv = lax.dynamic_slice_in_dim(
        packed[n_in:], head * heads * 2 * hd, heads * 2 * hd, 0
    ).reshape(heads, 2, hd)

    wide_sum = wide_sum.astype(f32)
    grad_w_in = wide_sum[:width]
    grad_w_back = wide_sum[width : width + hidden_dev]
    grad_w_out = wide_sum[width + hidden_dev :].reshape(heads, hd, width)
    return (
        jnp.transpose(result, (1, 0, 2)),
        jnp.transpose(d_tok, (1, 0, 2)),
        grad_w_qkv,
        grad_bias_qv,
        grad_w_out,
        small[0],
        small[1],
        small[2],
        grad_w_in,
        grad_bias_in,
        grad_w_back,
        small[3],
        small[4],
        small[5],
    )


def solution(mesh):
    seq_size, head_size = mesh.shape["seq"], mesh.shape["head"]

    def run(*args):
        seqs = args[0].shape[1]
        fine = Mesh(
            np.asarray(mesh.devices).reshape(seqs, seq_size // seqs, head_size // 2, 2),
            ("sq", "part", "hy", "hc"),
        )
        rows = P(("sq", "part", "hy", "hc"), None, None)
        placed = (
            rows,
            P(None, HEAD, None, None),
            P(HEAD, None, None),
            P(HEAD, None, None),
            P(),
            P(),
            P(),
            P(None, HEAD),
            P(HEAD),
            P(HEAD, None),
            P(),
            P(),
            P(),
            rows,
            P(),
            P(),
        )
        return jax.shard_map(
            per_device,
            mesh=fine,
            in_specs=placed,
            out_specs=(
                rows,
                rows,
                P(None, HEAD, None, None),
                P(HEAD, None, None),
                P(HEAD, None, None),
                P(),
                P(),
                P(),
                P(None, HEAD),
                P(HEAD),
                P(HEAD, None),
                P(),
                P(),
                P(),
            ),
            check_vma=False,
        )(*args)

    return run
```

```python
import functools

import jax
import jax.numpy as jnp
import numpy as np
from jax import lax
from jax.experimental import pallas as pl
from jax.experimental.pallas import tpu as pltpu
from jax.sharding import Mesh
from jax.sharding import PartitionSpec as P

BLOCK = 64
PICKS = 8
CHUNK = 512
NORM_EPS = 1e-12
MASK_FILL = -1000000000.0

f32 = jnp.float32
bf16 = jnp.bfloat16

PLANE = ("part", "hy", "hc")
HEAD = ("hy", "hc")
SEQ = ("sq", "part")


def norm_fwd(resid, gain, shift):
    row_mean = jnp.mean(resid, axis=-1, keepdims=True)
    centred = resid - row_mean
    inv_std = lax.rsqrt(jnp.mean(centred * centred, axis=-1, keepdims=True) + NORM_EPS)
    normed = centred * inv_std
    return (normed * gain + shift, normed, inv_std)


def norm_back(upstream, normed, inv_std, gain):
    d_normed = upstream * gain
    d_resid = inv_std * (
        d_normed
        - jnp.mean(d_normed, axis=-1, keepdims=True)
        - normed * jnp.mean(d_normed * normed, axis=-1, keepdims=True)
    )
    return (d_resid, jnp.sum(upstream * normed, axis=0), jnp.sum(upstream, axis=0))


def tanh_gelu(values):
    return jax.nn.gelu(values, approximate=True)


def gelu_back(preactivation_values, upstream):
    return jax.vjp(tanh_gelu, preactivation_values)[1](upstream)[0]


def dot_nt(a, b):
    return lax.dot_general(a, b, (((1,), (1,)), ((), ())), preferred_element_type=f32)


def dot_nn(a, b):
    return lax.dot_general(a, b, (((1,), (0,)), ((), ())), preferred_element_type=f32)


def dot_tn(a, b):
    return lax.dot_general(a, b, (((0,), (0,)), ((), ())), preferred_element_type=f32)


def gathered(kv_ref, table_ref, base, cols):
    return jnp.concatenate(
        [
            kv_ref[pl.ds(pl.multiple_of(table_ref[base + u] * BLOCK, BLOCK), BLOCK), cols]
            for u in range(PICKS)
        ],
        axis=0,
    )


def lane_pick(values, lane):
    lanes = lax.broadcasted_iota(jnp.int32, values.shape, 1)
    return jnp.sum(jnp.where(lanes == lane, values, 0.0), axis=1, keepdims=True)


def attn_fwd_kernel(heads, hd, table_ref, edge_ref, q_ref, kv_ref, bias_ref, mask_ref, o_ref, lse_ref, s_ref):
    wide = 2 * hd
    blocks = q_ref.shape[0] // BLOCK
    chunks = kv_ref.shape[0] // CHUNK
    lanes = lax.broadcasted_iota(jnp.int32, (BLOCK, 128), 1)

    def one(jl, carry):
        rows = pl.ds(pl.multiple_of(jl * BLOCK, BLOCK), BLOCK)
        outs = []
        lse_tile = jnp.zeros((BLOCK, 128), f32)
        for h in range(heads):
            cols = slice(h * wide, (h + 1) * wide)
            kvg = gathered(kv_ref, table_ref, (jl * heads + h) * PICKS, cols)
            s = dot_nt(q_ref[rows, cols], kvg) + bias_ref[jl, h : h + 1, :]
            top = jnp.max(s, axis=1, keepdims=True)
            p = jnp.exp(s - top)
            total = jnp.sum(p, axis=1, keepdims=True)
            low = (p * (1.0 / total)).astype(bf16)
            outs.append(dot_nn(low, kvg)[:, hd:])
            lse_tile = jnp.where(lanes == h, top + jnp.log(total), lse_tile)
        o_ref[rows, :] = jnp.concatenate(outs, axis=1).astype(bf16)
        lse_ref[rows, :] = lse_tile
        return carry

    lax.fori_loop(0, blocks, one, 0)

    def edge(jl):
        rows = slice(jl * BLOCK, (jl + 1) * BLOCK)
        outs = []
        lse_tile = jnp.zeros((BLOCK, 128), f32)
        for h in range(heads):
            cols = slice(h * wide, (h + 1) * wide)
            q = q_ref[rows, cols]

            def score(c, top):
                part = pl.ds(pl.multiple_of(c * CHUNK, CHUNK), CHUNK)
                s = dot_nt(q, kv_ref[part, cols]) + mask_ref[:, part]
                s_ref[:, part] = s
                return jnp.maximum(top, jnp.max(s, axis=1, keepdims=True))

            top = lax.fori_loop(0, chunks, score, jnp.full((BLOCK, 1), -3e38, f32))

            def add(c, total):
                part = pl.ds(pl.multiple_of(c * CHUNK, CHUNK), CHUNK)
                return total + jnp.sum(jnp.exp(s_ref[:, part] - top), axis=1, keepdims=True)

            total = lax.fori_loop(0, chunks, add, jnp.zeros((BLOCK, 1), f32))
            inv = 1.0 / total

            def out(c, acc):
                part = pl.ds(pl.multiple_of(c * CHUNK, CHUNK), CHUNK)
                low = (jnp.exp(s_ref[:, part] - top) * inv).astype(bf16)
                return acc + dot_nn(low, kv_ref[part, cols])

            acc = lax.fori_loop(0, chunks, out, jnp.zeros((BLOCK, wide), f32))
            outs.append(acc[:, hd:])
            lse_tile = jnp.where(lanes == h, top + jnp.log(total), lse_tile)
        o_ref[rows, :] = jnp.concatenate(outs, axis=1).astype(bf16)
        lse_ref[rows, :] = lse_tile

    @pl.when(edge_ref[0] == 1)
    def _():
        edge(0)

    @pl.when(edge_ref[1] == 1)
    def _():
        edge(blocks - 1)


def attn_bwd_kernel(
    heads, hd, scale, table_ref, edge_ref, qd_ref, kv_ref, bias_ref, mask_ref, lse_ref, dq_ref, dkv_ref, acc_ref, p_ref, dp_ref
):
    wide = 2 * hd
    blocks = qd_ref.shape[0] // BLOCK
    chunks = kv_ref.shape[0] // CHUNK
    left = lax.broadcasted_iota(jnp.int32, (BLOCK, wide), 1) < hd
    nil = jnp.zeros((BLOCK, wide), bf16)

    def clear(c, carry):
        part = pl.ds(pl.multiple_of(c * CHUNK, CHUNK), CHUNK)
        acc_ref[part, :] = jnp.zeros((CHUNK, heads * wide), f32)
        return carry

    lax.fori_loop(0, chunks, clear, 0)

    def stacked(qd):
        return jnp.concatenate([jnp.where(left, qd, nil), jnp.where(left, nil, qd)], axis=0)

    def one(jl, carry):
        rows = pl.ds(pl.multiple_of(jl * BLOCK, BLOCK), BLOCK)
        lse_tile = lse_ref[rows, :]
        outs = []
        for h in range(heads):
            cols = slice(h * wide, (h + 1) * wide)
            base = (jl * heads + h) * PICKS
            kvg = gathered(kv_ref, table_ref, base, cols)
            both = stacked(qd_ref[rows, cols])
            prod = dot_nt(both, kvg)
            p = jnp.exp(prod[:BLOCK] + bias_ref[jl, h : h + 1, :] - lane_pick(lse_tile, h))
            dp = prod[BLOCK:]
            dot_row = jnp.sum(p * dp, axis=1, keepdims=True)
            ds = (p * (dp - dot_row)).astype(bf16)
            outs.append(dot_nn(ds, kvg)[:, :hd])
            dkv = dot_tn(jnp.concatenate([ds, p.astype(bf16)], axis=0), both)
            for u in range(PICKS):
                place = pl.ds(pl.multiple_of(table_ref[base + u] * BLOCK, BLOCK), BLOCK)
                acc_ref[place, cols] += dkv[u * BLOCK : (u + 1) * BLOCK]
        dq_ref[rows, :] = (jnp.concatenate(outs, axis=1) * scale).astype(bf16)
        return carry

    lax.fori_loop(edge_ref[0], blocks - edge_ref[1], one, 0)

    def edge(jl):
        rows = slice(jl * BLOCK, (jl + 1) * BLOCK)
        lse_tile = lse_ref[rows, :]
        outs = []
        for h in range(heads):
            cols = slice(h * wide, (h + 1) * wide)
            both = stacked(qd_ref[rows, cols])
            lse = lane_pick(lse_tile, h)

            def first(c, total):
                part = pl.ds(pl.multiple_of(c * CHUNK, CHUNK), CHUNK)
                prod = dot_nt(both, kv_ref[part, cols])
                p = jnp.exp(prod[:BLOCK] + mask_ref[:, part] - lse)
                dp = prod[BLOCK:]
                p_ref[:, part] = p
                dp_ref[:, part] = dp
                return total + jnp.sum(p * dp, axis=1, keepdims=True)

            dot_row = lax.fori_loop(0, chunks, first, jnp.zeros((BLOCK, 1), f32))

            def second(c, dq):
                part = pl.ds(pl.multiple_of(c * CHUNK, CHUNK), CHUNK)
                p = p_ref[:, part]
                ds = (p * (dp_ref[:, part] - dot_row)).astype(bf16)
                acc_ref[part, cols] += dot_tn(jnp.concatenate([ds, p.astype(bf16)], axis=0), both)
                return dq + dot_nn(ds, kv_ref[part, cols])

            dq = lax.fori_loop(0, chunks, second, jnp.zeros((BLOCK, wide), f32))
            outs.append(dq[:, :hd])
        dq_ref[rows, :] = (jnp.concatenate(outs, axis=1) * scale).astype(bf16)

    @pl.when(edge_ref[0] == 1)
    def _():
        edge(0)

    @pl.when(edge_ref[1] == 1)
    def _():
        edge(blocks - 1)

    def put(c, carry):
        part = pl.ds(pl.multiple_of(c * CHUNK, CHUNK), CHUNK)
        dkv_ref[part, :] = acc_ref[part, :].astype(bf16)
        return carry

    lax.fori_loop(0, chunks, put, 0)


SMEM_SPEC = pl.BlockSpec(memory_space=pltpu.SMEM)
VMEM_SPEC = pl.BlockSpec(memory_space=pltpu.VMEM)
VMEM_LIMIT = 48 * 1024 * 1024


def attn_forward(heads, hd, table, edges, q, kv, bias, mask):
    rows, keys = q.shape[0], kv.shape[0]
    return pl.pallas_call(
        functools.partial(attn_fwd_kernel, heads, hd),
        out_shape=(
            jax.ShapeDtypeStruct((rows, heads * hd), bf16),
            jax.ShapeDtypeStruct((rows, 128), f32),
        ),
        in_specs=[SMEM_SPEC] * 2 + [VMEM_SPEC] * 4,
        out_specs=(VMEM_SPEC, VMEM_SPEC),
        scratch_shapes=[pltpu.VMEM((BLOCK, keys), f32)],
        compiler_params=pltpu.CompilerParams(vmem_limit_bytes=VMEM_LIMIT),
        cost_estimate=pl.CostEstimate(
            flops=4 * rows * heads * CHUNK * 2 * hd, bytes_accessed=8 << 20, transcendentals=rows * heads * CHUNK
        ),
        name="attn_forward",
    )(table, edges, q, kv, bias, mask)


def attn_backward(heads, hd, scale, table, edges, qd, kv, bias, mask, lse):
    rows, keys = qd.shape[0], kv.shape[0]
    return pl.pallas_call(
        functools.partial(attn_bwd_kernel, heads, hd, scale),
        out_shape=(
            jax.ShapeDtypeStruct((rows, heads * hd), bf16),
            jax.ShapeDtypeStruct((keys, heads * 2 * hd), bf16),
        ),
        in_specs=[SMEM_SPEC] * 2 + [VMEM_SPEC] * 5,
        out_specs=(VMEM_SPEC, VMEM_SPEC),
        scratch_shapes=[
            pltpu.VMEM((keys, heads * 2 * hd), f32),
            pltpu.VMEM((BLOCK, keys), f32),
            pltpu.VMEM((BLOCK, keys), f32),
        ],
        compiler_params=pltpu.CompilerParams(vmem_limit_bytes=VMEM_LIMIT),
        cost_estimate=pl.CostEstimate(
            flops=10 * rows * heads * CHUNK * 2 * hd, bytes_accessed=12 << 20, transcendentals=rows * heads * CHUNK
        ),
        name="attn_backward",
    )(table, edges, qd, kv, bias, mask, lse)


def general_layer(
    tokens,
    w_qkv,
    bias_qv,
    w_out,
    bias_out,
    gain_one,
    bias_one,
    up_weight,
    up_bias_vector,
    down_weight,
    down_bias_vector,
    gain_two,
    bias_two,
    d_out,
    key_mask,
    rand_idx,
):
    sq = lax.axis_index("sq")
    part = lax.axis_index("part")
    head = lax.axis_index(HEAD)
    parts = lax.axis_size("part")
    groups = lax.axis_size(HEAD)
    span, seqs, width = tokens.shape
    heads, hd = w_qkv.shape[1], w_qkv.shape[3]
    scale = hd ** (-0.5)
    length = key_mask.shape[1]
    blocks_all = length // BLOCK
    per_chunk = groups * span // BLOCK
    mine = seqs * per_chunk

    tok = lax.all_to_all(jnp.transpose(tokens, (1, 0, 2)), "sq", 0, 0, tiled=True)
    x_all = lax.all_gather(tok, PLANE, axis=0, tiled=False)
    d_res = lax.all_to_all(jnp.transpose(d_out, (1, 0, 2)), "sq", 0, 0, tiled=True)

    w_out_full = lax.all_gather(w_out.reshape(heads * hd, width), HEAD, axis=0, tiled=False)
    up_full = lax.all_gather(up_weight, HEAD, axis=0, tiled=False)
    down_full = lax.all_gather(down_weight, HEAD, axis=0, tiled=False)
    up_bias_full = lax.all_gather(up_bias_vector.astype(f32), HEAD, axis=0, tiled=False)

    chunk_ids = jnp.arange(seqs) * parts + part
    block_ids = (chunk_ids[:, None] * per_chunk + jnp.arange(per_chunk)[None, :]).reshape(mine)
    rand_seq = lax.dynamic_index_in_dim(rand_idx, sq, 0, keepdims=False)
    rand_head = lax.dynamic_slice_in_dim(rand_seq, head * heads, heads, 1)
    chosen = jnp.take(rand_head, block_ids, axis=0)
    window = block_ids[:, None] + jnp.arange(-1, 2)[None, :]
    window_ok = (window >= 1) & (window <= blocks_all - 2)
    fixed_ids = jnp.concatenate(
        [
            jnp.clip(window, 0, blocks_all - 1),
            jnp.broadcast_to(jnp.array([0, blocks_all - 1], jnp.int32), (mine, 2)),
        ],
        axis=1,
    )
    fixed_ok = jnp.concatenate([window_ok, jnp.ones((mine, 2), bool)], axis=1)
    table = jnp.concatenate(
        [jnp.broadcast_to(fixed_ids[:, None, :], (mine, heads, 5)), chosen], axis=2
    )
    table_ok = jnp.concatenate(
        [
            jnp.broadcast_to(fixed_ok[:, None, :], (mine, heads, 5)),
            jnp.ones((mine, heads, PICKS - 5), bool),
        ],
        axis=2,
    )
    mask_seq = lax.dynamic_index_in_dim(key_mask, sq, 0, keepdims=False)
    mask_blocks = (mask_seq == 1).reshape(blocks_all, BLOCK).astype(bf16)
    onehot = (table[..., None] == jnp.arange(blocks_all)).astype(bf16) * table_ok[..., None].astype(bf16)
    allowed = jnp.einsum("jhub,bk->jhuk", onehot, mask_blocks, preferred_element_type=f32)
    bias_rows = ((1.0 - allowed) * MASK_FILL).reshape(mine, heads, PICKS * BLOCK)
    mask_row = jnp.where(mask_seq == 1, 0.0, MASK_FILL).astype(f32).reshape(1, length)
    edges = jnp.stack([part == 0, part == parts - 1]).astype(jnp.int32)
    table = table.reshape(-1).astype(jnp.int32)

    w_kv = w_qkv[:, :, 1:].reshape(width, heads * 2 * hd)
    bias_kv = jnp.stack([jnp.zeros((heads, hd), f32), bias_qv[:, 1]], axis=1).reshape(heads * 2 * hd)
    w_q = w_qkv[:, :, 0].reshape(width, heads * hd)
    bias_q = bias_qv[:, 0].reshape(heads * hd)
    x_rows = x_all.reshape(parts, groups, seqs, span, width)
    x_mine = lax.dynamic_index_in_dim(x_rows, part, 0, keepdims=False)
    kv_rows = (jnp.einsum("pgzsd,dc->pgzsc", x_rows, w_kv, preferred_element_type=f32) + bias_kv).astype(bf16)
    kv = jnp.transpose(kv_rows, (2, 0, 1, 3, 4)).reshape(length, heads * 2 * hd)
    q_rows = (jnp.einsum("gzsd,dc->gzsc", x_mine, w_q, preferred_element_type=f32) + bias_q).astype(bf16)
    q_low = jnp.transpose(q_rows, (1, 0, 2, 3)).reshape(mine * BLOCK, heads, hd) * bf16(scale)
    q_pad = jnp.concatenate([q_low, jnp.zeros_like(q_low)], axis=-1).reshape(mine * BLOCK, heads * 2 * hd)

    attn_mine, lse = attn_forward(heads, hd, table, edges, q_pad, kv, bias_rows, mask_row)
    attn_send = jnp.transpose(attn_mine.reshape(seqs, groups, span, heads * hd), (1, 0, 2, 3))
    attn = lax.all_to_all(attn_send, HEAD, 0, 0, tiled=True).reshape(groups, seqs * span, heads * hd)

    rows = seqs * span
    tok_rows = tok.reshape(rows, width)
    branch = jnp.einsum("grc,gcd->rd", attn, w_out_full, preferred_element_type=f32) + bias_out
    y_one, normed_one, inv_one = norm_fwd(tok_rows.astype(f32) + branch, gain_one, bias_one)
    y_low = y_one.astype(bf16)
    pre = jnp.einsum("rd,gdf->grf", y_low, up_full, preferred_element_type=f32) + up_bias_full[:, None, :]
    hidden = tanh_gelu(pre).astype(bf16)
    ffn = jnp.einsum("grf,gfd->rd", hidden, down_full, preferred_element_type=f32) + down_bias_vector
    result, normed_two, inv_two = norm_fwd(y_one + ffn, gain_two, bias_two)
    result = lax.all_to_all(result.astype(bf16).reshape(seqs, span, width), "sq", 0, 0, tiled=True)
    d_two, grad_gain_two, grad_bias_two = norm_back(
        d_res.reshape(rows, width).astype(f32), normed_two, inv_two, gain_two
    )
    d_ffn = d_two.astype(bf16)
    grad_bias_back = jnp.sum(d_ffn.astype(f32), axis=0)
    d_hidden = jnp.einsum("rd,gfd->grf", d_ffn, down_full, preferred_element_type=f32)
    d_pre = gelu_back(pre, d_hidden).astype(bf16)
    d_y_ffn = jnp.einsum("grf,gdf->rd", d_pre, up_full, preferred_element_type=f32)
    grad_w_in = jnp.einsum("rd,grf->gdf", y_low, d_pre, preferred_element_type=f32).astype(bf16)
    grad_bias_in = jnp.sum(d_pre.astype(f32), axis=1)
    grad_w_back = jnp.einsum("grf,rd->gfd", hidden, d_ffn, preferred_element_type=f32).astype(bf16)
    d_one, grad_gain_one, grad_bias_one = norm_back(d_two + d_y_ffn, normed_one, inv_one, gain_one)
    d_branch = d_one.astype(bf16)
    grad_bias_out = jnp.sum(d_branch.astype(f32), axis=0)
    d_attn = jnp.einsum("rd,gcd->grc", d_branch, w_out_full, preferred_element_type=f32).astype(bf16)
    grad_w_out = jnp.einsum("grc,rd->gcd", attn, d_branch, preferred_element_type=f32).astype(bf16)

    d_attn_mine = lax.all_to_all(d_attn.reshape(groups, seqs, span, heads * hd), HEAD, 0, 0, tiled=True)
    d_attn_nat = jnp.transpose(d_attn_mine, (1, 0, 2, 3)).reshape(mine * BLOCK, heads, hd)
    qd = jnp.concatenate([q_low, d_attn_nat], axis=-1).reshape(mine * BLOCK, heads * 2 * hd)

    wide_part = jnp.concatenate([grad_w_in, grad_w_back, grad_w_out], axis=1)
    wide_sum = lax.psum_scatter(wide_part, HEAD, scatter_dimension=0, tiled=True)[0]
    wide_sum = lax.psum(wide_sum, SEQ)

    dq, dkv = attn_backward(heads, hd, scale, table, edges, qd, kv, bias_rows, mask_row, lse)
    dkv_rows = jnp.transpose(
        dkv.reshape(seqs, parts, groups, span, heads * 2 * hd), (1, 2, 0, 3, 4)
    )
    dq_rows = jnp.transpose(dq.reshape(seqs, groups, span, heads * hd), (1, 0, 2, 3))
    dq_all = lax.dynamic_update_index_in_dim(
        jnp.zeros((parts, groups, seqs, span, heads * hd), bf16), dq_rows, part, 0
    )
    d_x = jnp.einsum("pgzsc,dc->pgzsd", dkv_rows, w_kv, preferred_element_type=f32) + jnp.einsum(
        "pgzsc,dc->pgzsd", dq_all, w_q, preferred_element_type=f32
    )
    d_x = lax.psum_scatter(
        d_x.astype(bf16).reshape(parts * groups, seqs, span, width), PLANE, scatter_dimension=0, tiled=True
    )
    d_tok = (d_one + d_x.reshape(rows, width).astype(f32)).astype(bf16)
    d_tok = lax.all_to_all(d_tok.reshape(seqs, span, width), "sq", 0, 0, tiled=True)

    grad_kv = jnp.einsum("pgzsd,pgzsc->dc", x_rows, dkv_rows, preferred_element_type=f32)
    grad_q = jnp.einsum("gzsd,gzsc->dc", x_mine, dq_rows, preferred_element_type=f32)
    grad_w_qkv = jnp.concatenate(
        [grad_q.reshape(width, heads, 1, hd), grad_kv.reshape(width, heads, 2, hd)], axis=2
    )
    bias_q_sum = jnp.sum(dq_rows.astype(f32), axis=(0, 1, 2)).reshape(heads, 1, hd)
    bias_v_sum = jnp.sum(dkv_rows.astype(f32), axis=(0, 1, 2, 3)).reshape(heads, 2, hd)[:, 1:]
    grad_bias_qv = jnp.concatenate([bias_q_sum, bias_v_sum], axis=1)
    grad_w_qkv = lax.psum(grad_w_qkv.astype(bf16), SEQ).astype(f32)

    small = jnp.stack(
        [grad_bias_out, grad_gain_one, grad_bias_one, grad_bias_back, grad_gain_two, grad_bias_two]
    )
    all_bias_in = grad_bias_in
    bias_qv_all = lax.dynamic_update_index_in_dim(
        jnp.zeros((groups, heads * 2 * hd), f32), grad_bias_qv.reshape(-1), head, 0
    )
    packed = jnp.concatenate([small.reshape(-1), all_bias_in.reshape(-1), bias_qv_all.reshape(-1)])
    packed = lax.psum(packed, ("sq", "part", "hy", "hc"))
    n_small = 6 * width
    small = packed[:n_small].reshape(6, width)
    n_in = n_small + all_bias_in.size
    hidden_dev = up_weight.shape[1]
    grad_bias_in = lax.dynamic_slice_in_dim(packed[n_small:n_in], head * hidden_dev, hidden_dev, 0)
    grad_bias_qv = lax.dynamic_slice_in_dim(
        packed[n_in:], head * heads * 2 * hd, heads * 2 * hd, 0
    ).reshape(heads, 2, hd)

    wide_sum = wide_sum.astype(f32)
    grad_w_in = wide_sum[:width]
    grad_w_back = wide_sum[width : width + hidden_dev]
    grad_w_out = wide_sum[width + hidden_dev :].reshape(heads, hd, width)
    return (
        jnp.transpose(result, (1, 0, 2)),
        jnp.transpose(d_tok, (1, 0, 2)),
        grad_w_qkv,
        grad_bias_qv,
        grad_w_out,
        small[0],
        small[1],
        small[2],
        grad_w_in,
        grad_bias_in,
        grad_w_back,
        small[3],
        small[4],
        small[5],
    )


def swap(value, axis, step=1, name="swap"):
    size = lax.axis_size(axis)
    with jax.named_scope(name + "_" + axis + str(step)):
        return lax.ppermute(value, axis, [(i, i ^ step) for i in range(size)])


def flipped(value, bit, axis):
    return jnp.where(bit == 1, jnp.flip(value, axis), value)


def relative(value, place):
    shape = value.shape
    value = value.reshape((2, 2) + shape[1:])
    value = flipped(flipped(value, place // 2, 0), place % 2, 1)
    return value.reshape(shape)


ANY_SPEC = pl.BlockSpec(memory_space=pl.ANY)


def after(value, *orders):
    return pl.pallas_call(
        lambda *refs: None,
        out_shape=jax.ShapeDtypeStruct(value.shape, value.dtype),
        in_specs=[ANY_SPEC] * (1 + len(orders)),
        out_specs=ANY_SPEC,
        input_output_aliases={0: 0},
        name="after",
    )(value, *orders)


def params(limit_mb):
    return pltpu.CompilerParams(vmem_limit_bytes=limit_mb * 1024 * 1024)


def fill_tables(coord_ref, rand_ref, place_ref, nat_ref, heads, span):
    per_span = span // BLOCK

    def one(b, carry):
        own = b // per_span
        kz = (own // 8) ^ coord_ref[0]
        kx = (own // 4 % 2) ^ coord_ref[1]
        ky = (own // 2 % 2) ^ coord_ref[2]
        kc = (own % 2) ^ coord_ref[3]
        odd = kz % 2
        one, two = jnp.where(odd == 0, kx, ky), jnp.where(odd == 0, ky, kx)
        spot = ((((odd * 2 + kc) * 2 + two) * 2 + one) * 2 + kz // 2) * per_span + b % per_span
        place_ref[b] = spot
        nat_ref[spot] = b
        return carry

    lax.fori_loop(0, place_ref.shape[0], one, 0)


def natural_block(coord_ref, jl, per_span):
    kz = (jl // per_span % 2 * 2 + jl // (per_span * 2) % 2) ^ coord_ref[0]
    kc = jl // (per_span * 4) % 2 ^ coord_ref[3]
    ky = jl // (per_span * 8) ^ coord_ref[2]
    return (((kz * 2 + coord_ref[1]) * 2 + ky) * 2 + kc) * per_span + jl % per_span


def edge_of(coord_ref, blocks, per_span):
    last = coord_ref[1]
    kz = (last * 3) ^ coord_ref[0]
    ky = last ^ coord_ref[2]
    kc = last ^ coord_ref[3]
    return ((ky * 2 + kc) * 4 + kz % 2 * 2 + kz // 2) * per_span + last * (per_span - 1)


def picks_of(coord_ref, rand_ref, jl, h, heads, per_span, blocks_all):
    b = natural_block(coord_ref, jl, per_span)
    inner = (b > 0) & (b < blocks_all - 1)
    ids, rows = [], []
    for u in range(3):
        key = b + u - 1
        ids.append(jnp.clip(key, 0, blocks_all - 1))
        rows.append(jnp.where(inner & (key >= 1) & (key <= blocks_all - 2), key, blocks_all))
    for key in (0, blocks_all - 1):
        ids.append(key)
        rows.append(jnp.where(inner, key, blocks_all))
    for u in range(3):
        key = rand_ref[(b * heads + h) * 3 + u]
        ids.append(key)
        rows.append(jnp.where(inner, key, blocks_all))
    return ids, rows


def mask_of(mask_ref, rows, left):
    pairs = []
    for u in range(0, len(rows), 2):
        a, b = mask_ref[pl.ds(rows[u], 1), :], mask_ref[pl.ds(rows[u + 1], 1), :]
        pairs.append(jnp.where(left, a, b))
    return jnp.concatenate(pairs, axis=1)


def blocks_of(kv_ref, place_ref, ids, cols):
    return jnp.concatenate(
        [kv_ref[pl.ds(pl.multiple_of(place_ref[b] * BLOCK, BLOCK), BLOCK), cols] for b in ids], axis=0
    )


def query_pieces(pair):
    out = []
    for ky in range(2):
        for kc in range(2):
            at = (ky * 2 + kc) * 2 * pair
            out.append((at, kc * 2 + ky, 0))
            out.append((at + pair, 4 + kc * 2, ky * pair))
    return out


def project_and_attend_kernel(heads, hd, span, n_orders, coord_ref, rand_ref, *refs):
    x_refs = refs[:8]
    w_kv_ref, w_q_ref, b_kv_ref, b_q_ref, mask_ref = refs[8:13]
    refs = refs[13 + n_orders :]
    o_refs, (lse_ref, kv_ref, q_ref, s_ref, place_ref, nat_ref) = refs[:2], refs[2:]
    near = o_refs[0].shape[0] // BLOCK
    wide = 2 * hd
    piece, pair = 4 * span, 2 * span
    per_span = span // BLOCK
    blocks = q_ref.shape[0] // BLOCK
    blocks_all = kv_ref.shape[0] // BLOCK
    chunks = kv_ref.shape[0] // CHUNK
    lanes = lax.broadcasted_iota(jnp.int32, (BLOCK, 128), 1)
    left = lax.broadcasted_iota(jnp.int32, (1, 128), 1) < BLOCK
    fill_tables(coord_ref, rand_ref, place_ref, nat_ref, heads, span)

    for n, x_ref in enumerate(x_refs):
        kv_ref[n * piece : (n + 1) * piece, :] = (dot_nn(x_ref[...], w_kv_ref[...]) + b_kv_ref[...]).astype(bf16)
    for at, n, src in query_pieces(pair):
        x = x_refs[n][src : src + pair, :]
        q_ref[at : at + pair, :] = (dot_nn(x, w_q_ref[...]) + b_q_ref[...]).astype(bf16) * bf16(hd**-0.5)

    def finish(jl, accs, tops, totals):
        lse_tile = jnp.zeros((BLOCK, 128), f32)
        for h in range(heads):
            lse_tile = jnp.where(lanes == h, tops[h] + jnp.log(totals[h]), lse_tile)
        lse_ref[pl.ds(pl.multiple_of(jl * BLOCK, BLOCK), BLOCK), :] = lse_tile
        return jnp.concatenate([accs[h][:, hd:] * (1.0 / totals[h]) for h in range(heads)], axis=1).astype(bf16)

    def put(o_ref, jl, value):
        o_ref[pl.ds(pl.multiple_of(jl * BLOCK, BLOCK), BLOCK), :] = value

    unroll = 4

    def some(half, it, carry):
        items = [(half * near + it * unroll + u, h) for u in range(unroll) for h in range(heads)]
        scores, kvs = [], []
        for jl, h in items:
            rows = pl.ds(pl.multiple_of(jl * BLOCK, BLOCK), BLOCK)
            cols = slice(h * wide, (h + 1) * wide)
            ids, mask_rows = picks_of(coord_ref, rand_ref, jl, h, heads, per_span, blocks_all)
            kvg = blocks_of(kv_ref, place_ref, ids, cols)
            scores.append(dot_nt(q_ref[rows, cols], kvg) + mask_of(mask_ref, mask_rows, left))
            kvs.append(kvg)
        lows, tops, totals = [], [], []
        for s in scores:
            top = jnp.max(s, axis=1, keepdims=True)
            p = jnp.exp(s - top)
            totals.append(jnp.sum(p, axis=1, keepdims=True))
            tops.append(top)
            lows.append(p.astype(bf16))
        accs = [dot_nn(p, kvg) for p, kvg in zip(lows, kvs)]
        for u in range(unroll):
            of = slice(u * heads, (u + 1) * heads)
            jl = it * unroll + u
            put(o_refs[half], jl, finish(half * near + jl, accs[of], tops[of], totals[of]))
        return carry

    for half in range(2):
        lax.fori_loop(0, near // unroll, functools.partial(some, half), 0)

    edge = edge_of(coord_ref, blocks, per_span)
    rows = pl.ds(pl.multiple_of(edge * BLOCK, BLOCK), BLOCK)
    head_cols = [slice(h * wide, (h + 1) * wide) for h in range(heads)]
    qs = [q_ref[rows, cols] for cols in head_cols]

    def score(c, tops):
        part = pl.ds(pl.multiple_of(c * CHUNK, CHUNK), CHUNK)
        mask = mask_of(mask_ref, [nat_ref[c * PICKS + u] for u in range(PICKS)], left)
        ss = [dot_nt(qs[h], kv_ref[part, head_cols[h]]) + mask for h in range(heads)]
        for h in range(heads):
            s_ref[h, :, part] = ss[h]
        return tuple(jnp.maximum(tops[h], ss[h]) for h in range(heads))

    tops = lax.fori_loop(0, chunks, score, tuple(jnp.full((BLOCK, CHUNK), -3e38, f32) for _ in range(heads)))
    tops = [jnp.max(t, axis=1, keepdims=True) for t in tops]

    def out(c, carry):
        accs, sums = carry
        part = pl.ds(pl.multiple_of(c * CHUNK, CHUNK), CHUNK)
        ps = [jnp.exp(s_ref[h, :, part] - tops[h]) for h in range(heads)]
        accs = tuple(accs[h] + dot_nn(ps[h].astype(bf16), kv_ref[part, head_cols[h]]) for h in range(heads))
        sums = tuple(sums[h] + ps[h] for h in range(heads))
        return accs, sums

    accs, sums = lax.fori_loop(
        0,
        chunks,
        out,
        (
            tuple(jnp.zeros((BLOCK, wide), f32) for _ in range(heads)),
            tuple(jnp.zeros((BLOCK, CHUNK), f32) for _ in range(heads)),
        ),
    )
    value = finish(edge, accs, tops, [jnp.sum(t, axis=1, keepdims=True) for t in sums])

    @pl.when(edge < near)
    def _():
        put(o_refs[0], edge, value)

    @pl.when(edge >= near)
    def _():
        put(o_refs[1], edge - near, value)


def project_and_attend(heads, hd, span, coords, rand, xs, w_kv, w_q, b_kv, b_q, mask, orders):
    keys = 8 * xs[0].shape[0]
    rows = keys // 2
    cols = heads * 2 * hd
    return pl.pallas_call(
        functools.partial(project_and_attend_kernel, heads, hd, span, len(orders)),
        out_shape=(
            jax.ShapeDtypeStruct((rows // 2, heads * hd), bf16),
            jax.ShapeDtypeStruct((rows // 2, heads * hd), bf16),
            jax.ShapeDtypeStruct((rows, 128), f32),
            jax.ShapeDtypeStruct((keys, cols), bf16),
            jax.ShapeDtypeStruct((rows, cols), bf16),
        ),
        in_specs=[SMEM_SPEC] * 2 + [VMEM_SPEC] * 13 + [ANY_SPEC] * len(orders),
        out_specs=(VMEM_SPEC,) * 5,
        scratch_shapes=[
            pltpu.VMEM((heads, BLOCK, keys), f32),
            pltpu.SMEM((keys // BLOCK,), jnp.int32),
            pltpu.SMEM((keys // BLOCK,), jnp.int32),
        ],
        compiler_params=params(58),
        cost_estimate=pl.CostEstimate(
            flops=40 << 30, bytes_accessed=16 << 20, transcendentals=rows * heads * CHUNK
        ),
        name="project_and_attend",
    )(coords, rand, *xs, w_kv, w_q, b_kv, b_q, mask, *orders)


def attend_back_kernel(heads, hd, span, n_orders, coord_ref, rand_ref, q_ref, *refs):
    do_parts, o_parts = refs[:4], refs[4:6]
    kv_ref, mask_ref, lse_ref, w_kv_ref, w_q_ref = refs[6:11]
    dq_ref, dkv_ref, near_ref, far_ref, acc_ref, do_ref, o_ref, place_ref, nat_ref = refs[11 + n_orders :]
    own = do_parts[0].shape[0]
    for k, ref in enumerate(do_parts):
        do_ref[k * own : (k + 1) * own, :] = ref[0] if len(ref.shape) == 3 else ref[...]
    for k, ref in enumerate(o_parts):
        o_ref[k * 2 * own : (k + 1) * 2 * own, :] = ref[...]
    wide = 2 * hd
    piece = 4 * span
    per_span = span // BLOCK
    scale = hd**-0.5
    blocks = q_ref.shape[0] // BLOCK
    blocks_all = kv_ref.shape[0] // BLOCK
    chunks = kv_ref.shape[0] // CHUNK
    head_cols = [slice(h * wide, (h + 1) * wide) for h in range(heads)]
    nil = jnp.zeros((BLOCK, hd), bf16)
    left = lax.broadcasted_iota(jnp.int32, (1, 128), 1) < BLOCK
    fill_tables(coord_ref, rand_ref, place_ref, nat_ref, heads, span)

    def clear(c, carry):
        part = pl.ds(pl.multiple_of(c * CHUNK, CHUNK), CHUNK)
        acc_ref[part, :] = jnp.zeros((CHUNK, heads * wide), f32)
        return carry

    lax.fori_loop(0, chunks, clear, 0)

    def of_rows(rows):
        d_o = do_ref[rows, :]
        prod = d_o.astype(f32) * o_ref[rows, :].astype(f32)
        lse = lse_ref[rows, :]
        boths, dots, lses = [], [], []
        for h in range(heads):
            low = jnp.concatenate([nil, d_o[:, h * hd : (h + 1) * hd]], axis=1)
            boths.append(jnp.concatenate([q_ref[rows, head_cols[h]], low], axis=0))
            dots.append(jnp.sum(prod[:, h * hd : (h + 1) * hd], axis=1, keepdims=True))
            lses.append(lse[:, h : h + 1])
        return boths, dots, lses

    unroll = 2

    def some(it, carry):
        items, boths, dots, lses = [], [], [], []
        for u in range(unroll):
            jl = it * unroll + u
            rows = pl.ds(pl.multiple_of(jl * BLOCK, BLOCK), BLOCK)
            b, d, e = of_rows(rows)
            boths, dots, lses = boths + b, dots + d, lses + e
            items += [(jl, h) for h in range(heads)]
        kvs, prods, picks, masks = [], [], [], []
        for i, (jl, h) in enumerate(items):
            ids, mask_rows = picks_of(coord_ref, rand_ref, jl, h, heads, per_span, blocks_all)
            kvg = blocks_of(kv_ref, place_ref, ids, head_cols[h])
            prods.append(dot_nt(boths[i], kvg))
            masks.append(mask_of(mask_ref, mask_rows, left))
            kvs.append(kvg)
            picks.append(ids)
        dss, lows = [], []
        for i, (jl, h) in enumerate(items):
            p = jnp.exp(prods[i][:BLOCK] + masks[i] - lses[i])
            dss.append((p * (prods[i][BLOCK:] - dots[i])).astype(bf16))
            lows.append(p.astype(bf16))
        dqs = [dot_nn(ds, kvg)[:, :hd] for ds, kvg in zip(dss, kvs)]
        dkvs = [dot_tn(jnp.concatenate([ds, p], axis=0), both) for ds, p, both in zip(dss, lows, boths)]
        for i, (jl, h) in enumerate(items):
            for u in range(PICKS):
                place = pl.ds(pl.multiple_of(place_ref[picks[i][u]] * BLOCK, BLOCK), BLOCK)
                acc_ref[place, head_cols[h]] += dkvs[i][u * BLOCK : (u + 1) * BLOCK]
        for u in range(unroll):
            rows = pl.ds(pl.multiple_of((it * unroll + u) * BLOCK, BLOCK), BLOCK)
            dq_ref[rows, :] = (jnp.concatenate(dqs[u * heads : (u + 1) * heads], axis=1) * scale).astype(bf16)
        return carry

    lax.fori_loop(0, blocks // unroll, some, 0)

    rows = pl.ds(pl.multiple_of(edge_of(coord_ref, blocks, per_span) * BLOCK, BLOCK), BLOCK)
    boths, dots, lses = of_rows(rows)

    def edge(c, dqs):
        part = pl.ds(pl.multiple_of(c * CHUNK, CHUNK), CHUNK)
        mask = mask_of(mask_ref, [nat_ref[c * PICKS + u] for u in range(PICKS)], left)
        kvs = [kv_ref[part, cols] for cols in head_cols]
        prods = [dot_nt(boths[h], kvs[h]) for h in range(heads)]
        dss, lows = [], []
        for h in range(heads):
            p = jnp.exp(prods[h][:BLOCK] + mask - lses[h])
            dss.append((p * (prods[h][BLOCK:] - dots[h])).astype(bf16))
            lows.append(p.astype(bf16))
        new = tuple(dqs[h] + dot_nn(dss[h], kvs[h]) for h in range(heads))
        dkvs = [dot_tn(jnp.concatenate([dss[h], lows[h]], axis=0), boths[h]) for h in range(heads)]
        for h in range(heads):
            acc_ref[part, head_cols[h]] += dkvs[h]
        return new

    dqs = lax.fori_loop(0, chunks, edge, tuple(jnp.zeros((BLOCK, wide), f32) for _ in range(heads)))
    dq_ref[rows, :] = (jnp.concatenate([dq[:, :hd] for dq in dqs], axis=1) * scale).astype(bf16)

    pair = 2 * span
    mine = {(n, src): at for at, n, src in query_pieces(pair)}
    for n in range(8):
        kc = n // 2 % 2
        to = n % 2 * piece
        of = slice(n * piece, (n + 1) * piece)
        dkv = acc_ref[of, :].astype(bf16)
        dkv_ref[of, :] = dkv
        dx = dot_nt(dkv, w_kv_ref[...])
        for src in (0, pair):
            part = dx[src : src + pair]
            if (n, src) in mine:
                at = mine[n, src]
                part = part + dot_nt(dq_ref[at : at + pair, :], w_q_ref[...])
            (far_ref if kc else near_ref)[n // 4, to + src : to + src + pair, :] = part.astype(bf16)


def attend_back(heads, hd, span, coords, rand, q, d_os, os, kv, mask, lse, w_kv, w_q, orders):
    rows, keys = q.shape[0], kv.shape[0]
    width = w_kv.shape[0]
    piece = 4 * span
    return pl.pallas_call(
        functools.partial(attend_back_kernel, heads, hd, span, len(orders)),
        out_shape=(
            jax.ShapeDtypeStruct((rows, heads * hd), bf16),
            jax.ShapeDtypeStruct((keys, heads * 2 * hd), bf16),
        )
        + (jax.ShapeDtypeStruct((2, 2 * piece, width), bf16),) * 2,
        in_specs=[SMEM_SPEC] * 2 + [VMEM_SPEC] * 12 + [ANY_SPEC] * len(orders),
        out_specs=(VMEM_SPEC,) * 4,
        scratch_shapes=[
            pltpu.VMEM((keys, heads * 2 * hd), f32),
            pltpu.VMEM((rows, heads * hd), bf16),
            pltpu.VMEM((rows, heads * hd), bf16),
            pltpu.SMEM((keys // BLOCK,), jnp.int32),
            pltpu.SMEM((keys // BLOCK,), jnp.int32),
        ],
        compiler_params=params(58),
        cost_estimate=pl.CostEstimate(
            flops=60 << 30, bytes_accessed=24 << 20, transcendentals=rows * heads * CHUNK
        ),
        name="attend_back",
    )(coords, rand, q, *d_os, *os, kv, mask, lse, w_kv, w_q, *orders)


def split_low(value):
    top = value.astype(bf16)
    return jnp.concatenate([top, (value - top.astype(f32)).astype(bf16)], axis=0)


def joined(low):
    return low[:8].astype(f32) + low[8:16].astype(f32)


def qkv_grad_kernel(span, spot_ref, dq_ref, dkv_ref, keep_ref, got_ref, small_ref, *refs):
    x_refs, out_ref = refs[:8], refs[-1]
    piece = 4 * span
    n_kv = dkv_ref.shape[1]
    n_q = dq_ref.shape[1]
    rows, width = out_ref.shape[1], x_refs[0].shape[1]
    acc = jnp.zeros((n_kv, width), f32)
    acc_q = jnp.zeros((n_q, width), f32)
    for n, x_ref in enumerate(x_refs):
        acc = acc + dot_tn(dkv_ref[n * piece : (n + 1) * piece, :], x_ref[...])
    pair = 2 * span
    for at, n, src in query_pieces(pair):
        acc_q = acc_q + dot_tn(dq_ref[at : at + pair, :], x_refs[n][src : src + pair, :])
    out_ref[...] = jnp.zeros_like(out_ref)
    both = jnp.concatenate([acc, acc_q], axis=0)
    octets = [both[o * rows : (o + 1) * rows] for o in range(6)]
    w_out = keep_ref[keep_ref.shape[0] - 1].astype(f32) + got_ref[got_ref.shape[0] - 1].astype(f32)
    octets += [w_out[:, :width], w_out[:, width:]]
    sums = jnp.concatenate(
        [
            jnp.sum(dq_ref[...].astype(f32), axis=0, keepdims=True),
            jnp.sum(dkv_ref[...].astype(f32), axis=0, keepdims=True),
            jnp.zeros((1, 1024 - n_q - n_kv), f32),
        ],
        axis=1,
    )
    sums = jnp.concatenate([sums[:, i * 128 : (i + 1) * 128] for i in range(8)], axis=0)
    for o in range(8):
        spot = spot_ref[o]
        out_ref[spot, :, :width] = octets[o].astype(bf16)
        out_ref[spot, :16, width:] = split_low(small_ref[o] if o < 7 else sums)


def qkv_grad(span, spots, dq, dkv, keep, got, small, xs, orders):
    width = xs[0].shape[1]
    rows = (dq.shape[1] + dkv.shape[1]) // 6
    return pl.pallas_call(
        functools.partial(qkv_grad_kernel, span),
        out_shape=jax.ShapeDtypeStruct((8, rows, width + 128), bf16),
        in_specs=[SMEM_SPEC] + [VMEM_SPEC] * 13 + [ANY_SPEC] * len(orders),
        out_specs=VMEM_SPEC,
        compiler_params=params(48),
        cost_estimate=pl.CostEstimate(
            flops=14 << 30, bytes_accessed=12 << 20, transcendentals=0
        ),
        name="qkv_grad",
    )(spots, dq, dkv, keep, got, small, *xs, *orders)


def wide_sum_kernel(order_ref, keep_ref, y_ref, x_ref, out_ref):
    out_ref[...] = (keep_ref[...].astype(f32) + y_ref[...].astype(f32) + x_ref[...].astype(f32)).astype(bf16)


def wide_sum(order, keep, y_got, x_got):
    _, rows, cols = keep.shape
    octet = pl.BlockSpec((1, rows, cols), lambda i, order_ref: (i, 0, 0))
    return pl.pallas_call(
        wide_sum_kernel,
        grid_spec=pltpu.PrefetchScalarGridSpec(
            num_scalar_prefetch=1,
            grid=(4,),
            in_specs=[octet] * 3,
            out_specs=pl.BlockSpec((1, rows, cols), lambda i, order_ref: (order_ref[i], 0, 0)),
        ),
        out_shape=jax.ShapeDtypeStruct((4, rows, cols), bf16),
        compiler_params=params(58),
        cost_estimate=pl.CostEstimate(flops=1 << 28, bytes_accessed=6 << 20, transcendentals=0),
        name="wide_sum",
    )(order, keep, y_got, x_got)


def tail_sum_kernel(n_orders, tail_ref, got_ref, *refs):
    out_refs = refs[n_orders:]
    thin = tail_ref.shape[2] - 128
    for k in range(4):
        out_refs[k][:, :thin] = (tail_ref[k, :, :thin].astype(f32) + got_ref[k, :, :thin].astype(f32)).astype(bf16)
        out_refs[k][:, thin:] = jnp.zeros((tail_ref.shape[1], 128), bf16)
        out_refs[k][:16, thin:] = split_low(joined(tail_ref[k, :16, thin:]) + joined(got_ref[k, :16, thin:]))


def tail_sum(tail, tail_got, orders):
    _, rows, cols = tail.shape
    return pl.pallas_call(
        functools.partial(tail_sum_kernel, len(orders)),
        out_shape=(jax.ShapeDtypeStruct((rows, cols), bf16),) * 4,
        in_specs=[VMEM_SPEC] * 2 + [ANY_SPEC] * len(orders),
        out_specs=(VMEM_SPEC,) * 4,
        compiler_params=params(58),
        cost_estimate=pl.CostEstimate(flops=1 << 28, bytes_accessed=2 << 20, transcendentals=0),
        name="tail_sum",
    )(tail, tail_got, *orders)


def wide_end_kernel(wide_ref, top_ref, low_ref, out_ref):
    half = top_ref.shape[0]
    for i, more_ref in enumerate((top_ref, low_ref)):
        of = slice(i * half, (i + 1) * half)
        out_ref[of, :] = (wide_ref[of, :].astype(f32) + more_ref[...].astype(f32)).astype(bf16)


def wide_end(wide, top, low):
    return pl.pallas_call(
        wide_end_kernel,
        out_shape=jax.ShapeDtypeStruct(wide.shape, bf16),
        in_specs=[VMEM_SPEC] * 3,
        out_specs=VMEM_SPEC,
        compiler_params=params(58),
        cost_estimate=pl.CostEstimate(flops=1 << 28, bytes_accessed=3 << 20, transcendentals=0),
        name="wide_end",
    )(wide, top, low)


def tail_end_kernel(*refs):
    thin_refs, out_ref = refs[:4], refs[-1]
    thin = out_ref.shape[1] - 128
    out_ref[:, :thin] = sum(r[:, :thin].astype(f32) for r in thin_refs).astype(bf16)
    out_ref[:, thin:] = jnp.zeros((out_ref.shape[0], 128), bf16)
    out_ref[:16, thin:] = split_low(sum(joined(r[:16, thin:]) for r in thin_refs))


def tail_end(thins, orders):
    return pl.pallas_call(
        tail_end_kernel,
        out_shape=jax.ShapeDtypeStruct(thins[0].shape, bf16),
        in_specs=[VMEM_SPEC] * 4 + [ANY_SPEC] * len(orders),
        out_specs=VMEM_SPEC,
        compiler_params=params(58),
        cost_estimate=pl.CostEstimate(flops=1 << 28, bytes_accessed=3 << 20, transcendentals=0),
        name="tail_end",
    )(*thins, *orders)


def tail_place_kernel(spot_ref, *refs):
    ins, out_ref, small_ref = refs[:8], refs[8], refs[9]
    rows = ins[0].shape[0]
    cols = out_ref.shape[1]
    for n in range(8):
        spot = spot_ref[n]
        out_ref[pl.ds(pl.multiple_of(spot * rows, 16), rows), :] = ins[n][:, :cols]
        small_ref[spot] = joined(ins[n][:16, cols:])


def tail_place(spots, parts):
    rows, cols = parts[0].shape
    return pl.pallas_call(
        tail_place_kernel,
        out_shape=(
            jax.ShapeDtypeStruct((8 * rows, cols - 128), bf16),
            jax.ShapeDtypeStruct((8, 8, 128), f32),
        ),
        in_specs=[SMEM_SPEC] + [VMEM_SPEC] * 8,
        out_specs=(VMEM_SPEC,) * 2,
        compiler_params=params(58),
        cost_estimate=pl.CostEstimate(flops=1 << 28, bytes_accessed=3 << 20, transcendentals=0),
        name="tail_place",
    )(spots, *parts)


def across_sum_kernel(a_ref, b_ref, c_ref, d_ref, top_ref, low_ref):
    half = top_ref.shape[0]
    for i, out in enumerate((top_ref, low_ref)):
        of = slice(i * half, (i + 1) * half)
        out[...] = sum(r[of, :].astype(f32) for r in (a_ref, b_ref, c_ref, d_ref)).astype(bf16)


def across_sum(parts):
    rows, cols = parts[0].shape
    return pl.pallas_call(
        across_sum_kernel,
        out_shape=(jax.ShapeDtypeStruct((rows // 2, cols), bf16),) * 2,
        in_specs=[VMEM_SPEC] * 4,
        out_specs=(VMEM_SPEC,) * 2,
        compiler_params=params(58),
        cost_estimate=pl.CostEstimate(flops=1 << 24, bytes_accessed=1 << 20, transcendentals=0),
        name="across_sum",
    )(*parts)


def split_kernel(n_orders, coord_ref, rows_ref, *refs):
    value = rows_ref[...].astype(f32)
    pieces = [value[:, s, :] for s in range(4)]
    z = coord_ref[0]
    for k, out in enumerate(refs[n_orders:]):
        low = jnp.where((z ^ k) % 2 == 0, pieces[0], pieces[1])
        high = jnp.where((z ^ k) % 2 == 0, pieces[2], pieces[3])
        out[...] = jnp.where((z ^ k) // 2 == 0, low, high).astype(bf16)


def split(coords, rows, orders=()):
    span, seqs, width = rows.shape
    return pl.pallas_call(
        functools.partial(split_kernel, len(orders)),
        out_shape=(jax.ShapeDtypeStruct((span, width), bf16),) * seqs,
        in_specs=[SMEM_SPEC, VMEM_SPEC] + [ANY_SPEC] * len(orders),
        out_specs=(VMEM_SPEC,) * seqs,
        compiler_params=params(32),
        cost_estimate=pl.CostEstimate(flops=1 << 20, bytes_accessed=1 << 20, transcendentals=0),
        name="split",
    )(coords, rows, *orders)


def qkv_weights_kernel(n_orders, w_ref, b_ref, *refs):
    kv_ref, q_pad_ref, q_ref, b_kv_ref, b_q_ref = refs[n_orders:]
    width, heads, _, hd = w_ref.shape
    wide = 2 * hd
    value = w_ref[...].astype(f32)
    nil = jnp.zeros((width, hd), f32)
    qs = []
    for h in range(heads):
        q, k, v = [value[:, h, c, :] for c in range(3)]
        cols = slice(h * wide, (h + 1) * wide)
        kv_ref[:, cols] = jnp.concatenate([k, v], axis=1).astype(bf16)
        q_pad_ref[:, cols] = jnp.concatenate([q, nil], axis=1).astype(bf16)
        b_kv_ref[:, cols] = jnp.concatenate([nil[:1], b_ref[h, 1:2, :]], axis=1)
        b_q_ref[:, cols] = jnp.concatenate([b_ref[h, 0:1, :], nil[:1]], axis=1)
        qs.append(q)
    q_ref[...] = jnp.concatenate(qs, axis=1).astype(bf16)


def qkv_weights(w_qkv, bias_qv, orders):
    width, heads, _, hd = w_qkv.shape
    cols = heads * 2 * hd
    return pl.pallas_call(
        functools.partial(qkv_weights_kernel, len(orders)),
        out_shape=(
            jax.ShapeDtypeStruct((width, cols), bf16),
            jax.ShapeDtypeStruct((width, cols), bf16),
            jax.ShapeDtypeStruct((width, heads * hd), bf16),
            jax.ShapeDtypeStruct((1, cols), f32),
            jax.ShapeDtypeStruct((1, cols), f32),
        ),
        in_specs=[VMEM_SPEC] * 2 + [ANY_SPEC] * len(orders),
        out_specs=(VMEM_SPEC,) * 5,
        compiler_params=params(40),
        cost_estimate=pl.CostEstimate(flops=1 << 20, bytes_accessed=1 << 20, transcendentals=0),
        name="qkv_weights",
    )(w_qkv, bias_qv, *orders)


def pack_kernel(heads_rows, order_ref, up_ref, down_ref, out_ref_in, bias_ref, pack_ref, first_ref, up_rows_ref):
    width = up_ref.shape[0]
    eighth = down_ref.shape[0] // 8
    half = heads_rows // 2
    for i in range(0, down_ref.shape[0], 256):
        up_rows_ref[i : i + 256, :] = up_ref[:, i : i + 256].astype(f32).T.astype(bf16)
    pack_ref[:half, :width] = out_ref_in[:half, :]
    pack_ref[:half, width:] = out_ref_in[half:, :]
    pack_ref[half : half + 16, :width] = bias_ref[...]
    pack_ref[half : half + 16, width:] = jnp.zeros((16, width), bf16)
    for n in range(8):
        src = pl.ds(pl.multiple_of(order_ref[n] * eighth, 16), eighth)
        for ref, at in ((pack_ref, half + 16), (first_ref, 0))[: 2 if n < 2 else 1]:
            to = slice(at + n * eighth, at + (n + 1) * eighth)
            ref[to, :width] = up_rows_ref[src, :]
            ref[to, width:] = down_ref[src, :]


def pack(order, up, down, w_out, bias):
    hidden, width = down.shape
    rows = w_out.shape[0] // 2 + 16
    return pl.pallas_call(
        functools.partial(pack_kernel, w_out.shape[0]),
        out_shape=(
            jax.ShapeDtypeStruct((rows + hidden, 2 * width), bf16),
            jax.ShapeDtypeStruct((hidden // 4, 2 * width), bf16),
        ),
        in_specs=[SMEM_SPEC] + [VMEM_SPEC] * 4,
        out_specs=(VMEM_SPEC,) * 2,
        scratch_shapes=[pltpu.VMEM((hidden, width), bf16)],
        compiler_params=params(32),
        cost_estimate=pl.CostEstimate(flops=1 << 20, bytes_accessed=1 << 20, transcendentals=0),
        name="pack",
    )(order, up, down, w_out, bias)


def copies_kernel(n_orders, *refs):
    n = (len(refs) - n_orders) // 2
    for ref, out in zip(refs[:n], refs[n + n_orders :]):
        out[...] = ref[: out.shape[0], :]


def copies(values, rows, orders):
    return pl.pallas_call(
        functools.partial(copies_kernel, len(orders)),
        out_shape=tuple(jax.ShapeDtypeStruct((n, a.shape[1]), a.dtype) for a, n in zip(values, rows)),
        grid=(1,),
        in_specs=[pl.BlockSpec((n, a.shape[1]), lambda i: (0, 0)) for a, n in zip(values, rows)]
        + [ANY_SPEC] * len(orders),
        out_specs=tuple(pl.BlockSpec((n, a.shape[1]), lambda i: (0, 0)) for a, n in zip(values, rows)),
        compiler_params=params(58),
        cost_estimate=pl.CostEstimate(flops=1 << 20, bytes_accessed=1 << 20, transcendentals=0),
        name="copies",
    )(*values, *orders)


def rows_kernel(width, n_out, tile_rows, *refs):
    attn_refs, pack_refs = refs[:4], refs[4 : 4 + len(tile_rows)]
    refs = refs[4 + len(tile_rows) :]
    tok_refs, dres_refs, vec_ref = refs[:2], refs[2:6], refs[6]
    result_refs = refs[7:11]
    done_ref, hid_ref, dpre_ref, ylow_ref, dffn_ref, dbr_ref = refs[11:17]
    dattn_refs = refs[17:20]
    small_ref, bin_ref = refs[20:22]
    slope_ref = refs[22]
    bias_out, gain_one, bias_one, down_bias, gain_two, bias_two = [vec_ref[i : i + 1, :] for i in range(6)]
    step = pl.program_id(0)
    half = n_out // 2
    tiles, wos, biases = [], [], []
    for ref, first in zip(pack_refs, tile_rows):
        if first:
            wos.append(jnp.concatenate([ref[:half, :width], ref[:half, width:]], axis=0))
            biases.append(ref[half : half + 1, :width].astype(f32))
        left = ref.shape[0] - first
        if left == 0:
            continue
        size = min(left, width // 2)
        tiles += [ref.at[first + i * size : first + (i + 1) * size] for i in range(left // size)]
    up_bias = jnp.concatenate(biases, axis=1)

    def by_step(ones, twos):
        pairs = [jnp.where(step == 0, a[...].astype(f32), b[...].astype(f32)) for a, b in zip(ones, twos)]
        return pairs[0] if len(pairs) == 1 else jnp.concatenate(pairs, axis=0)

    @pl.when(pl.program_id(0) == 0)
    def _():
        small_ref[...] = jnp.zeros_like(small_ref)
        bin_ref[...] = jnp.zeros_like(bin_ref)

    branch = bias_out
    for k in range(4):
        branch = branch + dot_nn(attn_refs[k][...], wos[k])
    y_one, normed_one, inv_one = norm_fwd(by_step(tok_refs[:1], tok_refs[1:]) + branch, gain_one, bias_one)
    y_low = y_one.astype(bf16)
    ylow_ref[...] = y_low
    ffn = down_bias
    at = 0
    spans = []
    for tile in tiles:
        spans.append(slice(at, at + tile.shape[0]))
        at += tile.shape[0]
    for cols, tile in zip(spans, tiles):
        v = dot_nt(y_low, tile[:, :width]) + up_bias[:, cols]
        sq = v * v
        th = jnp.tanh(0.7978845608028654 * v * (1.0 + 0.044715 * sq))
        half = 0.5 * (1.0 + th)
        slope_ref[:, cols] = half + 0.5 * v * (1.0 - th * th) * (
            0.7978845608028654 * (1.0 + 3.0 * 0.044715 * sq)
        )
        hid = (v * half).astype(bf16)
        hid_ref[:, cols] = hid
        ffn = ffn + dot_nn(hid, tile[:, width:])
    result, normed_two, inv_two = norm_fwd(y_one + ffn, gain_two, bias_two)
    for s in range(2):

        @pl.when(step == s)
        def _(s=s):
            for k in range(2):
                ref = result_refs[s + 2 * k]
                ref[...] = result[k * ref.shape[0] : (k + 1) * ref.shape[0]].astype(bf16)

    d_two, g_gain_two, g_bias_two = norm_back(by_step(dres_refs[::2], dres_refs[1::2]), normed_two, inv_two, gain_two)
    d_ffn = d_two.astype(bf16)
    dffn_ref[...] = d_ffn
    g_bias_back = jnp.sum(d_ffn.astype(f32), axis=0)
    d_y = d_two
    for cols, tile in zip(spans, tiles):
        d_pre = (dot_nt(d_ffn, tile[:, width:]) * slope_ref[:, cols]).astype(bf16)
        dpre_ref[:, cols] = d_pre
        bin_ref[:, cols] += jnp.sum(d_pre.astype(f32), axis=0, keepdims=True)
        d_y = d_y + dot_nn(d_pre, tile[:, :width])
    d_one, g_gain_one, g_bias_one = norm_back(d_y, normed_one, inv_one, gain_one)
    done_ref[...] = d_one
    d_branch = d_one.astype(bf16)
    dbr_ref[...] = d_branch
    g_bias_out = jnp.sum(d_branch.astype(f32), axis=0)
    for k in range(4):
        d_attn = dot_nt(d_branch, wos[k]).astype(bf16)
        if k < 2:
            dattn_refs[k][...] = d_attn
        else:
            dattn_refs[2][k - 2] = d_attn
    sums = [g_bias_out, g_gain_one, g_bias_one, g_bias_back, g_gain_two, g_bias_two]
    for i, one in enumerate(sums):
        small_ref[i : i + 1, :] += one[None, :]


def rows_work(attns, packs, first_rows, toks, d_res, vecs):
    span, width = d_res[0].shape
    rows = 4 * span
    cols = attns[0].shape[1]
    hidden = sum(a.shape[0] - n for a, n in zip(packs, first_rows))
    tile = rows // 2

    def by_rows(n):
        return pl.BlockSpec((tile, n), lambda i: (i, 0))

    def whole(a):
        return pl.BlockSpec(a.shape, lambda i, nd=a.ndim: (0,) * nd, pipeline_mode=pl.Buffered(1))

    def fixed(shape):
        return pl.BlockSpec(shape, lambda i: (0, 0))

    low = functools.partial(jax.ShapeDtypeStruct, dtype=bf16)
    return pl.pallas_call(
        functools.partial(rows_kernel, width, cols, first_rows),
        grid=(rows // tile,),
        out_shape=(low((span, width)),) * 4
        + (
            jax.ShapeDtypeStruct((rows, width), f32),
            low((rows, hidden)),
            low((rows, hidden)),
            low((rows, width)),
            low((rows, width)),
            low((rows, width)),
            low((rows, cols)),
            low((rows, cols)),
            low((2, rows, cols)),
            jax.ShapeDtypeStruct((8, width), f32),
            jax.ShapeDtypeStruct((1, hidden), f32),
        ),
        in_specs=[by_rows(cols)] * 4 + [whole(a) for a in (*packs, *toks, *d_res, vecs)],
        out_specs=(fixed((span, width)),) * 4
        + (
            by_rows(width),
            by_rows(hidden),
            by_rows(hidden),
            by_rows(width),
            by_rows(width),
            by_rows(width),
            by_rows(cols),
            by_rows(cols),
            pl.BlockSpec((2, tile, cols), lambda i: (0, i, 0)),
            fixed((8, width)),
            fixed((1, hidden)),
        ),
        scratch_shapes=[pltpu.VMEM((tile, hidden), f32)],
        compiler_params=params(58),
        cost_estimate=pl.CostEstimate(flops=50 << 30, bytes_accessed=30 << 20, transcendentals=rows * hidden),
        name="rows_work",
    )(*attns, *packs, *toks, *d_res, vecs)


def tile_grads(ylow_ref, dpre_ref, hid_ref, dffn_ref):
    return dot_tn(dpre_ref[...], ylow_ref[...]), dot_tn(hid_ref[...], dffn_ref[...])


def far_grad_kernel(ylow_ref, dpre_ref, hid_ref, dffn_ref, dbr_ref, attn0_ref, attn1_ref, out_ref):
    width = ylow_ref.shape[1]
    eighth = out_ref.shape[1]

    @pl.when(pl.program_id(0) < 4)
    def _():
        g_in, g_back = tile_grads(ylow_ref, dpre_ref, hid_ref, dffn_ref)
        for n in range(4):
            out_ref[n, :, :width] = g_in[n * eighth : (n + 1) * eighth].astype(bf16)
            out_ref[n, :, width:] = g_back[n * eighth : (n + 1) * eighth].astype(bf16)

    @pl.when(pl.program_id(0) == 4)
    def _():
        for k, attn_ref in enumerate((attn0_ref, attn1_ref)):
            g_out = dot_tn(attn_ref[...], dbr_ref[...]).astype(bf16)
            out_ref[k, :, :width] = g_out[:eighth]
            out_ref[k, :, width:] = g_out[eighth:]
            out_ref[2 + k] = jnp.zeros_like(out_ref[2 + k])


def near_grad_kernel(
    n_orders, ylow_ref, dpre_ref, hid_ref, dffn_ref, dbr_ref, attn0_ref, attn1_ref, got_ref, *refs
):
    keep_ref, y_ref, x_ref, *across_refs, held_ref, sems = refs[n_orders:]
    width = ylow_ref.shape[1]
    eighth = got_ref.shape[1]
    step = pl.program_id(0)

    def moves(n):
        if n == 0:
            pairs = [(held_ref.at[0], keep_ref.at[0:4])]
        elif n == 1:
            pairs = [(held_ref.at[1], x_ref.at[0:4])]
        elif n == 2:
            pairs = [(held_ref.at[0], y_ref.at[0:4])]
        elif n == 3:
            pairs = [(held_ref.at[1, k], across_refs[k]) for k in range(4)]
        else:
            pairs = [(held_ref.at[0, 0], keep_ref.at[4]), (held_ref.at[0, 1], y_ref.at[4])]
        return [pltpu.make_async_copy(a, b, sems.at[n, i]) for i, (a, b) in enumerate(pairs)]

    for n in range(5):

        @pl.when(step == n)
        def _(n=n):
            if n >= 2:
                for copy in moves(n - 2):
                    copy.wait()
            if n < 4:
                g_in, g_back = tile_grads(ylow_ref, dpre_ref, hid_ref, dffn_ref)
                for k in range(4):
                    rows = slice(k * eighth, (k + 1) * eighth)
                    held_ref[n % 2, k, :, :width] = (g_in[rows] + got_ref[k, :, :width].astype(f32)).astype(bf16)
                    held_ref[n % 2, k, :, width:] = (g_back[rows] + got_ref[k, :, width:].astype(f32)).astype(bf16)
            else:
                for k, attn_ref in enumerate((attn0_ref, attn1_ref)):
                    g_out = dot_tn(attn_ref[...], dbr_ref[...])
                    held_ref[0, k, :, :width] = (g_out[:eighth] + got_ref[k, :, :width].astype(f32)).astype(bf16)
                    held_ref[0, k, :, width:] = (g_out[eighth:] + got_ref[k, :, width:].astype(f32)).astype(bf16)
            for copy in moves(n):
                copy.start()
            if n == 4:
                for copy in moves(3) + moves(4):
                    copy.wait()


def rows_grad(kc, y_low, d_pre, hidden, d_ffn, d_branch, attn0, attn1, got=None, orders=()):
    rows, width = y_low.shape
    part = hidden.shape[1] // 8
    eighth = part // 4
    block = (4, eighth, 2 * width)

    def fixed(n):
        return pl.BlockSpec((rows, n), lambda i: (0, 0), pipeline_mode=pl.Buffered(1))

    def tile_of(i):
        i = jnp.minimum(i, 3)
        return (0, (i // 2) * 4 + kc * 2 + i % 2)

    tile = pl.BlockSpec((rows, part), tile_of)
    in_specs = [fixed(width), tile, tile, fixed(width), fixed(width), fixed(attn0.shape[1]), fixed(attn1.shape[1])]
    octets = pl.BlockSpec(block, lambda i: (i, 0, 0))
    cost = pl.CostEstimate(flops=8 << 30, bytes_accessed=16 << 20, transcendentals=0)
    operands = (y_low, d_pre, hidden, d_ffn, d_branch, attn0, attn1)
    if kc == 1:
        return pl.pallas_call(
            far_grad_kernel,
            grid=(5,),
            out_shape=jax.ShapeDtypeStruct((20,) + block[1:], bf16),
            in_specs=in_specs,
            out_specs=octets,
            compiler_params=params(58),
            cost_estimate=cost,
            name="far_grad",
        )(*operands)
    return pl.pallas_call(
        functools.partial(near_grad_kernel, len(orders)),
        grid=(5,),
        out_shape=tuple(jax.ShapeDtypeStruct((n,) + block[1:], bf16) for n in (5, 5, 4))
        + (jax.ShapeDtypeStruct(block[1:], bf16),) * 4,
        in_specs=in_specs + [octets] + [ANY_SPEC] * len(orders),
        out_specs=(ANY_SPEC,) * 7,
        scratch_shapes=[pltpu.VMEM((2,) + block, bf16), pltpu.SemaphoreType.DMA((5, 4))],
        compiler_params=params(58),
        cost_estimate=cost,
        name="near_grad",
    )(*operands, got, *orders)


def row_sum_one_kernel(near_ref, got_ref, *refs):
    for i, out in enumerate(refs[-2:]):

        @pl.when(pl.program_id(0) == i)
        def _(out=out):
            out[...] = (near_ref[0].astype(f32) + got_ref[0].astype(f32)).astype(bf16)


def row_sum_one(near, got, orders):
    _, rows, width = near.shape
    far = pl.BlockSpec((1, rows // 2, width), lambda i: (i, 1, 0))
    return pl.pallas_call(
        row_sum_one_kernel,
        grid=(2,),
        out_shape=(jax.ShapeDtypeStruct((rows // 2, width), bf16),) * 2,
        in_specs=[far] * 2 + [ANY_SPEC] * len(orders),
        out_specs=(pl.BlockSpec((rows // 2, width), lambda i: (0, 0)),) * 2,
        compiler_params=params(58),
        cost_estimate=pl.CostEstimate(flops=1 << 28, bytes_accessed=6 << 20, transcendentals=0),
        name="row_sum_one",
    )(near, got, *orders)


def row_sum_two_kernel(near_ref, got_ref, even_ref, odd_ref, *refs):
    for i, (src, out) in enumerate(zip((even_ref, odd_ref), refs[-2:])):

        @pl.when(pl.program_id(0) == i)
        def _(src=src, out=out):
            out[...] = (near_ref[0].astype(f32) + got_ref[0].astype(f32) + src[...].astype(f32)).astype(bf16)


def row_sum_two(near, got, even, odd, orders):
    quarter, width = near.shape[1] // 4, near.shape[2]
    part = pl.BlockSpec((1, quarter, width), lambda i: (i, 1, 0))
    return pl.pallas_call(
        row_sum_two_kernel,
        grid=(2,),
        out_shape=(jax.ShapeDtypeStruct((quarter, width), bf16),) * 2,
        in_specs=[part] * 2 + [pl.BlockSpec((quarter, width), lambda i: (1, 0))] * 2 + [ANY_SPEC] * len(orders),
        out_specs=(pl.BlockSpec((quarter, width), lambda i: (0, 0)),) * 2,
        compiler_params=params(58),
        cost_estimate=pl.CostEstimate(flops=1 << 28, bytes_accessed=4 << 20, transcendentals=0),
        name="row_sum_two",
    )(near, got, even, odd, *orders)


def row_sum_three_kernel(near_ref, got_ref, even_ref, odd_ref, even_got, odd_got, done_ref, *out_refs):
    rows = near_ref.shape[1]
    for i, (one, two) in enumerate(((even_ref, even_got), (odd_ref, odd_got))):

        @pl.when(pl.program_id(0) == i)
        def _(i=i, one=one, two=two):
            total = (
                near_ref[0].astype(f32)
                + got_ref[0].astype(f32)
                + one[:rows, :].astype(f32)
                + two[:rows, :].astype(f32)
                + done_ref[...]
            ).astype(bf16)
            out_refs[i][...] = total[: rows // 2]
            out_refs[i + 2][...] = total[rows // 2 :]


def row_sum_three(near, got, even, odd, even_got, odd_got, d_one):
    quarter, width = near.shape[1] // 4, near.shape[2]
    part = pl.BlockSpec((1, quarter, width), lambda i: (i, 0, 0))
    first = pl.BlockSpec((quarter, width), lambda i: (0, 0))
    out = pl.BlockSpec((quarter // 2, width), lambda i: (0, 0))
    return pl.pallas_call(
        row_sum_three_kernel,
        grid=(2,),
        out_shape=(jax.ShapeDtypeStruct((quarter // 2, width), bf16),) * 4,
        in_specs=[part] * 2 + [first] * 4 + [pl.BlockSpec((quarter, width), lambda i: (i, 0))],
        out_specs=(out,) * 4,
        compiler_params=params(58),
        cost_estimate=pl.CostEstimate(flops=1 << 28, bytes_accessed=4 << 20, transcendentals=0),
        name="row_sum_three",
    )(near, got, even, odd, even_got, odd_got, d_one)


def plane_layer(
    tokens,
    w_qkv,
    bias_qv,
    w_out,
    bias_out,
    gain_one,
    bias_one,
    up_weight,
    up_bias_vector,
    down_weight,
    down_bias_vector,
    gain_two,
    bias_two,
    d_out,
    key_mask,
    rand_idx,
):
    z = lax.axis_index("sq")
    px = lax.axis_index("part")
    hy = lax.axis_index("hy")
    hc = lax.axis_index("hc")
    head = hy * 2 + hc
    span, seqs, width = tokens.shape
    heads, hd = w_qkv.shape[1], w_qkv.shape[3]
    n_o, n_kv = heads * hd, heads * 2 * hd
    hidden_dev = up_weight.shape[1]
    eighth = hidden_dev // 8
    length = key_mask.shape[1]
    blocks_all = length // BLOCK
    rows = seqs * span
    coords = jnp.stack([z, px, hy, hc]).astype(jnp.int32)
    octet = jnp.arange(8)

    def turn_octets(value):
        shape = value.shape
        value = flipped(value.reshape((2, 2, 2) + shape[1:]), z // 2, 0)
        return flipped(flipped(value, z % 2, 1), px, 2).reshape(shape)

    held_zd = octet // 2 % 2 + octet % 2 * 2
    held_order = ((held_zd ^ z) * 2 + ((octet // 4) ^ px)).astype(jnp.int32)
    bias_row = jnp.moveaxis(turn_octets(up_bias_vector.reshape(8, eighth)).reshape(2, 2, 2, eighth), (0, 2), (2, 0))
    bias_row = jnp.pad(bias_row.reshape(1, hidden_dev), ((0, 15), (0, 0)))
    wf, wf_first = pack(held_order, up_weight, down_weight, w_out.reshape(n_o, width), bias_row)
    n_wo = n_o // 2 + 16
    quarter = swap(wf_first, "hy", name="weight")

    raw = split(coords, tokens, [wf])
    tok = [raw[0]] + [swap(raw[k], "sq", k, name="tok") for k in range(1, 4)]
    w_kv, w_q_pad, w_q, b_kv, b_q = qkv_weights(w_qkv, bias_qv, raw)
    even = after(jnp.concatenate([tok[0], tok[2]], axis=0), *tok, w_kv, quarter)
    odd = after(jnp.concatenate([tok[1], tok[3]], axis=0), *tok, w_kv, quarter)
    even_x = swap(even, "part", name="tok")
    odd_y = swap(odd, "hy", name="tok")
    units = copies([quarter], [2 * eighth], [even, odd])[0]
    wf_z = swap(units, "sq", 1, name="weight")
    even_near = after(jnp.concatenate([even, even_x], axis=0), units)
    odd_near = after(jnp.concatenate([odd, odd_y], axis=0), units)
    even_far = swap(even_near, "hy", name="tok")
    odd_far = swap(odd_near, "part", name="tok")
    xs = [even_near, even_far, swap(even_near, "hc", name="tok"), swap(even_far, "hc", name="tok")]
    xs += [odd_near, odd_far, swap(odd_near, "hc", name="tok"), swap(odd_far, "hc", name="tok")]
    dres_raw = split(coords, d_out, [even_near, odd_near])
    dres = [dres_raw[0]] + [swap(dres_raw[k], "sq", k, name="dres") for k in range(1, 4)]

    mask_seq = lax.dynamic_index_in_dim(key_mask, z, 0, keepdims=False).reshape(blocks_all, BLOCK)
    mask = jnp.where(mask_seq == 1, 0.0, MASK_FILL).astype(f32)
    mask = jnp.pad(jnp.concatenate([mask, mask], axis=1), ((0, 8), (0, 0)), constant_values=MASK_FILL)
    rand = lax.dynamic_slice(rand_idx, (z, 0, head * heads, 0), (1, blocks_all, heads, 3)).reshape(-1)
    vecs = jnp.stack([bias_out, gain_one, bias_one, down_bias_vector, gain_two, bias_two])
    vecs = jnp.pad(vecs, ((0, 2), (0, 0)))

    wf_c = swap(wf, "hc", name="weight")
    quarter_c = swap(quarter, "hc", name="weight")
    wf_zc = swap(wf_z, "hc", name="weight")
    units, units_z, wo = copies([quarter, wf_z, wf], [2 * eighth, 2 * eighth, n_wo], xs)
    wo_y = swap(wo, "hy", name="weight")
    wf_x = swap(units, "part", name="weight")
    wf_zx = swap(units_z, "part", name="weight")

    o_near, o_far, lse, kv, q = project_and_attend(
        heads, hd, span, coords, rand, xs, w_kv, w_q_pad, b_kv, b_q, mask, [wf_c, quarter_c, wf_zc, units, *dres_raw]
    )
    o_far = after(o_far, *dres[1:])
    wo_y, wf_x, wf_zx = after(wo_y, o_near), after(wf_x, o_near), after(wf_zx, o_near)
    wo_yc = swap(wo_y, "hc", name="weight")
    wf_xc = swap(wf_x, "hc", name="weight")
    wf_zxc = swap(wf_zx, "hc", name="weight")
    attn_y = swap(o_far, "hy", name="attn")
    attn_c = swap(o_near[rows:], "hc", name="attn")
    attn_yc = swap(attn_y[rows:], "hc", name="attn")

    packs = [wf, wf_c, wo_y, quarter, wf_z, wf_x, wf_zx, wo_yc, quarter_c, wf_zc, wf_xc, wf_zxc]
    first_rows = (n_wo, n_wo, n_wo, 0, 0, 0, 0, n_wo, 0, 0, 0, 0)
    out = rows_work([o_near, attn_c, attn_y, attn_yc], packs, first_rows, [even, odd], dres, vecs)
    result, (d_one, hidden, d_pre, y_low, d_ffn, d_branch, d_00, d_01, d_far, small, bin_sum) = out[:4], out[4:]

    d_y = swap(d_far, "hy", name="dattn")
    d_c = swap(d_01, "hc", name="dattn")
    d_yc = swap(d_y[1], "hc", name="dattn")

    other = rows_grad(1, y_low, d_pre, hidden, d_ffn, d_branch, attn_c, attn_yc)
    wide_got = swap(other, "hc", name="wide")
    res = [result[0]] + [swap(result[k], "sq", k, name="result") for k in range(1, 4)]
    keep, to_y, to_x, *across = rows_grad(0, y_low, d_pre, hidden, d_ffn, d_branch, o_near, attn_y, wide_got, [d_y, d_c])
    y_got = swap(to_y, "hy", name="wide")
    x_got = swap(to_x, "part", name="wide")
    across_got = [swap(across[p], "sq", k, name="wide") for p, k in ((2, 1), (1, 2), (3, 3))]

    dq, dkv, dx, dx_far = attend_back(
        heads,
        hd,
        span,
        coords,
        rand,
        q,
        [d_00, d_c, d_y, d_yc],
        [o_near, o_far],
        kv,
        mask,
        lse,
        w_kv,
        w_q,
        [to_y, to_x, *across, *res[1:]],
    )
    dx_far = after(dx_far, y_got, x_got, *across_got)

    b_in = bin_sum.reshape(4, hidden_dev)
    flat = small[:6].reshape(-1)
    n_flat = flat.size
    got = swap(after(jnp.concatenate([flat, b_in[1], b_in[3]]), dq), "hc", name="small")
    flat = flat + got[:n_flat]
    b_in = jnp.stack([b_in[0], b_in[2]]) + got[n_flat:].reshape(2, hidden_dev)
    got = swap(jnp.concatenate([flat, b_in[1]]), "hy", name="small")
    flat = flat + got[:n_flat]
    b_in = (b_in[0] + got[n_flat:]).reshape(2, 2, 2, eighth)
    b_in = turn_octets(jnp.moveaxis(b_in, (2, 0), (0, 2)).reshape(8, eighth)).reshape(1, hidden_dev)
    small = jnp.concatenate([flat.reshape(6, width), b_in, jnp.zeros((1, width), f32)], axis=0)
    small = jnp.pad(small.reshape(8, width // 128, 128), ((0, 0), (0, 8 - width // 128), (0, 0)))

    dx_got = swap(dx_far, "hc", name="dtok")
    octets = octet[:4]
    wide = wide_sum(((octets // 2 + octets % 2 * 2) ^ z).astype(jnp.int32), keep, y_got, x_got)
    top, low = across_sum([across[0]] + across_got)
    sent = row_sum_one(dx, dx_got, [wide, top, low])
    wide = lax.psum_scatter(wide, "sq", scatter_dimension=0, tiled=True)[0]
    top, low = swap(top, "part", name="across"), swap(low, "hy", name="across")
    even_got, odd_got = swap(sent[0], "hy", name="dtok"), swap(sent[1], "part", name="dtok")

    zq, xq = octet // 2, octet % 2
    zd = zq ^ z
    spots = ((xq ^ px) * 4 + (zd % 2) * 2 + zd // 2).astype(jnp.int32)
    tail = qkv_grad(span, spots, dq, dkv, keep, y_got, small, xs, [*sent, top, low])
    top, low = swap(top, "hy", name="across"), swap(low, "part", name="across")
    tail_got = swap(tail[4:], "part", name="tail")
    wide = wide_end(wide, top, low)
    sent_two = row_sum_two(dx, dx_got, even_got, odd_got, [wide])
    wide = lax.all_gather(wide, SEQ, axis=0, tiled=True)
    even_got2, odd_got2 = swap(sent_two[0], "part", name="dtok"), swap(sent_two[1], "hy", name="dtok")
    thins = tail_sum(tail, tail_got, [*sent_two])
    thins = [thins[0]] + [swap(thins[p], "sq", k, name="tail") for p, k in ((2, 1), (1, 2), (3, 3))]
    back_sent = row_sum_three(dx, dx_got, even_got, odd_got, even_got2, odd_got2, d_one)
    back = [back_sent[0]] + [swap(back_sent[k], "sq", k, name="dtok") for k in range(1, 4)]

    back_spots = (((octet % 4) ^ z) * 2 + ((octet // 4) ^ px)).astype(jnp.int32)
    thin_held = tail_end(thins, [*back_sent])
    thin_held = [thin_held] + [swap(thin_held, "sq", k, name="tail") for k in range(1, 4)]
    thin_held += [swap(a, "part", name="tail") for a in thin_held]
    grad_w_in = jnp.transpose(wide[:, :width]).astype(f32)
    grad_w_back = wide[:, width:].astype(f32)
    thin, small = tail_place(back_spots, thin_held)
    g_kv = jnp.transpose(thin[:n_kv]).reshape(width, heads, 2, hd)
    g_q = jnp.transpose(thin[n_kv : n_kv + n_o]).reshape(width, heads, 1, hd)
    grad_w_qkv = jnp.concatenate([g_q, g_kv], axis=2).astype(f32)
    grad_w_out = thin[n_kv + n_o :].reshape(heads, hd, width).astype(f32)
    small = small.reshape(8, 1024)
    grad_bias_qv = jnp.stack(
        [small[7, :n_o].reshape(heads, hd), small[7, n_o : n_o + n_kv].reshape(heads, 2, hd)[:, 1]], axis=1
    )
    small = small[:, :width]
    return (
        jnp.transpose(relative(jnp.stack(res), z), (1, 0, 2)),
        jnp.transpose(relative(jnp.stack(back), z), (1, 0, 2)),
        grad_w_qkv,
        grad_bias_qv,
        grad_w_out,
        small[0],
        small[1],
        small[2],
        grad_w_in,
        small[6],
        grad_w_back,
        small[3],
        small[4],
        small[5],
    )


def solution(mesh):
    seq_size, head_size = mesh.shape["seq"], mesh.shape["head"]

    def run(*args):
        seqs = args[0].shape[1]
        fine = Mesh(
            np.asarray(mesh.devices).reshape(seqs, seq_size // seqs, head_size // 2, 2),
            ("sq", "part", "hy", "hc"),
        )
        rows = P(("sq", "part", "hy", "hc"), None, None)
        span = args[0].shape[0] // (seq_size * head_size)
        fits = seqs == 4 and seq_size == 8 and head_size == 4 and span % BLOCK == 0
        layer = plane_layer if fits else general_layer
        placed = (
            rows,
            P(None, HEAD, None, None),
            P(HEAD, None, None),
            P(HEAD, None, None),
            P(),
            P(),
            P(),
            P(None, HEAD),
            P(HEAD),
            P(HEAD, None),
            P(),
            P(),
            P(),
            rows,
            P(),
            P(),
        )
        return jax.shard_map(
            layer,
            mesh=fine,
            in_specs=placed,
            out_specs=(
                rows,
                rows,
                P(None, HEAD, None, None),
                P(HEAD, None, None),
                P(HEAD, None, None),
                P(),
                P(),
                P(),
                P(None, HEAD),
                P(HEAD),
                P(HEAD, None),
                P(),
                P(),
                P(),
            ),
            check_vma=False,
        )(*args)

    return run
```

```python
import functools

import jax
import jax.numpy as jnp
import numpy as np
from jax import lax
from jax.experimental import pallas as pl
from jax.experimental.pallas import tpu as pltpu
from jax.sharding import Mesh
from jax.sharding import PartitionSpec as P

BLOCK = 64
PICKS = 8
CHUNK = 512
NORM_EPS = 1e-12
MASK_FILL = -1000000000.0

f32 = jnp.float32
bf16 = jnp.bfloat16

PLANE = ("part", "hy", "hc")
HEAD = ("hy", "hc")
SEQ = ("sq", "part")


def norm_fwd(resid, gain, shift):
    row_mean = jnp.mean(resid, axis=-1, keepdims=True)
    centred = resid - row_mean
    inv_std = lax.rsqrt(jnp.mean(centred * centred, axis=-1, keepdims=True) + NORM_EPS)
    normed = centred * inv_std
    return (normed * gain + shift, normed, inv_std)


def norm_back(upstream, normed, inv_std, gain):
    d_normed = upstream * gain
    d_resid = inv_std * (
        d_normed
        - jnp.mean(d_normed, axis=-1, keepdims=True)
        - normed * jnp.mean(d_normed * normed, axis=-1, keepdims=True)
    )
    return (d_resid, jnp.sum(upstream * normed, axis=0), jnp.sum(upstream, axis=0))


def tanh_gelu(values):
    return jax.nn.gelu(values, approximate=True)


def gelu_back(preactivation_values, upstream):
    return jax.vjp(tanh_gelu, preactivation_values)[1](upstream)[0]


def dot_nt(a, b):
    return lax.dot_general(a, b, (((1,), (1,)), ((), ())), preferred_element_type=f32)


def dot_nn(a, b):
    return lax.dot_general(a, b, (((1,), (0,)), ((), ())), preferred_element_type=f32)


def dot_tn(a, b):
    return lax.dot_general(a, b, (((0,), (0,)), ((), ())), preferred_element_type=f32)


def gathered(kv_ref, table_ref, base, cols):
    return jnp.concatenate(
        [
            kv_ref[pl.ds(pl.multiple_of(table_ref[base + u] * BLOCK, BLOCK), BLOCK), cols]
            for u in range(PICKS)
        ],
        axis=0,
    )


def lane_pick(values, lane):
    lanes = lax.broadcasted_iota(jnp.int32, values.shape, 1)
    return jnp.sum(jnp.where(lanes == lane, values, 0.0), axis=1, keepdims=True)


def attn_fwd_kernel(heads, hd, table_ref, edge_ref, q_ref, kv_ref, bias_ref, mask_ref, o_ref, lse_ref, s_ref):
    wide = 2 * hd
    blocks = q_ref.shape[0] // BLOCK
    chunks = kv_ref.shape[0] // CHUNK
    lanes = lax.broadcasted_iota(jnp.int32, (BLOCK, 128), 1)

    def one(jl, carry):
        rows = pl.ds(pl.multiple_of(jl * BLOCK, BLOCK), BLOCK)
        outs = []
        lse_tile = jnp.zeros((BLOCK, 128), f32)
        for h in range(heads):
            cols = slice(h * wide, (h + 1) * wide)
            kvg = gathered(kv_ref, table_ref, (jl * heads + h) * PICKS, cols)
            s = dot_nt(q_ref[rows, cols], kvg) + bias_ref[jl, h : h + 1, :]
            top = jnp.max(s, axis=1, keepdims=True)
            p = jnp.exp(s - top)
            total = jnp.sum(p, axis=1, keepdims=True)
            low = (p * (1.0 / total)).astype(bf16)
            outs.append(dot_nn(low, kvg)[:, hd:])
            lse_tile = jnp.where(lanes == h, top + jnp.log(total), lse_tile)
        o_ref[rows, :] = jnp.concatenate(outs, axis=1).astype(bf16)
        lse_ref[rows, :] = lse_tile
        return carry

    lax.fori_loop(0, blocks, one, 0)

    def edge(jl):
        rows = slice(jl * BLOCK, (jl + 1) * BLOCK)
        outs = []
        lse_tile = jnp.zeros((BLOCK, 128), f32)
        for h in range(heads):
            cols = slice(h * wide, (h + 1) * wide)
            q = q_ref[rows, cols]

            def score(c, top):
                part = pl.ds(pl.multiple_of(c * CHUNK, CHUNK), CHUNK)
                s = dot_nt(q, kv_ref[part, cols]) + mask_ref[:, part]
                s_ref[:, part] = s
                return jnp.maximum(top, jnp.max(s, axis=1, keepdims=True))

            top = lax.fori_loop(0, chunks, score, jnp.full((BLOCK, 1), -3e38, f32))

            def add(c, total):
                part = pl.ds(pl.multiple_of(c * CHUNK, CHUNK), CHUNK)
                return total + jnp.sum(jnp.exp(s_ref[:, part] - top), axis=1, keepdims=True)

            total = lax.fori_loop(0, chunks, add, jnp.zeros((BLOCK, 1), f32))
            inv = 1.0 / total

            def out(c, acc):
                part = pl.ds(pl.multiple_of(c * CHUNK, CHUNK), CHUNK)
                low = (jnp.exp(s_ref[:, part] - top) * inv).astype(bf16)
                return acc + dot_nn(low, kv_ref[part, cols])

            acc = lax.fori_loop(0, chunks, out, jnp.zeros((BLOCK, wide), f32))
            outs.append(acc[:, hd:])
            lse_tile = jnp.where(lanes == h, top + jnp.log(total), lse_tile)
        o_ref[rows, :] = jnp.concatenate(outs, axis=1).astype(bf16)
        lse_ref[rows, :] = lse_tile

    @pl.when(edge_ref[0] == 1)
    def _():
        edge(0)

    @pl.when(edge_ref[1] == 1)
    def _():
        edge(blocks - 1)


def attn_bwd_kernel(
    heads, hd, scale, table_ref, edge_ref, qd_ref, kv_ref, bias_ref, mask_ref, lse_ref, dq_ref, dkv_ref, acc_ref, p_ref, dp_ref
):
    wide = 2 * hd
    blocks = qd_ref.shape[0] // BLOCK
    chunks = kv_ref.shape[0] // CHUNK
    left = lax.broadcasted_iota(jnp.int32, (BLOCK, wide), 1) < hd
    nil = jnp.zeros((BLOCK, wide), bf16)

    def clear(c, carry):
        part = pl.ds(pl.multiple_of(c * CHUNK, CHUNK), CHUNK)
        acc_ref[part, :] = jnp.zeros((CHUNK, heads * wide), f32)
        return carry

    lax.fori_loop(0, chunks, clear, 0)

    def stacked(qd):
        return jnp.concatenate([jnp.where(left, qd, nil), jnp.where(left, nil, qd)], axis=0)

    def one(jl, carry):
        rows = pl.ds(pl.multiple_of(jl * BLOCK, BLOCK), BLOCK)
        lse_tile = lse_ref[rows, :]
        outs = []
        for h in range(heads):
            cols = slice(h * wide, (h + 1) * wide)
            base = (jl * heads + h) * PICKS
            kvg = gathered(kv_ref, table_ref, base, cols)
            both = stacked(qd_ref[rows, cols])
            prod = dot_nt(both, kvg)
            p = jnp.exp(prod[:BLOCK] + bias_ref[jl, h : h + 1, :] - lane_pick(lse_tile, h))
            dp = prod[BLOCK:]
            dot_row = jnp.sum(p * dp, axis=1, keepdims=True)
            ds = (p * (dp - dot_row)).astype(bf16)
            outs.append(dot_nn(ds, kvg)[:, :hd])
            dkv = dot_tn(jnp.concatenate([ds, p.astype(bf16)], axis=0), both)
            for u in range(PICKS):
                place = pl.ds(pl.multiple_of(table_ref[base + u] * BLOCK, BLOCK), BLOCK)
                acc_ref[place, cols] += dkv[u * BLOCK : (u + 1) * BLOCK]
        dq_ref[rows, :] = (jnp.concatenate(outs, axis=1) * scale).astype(bf16)
        return carry

    lax.fori_loop(edge_ref[0], blocks - edge_ref[1], one, 0)

    def edge(jl):
        rows = slice(jl * BLOCK, (jl + 1) * BLOCK)
        lse_tile = lse_ref[rows, :]
        outs = []
        for h in range(heads):
            cols = slice(h * wide, (h + 1) * wide)
            both = stacked(qd_ref[rows, cols])
            lse = lane_pick(lse_tile, h)

            def first(c, total):
                part = pl.ds(pl.multiple_of(c * CHUNK, CHUNK), CHUNK)
                prod = dot_nt(both, kv_ref[part, cols])
                p = jnp.exp(prod[:BLOCK] + mask_ref[:, part] - lse)
                dp = prod[BLOCK:]
                p_ref[:, part] = p
                dp_ref[:, part] = dp
                return total + jnp.sum(p * dp, axis=1, keepdims=True)

            dot_row = lax.fori_loop(0, chunks, first, jnp.zeros((BLOCK, 1), f32))

            def second(c, dq):
                part = pl.ds(pl.multiple_of(c * CHUNK, CHUNK), CHUNK)
                p = p_ref[:, part]
                ds = (p * (dp_ref[:, part] - dot_row)).astype(bf16)
                acc_ref[part, cols] += dot_tn(jnp.concatenate([ds, p.astype(bf16)], axis=0), both)
                return dq + dot_nn(ds, kv_ref[part, cols])

            dq = lax.fori_loop(0, chunks, second, jnp.zeros((BLOCK, wide), f32))
            outs.append(dq[:, :hd])
        dq_ref[rows, :] = (jnp.concatenate(outs, axis=1) * scale).astype(bf16)

    @pl.when(edge_ref[0] == 1)
    def _():
        edge(0)

    @pl.when(edge_ref[1] == 1)
    def _():
        edge(blocks - 1)

    def put(c, carry):
        part = pl.ds(pl.multiple_of(c * CHUNK, CHUNK), CHUNK)
        dkv_ref[part, :] = acc_ref[part, :].astype(bf16)
        return carry

    lax.fori_loop(0, chunks, put, 0)


SMEM_SPEC = pl.BlockSpec(memory_space=pltpu.SMEM)
VMEM_SPEC = pl.BlockSpec(memory_space=pltpu.VMEM)
VMEM_LIMIT = 48 * 1024 * 1024


def attn_forward(heads, hd, table, edges, q, kv, bias, mask):
    rows, keys = q.shape[0], kv.shape[0]
    return pl.pallas_call(
        functools.partial(attn_fwd_kernel, heads, hd),
        out_shape=(
            jax.ShapeDtypeStruct((rows, heads * hd), bf16),
            jax.ShapeDtypeStruct((rows, 128), f32),
        ),
        in_specs=[SMEM_SPEC] * 2 + [VMEM_SPEC] * 4,
        out_specs=(VMEM_SPEC, VMEM_SPEC),
        scratch_shapes=[pltpu.VMEM((BLOCK, keys), f32)],
        compiler_params=pltpu.CompilerParams(vmem_limit_bytes=VMEM_LIMIT),
        cost_estimate=pl.CostEstimate(
            flops=4 * rows * heads * CHUNK * 2 * hd, bytes_accessed=8 << 20, transcendentals=rows * heads * CHUNK
        ),
        name="attn_forward",
    )(table, edges, q, kv, bias, mask)


def attn_backward(heads, hd, scale, table, edges, qd, kv, bias, mask, lse):
    rows, keys = qd.shape[0], kv.shape[0]
    return pl.pallas_call(
        functools.partial(attn_bwd_kernel, heads, hd, scale),
        out_shape=(
            jax.ShapeDtypeStruct((rows, heads * hd), bf16),
            jax.ShapeDtypeStruct((keys, heads * 2 * hd), bf16),
        ),
        in_specs=[SMEM_SPEC] * 2 + [VMEM_SPEC] * 5,
        out_specs=(VMEM_SPEC, VMEM_SPEC),
        scratch_shapes=[
            pltpu.VMEM((keys, heads * 2 * hd), f32),
            pltpu.VMEM((BLOCK, keys), f32),
            pltpu.VMEM((BLOCK, keys), f32),
        ],
        compiler_params=pltpu.CompilerParams(vmem_limit_bytes=VMEM_LIMIT),
        cost_estimate=pl.CostEstimate(
            flops=10 * rows * heads * CHUNK * 2 * hd, bytes_accessed=12 << 20, transcendentals=rows * heads * CHUNK
        ),
        name="attn_backward",
    )(table, edges, qd, kv, bias, mask, lse)


def general_layer(
    tokens,
    w_qkv,
    bias_qv,
    w_out,
    bias_out,
    gain_one,
    bias_one,
    up_weight,
    up_bias_vector,
    down_weight,
    down_bias_vector,
    gain_two,
    bias_two,
    d_out,
    key_mask,
    rand_idx,
):
    sq = lax.axis_index("sq")
    part = lax.axis_index("part")
    head = lax.axis_index(HEAD)
    parts = lax.axis_size("part")
    groups = lax.axis_size(HEAD)
    span, seqs, width = tokens.shape
    heads, hd = w_qkv.shape[1], w_qkv.shape[3]
    scale = hd ** (-0.5)
    length = key_mask.shape[1]
    blocks_all = length // BLOCK
    per_chunk = groups * span // BLOCK
    mine = seqs * per_chunk

    tok = lax.all_to_all(jnp.transpose(tokens, (1, 0, 2)), "sq", 0, 0, tiled=True)
    x_all = lax.all_gather(tok, PLANE, axis=0, tiled=False)
    d_res = lax.all_to_all(jnp.transpose(d_out, (1, 0, 2)), "sq", 0, 0, tiled=True)

    w_out_full = lax.all_gather(w_out.reshape(heads * hd, width), HEAD, axis=0, tiled=False)
    up_full = lax.all_gather(up_weight, HEAD, axis=0, tiled=False)
    down_full = lax.all_gather(down_weight, HEAD, axis=0, tiled=False)
    up_bias_full = lax.all_gather(up_bias_vector.astype(f32), HEAD, axis=0, tiled=False)

    chunk_ids = jnp.arange(seqs) * parts + part
    block_ids = (chunk_ids[:, None] * per_chunk + jnp.arange(per_chunk)[None, :]).reshape(mine)
    rand_seq = lax.dynamic_index_in_dim(rand_idx, sq, 0, keepdims=False)
    rand_head = lax.dynamic_slice_in_dim(rand_seq, head * heads, heads, 1)
    chosen = jnp.take(rand_head, block_ids, axis=0)
    window = block_ids[:, None] + jnp.arange(-1, 2)[None, :]
    window_ok = (window >= 1) & (window <= blocks_all - 2)
    fixed_ids = jnp.concatenate(
        [
            jnp.clip(window, 0, blocks_all - 1),
            jnp.broadcast_to(jnp.array([0, blocks_all - 1], jnp.int32), (mine, 2)),
        ],
        axis=1,
    )
    fixed_ok = jnp.concatenate([window_ok, jnp.ones((mine, 2), bool)], axis=1)
    table = jnp.concatenate(
        [jnp.broadcast_to(fixed_ids[:, None, :], (mine, heads, 5)), chosen], axis=2
    )
    table_ok = jnp.concatenate(
        [
            jnp.broadcast_to(fixed_ok[:, None, :], (mine, heads, 5)),
            jnp.ones((mine, heads, PICKS - 5), bool),
        ],
        axis=2,
    )
    mask_seq = lax.dynamic_index_in_dim(key_mask, sq, 0, keepdims=False)
    mask_blocks = (mask_seq == 1).reshape(blocks_all, BLOCK).astype(bf16)
    onehot = (table[..., None] == jnp.arange(blocks_all)).astype(bf16) * table_ok[..., None].astype(bf16)
    allowed = jnp.einsum("jhub,bk->jhuk", onehot, mask_blocks, preferred_element_type=f32)
    bias_rows = ((1.0 - allowed) * MASK_FILL).reshape(mine, heads, PICKS * BLOCK)
    mask_row = jnp.where(mask_seq == 1, 0.0, MASK_FILL).astype(f32).reshape(1, length)
    edges = jnp.stack([part == 0, part == parts - 1]).astype(jnp.int32)
    table = table.reshape(-1).astype(jnp.int32)

    w_kv = w_qkv[:, :, 1:].reshape(width, heads * 2 * hd)
    bias_kv = jnp.stack([jnp.zeros((heads, hd), f32), bias_qv[:, 1]], axis=1).reshape(heads * 2 * hd)
    w_q = w_qkv[:, :, 0].reshape(width, heads * hd)
    bias_q = bias_qv[:, 0].reshape(heads * hd)
    x_rows = x_all.reshape(parts, groups, seqs, span, width)
    x_mine = lax.dynamic_index_in_dim(x_rows, part, 0, keepdims=False)
    kv_rows = (jnp.einsum("pgzsd,dc->pgzsc", x_rows, w_kv, preferred_element_type=f32) + bias_kv).astype(bf16)
    kv = jnp.transpose(kv_rows, (2, 0, 1, 3, 4)).reshape(length, heads * 2 * hd)
    q_rows = (jnp.einsum("gzsd,dc->gzsc", x_mine, w_q, preferred_element_type=f32) + bias_q).astype(bf16)
    q_low = jnp.transpose(q_rows, (1, 0, 2, 3)).reshape(mine * BLOCK, heads, hd) * bf16(scale)
    q_pad = jnp.concatenate([q_low, jnp.zeros_like(q_low)], axis=-1).reshape(mine * BLOCK, heads * 2 * hd)

    attn_mine, lse = attn_forward(heads, hd, table, edges, q_pad, kv, bias_rows, mask_row)
    attn_send = jnp.transpose(attn_mine.reshape(seqs, groups, span, heads * hd), (1, 0, 2, 3))
    attn = lax.all_to_all(attn_send, HEAD, 0, 0, tiled=True).reshape(groups, seqs * span, heads * hd)

    rows = seqs * span
    tok_rows = tok.reshape(rows, width)
    branch = jnp.einsum("grc,gcd->rd", attn, w_out_full, preferred_element_type=f32) + bias_out
    y_one, normed_one, inv_one = norm_fwd(tok_rows.astype(f32) + branch, gain_one, bias_one)
    y_low = y_one.astype(bf16)
    pre = jnp.einsum("rd,gdf->grf", y_low, up_full, preferred_element_type=f32) + up_bias_full[:, None, :]
    hidden = tanh_gelu(pre).astype(bf16)
    ffn = jnp.einsum("grf,gfd->rd", hidden, down_full, preferred_element_type=f32) + down_bias_vector
    result, normed_two, inv_two = norm_fwd(y_one + ffn, gain_two, bias_two)
    result = lax.all_to_all(result.astype(bf16).reshape(seqs, span, width), "sq", 0, 0, tiled=True)
    d_two, grad_gain_two, grad_bias_two = norm_back(
        d_res.reshape(rows, width).astype(f32), normed_two, inv_two, gain_two
    )
    d_ffn = d_two.astype(bf16)
    grad_bias_back = jnp.sum(d_ffn.astype(f32), axis=0)
    d_hidden = jnp.einsum("rd,gfd->grf", d_ffn, down_full, preferred_element_type=f32)
    d_pre = gelu_back(pre, d_hidden).astype(bf16)
    d_y_ffn = jnp.einsum("grf,gdf->rd", d_pre, up_full, preferred_element_type=f32)
    grad_w_in = jnp.einsum("rd,grf->gdf", y_low, d_pre, preferred_element_type=f32).astype(bf16)
    grad_bias_in = jnp.sum(d_pre.astype(f32), axis=1)
    grad_w_back = jnp.einsum("grf,rd->gfd", hidden, d_ffn, preferred_element_type=f32).astype(bf16)
    d_one, grad_gain_one, grad_bias_one = norm_back(d_two + d_y_ffn, normed_one, inv_one, gain_one)
    d_branch = d_one.astype(bf16)
    grad_bias_out = jnp.sum(d_branch.astype(f32), axis=0)
    d_attn = jnp.einsum("rd,gcd->grc", d_branch, w_out_full, preferred_element_type=f32).astype(bf16)
    grad_w_out = jnp.einsum("grc,rd->gcd", attn, d_branch, preferred_element_type=f32).astype(bf16)

    d_attn_mine = lax.all_to_all(d_attn.reshape(groups, seqs, span, heads * hd), HEAD, 0, 0, tiled=True)
    d_attn_nat = jnp.transpose(d_attn_mine, (1, 0, 2, 3)).reshape(mine * BLOCK, heads, hd)
    qd = jnp.concatenate([q_low, d_attn_nat], axis=-1).reshape(mine * BLOCK, heads * 2 * hd)

    wide_part = jnp.concatenate([grad_w_in, grad_w_back, grad_w_out], axis=1)
    wide_sum = lax.psum_scatter(wide_part, HEAD, scatter_dimension=0, tiled=True)[0]
    wide_sum = lax.psum(wide_sum, SEQ)

    dq, dkv = attn_backward(heads, hd, scale, table, edges, qd, kv, bias_rows, mask_row, lse)
    dkv_rows = jnp.transpose(
        dkv.reshape(seqs, parts, groups, span, heads * 2 * hd), (1, 2, 0, 3, 4)
    )
    dq_rows = jnp.transpose(dq.reshape(seqs, groups, span, heads * hd), (1, 0, 2, 3))
    dq_all = lax.dynamic_update_index_in_dim(
        jnp.zeros((parts, groups, seqs, span, heads * hd), bf16), dq_rows, part, 0
    )
    d_x = jnp.einsum("pgzsc,dc->pgzsd", dkv_rows, w_kv, preferred_element_type=f32) + jnp.einsum(
        "pgzsc,dc->pgzsd", dq_all, w_q, preferred_element_type=f32
    )
    d_x = lax.psum_scatter(
        d_x.astype(bf16).reshape(parts * groups, seqs, span, width), PLANE, scatter_dimension=0, tiled=True
    )
    d_tok = (d_one + d_x.reshape(rows, width).astype(f32)).astype(bf16)
    d_tok = lax.all_to_all(d_tok.reshape(seqs, span, width), "sq", 0, 0, tiled=True)

    grad_kv = jnp.einsum("pgzsd,pgzsc->dc", x_rows, dkv_rows, preferred_element_type=f32)
    grad_q = jnp.einsum("gzsd,gzsc->dc", x_mine, dq_rows, preferred_element_type=f32)
    grad_w_qkv = jnp.concatenate(
        [grad_q.reshape(width, heads, 1, hd), grad_kv.reshape(width, heads, 2, hd)], axis=2
    )
    bias_q_sum = jnp.sum(dq_rows.astype(f32), axis=(0, 1, 2)).reshape(heads, 1, hd)
    bias_v_sum = jnp.sum(dkv_rows.astype(f32), axis=(0, 1, 2, 3)).reshape(heads, 2, hd)[:, 1:]
    grad_bias_qv = jnp.concatenate([bias_q_sum, bias_v_sum], axis=1)
    grad_w_qkv = lax.psum(grad_w_qkv.astype(bf16), SEQ).astype(f32)

    small = jnp.stack(
        [grad_bias_out, grad_gain_one, grad_bias_one, grad_bias_back, grad_gain_two, grad_bias_two]
    )
    all_bias_in = grad_bias_in
    bias_qv_all = lax.dynamic_update_index_in_dim(
        jnp.zeros((groups, heads * 2 * hd), f32), grad_bias_qv.reshape(-1), head, 0
    )
    packed = jnp.concatenate([small.reshape(-1), all_bias_in.reshape(-1), bias_qv_all.reshape(-1)])
    packed = lax.psum(packed, ("sq", "part", "hy", "hc"))
    n_small = 6 * width
    small = packed[:n_small].reshape(6, width)
    n_in = n_small + all_bias_in.size
    hidden_dev = up_weight.shape[1]
    grad_bias_in = lax.dynamic_slice_in_dim(packed[n_small:n_in], head * hidden_dev, hidden_dev, 0)
    grad_bias_qv = lax.dynamic_slice_in_dim(
        packed[n_in:], head * heads * 2 * hd, heads * 2 * hd, 0
    ).reshape(heads, 2, hd)

    wide_sum = wide_sum.astype(f32)
    grad_w_in = wide_sum[:width]
    grad_w_back = wide_sum[width : width + hidden_dev]
    grad_w_out = wide_sum[width + hidden_dev :].reshape(heads, hd, width)
    return (
        jnp.transpose(result, (1, 0, 2)),
        jnp.transpose(d_tok, (1, 0, 2)),
        grad_w_qkv,
        grad_bias_qv,
        grad_w_out,
        small[0],
        small[1],
        small[2],
        grad_w_in,
        grad_bias_in,
        grad_w_back,
        small[3],
        small[4],
        small[5],
    )


def swap(value, axis, step=1, name="swap"):
    size = lax.axis_size(axis)
    with jax.named_scope(name + "_" + axis + str(step)):
        return lax.ppermute(value, axis, [(i, i ^ step) for i in range(size)])


def flipped(value, bit, axis):
    return jnp.where(bit == 1, jnp.flip(value, axis), value)


def relative(value, place):
    shape = value.shape
    value = value.reshape((2, 2) + shape[1:])
    value = flipped(flipped(value, place // 2, 0), place % 2, 1)
    return value.reshape(shape)


ANY_SPEC = pl.BlockSpec(memory_space=pl.ANY)


def after(value, *orders):
    return pl.pallas_call(
        lambda *refs: None,
        out_shape=jax.ShapeDtypeStruct(value.shape, value.dtype),
        in_specs=[ANY_SPEC] * (1 + len(orders)),
        out_specs=ANY_SPEC,
        input_output_aliases={0: 0},
        name="after",
    )(value, *orders)


def params(limit_mb):
    return pltpu.CompilerParams(vmem_limit_bytes=limit_mb * 1024 * 1024)


def fill_tables(coord_ref, rand_ref, place_ref, nat_ref, heads, span):
    per_span = span // BLOCK

    def one(b, carry):
        own = b // per_span
        kz = (own // 8) ^ coord_ref[0]
        kx = (own // 4 % 2) ^ coord_ref[1]
        ky = (own // 2 % 2) ^ coord_ref[2]
        kc = (own % 2) ^ coord_ref[3]
        odd = kz % 2
        one, two = jnp.where(odd == 0, kx, ky), jnp.where(odd == 0, ky, kx)
        spot = ((((odd * 2 + kc) * 2 + two) * 2 + one) * 2 + kz // 2) * per_span + b % per_span
        place_ref[b] = spot
        nat_ref[spot] = b
        return carry

    lax.fori_loop(0, place_ref.shape[0], one, 0)


def natural_block(coord_ref, jl, per_span):
    kz = (jl // per_span % 2 * 2 + jl // (per_span * 2) % 2) ^ coord_ref[0]
    kc = jl // (per_span * 4) % 2 ^ coord_ref[3]
    ky = jl // (per_span * 8) ^ coord_ref[2]
    return (((kz * 2 + coord_ref[1]) * 2 + ky) * 2 + kc) * per_span + jl % per_span


def edge_of(coord_ref, blocks, per_span):
    last = coord_ref[1]
    kz = (last * 3) ^ coord_ref[0]
    ky = last ^ coord_ref[2]
    kc = last ^ coord_ref[3]
    return ((ky * 2 + kc) * 4 + kz % 2 * 2 + kz // 2) * per_span + last * (per_span - 1)


def picks_of(coord_ref, rand_ref, jl, h, heads, per_span, blocks_all):
    b = natural_block(coord_ref, jl, per_span)
    inner = (b > 0) & (b < blocks_all - 1)
    ids, rows = [], []
    for u in range(3):
        key = b + u - 1
        ids.append(jnp.clip(key, 0, blocks_all - 1))
        rows.append(jnp.where(inner & (key >= 1) & (key <= blocks_all - 2), key, blocks_all))
    for key in (0, blocks_all - 1):
        ids.append(key)
        rows.append(jnp.where(inner, key, blocks_all))
    for u in range(3):
        key = rand_ref[(b * heads + h) * 3 + u]
        ids.append(key)
        rows.append(jnp.where(inner, key, blocks_all))
    return ids, rows


def mask_of(mask_ref, rows, left):
    pairs = []
    for u in range(0, len(rows), 2):
        a, b = mask_ref[pl.ds(rows[u], 1), :], mask_ref[pl.ds(rows[u + 1], 1), :]
        pairs.append(jnp.where(left, a, b))
    return jnp.concatenate(pairs, axis=1)


def blocks_of(kv_ref, place_ref, ids, cols):
    return jnp.concatenate(
        [kv_ref[pl.ds(pl.multiple_of(place_ref[b] * BLOCK, BLOCK), BLOCK), cols] for b in ids], axis=0
    )


def query_pieces(pair):
    out = []
    for ky in range(2):
        for kc in range(2):
            at = (ky * 2 + kc) * 2 * pair
            out.append((at, kc * 2 + ky, 0))
            out.append((at + pair, 4 + kc * 2, ky * pair))
    return out


def project_and_attend_kernel(heads, hd, span, n_orders, coord_ref, rand_ref, *refs):
    x_from = refs[:8]
    w_from, (b_kv_ref, b_q_ref, mask_ref) = refs[8:10], refs[10:13]
    refs = refs[13 + n_orders :]
    outs, refs = refs[:5], refs[5:]
    x_refs, (w_kv_ref, w_q_ref), o_refs = refs[:8], refs[8:10], refs[10:12]
    lse_ref, kv_ref, q_ref, s_ref, place_ref, nat_ref, in_sems, out_sems = refs[12:]
    arriving = [
        pltpu.make_async_copy(a, b, in_sems.at[i])
        for i, (a, b) in enumerate(zip((*w_from, *x_from), (w_kv_ref, w_q_ref, *x_refs)))
    ]
    for copy in arriving:
        copy.start()
    leaving = []

    def leave(src, dst):
        leaving.append(pltpu.make_async_copy(src, dst, out_sems.at[len(leaving)]))
        leaving[-1].start()

    near = o_refs[0].shape[0] // BLOCK
    wide = 2 * hd
    piece, pair = 4 * span, 2 * span
    per_span = span // BLOCK
    blocks = q_ref.shape[0] // BLOCK
    blocks_all = kv_ref.shape[0] // BLOCK
    chunks = kv_ref.shape[0] // CHUNK
    lanes = lax.broadcasted_iota(jnp.int32, (BLOCK, 128), 1)
    left = lax.broadcasted_iota(jnp.int32, (1, 128), 1) < BLOCK
    fill_tables(coord_ref, rand_ref, place_ref, nat_ref, heads, span)

    arriving[0].wait()
    arriving[1].wait()
    for n, x_ref in enumerate(x_refs):
        arriving[2 + n].wait()
        of = slice(n * piece, (n + 1) * piece)
        kv_ref[of, :] = (dot_nn(x_ref[...], w_kv_ref[...]) + b_kv_ref[...]).astype(bf16)
        leave(kv_ref.at[of], outs[3].at[of])
    for at, n, src in query_pieces(pair):
        x = x_refs[n][src : src + pair, :]
        q_ref[at : at + pair, :] = (dot_nn(x, w_q_ref[...]) + b_q_ref[...]).astype(bf16) * bf16(hd**-0.5)
    leave(q_ref, outs[4])

    def finish(jl, accs, tops, totals):
        lse_tile = jnp.zeros((BLOCK, 128), f32)
        for h in range(heads):
            lse_tile = jnp.where(lanes == h, tops[h] + jnp.log(totals[h]), lse_tile)
        lse_ref[pl.ds(pl.multiple_of(jl * BLOCK, BLOCK), BLOCK), :] = lse_tile
        return jnp.concatenate([accs[h][:, hd:] * (1.0 / totals[h]) for h in range(heads)], axis=1).astype(bf16)

    def put(o_ref, jl, value):
        o_ref[pl.ds(pl.multiple_of(jl * BLOCK, BLOCK), BLOCK), :] = value

    unroll = 4

    def some(half, it, carry):
        items = [(half * near + it * unroll + u, h) for u in range(unroll) for h in range(heads)]
        scores, kvs = [], []
        for jl, h in items:
            rows = pl.ds(pl.multiple_of(jl * BLOCK, BLOCK), BLOCK)
            cols = slice(h * wide, (h + 1) * wide)
            ids, mask_rows = picks_of(coord_ref, rand_ref, jl, h, heads, per_span, blocks_all)
            kvg = blocks_of(kv_ref, place_ref, ids, cols)
            scores.append(dot_nt(q_ref[rows, cols], kvg) + mask_of(mask_ref, mask_rows, left))
            kvs.append(kvg)
        lows, tops, totals = [], [], []
        for s in scores:
            top = jnp.max(s, axis=1, keepdims=True)
            p = jnp.exp(s - top)
            totals.append(jnp.sum(p, axis=1, keepdims=True))
            tops.append(top)
            lows.append(p.astype(bf16))
        accs = [dot_nn(p, kvg) for p, kvg in zip(lows, kvs)]
        for u in range(unroll):
            of = slice(u * heads, (u + 1) * heads)
            jl = it * unroll + u
            put(o_refs[half], jl, finish(half * near + jl, accs[of], tops[of], totals[of]))
        return carry

    for half in range(2):
        lax.fori_loop(0, near // unroll, functools.partial(some, half), 0)

    edge = edge_of(coord_ref, blocks, per_span)
    rows = pl.ds(pl.multiple_of(edge * BLOCK, BLOCK), BLOCK)
    head_cols = [slice(h * wide, (h + 1) * wide) for h in range(heads)]
    qs = [q_ref[rows, cols] for cols in head_cols]

    def score(c, tops):
        parts = [pl.ds(pl.multiple_of((c * 2 + i) * CHUNK, CHUNK), CHUNK) for i in range(2)]
        masks = [
            mask_of(mask_ref, [nat_ref[(c * 2 + i) * PICKS + u] for u in range(PICKS)], left) for i in range(2)
        ]
        ss = [
            [dot_nt(qs[h], kv_ref[parts[i], head_cols[h]]) + masks[i] for h in range(heads)] for i in range(2)
        ]
        for i in range(2):
            for h in range(heads):
                s_ref[h, :, parts[i]] = ss[i][h]
        return tuple(jnp.maximum(tops[h], jnp.maximum(ss[0][h], ss[1][h])) for h in range(heads))

    tops = lax.fori_loop(0, chunks // 2, score, tuple(jnp.full((BLOCK, CHUNK), -3e38, f32) for _ in range(heads)))
    tops = [jnp.max(t, axis=1, keepdims=True) for t in tops]

    def out(c, carry):
        accs, sums = carry
        parts = [pl.ds(pl.multiple_of((c * 2 + i) * CHUNK, CHUNK), CHUNK) for i in range(2)]
        ps = [[jnp.exp(s_ref[h, :, part] - tops[h]) for h in range(heads)] for part in parts]
        adds = [
            [dot_nn(ps[i][h].astype(bf16), kv_ref[parts[i], head_cols[h]]) for h in range(heads)] for i in range(2)
        ]
        accs = tuple(accs[h] + (adds[0][h] + adds[1][h]) for h in range(heads))
        sums = tuple(sums[h] + (ps[0][h] + ps[1][h]) for h in range(heads))
        return accs, sums

    accs, sums = lax.fori_loop(
        0,
        chunks // 2,
        out,
        (
            tuple(jnp.zeros((BLOCK, wide), f32) for _ in range(heads)),
            tuple(jnp.zeros((BLOCK, CHUNK), f32) for _ in range(heads)),
        ),
    )
    value = finish(edge, accs, tops, [jnp.sum(t, axis=1, keepdims=True) for t in sums])

    @pl.when(edge < near)
    def _():
        put(o_refs[0], edge, value)

    @pl.when(edge >= near)
    def _():
        put(o_refs[1], edge - near, value)

    for src, dst in zip((*o_refs, lse_ref), outs):
        leave(src, dst)
    for copy in leaving:
        copy.wait()


def project_and_attend(heads, hd, span, coords, rand, xs, w_kv, w_q, b_kv, b_q, mask, orders):
    keys = 8 * xs[0].shape[0]
    rows = keys // 2
    cols = heads * 2 * hd
    return pl.pallas_call(
        functools.partial(project_and_attend_kernel, heads, hd, span, len(orders)),
        out_shape=(
            jax.ShapeDtypeStruct((rows // 2, heads * hd), bf16),
            jax.ShapeDtypeStruct((rows // 2, heads * hd), bf16),
            jax.ShapeDtypeStruct((rows, 128), f32),
            jax.ShapeDtypeStruct((keys, cols), bf16),
            jax.ShapeDtypeStruct((rows, cols), bf16),
        ),
        in_specs=[SMEM_SPEC] * 2 + [ANY_SPEC] * 10 + [VMEM_SPEC] * 3 + [ANY_SPEC] * len(orders),
        out_specs=(ANY_SPEC,) * 5,
        scratch_shapes=[pltpu.VMEM(a.shape, bf16) for a in (*xs, w_kv, w_q)]
        + [pltpu.VMEM((rows // 2, heads * hd), bf16)] * 2
        + [
            pltpu.VMEM((rows, 128), f32),
            pltpu.VMEM((keys, cols), bf16),
            pltpu.VMEM((rows, cols), bf16),
            pltpu.VMEM((heads, BLOCK, keys), f32),
            pltpu.SMEM((keys // BLOCK,), jnp.int32),
            pltpu.SMEM((keys // BLOCK,), jnp.int32),
            pltpu.SemaphoreType.DMA((10,)),
            pltpu.SemaphoreType.DMA((12,)),
        ],
        compiler_params=params(60),
        cost_estimate=pl.CostEstimate(
            flops=40 << 30, bytes_accessed=16 << 20, transcendentals=rows * heads * CHUNK
        ),
        name="project_and_attend",
    )(coords, rand, *xs, w_kv, w_q, b_kv, b_q, mask, *orders)


def attend_back_kernel(heads, hd, span, n_orders, coord_ref, rand_ref, q_from, *refs):
    do_parts, o_parts, (kv_from, lse_from, w_kv_from, w_q_from, mask_ref) = refs[:4], refs[4:6], refs[6:11]
    refs = refs[11 + n_orders :]
    dq_out, dkv_out, near_out, far_out, acc_ref, do_ref, o_ref, place_ref, nat_ref = refs[:9]
    q_ref, kv_ref, lse_ref, w_kv_ref, w_q_ref, dq_ref, dkv_ref, dx_ref, in_sems, out_sems = refs[9:]
    own = do_parts[0].shape[0]
    pairs = [(q_from, q_ref), (kv_from, kv_ref), (lse_from, lse_ref)]
    for k, ref in enumerate(do_parts):
        pairs.append((ref.at[0] if len(ref.shape) == 3 else ref, do_ref.at[k * own : (k + 1) * own]))
    for k, ref in enumerate(o_parts):
        pairs.append((ref, o_ref.at[k * 2 * own : (k + 1) * 2 * own]))
    pairs += [(w_kv_from, w_kv_ref), (w_q_from, w_q_ref)]
    arriving = [pltpu.make_async_copy(a, b, in_sems.at[i]) for i, (a, b) in enumerate(pairs)]
    for copy in arriving:
        copy.start()
    wide = 2 * hd
    piece = 4 * span
    per_span = span // BLOCK
    scale = hd**-0.5
    blocks = q_ref.shape[0] // BLOCK
    blocks_all = kv_ref.shape[0] // BLOCK
    chunks = kv_ref.shape[0] // CHUNK
    head_cols = [slice(h * wide, (h + 1) * wide) for h in range(heads)]
    nil = jnp.zeros((BLOCK, hd), bf16)
    left = lax.broadcasted_iota(jnp.int32, (1, 128), 1) < BLOCK
    fill_tables(coord_ref, rand_ref, place_ref, nat_ref, heads, span)

    def clear(c, carry):
        part = pl.ds(pl.multiple_of(c * CHUNK, CHUNK), CHUNK)
        acc_ref[part, :] = jnp.zeros((CHUNK, heads * wide), f32)
        return carry

    lax.fori_loop(0, chunks, clear, 0)
    for copy in arriving[:-2]:
        copy.wait()

    def of_rows(rows):
        d_o = do_ref[rows, :]
        prod = d_o.astype(f32) * o_ref[rows, :].astype(f32)
        lse = lse_ref[rows, :]
        boths, dots, lses = [], [], []
        for h in range(heads):
            low = jnp.concatenate([nil, d_o[:, h * hd : (h + 1) * hd]], axis=1)
            boths.append(jnp.concatenate([q_ref[rows, head_cols[h]], low], axis=0))
            dots.append(jnp.sum(prod[:, h * hd : (h + 1) * hd], axis=1, keepdims=True))
            lses.append(lse[:, h : h + 1])
        return boths, dots, lses

    unroll = 4

    def some(it, carry):
        items, boths, dots, lses = [], [], [], []
        for u in range(unroll):
            jl = it * unroll + u
            rows = pl.ds(pl.multiple_of(jl * BLOCK, BLOCK), BLOCK)
            b, d, e = of_rows(rows)
            boths, dots, lses = boths + b, dots + d, lses + e
            items += [(jl, h) for h in range(heads)]
        kvs, prods, picks, masks = [], [], [], []
        for i, (jl, h) in enumerate(items):
            ids, mask_rows = picks_of(coord_ref, rand_ref, jl, h, heads, per_span, blocks_all)
            kvg = blocks_of(kv_ref, place_ref, ids, head_cols[h])
            prods.append(dot_nt(boths[i], kvg))
            masks.append(mask_of(mask_ref, mask_rows, left))
            kvs.append(kvg)
            picks.append(ids)
        dss, lows = [], []
        for i, (jl, h) in enumerate(items):
            p = jnp.exp(prods[i][:BLOCK] + masks[i] - lses[i])
            dss.append((p * (prods[i][BLOCK:] - dots[i])).astype(bf16))
            lows.append(p.astype(bf16))
        dqs = [dot_nn(ds, kvg)[:, :hd] for ds, kvg in zip(dss, kvs)]
        dkvs = [dot_tn(jnp.concatenate([ds, p], axis=0), both) for ds, p, both in zip(dss, lows, boths)]
        for i, (jl, h) in enumerate(items):
            for u in range(PICKS):
                place = pl.ds(pl.multiple_of(place_ref[picks[i][u]] * BLOCK, BLOCK), BLOCK)
                acc_ref[place, head_cols[h]] += dkvs[i][u * BLOCK : (u + 1) * BLOCK]
        for u in range(unroll):
            rows = pl.ds(pl.multiple_of((it * unroll + u) * BLOCK, BLOCK), BLOCK)
            dq_ref[rows, :] = (jnp.concatenate(dqs[u * heads : (u + 1) * heads], axis=1) * scale).astype(bf16)
        return carry

    lax.fori_loop(0, blocks // unroll, some, 0)

    rows = pl.ds(pl.multiple_of(edge_of(coord_ref, blocks, per_span) * BLOCK, BLOCK), BLOCK)
    boths, dots, lses = of_rows(rows)

    def edge(c, dqs):
        items = [(i, h) for i in range(2) for h in range(heads)]
        parts = [pl.ds(pl.multiple_of((c * 2 + i) * CHUNK, CHUNK), CHUNK) for i in range(2)]
        masks = [
            mask_of(mask_ref, [nat_ref[(c * 2 + i) * PICKS + u] for u in range(PICKS)], left) for i in range(2)
        ]
        kvs = [kv_ref[parts[i], head_cols[h]] for i, h in items]
        prods = [dot_nt(boths[h], kvg) for (i, h), kvg in zip(items, kvs)]
        dss, lows = [], []
        for (i, h), prod in zip(items, prods):
            p = jnp.exp(prod[:BLOCK] + masks[i] - lses[h])
            dss.append((p * (prod[BLOCK:] - dots[h])).astype(bf16))
            lows.append(p.astype(bf16))
        adds = [dot_nn(ds, kvg) for ds, kvg in zip(dss, kvs)]
        dkvs = [dot_tn(jnp.concatenate([ds, p], axis=0), boths[h]) for (i, h), ds, p in zip(items, dss, lows)]
        for (i, h), dkv in zip(items, dkvs):
            acc_ref[parts[i], head_cols[h]] += dkv
        return tuple(dqs[h] + (adds[h] + adds[heads + h]) for h in range(heads))

    dqs = lax.fori_loop(0, chunks // 2, edge, tuple(jnp.zeros((BLOCK, wide), f32) for _ in range(heads)))
    dq_ref[rows, :] = (jnp.concatenate([dq[:, :hd] for dq in dqs], axis=1) * scale).astype(bf16)

    pair = 2 * span
    mine = {(n, src): at for at, n, src in query_pieces(pair)}
    leaving = [pltpu.make_async_copy(dq_ref, dq_out, out_sems.at[0])]
    leaving[0].start()
    arriving[-2].wait()
    arriving[-1].wait()
    moves = []
    for i, n in enumerate((2, 3, 6, 7, 0, 1, 4, 5)):
        kc = n // 2 % 2
        to = n % 2 * piece
        of = slice(n * piece, (n + 1) * piece)
        slot = i % 2
        if i >= 2:
            for copy in moves[i - 2]:
                copy.wait()
        dkv = acc_ref[of, :].astype(bf16)
        dkv_ref[slot] = dkv
        dx = dot_nt(dkv, w_kv_ref[...])
        for src in (0, pair):
            part = dx[src : src + pair]
            if (n, src) in mine:
                at = mine[n, src]
                part = part + dot_nt(dq_ref[at : at + pair, :], w_q_ref[...])
            dx_ref[slot, src : src + pair, :] = part.astype(bf16)
        dx_out = (far_out if kc else near_out).at[n // 4, to : to + piece]
        moves.append(
            [
                pltpu.make_async_copy(dkv_ref.at[slot], dkv_out.at[of], out_sems.at[1 + 2 * i]),
                pltpu.make_async_copy(dx_ref.at[slot], dx_out, out_sems.at[2 + 2 * i]),
            ]
        )
        for copy in moves[-1]:
            copy.start()
    for copy in (*leaving, *moves[-2], *moves[-1]):
        copy.wait()


def attend_back(heads, hd, span, coords, rand, q, d_os, os, kv, mask, lse, w_kv, w_q, orders):
    rows, keys = q.shape[0], kv.shape[0]
    width = w_kv.shape[0]
    piece = 4 * span
    return pl.pallas_call(
        functools.partial(attend_back_kernel, heads, hd, span, len(orders)),
        out_shape=(
            jax.ShapeDtypeStruct((rows, heads * hd), bf16),
            jax.ShapeDtypeStruct((keys, heads * 2 * hd), bf16),
        )
        + (jax.ShapeDtypeStruct((2, 2 * piece, width), bf16),) * 2,
        in_specs=[SMEM_SPEC] * 2 + [ANY_SPEC] * 11 + [VMEM_SPEC] + [ANY_SPEC] * len(orders),
        out_specs=(ANY_SPEC,) * 4,
        scratch_shapes=[
            pltpu.VMEM((keys, heads * 2 * hd), f32),
            pltpu.VMEM((rows, heads * hd), bf16),
            pltpu.VMEM((rows, heads * hd), bf16),
            pltpu.SMEM((keys // BLOCK,), jnp.int32),
            pltpu.SMEM((keys // BLOCK,), jnp.int32),
            pltpu.VMEM(q.shape, bf16),
            pltpu.VMEM(kv.shape, bf16),
            pltpu.VMEM(lse.shape, f32),
            pltpu.VMEM(w_kv.shape, bf16),
            pltpu.VMEM(w_q.shape, bf16),
            pltpu.VMEM((rows, heads * hd), bf16),
            pltpu.VMEM((2, piece, heads * 2 * hd), bf16),
            pltpu.VMEM((2, piece, width), bf16),
            pltpu.SemaphoreType.DMA((11,)),
            pltpu.SemaphoreType.DMA((17,)),
        ],
        compiler_params=params(60),
        cost_estimate=pl.CostEstimate(
            flops=60 << 30, bytes_accessed=24 << 20, transcendentals=rows * heads * CHUNK
        ),
        name="attend_back",
    )(coords, rand, q, *d_os, *os, kv, lse, w_kv, w_q, mask, *orders)


def split_low(value):
    top = value.astype(bf16)
    return jnp.concatenate([top, (value - top.astype(f32)).astype(bf16)], axis=0)


def joined(low):
    return low[:8].astype(f32) + low[8:16].astype(f32)


def qkv_grad_kernel(span, spot_ref, coord_ref, dq_ref, dkv_ref, keep_ref, got_ref, small_ref, *refs):
    x_refs, out_ref = refs[:8], refs[-1]
    piece = 4 * span
    n_kv = dkv_ref.shape[1]
    n_q = dq_ref.shape[1]
    rows, width = out_ref.shape[1], x_refs[0].shape[1]
    acc = jnp.zeros((n_kv, width), f32)
    acc_q = jnp.zeros((n_q, width), f32)
    for n, x_ref in enumerate(x_refs):
        acc = acc + dot_tn(dkv_ref[n * piece : (n + 1) * piece, :], x_ref[...])
    pair = 2 * span
    for at, n, src in query_pieces(pair):
        acc_q = acc_q + dot_tn(dq_ref[at : at + pair, :], x_refs[n][src : src + pair, :])
    out_ref[...] = jnp.zeros_like(out_ref)
    both = jnp.concatenate([acc, acc_q], axis=0)
    octets = [both[o * rows : (o + 1) * rows] for o in range(6)]
    w_out = keep_ref[4].astype(f32) + got_ref[4 * rows : 5 * rows, :].astype(f32)
    octets += [w_out[:, :width], w_out[:, width:]]
    sums = jnp.concatenate(
        [
            jnp.sum(dq_ref[...].astype(f32), axis=0, keepdims=True),
            jnp.sum(dkv_ref[...].astype(f32), axis=0, keepdims=True),
            jnp.zeros((1, 1024 - n_q - n_kv), f32),
        ],
        axis=1,
    )
    sums = jnp.concatenate([sums[:, i * 128 : (i + 1) * 128] for i in range(8)], axis=0)

    others = joined(got_ref[5 * rows :, :width])
    own = joined(split_low(small_ref[...]))
    small = own + others
    held = split_low(own + pltpu.roll(others, 7, 0))
    unit = lax.broadcasted_iota(jnp.int32, (width, width), 0)
    octet = unit // rows
    zq = (octet // 2 % 2 + octet % 2 * 2) ^ coord_ref[0]
    own_unit = (zq * 2 + (octet // 4 ^ coord_ref[1])) * rows + unit % rows
    turn = jnp.where(own_unit == lax.broadcasted_iota(jnp.int32, (width, width), 1), 1.0, 0.0).astype(bf16)
    b_in = joined(dot_nn(held, turn))[6:7]

    def lanes_down(row):
        parts = [row[:, i * 128 : (i + 1) * 128] for i in range(width // 128)]
        return jnp.concatenate(parts + [jnp.zeros((8 - width // 128, 128), f32)], axis=0)

    vectors = [lanes_down(small[i : i + 1]) for i in range(6)] + [lanes_down(b_in), sums]
    for o in range(8):
        spot = spot_ref[o]
        out_ref[spot, :, :width] = octets[o].astype(bf16)
        out_ref[spot, :16, width:] = split_low(vectors[o])


def qkv_grad(span, spots, coords, dq, dkv, keep, got, small, xs, orders):
    width = xs[0].shape[1]
    rows = (dq.shape[1] + dkv.shape[1]) // 6
    return pl.pallas_call(
        functools.partial(qkv_grad_kernel, span),
        out_shape=jax.ShapeDtypeStruct((8, rows, width + 128), bf16),
        in_specs=[SMEM_SPEC] * 2 + [VMEM_SPEC] * 13 + [ANY_SPEC] * len(orders),
        out_specs=VMEM_SPEC,
        compiler_params=params(60),
        cost_estimate=pl.CostEstimate(
            flops=14 << 30, bytes_accessed=12 << 20, transcendentals=0
        ),
        name="qkv_grad",
    )(spots, coords, dq, dkv, keep, got, small, *xs, *orders)


def wide_sum_kernel(order_ref, keep_ref, y_ref, x_ref, a_ref, b_ref, c_ref, d_ref, out_ref, top_ref, low_ref):
    rows = keep_ref.shape[1]
    half = rows // 2
    for i, out in enumerate((top_ref, low_ref)):
        of = slice(i * half, (i + 1) * half)
        out[...] = sum(r[of, :].astype(f32) for r in (a_ref, b_ref, c_ref, d_ref)).astype(bf16)
    for k in range(4):
        of = slice(k * rows, (k + 1) * rows)
        out_ref[order_ref[k]] = (keep_ref[k].astype(f32) + y_ref[of, :].astype(f32) + x_ref[k].astype(f32)).astype(bf16)


def wide_sum(order, keep, y_got, x_got, across):
    _, rows, cols = keep.shape
    four = pl.BlockSpec((4, rows, cols), lambda i: (0, 0, 0))
    octet = pl.BlockSpec((rows, cols), lambda i: (0, 0))
    half = pl.BlockSpec((rows // 2, cols), lambda i: (0, 0))
    return pl.pallas_call(
        wide_sum_kernel,
        grid=(1,),
        in_specs=[SMEM_SPEC, four, pl.BlockSpec((4 * rows, cols), lambda i: (0, 0)), four] + [octet] * 4,
        out_specs=(four, half, half),
        out_shape=(
            jax.ShapeDtypeStruct((4, rows, cols), bf16),
            jax.ShapeDtypeStruct((rows // 2, cols), bf16),
            jax.ShapeDtypeStruct((rows // 2, cols), bf16),
        ),
        compiler_params=params(60),
        cost_estimate=pl.CostEstimate(flops=1 << 28, bytes_accessed=6 << 20, transcendentals=0),
        name="wide_sum",
    )(order, keep, y_got, x_got, *across)


def tail_sum_kernel(n_orders, tail_ref, got_ref, *refs):
    out_refs = refs[n_orders:]
    thin = tail_ref.shape[2] - 128
    for k in range(4):
        out_refs[k][:, :thin] = (tail_ref[k, :, :thin].astype(f32) + got_ref[k, :, :thin].astype(f32)).astype(bf16)
        out_refs[k][:, thin:] = jnp.zeros((tail_ref.shape[1], 128), bf16)
        out_refs[k][:16, thin:] = split_low(joined(tail_ref[k, :16, thin:]) + joined(got_ref[k, :16, thin:]))


def tail_sum(tail, tail_got, orders):
    _, rows, cols = tail.shape
    return pl.pallas_call(
        functools.partial(tail_sum_kernel, len(orders)),
        out_shape=(jax.ShapeDtypeStruct((rows, cols), bf16),) * 4,
        in_specs=[VMEM_SPEC] * 2 + [ANY_SPEC] * len(orders),
        out_specs=(VMEM_SPEC,) * 4,
        compiler_params=params(60),
        cost_estimate=pl.CostEstimate(flops=1 << 28, bytes_accessed=2 << 20, transcendentals=0),
        name="tail_sum",
    )(tail, tail_got, *orders)


def wide_end_kernel(wide_ref, top_ref, low_ref, *refs):
    out_ref = refs[-1]
    half = top_ref.shape[0]
    for i, more_ref in enumerate((top_ref, low_ref)):
        of = slice(i * half, (i + 1) * half)
        out_ref[of, :] = (wide_ref[of, :].astype(f32) + more_ref[...].astype(f32)).astype(bf16)


def wide_end(wide, top, low, orders):
    return pl.pallas_call(
        wide_end_kernel,
        out_shape=jax.ShapeDtypeStruct(wide.shape, bf16),
        in_specs=[VMEM_SPEC] * 3 + [ANY_SPEC] * len(orders),
        out_specs=VMEM_SPEC,
        compiler_params=params(60),
        cost_estimate=pl.CostEstimate(flops=1 << 28, bytes_accessed=3 << 20, transcendentals=0),
        name="wide_end",
    )(wide, top, low, *orders)


def tail_end_kernel(*refs):
    thin_refs, out_ref = refs[:4], refs[-1]
    thin = out_ref.shape[1] - 128
    out_ref[:, :thin] = sum(r[:, :thin].astype(f32) for r in thin_refs).astype(bf16)
    out_ref[:, thin:] = jnp.zeros((out_ref.shape[0], 128), bf16)
    out_ref[:16, thin:] = split_low(sum(joined(r[:16, thin:]) for r in thin_refs))


def tail_end(thins, orders):
    return pl.pallas_call(
        tail_end_kernel,
        out_shape=jax.ShapeDtypeStruct(thins[0].shape, bf16),
        in_specs=[VMEM_SPEC] * 4 + [ANY_SPEC] * len(orders),
        out_specs=VMEM_SPEC,
        compiler_params=params(60),
        cost_estimate=pl.CostEstimate(flops=1 << 28, bytes_accessed=3 << 20, transcendentals=0),
        name="tail_end",
    )(*thins, *orders)


def tail_place_kernel(n_qkv, heads, spot_ref, *refs):
    ins, (qkv_ref, w_out_ref, small_ref, held_ref) = refs[:8], refs[-4:]
    rows = ins[0].shape[0]
    cols = held_ref.shape[1]
    for n in range(8):
        spot = spot_ref[n]
        held_ref[pl.ds(pl.multiple_of(spot * rows, 16), rows), :] = ins[n][:, :cols].astype(f32)
        small_ref[spot] = joined(ins[n][:16, cols:])
    w_out_ref[...] = held_ref[n_qkv:, :]
    hd = n_qkv // 3 // heads
    parts = []
    for h in range(heads):
        q_at, kv_at = 2 * heads * hd + h * hd, 2 * h * hd
        parts += [held_ref[q_at : q_at + hd, :], held_ref[kv_at : kv_at + 2 * hd, :]]
    qkv_ref[...] = jnp.concatenate(parts, axis=0).T


def tail_place(spots, parts, n_qkv, heads, orders):
    rows, cols = parts[0].shape
    width = cols - 128
    return pl.pallas_call(
        functools.partial(tail_place_kernel, n_qkv, heads),
        out_shape=(
            jax.ShapeDtypeStruct((width, n_qkv), f32),
            jax.ShapeDtypeStruct((8 * rows - n_qkv, width), f32),
            jax.ShapeDtypeStruct((8, 8, 128), f32),
        ),
        in_specs=[SMEM_SPEC] + [VMEM_SPEC] * 8 + [ANY_SPEC] * len(orders),
        out_specs=(VMEM_SPEC,) * 3,
        scratch_shapes=[pltpu.VMEM((8 * rows, width), f32)],
        compiler_params=params(60),
        cost_estimate=pl.CostEstimate(flops=1 << 28, bytes_accessed=3 << 20, transcendentals=0),
        name="tail_place",
    )(spots, *parts, *orders)


def split_kernel(n_orders, coord_ref, rows_ref, *refs):
    value = rows_ref[...].astype(f32)
    pieces = [value[:, s, :] for s in range(4)]
    z = coord_ref[0]
    for k, out in enumerate(refs[n_orders:]):
        low = jnp.where((z ^ k) % 2 == 0, pieces[0], pieces[1])
        high = jnp.where((z ^ k) % 2 == 0, pieces[2], pieces[3])
        out[...] = jnp.where((z ^ k) // 2 == 0, low, high).astype(bf16)


def split(coords, rows, orders=()):
    span, seqs, width = rows.shape
    return pl.pallas_call(
        functools.partial(split_kernel, len(orders)),
        out_shape=(jax.ShapeDtypeStruct((span, width), bf16),) * seqs,
        in_specs=[SMEM_SPEC, VMEM_SPEC] + [ANY_SPEC] * len(orders),
        out_specs=(VMEM_SPEC,) * seqs,
        compiler_params=params(32),
        cost_estimate=pl.CostEstimate(flops=1 << 20, bytes_accessed=1 << 20, transcendentals=0),
        name="split",
    )(coords, rows, *orders)


def qkv_weights_kernel(n_orders, w_ref, b_ref, *refs):
    kv_ref, q_pad_ref, q_ref, b_kv_ref, b_q_ref = refs[n_orders:]
    width, heads, _, hd = w_ref.shape
    wide = 2 * hd
    value = w_ref[...].astype(f32)
    nil = jnp.zeros((width, hd), f32)
    qs = []
    for h in range(heads):
        q, k, v = [value[:, h, c, :] for c in range(3)]
        cols = slice(h * wide, (h + 1) * wide)
        kv_ref[:, cols] = jnp.concatenate([k, v], axis=1).astype(bf16)
        q_pad_ref[:, cols] = jnp.concatenate([q, nil], axis=1).astype(bf16)
        b_kv_ref[:, cols] = jnp.concatenate([nil[:1], b_ref[h, 1:2, :]], axis=1)
        b_q_ref[:, cols] = jnp.concatenate([b_ref[h, 0:1, :], nil[:1]], axis=1)
        qs.append(q)
    q_ref[...] = jnp.concatenate(qs, axis=1).astype(bf16)


def qkv_weights(w_qkv, bias_qv, orders):
    width, heads, _, hd = w_qkv.shape
    cols = heads * 2 * hd
    return pl.pallas_call(
        functools.partial(qkv_weights_kernel, len(orders)),
        out_shape=(
            jax.ShapeDtypeStruct((width, cols), bf16),
            jax.ShapeDtypeStruct((width, cols), bf16),
            jax.ShapeDtypeStruct((width, heads * hd), bf16),
            jax.ShapeDtypeStruct((1, cols), f32),
            jax.ShapeDtypeStruct((1, cols), f32),
        ),
        in_specs=[VMEM_SPEC] * 2 + [ANY_SPEC] * len(orders),
        out_specs=(VMEM_SPEC,) * 5,
        compiler_params=params(40),
        cost_estimate=pl.CostEstimate(flops=1 << 20, bytes_accessed=1 << 20, transcendentals=0),
        name="qkv_weights",
    )(w_qkv, bias_qv, *orders)


def pack_kernel(n_orders, order_ref, up_ref, down_ref, w_out_ref, bias_ref, *refs):
    pack_ref, first_ref, out_ref, up_rows_ref = refs[n_orders:]
    width = up_ref.shape[0]
    eighth = down_ref.shape[0] // 8
    half = w_out_ref.shape[0] // 2
    for i in range(0, down_ref.shape[0], 256):
        up_rows_ref[i : i + 256, :] = up_ref[:, i : i + 256].astype(f32).T.astype(bf16)
    for ref in (pack_ref, out_ref):
        ref[:half, :width] = w_out_ref[:half, :]
        ref[:half, width:] = w_out_ref[half:, :]
        ref[half : half + 16, :width] = bias_ref[...]
        ref[half : half + 16, width:] = jnp.zeros((16, width), bf16)
    for n in range(8):
        src = pl.ds(pl.multiple_of(order_ref[n] * eighth, 16), eighth)
        for ref, at in ((pack_ref, half + 16), (first_ref, 0))[: 2 if n < 4 else 1]:
            to = slice(at + n * eighth, at + (n + 1) * eighth)
            ref[to, :width] = up_rows_ref[src, :]
            ref[to, width:] = down_ref[src, :]


def pack(order, up, down, w_out, bias, orders):
    hidden, width = down.shape
    rows = w_out.shape[0] // 2 + 16
    return pl.pallas_call(
        functools.partial(pack_kernel, len(orders)),
        out_shape=(
            jax.ShapeDtypeStruct((rows + hidden, 2 * width), bf16),
            jax.ShapeDtypeStruct((hidden // 2, 2 * width), bf16),
            jax.ShapeDtypeStruct((rows, 2 * width), bf16),
        ),
        in_specs=[SMEM_SPEC] + [VMEM_SPEC] * 4 + [ANY_SPEC] * len(orders),
        out_specs=(VMEM_SPEC,) * 3,
        scratch_shapes=[pltpu.VMEM((hidden, width), bf16)],
        compiler_params=params(32),
        cost_estimate=pl.CostEstimate(flops=1 << 20, bytes_accessed=1 << 20, transcendentals=0),
        name="pack",
    )(order, up, down, w_out, bias, *orders)


def rows_kernel(width, n_out, tile_rows, *refs):
    attn_refs, pack_refs = refs[:4], refs[4 : 4 + len(tile_rows)]
    refs = refs[4 + len(tile_rows) :]
    tok_refs, dres_refs, vec_ref = refs[:2], refs[2:6], refs[6]
    result_refs = refs[7:11]
    done_ref, hid_ref, dpre_ref, ylow_ref, dffn_ref, dbr_ref = refs[11:17]
    dattn_refs = refs[17:20]
    small_ref, bin_ref = refs[20:22]
    slope_ref = refs[22]
    bias_out, gain_one, bias_one, down_bias, gain_two, bias_two = [vec_ref[i : i + 1, :] for i in range(6)]
    step = pl.program_id(0)
    half = n_out // 2
    tiles, wos, biases = [], [], []
    for ref, (first, whole) in zip(pack_refs, tile_rows):
        if whole:
            wos.append(jnp.concatenate([ref[:half, :width], ref[:half, width:]], axis=0))
            biases.append(ref[half : half + 1, :width].astype(f32))
        left = ref.shape[0] - first
        if left == 0:
            continue
        size = min(left, width // 2)
        tiles += [ref.at[first + i * size : first + (i + 1) * size] for i in range(left // size)]
    up_bias = jnp.concatenate(biases, axis=1)

    def by_step(ones, twos):
        pairs = [jnp.where(step == 0, a[...].astype(f32), b[...].astype(f32)) for a, b in zip(ones, twos)]
        return pairs[0] if len(pairs) == 1 else jnp.concatenate(pairs, axis=0)

    @pl.when(pl.program_id(0) == 0)
    def _():
        small_ref[...] = jnp.zeros_like(small_ref)
        bin_ref[...] = jnp.zeros_like(bin_ref)

    branch = bias_out
    for k in range(4):
        branch = branch + dot_nn(attn_refs[k][...], wos[k])
    y_one, normed_one, inv_one = norm_fwd(by_step(tok_refs[:1], tok_refs[1:]) + branch, gain_one, bias_one)
    y_low = y_one.astype(bf16)
    ylow_ref[...] = y_low
    ffn = down_bias
    at = 0
    spans = []
    for tile in tiles:
        spans.append(slice(at, at + tile.shape[0]))
        at += tile.shape[0]
    for cols, tile in zip(spans, tiles):
        v = dot_nt(y_low, tile[:, :width]) + up_bias[:, cols]
        sq = v * v
        th = jnp.tanh(0.7978845608028654 * v * (1.0 + 0.044715 * sq))
        half = 0.5 * (1.0 + th)
        slope_ref[:, cols] = half + 0.5 * v * (1.0 - th * th) * (
            0.7978845608028654 * (1.0 + 3.0 * 0.044715 * sq)
        )
        hid = (v * half).astype(bf16)
        hid_ref[:, cols] = hid
        ffn = ffn + dot_nn(hid, tile[:, width:])
    result, normed_two, inv_two = norm_fwd(y_one + ffn, gain_two, bias_two)
    for s in range(2):

        @pl.when(step == s)
        def _(s=s):
            for k in range(2):
                ref = result_refs[s + 2 * k]
                ref[...] = result[k * ref.shape[0] : (k + 1) * ref.shape[0]].astype(bf16)

    d_two, g_gain_two, g_bias_two = norm_back(by_step(dres_refs[::2], dres_refs[1::2]), normed_two, inv_two, gain_two)
    d_ffn = d_two.astype(bf16)
    dffn_ref[...] = d_ffn
    g_bias_back = jnp.sum(d_ffn.astype(f32), axis=0)
    d_y = d_two
    for cols, tile in zip(spans, tiles):
        d_pre = (dot_nt(d_ffn, tile[:, width:]) * slope_ref[:, cols]).astype(bf16)
        dpre_ref[:, cols] = d_pre
        bin_ref[:, cols] += jnp.sum(d_pre.astype(f32), axis=0, keepdims=True)
        d_y = d_y + dot_nn(d_pre, tile[:, :width])
    d_one, g_gain_one, g_bias_one = norm_back(d_y, normed_one, inv_one, gain_one)
    done_ref[...] = d_one
    d_branch = d_one.astype(bf16)
    dbr_ref[...] = d_branch
    g_bias_out = jnp.sum(d_branch.astype(f32), axis=0)
    for k in range(4):
        d_attn = dot_nt(d_branch, wos[k]).astype(bf16)
        if k < 2:
            dattn_refs[k][...] = d_attn
        else:
            dattn_refs[2][k - 2] = d_attn
    sums = [g_bias_out, g_gain_one, g_bias_one, g_bias_back, g_gain_two, g_bias_two]
    for i, one in enumerate(sums):
        small_ref[i : i + 1, :] += one[None, :]


def rows_work(attns, packs, first_rows, toks, d_res, vecs):
    span, width = d_res[0].shape
    rows = 4 * span
    cols = attns[0].shape[1]
    hidden = sum(a.shape[0] - n for a, (n, _) in zip(packs, first_rows))
    tile = rows // 2

    def by_rows(n):
        return pl.BlockSpec((tile, n), lambda i: (i, 0))

    def whole(a):
        return pl.BlockSpec(a.shape, lambda i, nd=a.ndim: (0,) * nd, pipeline_mode=pl.Buffered(1))

    def fixed(shape):
        return pl.BlockSpec(shape, lambda i: (0, 0))

    low = functools.partial(jax.ShapeDtypeStruct, dtype=bf16)
    return pl.pallas_call(
        functools.partial(rows_kernel, width, cols, first_rows),
        grid=(rows // tile,),
        out_shape=(low((span, width)),) * 4
        + (
            jax.ShapeDtypeStruct((rows, width), f32),
            low((rows, hidden)),
            low((rows, hidden)),
            low((rows, width)),
            low((rows, width)),
            low((rows, width)),
            low((rows, cols)),
            low((rows, cols)),
            low((2, rows, cols)),
            jax.ShapeDtypeStruct((8, width), f32),
            jax.ShapeDtypeStruct((1, hidden), f32),
        ),
        in_specs=[by_rows(cols)] * 4 + [whole(a) for a in (*packs, *toks, *d_res, vecs)],
        out_specs=(fixed((span, width)),) * 4
        + (
            by_rows(width),
            by_rows(hidden),
            by_rows(hidden),
            by_rows(width),
            by_rows(width),
            by_rows(width),
            by_rows(cols),
            by_rows(cols),
            pl.BlockSpec((2, tile, cols), lambda i: (0, i, 0)),
            fixed((8, width)),
            fixed((1, hidden)),
        ),
        scratch_shapes=[pltpu.VMEM((tile, hidden), f32)],
        compiler_params=params(60),
        cost_estimate=pl.CostEstimate(flops=50 << 30, bytes_accessed=30 << 20, transcendentals=rows * hidden),
        name="rows_work",
    )(*attns, *packs, *toks, *d_res, vecs)


def small_rows(kc, small_ref, bin_ref):
    width = small_ref.shape[1]
    ends = [bin_ref[:, (ky * 2 + kc) * width : (ky * 2 + kc + 1) * width] for ky in range(2)]
    return jnp.concatenate([small_ref[:6, :]] + ends, axis=0)


def rows_grad_kernel(kc, n_orders, *refs):
    *sources, small_ref, bin_ref = refs[:9]
    refs = refs[9:]
    got_from = refs[0] if kc == 0 else None
    refs = refs[(1 if kc == 0 else 0) + n_orders :]
    n_outs = 1 if kc else 8
    outs, (ylow_ref, dpre_ref, hid_ref, dffn_ref, dbr_ref, attn0_ref, attn1_ref, held_ref, got_ref, low_ref) = (
        refs[:n_outs],
        refs[n_outs : n_outs + 10],
    )
    in_sems, got_sems, out_sems = refs[n_outs + 10 :]
    width = ylow_ref.shape[1]
    rows = ylow_ref.shape[0]
    part = width // 2
    eighth = held_ref.shape[1]

    def cols_of(n):
        at = ((n // 2) * 4 + kc * 2 + n % 2) * part
        return slice(at, at + part)

    pairs = [(sources[0], ylow_ref), (sources[3], dffn_ref)]
    for n in range(4):
        pairs.append((sources[1].at[:, cols_of(n)], dpre_ref.at[n]))
        pairs.append((sources[2].at[:, cols_of(n)], hid_ref.at[n]))
    pairs += [(sources[4], dbr_ref)]
    pairs += [(source.at[0:rows], ref) for source, ref in zip(sources[5:], (attn0_ref, attn1_ref))]
    arriving = [pltpu.make_async_copy(a, b, in_sems.at[i]) for i, (a, b) in enumerate(pairs)]
    gots = []
    if kc == 0:
        gots = [
            pltpu.make_async_copy(got_from.at[4 * n : 4 * n + 4], got_ref.at[4 * n : 4 * n + 4], got_sems.at[n])
            for n in range(5)
        ]
    for i, copy in enumerate(arriving):
        copy.start()
        if gots and i in (3, 5, 7, 9):
            gots[(i - 3) // 2].start()
    if gots:
        gots[4].start()
    arriving[0].wait()
    arriving[1].wait()
    leaving = []

    def leave(src, dst):
        leaving.append(pltpu.make_async_copy(src, dst, out_sems.at[len(leaving)]))
        leaving[-1].start()

    def put(at, k, lanes, value):
        if gots:
            value = value + got_ref[at + k, :, lanes].astype(f32)
        held_ref[at + k, :, lanes] = value.astype(bf16)

    left, right = slice(0, width), slice(width, 2 * width)
    for n in range(4):
        arriving[2 + 2 * n].wait()
        arriving[3 + 2 * n].wait()
        g_in = dot_tn(dpre_ref[n], ylow_ref[...])
        g_back = dot_tn(hid_ref[n], dffn_ref[...])
        if gots:
            gots[n].wait()
        for k in range(4):
            put(4 * n, k, left, g_in[k * eighth : (k + 1) * eighth])
            put(4 * n, k, right, g_back[k * eighth : (k + 1) * eighth])
        if kc:
            leave(held_ref.at[4 * n : 4 * n + 4], outs[0].at[4 * n : 4 * n + 4])
        elif n < 2:
            leave(held_ref.at[4 * n : 4 * n + 4], outs[2 * n].at[0:4])
        elif n == 2:
            for k in range(4):
                leave(held_ref.at[8 + k], outs[1].at[k * eighth : (k + 1) * eighth])
        else:
            for k in range(4):
                leave(held_ref.at[12 + k], outs[3 + k])
    for copy in arriving[10:]:
        copy.wait()
    if gots:
        gots[4].wait()
    for ky, attn_ref in enumerate((attn0_ref, attn1_ref)):
        g_out = dot_tn(attn_ref[...], dbr_ref[...])
        put(16, ky, left, g_out[:eighth])
        put(16, ky, right, g_out[eighth:])
    low_ref[...] = jnp.zeros_like(low_ref)
    if kc:
        low_ref[:16, :width] = split_low(small_rows(1, small_ref, bin_ref))
        leave(held_ref.at[16:18], outs[0].at[16:18])
        leave(low_ref, outs[0].at[18])
        leave(low_ref, outs[0].at[19])
    else:
        sums = joined(split_low(small_rows(0, small_ref, bin_ref))) + joined(got_ref[18, :16, :width])
        outs[7][...] = sums
        low_ref[:16, :width] = split_low(sums)
        leave(held_ref.at[16], outs[0].at[4])
        leave(held_ref.at[17], outs[1].at[4 * eighth : 5 * eighth])
        leave(low_ref.at[0:16], outs[1].at[5 * eighth : 5 * eighth + 16])
    for copy in leaving:
        copy.wait()


def rows_grad(kc, y_low, d_pre, hidden, d_ffn, d_branch, attn0, attn1, small, bin_sum, got=None, orders=()):
    rows, width = y_low.shape
    part = hidden.shape[1] // 8
    eighth = part // 4
    octet = (eighth, 2 * width)
    low = functools.partial(jax.ShapeDtypeStruct, dtype=bf16)
    if kc == 1:
        out_shape = (low((20,) + octet),)
        out_specs = (ANY_SPEC,)
    else:
        out_shape = (low((5,) + octet), low((5 * eighth + 16, 2 * width)), low((4,) + octet)) + (low(octet),) * 4
        out_shape += (jax.ShapeDtypeStruct((8, width), f32),)
        out_specs = (ANY_SPEC,) * 7 + (VMEM_SPEC,)
    extra = () if got is None else (got,)
    out = pl.pallas_call(
        functools.partial(rows_grad_kernel, kc, len(orders)),
        out_shape=out_shape,
        in_specs=[ANY_SPEC] * 7 + [VMEM_SPEC] * 2 + [ANY_SPEC] * (len(extra) + len(orders)),
        out_specs=out_specs,
        scratch_shapes=[
            pltpu.VMEM((rows, width), bf16),
            pltpu.VMEM((4, rows, part), bf16),
            pltpu.VMEM((4, rows, part), bf16),
            pltpu.VMEM((rows, width), bf16),
            pltpu.VMEM((rows, width), bf16),
            pltpu.VMEM((rows, attn0.shape[1]), bf16),
            pltpu.VMEM((rows, attn1.shape[1]), bf16),
            pltpu.VMEM((18,) + octet, bf16),
            pltpu.VMEM((20,) + octet, bf16),
            pltpu.VMEM(octet, bf16),
            pltpu.SemaphoreType.DMA((13,)),
            pltpu.SemaphoreType.DMA((5,)),
            pltpu.SemaphoreType.DMA((16,)),
        ],
        compiler_params=params(60),
        cost_estimate=pl.CostEstimate(flops=8 << 30, bytes_accessed=16 << 20, transcendentals=0),
        name="far_grad" if kc else "near_grad",
    )(y_low, d_pre, hidden, d_ffn, d_branch, attn0, attn1, small, bin_sum, *extra, *orders)
    return out[0] if kc else out


def row_sum_one_kernel(near_ref, got_ref, *refs):
    for i, out in enumerate(refs[-2:]):

        @pl.when(pl.program_id(0) == i)
        def _(out=out):
            out[...] = (near_ref[0].astype(f32) + got_ref[0].astype(f32)).astype(bf16)


def row_sum_one(near, got, orders):
    _, rows, width = near.shape
    far = pl.BlockSpec((1, rows // 2, width), lambda i: (i, 1, 0))
    return pl.pallas_call(
        row_sum_one_kernel,
        grid=(2,),
        out_shape=(jax.ShapeDtypeStruct((rows // 2, width), bf16),) * 2,
        in_specs=[far] * 2 + [ANY_SPEC] * len(orders),
        out_specs=(pl.BlockSpec((rows // 2, width), lambda i: (0, 0)),) * 2,
        compiler_params=params(60),
        cost_estimate=pl.CostEstimate(flops=1 << 28, bytes_accessed=6 << 20, transcendentals=0),
        name="row_sum_one",
    )(near, got, *orders)


def row_sum_two_kernel(near_ref, got_ref, even_ref, odd_ref, *refs):
    for i, (src, out) in enumerate(zip((even_ref, odd_ref), refs[-2:])):

        @pl.when(pl.program_id(0) == i)
        def _(src=src, out=out):
            out[...] = (near_ref[0].astype(f32) + got_ref[0].astype(f32) + src[...].astype(f32)).astype(bf16)


def row_sum_two(near, got, even, odd, orders):
    quarter, width = near.shape[1] // 4, near.shape[2]
    part = pl.BlockSpec((1, quarter, width), lambda i: (i, 1, 0))
    return pl.pallas_call(
        row_sum_two_kernel,
        grid=(2,),
        out_shape=(jax.ShapeDtypeStruct((quarter, width), bf16),) * 2,
        in_specs=[part] * 2 + [pl.BlockSpec((quarter, width), lambda i: (1, 0))] * 2 + [ANY_SPEC] * len(orders),
        out_specs=(pl.BlockSpec((quarter, width), lambda i: (0, 0)),) * 2,
        compiler_params=params(60),
        cost_estimate=pl.CostEstimate(flops=1 << 28, bytes_accessed=4 << 20, transcendentals=0),
        name="row_sum_two",
    )(near, got, even, odd, *orders)


def row_sum_three_kernel(near_ref, got_ref, even_ref, odd_ref, even_got, odd_got, done_ref, *out_refs):
    rows = near_ref.shape[1]
    for i, (one, two) in enumerate(((even_ref, even_got), (odd_ref, odd_got))):

        @pl.when(pl.program_id(0) == i)
        def _(i=i, one=one, two=two):
            total = (
                near_ref[0].astype(f32)
                + got_ref[0].astype(f32)
                + one[:rows, :].astype(f32)
                + two[:rows, :].astype(f32)
                + done_ref[...]
            ).astype(bf16)
            out_refs[i][...] = total[: rows // 2]
            out_refs[i + 2][...] = total[rows // 2 :]


def row_sum_three(near, got, even, odd, even_got, odd_got, d_one):
    quarter, width = near.shape[1] // 4, near.shape[2]
    part = pl.BlockSpec((1, quarter, width), lambda i: (i, 0, 0))
    first = pl.BlockSpec((quarter, width), lambda i: (0, 0))
    out = pl.BlockSpec((quarter // 2, width), lambda i: (0, 0))
    return pl.pallas_call(
        row_sum_three_kernel,
        grid=(2,),
        out_shape=(jax.ShapeDtypeStruct((quarter // 2, width), bf16),) * 4,
        in_specs=[part] * 2 + [first] * 4 + [pl.BlockSpec((quarter, width), lambda i: (i, 0))],
        out_specs=(out,) * 4,
        compiler_params=params(60),
        cost_estimate=pl.CostEstimate(flops=1 << 28, bytes_accessed=4 << 20, transcendentals=0),
        name="row_sum_three",
    )(near, got, even, odd, even_got, odd_got, d_one)


def plane_layer(
    tokens,
    w_qkv,
    bias_qv,
    w_out,
    bias_out,
    gain_one,
    bias_one,
    up_weight,
    up_bias_vector,
    down_weight,
    down_bias_vector,
    gain_two,
    bias_two,
    d_out,
    key_mask,
    rand_idx,
):
    z = lax.axis_index("sq")
    px = lax.axis_index("part")
    hy = lax.axis_index("hy")
    hc = lax.axis_index("hc")
    head = hy * 2 + hc
    span, seqs, width = tokens.shape
    heads, hd = w_qkv.shape[1], w_qkv.shape[3]
    n_o, n_kv = heads * hd, heads * 2 * hd
    hidden_dev = up_weight.shape[1]
    eighth = hidden_dev // 8
    length = key_mask.shape[1]
    blocks_all = length // BLOCK
    rows = seqs * span
    coords = jnp.stack([z, px, hy, hc]).astype(jnp.int32)
    octet = jnp.arange(8)

    def turn_octets(value):
        shape = value.shape
        value = flipped(value.reshape((2, 2, 2) + shape[1:]), z // 2, 0)
        return flipped(flipped(value, z % 2, 1), px, 2).reshape(shape)

    held_zd = octet // 2 % 2 + octet % 2 * 2
    held_order = ((held_zd ^ z) * 2 + ((octet // 4) ^ px)).astype(jnp.int32)
    bias_row = jnp.moveaxis(turn_octets(up_bias_vector.reshape(8, eighth)).reshape(2, 2, 2, eighth), (0, 2), (2, 0))
    bias_row = jnp.pad(bias_row.reshape(1, hidden_dev), ((0, 15), (0, 0)))
    n_wo = n_o // 2 + 16
    wf, wf_first, wo = pack(held_order, up_weight, down_weight, w_out.reshape(n_o, width), bias_row, [])
    wf_y = swap(wf_first, "hy", name="weight")
    wf_c = swap(wf, "hc", name="weight")

    raw = split(coords, tokens, [wf])
    tok = [raw[0]] + [swap(raw[k], "sq", k, name="tok") for k in range(1, 4)]
    w_kv, w_q_pad, w_q, b_kv, b_q = qkv_weights(w_qkv, bias_qv, raw)
    dres_raw = split(coords, d_out, raw)
    dres = [dres_raw[0]] + [swap(dres_raw[k], "sq", k, name="dres") for k in range(1, 4)]
    odd = after(jnp.concatenate([tok[1], tok[3]], axis=0), *tok, w_kv, wf_y, wf_c, *dres_raw)
    even = after(jnp.concatenate([tok[0], tok[2]], axis=0), *tok, w_kv, wf_y, wf_c, *dres_raw)
    even_x = swap(even, "part", name="tok")
    odd_y = swap(odd, "hy", name="tok")
    wo_y = swap(after(wo, odd), "hy", name="weight")
    even_near = after(jnp.concatenate([even, even_x], axis=0), odd_y, wo_y)
    odd_near = after(jnp.concatenate([odd, odd_y], axis=0), even_x)
    even_far = swap(even_near, "hy", name="tok")
    odd_far = swap(odd_near, "part", name="tok")
    mask_seq = lax.dynamic_index_in_dim(key_mask, z, 0, keepdims=False).reshape(blocks_all, BLOCK)
    mask = jnp.where(mask_seq == 1, 0.0, MASK_FILL).astype(f32)
    mask = jnp.pad(jnp.concatenate([mask, mask], axis=1), ((0, 8), (0, 0)), constant_values=MASK_FILL)
    rand = lax.dynamic_slice(rand_idx, (z, 0, head * heads, 0), (1, blocks_all, heads, 3)).reshape(-1)
    even_far = after(even_far, mask, rand, *dres[1:])
    xs = [even_near, even_far, swap(even_near, "hc", name="tok"), swap(even_far, "hc", name="tok")]
    xs += [odd_near, odd_far, swap(odd_near, "hc", name="tok"), swap(odd_far, "hc", name="tok")]
    vecs = jnp.stack([bias_out, gain_one, bias_one, down_bias_vector, gain_two, bias_two])
    vecs = jnp.pad(vecs, ((0, 2), (0, 0)))

    wf_yc = swap(wf_y, "hc", name="weight")
    wf_x = swap(wf_y, "part", name="weight")
    wo_yc = swap(wo_y, "hc", name="weight")

    o_near, o_far, lse, kv, q = project_and_attend(
        heads, hd, span, coords, rand, xs, w_kv, w_q_pad, b_kv, b_q, mask, []
    )
    attn_y = swap(o_far, "hy", name="attn")
    attn_c = swap(o_near[rows:], "hc", name="attn")
    attn_yc = swap(attn_y[rows:], "hc", name="attn")
    wf_x = after(wf_x, attn_c)
    wf_xc = swap(wf_x, "hc", name="weight")

    packs = [wf, wf_c, wo_y, wf_y, wf_x, wo_yc, wf_yc, wf_xc]
    first_rows = tuple((n, n > 0) for n in (n_wo, n_wo, n_wo, 0, 0, n_wo, 0, 0))
    out = rows_work([o_near, attn_c, attn_y, attn_yc], packs, first_rows, [even, odd], dres, vecs)
    result, (d_one, hidden, d_pre, y_low, d_ffn, d_branch, d_00, d_01, d_far, small, bin_sum) = out[:4], out[4:]

    d_y = swap(d_far, "hy", name="dattn")
    d_c = swap(d_01, "hc", name="dattn")
    d_yc = swap(d_y[1], "hc", name="dattn")

    other = rows_grad(1, y_low, d_pre, hidden, d_ffn, d_branch, attn_c, attn_yc, small, bin_sum)
    wide_got = swap(other, "hc", name="wide")
    res = [result[0]] + [swap(result[k], "sq", k, name="result") for k in range(1, 4)]
    keep, to_y, to_x, *across, small = rows_grad(
        0, y_low, d_pre, hidden, d_ffn, d_branch, o_near, attn_y, small, bin_sum, wide_got, [d_y, d_c]
    )
    y_got = swap(to_y, "hy", name="wide")
    x_got = swap(to_x, "part", name="wide")
    across_got = [swap(across[p], "sq", k, name="wide") for p, k in ((2, 1), (1, 2), (3, 3))]

    dq, dkv, dx, dx_far = attend_back(
        heads,
        hd,
        span,
        coords,
        rand,
        q,
        [d_00, d_c, d_y, d_yc],
        [o_near, o_far],
        kv,
        mask,
        lse,
        w_kv,
        w_q,
        [to_y, to_x, *across, *res[1:]],
    )
    dx_far = after(dx_far, y_got, x_got, *across_got)

    dx_got = swap(dx_far, "hc", name="dtok")
    octets = octet[:4]
    wide, top, low = wide_sum(
        ((octets // 2 + octets % 2 * 2) ^ z).astype(jnp.int32), keep, y_got, x_got, [across[0]] + across_got
    )
    sent = row_sum_one(dx, dx_got, [wide, top, low])
    wide = lax.psum_scatter(wide, "sq", scatter_dimension=0, tiled=True)[0]
    top, low = swap(top, "part", name="across"), swap(low, "hy", name="across")
    even_got, odd_got = swap(sent[0], "hy", name="dtok"), swap(sent[1], "part", name="dtok")

    zq, xq = octet // 2, octet % 2
    zd = zq ^ z
    spots = ((xq ^ px) * 4 + (zd % 2) * 2 + zd // 2).astype(jnp.int32)
    tail = qkv_grad(span, spots, coords, dq, dkv, keep, y_got, small, xs, [*sent])
    top, low = after(top, tail), after(low, tail)
    top, low = swap(top, "hy", name="across"), swap(low, "part", name="across")
    tail_got = swap(tail[4:], "part", name="tail")
    wide = wide_end(wide, top, low, [tail, even_got, odd_got])
    sent_two = row_sum_two(dx, dx_got, even_got, odd_got, [tail])
    wide = lax.all_gather(wide, SEQ, axis=0, tiled=True)
    even_got2, odd_got2 = swap(sent_two[0], "part", name="dtok"), swap(sent_two[1], "hy", name="dtok")
    thins = tail_sum(tail, tail_got, [*sent_two])
    thins = [thins[0]] + [swap(thins[p], "sq", k, name="tail") for p, k in ((2, 1), (1, 2), (3, 3))]
    back_sent = row_sum_three(dx, dx_got, even_got, odd_got, even_got2, odd_got2, d_one)
    back = [back_sent[0]] + [swap(back_sent[k], "sq", k, name="dtok") for k in range(1, 4)]

    back_spots = (((octet % 4) ^ z) * 2 + ((octet // 4) ^ px)).astype(jnp.int32)
    thin_held = tail_end(thins, [*back_sent])
    thin_held = [thin_held] + [swap(thin_held, "sq", k, name="tail") for k in range(1, 4)]
    thin_held += [swap(a, "part", name="tail") for a in thin_held]
    grad_w_in = jnp.transpose(wide[:, :width]).astype(f32)
    grad_w_back = wide[:, width:].astype(f32)
    thin, grad_w_out, small = tail_place(
        back_spots, thin_held, n_o + n_kv, heads, [grad_w_in, grad_w_back]
    )
    grad_w_out = grad_w_out.reshape(heads, hd, width)
    grad_w_qkv = thin.reshape(width, heads, 3, hd)
    small = small.reshape(8, 1024)
    grad_bias_qv = jnp.stack(
        [small[7, :n_o].reshape(heads, hd), small[7, n_o : n_o + n_kv].reshape(heads, 2, hd)[:, 1]], axis=1
    )
    small = small[:, :width]
    return (
        jnp.transpose(relative(jnp.stack(res), z), (1, 0, 2)),
        jnp.transpose(relative(jnp.stack(back), z), (1, 0, 2)),
        grad_w_qkv,
        grad_bias_qv,
        grad_w_out,
        small[0],
        small[1],
        small[2],
        grad_w_in,
        small[6],
        grad_w_back,
        small[3],
        small[4],
        small[5],
    )


def solution(mesh):
    seq_size, head_size = mesh.shape["seq"], mesh.shape["head"]

    def run(*args):
        seqs = args[0].shape[1]
        fine = Mesh(
            np.asarray(mesh.devices).reshape(seqs, seq_size // seqs, head_size // 2, 2),
            ("sq", "part", "hy", "hc"),
        )
        rows = P(("sq", "part", "hy", "hc"), None, None)
        span = args[0].shape[0] // (seq_size * head_size)
        fits = seqs == 4 and seq_size == 8 and head_size == 4 and span % BLOCK == 0
        layer = plane_layer if fits else general_layer
        placed = (
            rows,
            P(None, HEAD, None, None),
            P(HEAD, None, None),
            P(HEAD, None, None),
            P(),
            P(),
            P(),
            P(None, HEAD),
            P(HEAD),
            P(HEAD, None),
            P(),
            P(),
            P(),
            rows,
            P(),
            P(),
        )
        return jax.shard_map(
            layer,
            mesh=fine,
            in_specs=placed,
            out_specs=(
                rows,
                rows,
                P(None, HEAD, None, None),
                P(HEAD, None, None),
                P(HEAD, None, None),
                P(),
                P(),
                P(),
                P(None, HEAD),
                P(HEAD),
                P(HEAD, None),
                P(),
                P(),
                P(),
            ),
            check_vma=False,
        )(*args)

    return run
```

```python
import functools

import jax
import jax.numpy as jnp
import numpy as np
from jax import lax
from jax.experimental import pallas as pl
from jax.experimental.pallas import tpu as pltpu
from jax.sharding import Mesh
from jax.sharding import PartitionSpec as P

BLOCK = 64
PICKS = 8
CHUNK = 512
NORM_EPS = 1e-12
MASK_FILL = -1000000000.0

f32 = jnp.float32
bf16 = jnp.bfloat16

PLANE = ("part", "hy", "hc")
HEAD = ("hy", "hc")
SEQ = ("sq", "part")


def norm_fwd(resid, gain, shift):
    row_mean = jnp.mean(resid, axis=-1, keepdims=True)
    centred = resid - row_mean
    inv_std = lax.rsqrt(jnp.mean(centred * centred, axis=-1, keepdims=True) + NORM_EPS)
    normed = centred * inv_std
    return (normed * gain + shift, normed, inv_std)


def norm_back(upstream, normed, inv_std, gain):
    d_normed = upstream * gain
    d_resid = inv_std * (
        d_normed
        - jnp.mean(d_normed, axis=-1, keepdims=True)
        - normed * jnp.mean(d_normed * normed, axis=-1, keepdims=True)
    )
    return (d_resid, jnp.sum(upstream * normed, axis=0), jnp.sum(upstream, axis=0))


def tanh_gelu(values):
    return jax.nn.gelu(values, approximate=True)


def gelu_back(preactivation_values, upstream):
    return jax.vjp(tanh_gelu, preactivation_values)[1](upstream)[0]


def dot_nt(a, b):
    return lax.dot_general(a, b, (((1,), (1,)), ((), ())), preferred_element_type=f32)


def dot_nn(a, b):
    return lax.dot_general(a, b, (((1,), (0,)), ((), ())), preferred_element_type=f32)


def dot_tn(a, b):
    return lax.dot_general(a, b, (((0,), (0,)), ((), ())), preferred_element_type=f32)


def gathered(kv_ref, table_ref, base, cols):
    return jnp.concatenate(
        [
            kv_ref[pl.ds(pl.multiple_of(table_ref[base + u] * BLOCK, BLOCK), BLOCK), cols]
            for u in range(PICKS)
        ],
        axis=0,
    )


def lane_pick(values, lane):
    lanes = lax.broadcasted_iota(jnp.int32, values.shape, 1)
    return jnp.sum(jnp.where(lanes == lane, values, 0.0), axis=1, keepdims=True)


def attn_fwd_kernel(heads, hd, table_ref, edge_ref, q_ref, kv_ref, bias_ref, mask_ref, o_ref, lse_ref, s_ref):
    wide = 2 * hd
    blocks = q_ref.shape[0] // BLOCK
    chunks = kv_ref.shape[0] // CHUNK
    lanes = lax.broadcasted_iota(jnp.int32, (BLOCK, 128), 1)

    def one(jl, carry):
        rows = pl.ds(pl.multiple_of(jl * BLOCK, BLOCK), BLOCK)
        outs = []
        lse_tile = jnp.zeros((BLOCK, 128), f32)
        for h in range(heads):
            cols = slice(h * wide, (h + 1) * wide)
            kvg = gathered(kv_ref, table_ref, (jl * heads + h) * PICKS, cols)
            s = dot_nt(q_ref[rows, cols], kvg) + bias_ref[jl, h : h + 1, :]
            top = jnp.max(s, axis=1, keepdims=True)
            p = jnp.exp(s - top)
            total = jnp.sum(p, axis=1, keepdims=True)
            low = (p * (1.0 / total)).astype(bf16)
            outs.append(dot_nn(low, kvg)[:, hd:])
            lse_tile = jnp.where(lanes == h, top + jnp.log(total), lse_tile)
        o_ref[rows, :] = jnp.concatenate(outs, axis=1).astype(bf16)
        lse_ref[rows, :] = lse_tile
        return carry

    lax.fori_loop(0, blocks, one, 0)

    def edge(jl):
        rows = slice(jl * BLOCK, (jl + 1) * BLOCK)
        outs = []
        lse_tile = jnp.zeros((BLOCK, 128), f32)
        for h in range(heads):
            cols = slice(h * wide, (h + 1) * wide)
            q = q_ref[rows, cols]

            def score(c, top):
                part = pl.ds(pl.multiple_of(c * CHUNK, CHUNK), CHUNK)
                s = dot_nt(q, kv_ref[part, cols]) + mask_ref[:, part]
                s_ref[:, part] = s
                return jnp.maximum(top, jnp.max(s, axis=1, keepdims=True))

            top = lax.fori_loop(0, chunks, score, jnp.full((BLOCK, 1), -3e38, f32))

            def add(c, total):
                part = pl.ds(pl.multiple_of(c * CHUNK, CHUNK), CHUNK)
                return total + jnp.sum(jnp.exp(s_ref[:, part] - top), axis=1, keepdims=True)

            total = lax.fori_loop(0, chunks, add, jnp.zeros((BLOCK, 1), f32))
            inv = 1.0 / total

            def out(c, acc):
                part = pl.ds(pl.multiple_of(c * CHUNK, CHUNK), CHUNK)
                low = (jnp.exp(s_ref[:, part] - top) * inv).astype(bf16)
                return acc + dot_nn(low, kv_ref[part, cols])

            acc = lax.fori_loop(0, chunks, out, jnp.zeros((BLOCK, wide), f32))
            outs.append(acc[:, hd:])
            lse_tile = jnp.where(lanes == h, top + jnp.log(total), lse_tile)
        o_ref[rows, :] = jnp.concatenate(outs, axis=1).astype(bf16)
        lse_ref[rows, :] = lse_tile

    @pl.when(edge_ref[0] == 1)
    def _():
        edge(0)

    @pl.when(edge_ref[1] == 1)
    def _():
        edge(blocks - 1)


def attn_bwd_kernel(
    heads, hd, scale, table_ref, edge_ref, qd_ref, kv_ref, bias_ref, mask_ref, lse_ref, dq_ref, dkv_ref, acc_ref, p_ref, dp_ref
):
    wide = 2 * hd
    blocks = qd_ref.shape[0] // BLOCK
    chunks = kv_ref.shape[0] // CHUNK
    left = lax.broadcasted_iota(jnp.int32, (BLOCK, wide), 1) < hd
    nil = jnp.zeros((BLOCK, wide), bf16)

    def clear(c, carry):
        part = pl.ds(pl.multiple_of(c * CHUNK, CHUNK), CHUNK)
        acc_ref[part, :] = jnp.zeros((CHUNK, heads * wide), f32)
        return carry

    lax.fori_loop(0, chunks, clear, 0)

    def stacked(qd):
        return jnp.concatenate([jnp.where(left, qd, nil), jnp.where(left, nil, qd)], axis=0)

    def one(jl, carry):
        rows = pl.ds(pl.multiple_of(jl * BLOCK, BLOCK), BLOCK)
        lse_tile = lse_ref[rows, :]
        outs = []
        for h in range(heads):
            cols = slice(h * wide, (h + 1) * wide)
            base = (jl * heads + h) * PICKS
            kvg = gathered(kv_ref, table_ref, base, cols)
            both = stacked(qd_ref[rows, cols])
            prod = dot_nt(both, kvg)
            p = jnp.exp(prod[:BLOCK] + bias_ref[jl, h : h + 1, :] - lane_pick(lse_tile, h))
            dp = prod[BLOCK:]
            dot_row = jnp.sum(p * dp, axis=1, keepdims=True)
            ds = (p * (dp - dot_row)).astype(bf16)
            outs.append(dot_nn(ds, kvg)[:, :hd])
            dkv = dot_tn(jnp.concatenate([ds, p.astype(bf16)], axis=0), both)
            for u in range(PICKS):
                place = pl.ds(pl.multiple_of(table_ref[base + u] * BLOCK, BLOCK), BLOCK)
                acc_ref[place, cols] += dkv[u * BLOCK : (u + 1) * BLOCK]
        dq_ref[rows, :] = (jnp.concatenate(outs, axis=1) * scale).astype(bf16)
        return carry

    lax.fori_loop(edge_ref[0], blocks - edge_ref[1], one, 0)

    def edge(jl):
        rows = slice(jl * BLOCK, (jl + 1) * BLOCK)
        lse_tile = lse_ref[rows, :]
        outs = []
        for h in range(heads):
            cols = slice(h * wide, (h + 1) * wide)
            both = stacked(qd_ref[rows, cols])
            lse = lane_pick(lse_tile, h)

            def first(c, total):
                part = pl.ds(pl.multiple_of(c * CHUNK, CHUNK), CHUNK)
                prod = dot_nt(both, kv_ref[part, cols])
                p = jnp.exp(prod[:BLOCK] + mask_ref[:, part] - lse)
                dp = prod[BLOCK:]
                p_ref[:, part] = p
                dp_ref[:, part] = dp
                return total + jnp.sum(p * dp, axis=1, keepdims=True)

            dot_row = lax.fori_loop(0, chunks, first, jnp.zeros((BLOCK, 1), f32))

            def second(c, dq):
                part = pl.ds(pl.multiple_of(c * CHUNK, CHUNK), CHUNK)
                p = p_ref[:, part]
                ds = (p * (dp_ref[:, part] - dot_row)).astype(bf16)
                acc_ref[part, cols] += dot_tn(jnp.concatenate([ds, p.astype(bf16)], axis=0), both)
                return dq + dot_nn(ds, kv_ref[part, cols])

            dq = lax.fori_loop(0, chunks, second, jnp.zeros((BLOCK, wide), f32))
            outs.append(dq[:, :hd])
        dq_ref[rows, :] = (jnp.concatenate(outs, axis=1) * scale).astype(bf16)

    @pl.when(edge_ref[0] == 1)
    def _():
        edge(0)

    @pl.when(edge_ref[1] == 1)
    def _():
        edge(blocks - 1)

    def put(c, carry):
        part = pl.ds(pl.multiple_of(c * CHUNK, CHUNK), CHUNK)
        dkv_ref[part, :] = acc_ref[part, :].astype(bf16)
        return carry

    lax.fori_loop(0, chunks, put, 0)


SMEM_SPEC = pl.BlockSpec(memory_space=pltpu.SMEM)
VMEM_SPEC = pl.BlockSpec(memory_space=pltpu.VMEM)
VMEM_LIMIT = 48 * 1024 * 1024


def attn_forward(heads, hd, table, edges, q, kv, bias, mask):
    rows, keys = q.shape[0], kv.shape[0]
    return pl.pallas_call(
        functools.partial(attn_fwd_kernel, heads, hd),
        out_shape=(
            jax.ShapeDtypeStruct((rows, heads * hd), bf16),
            jax.ShapeDtypeStruct((rows, 128), f32),
        ),
        in_specs=[SMEM_SPEC] * 2 + [VMEM_SPEC] * 4,
        out_specs=(VMEM_SPEC, VMEM_SPEC),
        scratch_shapes=[pltpu.VMEM((BLOCK, keys), f32)],
        compiler_params=pltpu.CompilerParams(vmem_limit_bytes=VMEM_LIMIT),
        cost_estimate=pl.CostEstimate(
            flops=4 * rows * heads * CHUNK * 2 * hd, bytes_accessed=8 << 20, transcendentals=rows * heads * CHUNK
        ),
        name="attn_forward",
    )(table, edges, q, kv, bias, mask)


def attn_backward(heads, hd, scale, table, edges, qd, kv, bias, mask, lse):
    rows, keys = qd.shape[0], kv.shape[0]
    return pl.pallas_call(
        functools.partial(attn_bwd_kernel, heads, hd, scale),
        out_shape=(
            jax.ShapeDtypeStruct((rows, heads * hd), bf16),
            jax.ShapeDtypeStruct((keys, heads * 2 * hd), bf16),
        ),
        in_specs=[SMEM_SPEC] * 2 + [VMEM_SPEC] * 5,
        out_specs=(VMEM_SPEC, VMEM_SPEC),
        scratch_shapes=[
            pltpu.VMEM((keys, heads * 2 * hd), f32),
            pltpu.VMEM((BLOCK, keys), f32),
            pltpu.VMEM((BLOCK, keys), f32),
        ],
        compiler_params=pltpu.CompilerParams(vmem_limit_bytes=VMEM_LIMIT),
        cost_estimate=pl.CostEstimate(
            flops=10 * rows * heads * CHUNK * 2 * hd, bytes_accessed=12 << 20, transcendentals=rows * heads * CHUNK
        ),
        name="attn_backward",
    )(table, edges, qd, kv, bias, mask, lse)


def general_layer(
    tokens,
    w_qkv,
    bias_qv,
    w_out,
    bias_out,
    gain_one,
    bias_one,
    up_weight,
    up_bias_vector,
    down_weight,
    down_bias_vector,
    gain_two,
    bias_two,
    d_out,
    key_mask,
    rand_idx,
):
    sq = lax.axis_index("sq")
    part = lax.axis_index("part")
    head = lax.axis_index(HEAD)
    parts = lax.axis_size("part")
    groups = lax.axis_size(HEAD)
    span, seqs, width = tokens.shape
    heads, hd = w_qkv.shape[1], w_qkv.shape[3]
    scale = hd ** (-0.5)
    length = key_mask.shape[1]
    blocks_all = length // BLOCK
    per_chunk = groups * span // BLOCK
    mine = seqs * per_chunk

    tok = lax.all_to_all(jnp.transpose(tokens, (1, 0, 2)), "sq", 0, 0, tiled=True)
    x_all = lax.all_gather(tok, PLANE, axis=0, tiled=False)
    d_res = lax.all_to_all(jnp.transpose(d_out, (1, 0, 2)), "sq", 0, 0, tiled=True)

    w_out_full = lax.all_gather(w_out.reshape(heads * hd, width), HEAD, axis=0, tiled=False)
    up_full = lax.all_gather(up_weight, HEAD, axis=0, tiled=False)
    down_full = lax.all_gather(down_weight, HEAD, axis=0, tiled=False)
    up_bias_full = lax.all_gather(up_bias_vector.astype(f32), HEAD, axis=0, tiled=False)

    chunk_ids = jnp.arange(seqs) * parts + part
    block_ids = (chunk_ids[:, None] * per_chunk + jnp.arange(per_chunk)[None, :]).reshape(mine)
    rand_seq = lax.dynamic_index_in_dim(rand_idx, sq, 0, keepdims=False)
    rand_head = lax.dynamic_slice_in_dim(rand_seq, head * heads, heads, 1)
    chosen = jnp.take(rand_head, block_ids, axis=0)
    window = block_ids[:, None] + jnp.arange(-1, 2)[None, :]
    window_ok = (window >= 1) & (window <= blocks_all - 2)
    fixed_ids = jnp.concatenate(
        [
            jnp.clip(window, 0, blocks_all - 1),
            jnp.broadcast_to(jnp.array([0, blocks_all - 1], jnp.int32), (mine, 2)),
        ],
        axis=1,
    )
    fixed_ok = jnp.concatenate([window_ok, jnp.ones((mine, 2), bool)], axis=1)
    table = jnp.concatenate(
        [jnp.broadcast_to(fixed_ids[:, None, :], (mine, heads, 5)), chosen], axis=2
    )
    table_ok = jnp.concatenate(
        [
            jnp.broadcast_to(fixed_ok[:, None, :], (mine, heads, 5)),
            jnp.ones((mine, heads, PICKS - 5), bool),
        ],
        axis=2,
    )
    mask_seq = lax.dynamic_index_in_dim(key_mask, sq, 0, keepdims=False)
    mask_blocks = (mask_seq == 1).reshape(blocks_all, BLOCK).astype(bf16)
    onehot = (table[..., None] == jnp.arange(blocks_all)).astype(bf16) * table_ok[..., None].astype(bf16)
    allowed = jnp.einsum("jhub,bk->jhuk", onehot, mask_blocks, preferred_element_type=f32)
    bias_rows = ((1.0 - allowed) * MASK_FILL).reshape(mine, heads, PICKS * BLOCK)
    mask_row = jnp.where(mask_seq == 1, 0.0, MASK_FILL).astype(f32).reshape(1, length)
    edges = jnp.stack([part == 0, part == parts - 1]).astype(jnp.int32)
    table = table.reshape(-1).astype(jnp.int32)

    w_kv = w_qkv[:, :, 1:].reshape(width, heads * 2 * hd)
    bias_kv = jnp.stack([jnp.zeros((heads, hd), f32), bias_qv[:, 1]], axis=1).reshape(heads * 2 * hd)
    w_q = w_qkv[:, :, 0].reshape(width, heads * hd)
    bias_q = bias_qv[:, 0].reshape(heads * hd)
    x_rows = x_all.reshape(parts, groups, seqs, span, width)
    x_mine = lax.dynamic_index_in_dim(x_rows, part, 0, keepdims=False)
    kv_rows = (jnp.einsum("pgzsd,dc->pgzsc", x_rows, w_kv, preferred_element_type=f32) + bias_kv).astype(bf16)
    kv = jnp.transpose(kv_rows, (2, 0, 1, 3, 4)).reshape(length, heads * 2 * hd)
    q_rows = (jnp.einsum("gzsd,dc->gzsc", x_mine, w_q, preferred_element_type=f32) + bias_q).astype(bf16)
    q_low = jnp.transpose(q_rows, (1, 0, 2, 3)).reshape(mine * BLOCK, heads, hd) * bf16(scale)
    q_pad = jnp.concatenate([q_low, jnp.zeros_like(q_low)], axis=-1).reshape(mine * BLOCK, heads * 2 * hd)

    attn_mine, lse = attn_forward(heads, hd, table, edges, q_pad, kv, bias_rows, mask_row)
    attn_send = jnp.transpose(attn_mine.reshape(seqs, groups, span, heads * hd), (1, 0, 2, 3))
    attn = lax.all_to_all(attn_send, HEAD, 0, 0, tiled=True).reshape(groups, seqs * span, heads * hd)

    rows = seqs * span
    tok_rows = tok.reshape(rows, width)
    branch = jnp.einsum("grc,gcd->rd", attn, w_out_full, preferred_element_type=f32) + bias_out
    y_one, normed_one, inv_one = norm_fwd(tok_rows.astype(f32) + branch, gain_one, bias_one)
    y_low = y_one.astype(bf16)
    pre = jnp.einsum("rd,gdf->grf", y_low, up_full, preferred_element_type=f32) + up_bias_full[:, None, :]
    hidden = tanh_gelu(pre).astype(bf16)
    ffn = jnp.einsum("grf,gfd->rd", hidden, down_full, preferred_element_type=f32) + down_bias_vector
    result, normed_two, inv_two = norm_fwd(y_one + ffn, gain_two, bias_two)
    result = lax.all_to_all(result.astype(bf16).reshape(seqs, span, width), "sq", 0, 0, tiled=True)
    d_two, grad_gain_two, grad_bias_two = norm_back(
        d_res.reshape(rows, width).astype(f32), normed_two, inv_two, gain_two
    )
    d_ffn = d_two.astype(bf16)
    grad_bias_back = jnp.sum(d_ffn.astype(f32), axis=0)
    d_hidden = jnp.einsum("rd,gfd->grf", d_ffn, down_full, preferred_element_type=f32)
    d_pre = gelu_back(pre, d_hidden).astype(bf16)
    d_y_ffn = jnp.einsum("grf,gdf->rd", d_pre, up_full, preferred_element_type=f32)
    grad_w_in = jnp.einsum("rd,grf->gdf", y_low, d_pre, preferred_element_type=f32).astype(bf16)
    grad_bias_in = jnp.sum(d_pre.astype(f32), axis=1)
    grad_w_back = jnp.einsum("grf,rd->gfd", hidden, d_ffn, preferred_element_type=f32).astype(bf16)
    d_one, grad_gain_one, grad_bias_one = norm_back(d_two + d_y_ffn, normed_one, inv_one, gain_one)
    d_branch = d_one.astype(bf16)
    grad_bias_out = jnp.sum(d_branch.astype(f32), axis=0)
    d_attn = jnp.einsum("rd,gcd->grc", d_branch, w_out_full, preferred_element_type=f32).astype(bf16)
    grad_w_out = jnp.einsum("grc,rd->gcd", attn, d_branch, preferred_element_type=f32).astype(bf16)

    d_attn_mine = lax.all_to_all(d_attn.reshape(groups, seqs, span, heads * hd), HEAD, 0, 0, tiled=True)
    d_attn_nat = jnp.transpose(d_attn_mine, (1, 0, 2, 3)).reshape(mine * BLOCK, heads, hd)
    qd = jnp.concatenate([q_low, d_attn_nat], axis=-1).reshape(mine * BLOCK, heads * 2 * hd)

    wide_part = jnp.concatenate([grad_w_in, grad_w_back, grad_w_out], axis=1)
    wide_sum = lax.psum_scatter(wide_part, HEAD, scatter_dimension=0, tiled=True)[0]
    wide_sum = lax.psum(wide_sum, SEQ)

    dq, dkv = attn_backward(heads, hd, scale, table, edges, qd, kv, bias_rows, mask_row, lse)
    dkv_rows = jnp.transpose(
        dkv.reshape(seqs, parts, groups, span, heads * 2 * hd), (1, 2, 0, 3, 4)
    )
    dq_rows = jnp.transpose(dq.reshape(seqs, groups, span, heads * hd), (1, 0, 2, 3))
    dq_all = lax.dynamic_update_index_in_dim(
        jnp.zeros((parts, groups, seqs, span, heads * hd), bf16), dq_rows, part, 0
    )
    d_x = jnp.einsum("pgzsc,dc->pgzsd", dkv_rows, w_kv, preferred_element_type=f32) + jnp.einsum(
        "pgzsc,dc->pgzsd", dq_all, w_q, preferred_element_type=f32
    )
    d_x = lax.psum_scatter(
        d_x.astype(bf16).reshape(parts * groups, seqs, span, width), PLANE, scatter_dimension=0, tiled=True
    )
    d_tok = (d_one + d_x.reshape(rows, width).astype(f32)).astype(bf16)
    d_tok = lax.all_to_all(d_tok.reshape(seqs, span, width), "sq", 0, 0, tiled=True)

    grad_kv = jnp.einsum("pgzsd,pgzsc->dc", x_rows, dkv_rows, preferred_element_type=f32)
    grad_q = jnp.einsum("gzsd,gzsc->dc", x_mine, dq_rows, preferred_element_type=f32)
    grad_w_qkv = jnp.concatenate(
        [grad_q.reshape(width, heads, 1, hd), grad_kv.reshape(width, heads, 2, hd)], axis=2
    )
    bias_q_sum = jnp.sum(dq_rows.astype(f32), axis=(0, 1, 2)).reshape(heads, 1, hd)
    bias_v_sum = jnp.sum(dkv_rows.astype(f32), axis=(0, 1, 2, 3)).reshape(heads, 2, hd)[:, 1:]
    grad_bias_qv = jnp.concatenate([bias_q_sum, bias_v_sum], axis=1)
    grad_w_qkv = lax.psum(grad_w_qkv.astype(bf16), SEQ).astype(f32)

    small = jnp.stack(
        [grad_bias_out, grad_gain_one, grad_bias_one, grad_bias_back, grad_gain_two, grad_bias_two]
    )
    all_bias_in = grad_bias_in
    bias_qv_all = lax.dynamic_update_index_in_dim(
        jnp.zeros((groups, heads * 2 * hd), f32), grad_bias_qv.reshape(-1), head, 0
    )
    packed = jnp.concatenate([small.reshape(-1), all_bias_in.reshape(-1), bias_qv_all.reshape(-1)])
    packed = lax.psum(packed, ("sq", "part", "hy", "hc"))
    n_small = 6 * width
    small = packed[:n_small].reshape(6, width)
    n_in = n_small + all_bias_in.size
    hidden_dev = up_weight.shape[1]
    grad_bias_in = lax.dynamic_slice_in_dim(packed[n_small:n_in], head * hidden_dev, hidden_dev, 0)
    grad_bias_qv = lax.dynamic_slice_in_dim(
        packed[n_in:], head * heads * 2 * hd, heads * 2 * hd, 0
    ).reshape(heads, 2, hd)

    wide_sum = wide_sum.astype(f32)
    grad_w_in = wide_sum[:width]
    grad_w_back = wide_sum[width : width + hidden_dev]
    grad_w_out = wide_sum[width + hidden_dev :].reshape(heads, hd, width)
    return (
        jnp.transpose(result, (1, 0, 2)),
        jnp.transpose(d_tok, (1, 0, 2)),
        grad_w_qkv,
        grad_bias_qv,
        grad_w_out,
        small[0],
        small[1],
        small[2],
        grad_w_in,
        grad_bias_in,
        grad_w_back,
        small[3],
        small[4],
        small[5],
    )


def swap(value, axis, step=1, name="swap"):
    size = lax.axis_size(axis)
    with jax.named_scope(name + "_" + axis + str(step)):
        return lax.ppermute(value, axis, [(i, i ^ step) for i in range(size)])


def flipped(value, bit, axis):
    return jnp.where(bit == 1, jnp.flip(value, axis), value)


def relative(value, place):
    shape = value.shape
    value = value.reshape((2, 2) + shape[1:])
    value = flipped(flipped(value, place // 2, 0), place % 2, 1)
    return value.reshape(shape)


def swap_both(value, name):
    order = [(i, i ^ 3) for i in range(4)]
    with jax.named_scope(name + "_both"):
        return lax.ppermute(value, ("part", "hy"), order)


ANY_SPEC = pl.BlockSpec(memory_space=pl.ANY)


def after(value, *orders):
    return pl.pallas_call(
        lambda *refs: None,
        out_shape=jax.ShapeDtypeStruct(value.shape, value.dtype),
        in_specs=[ANY_SPEC] * (1 + len(orders)),
        out_specs=ANY_SPEC,
        input_output_aliases={0: 0},
        name="after",
    )(value, *orders)


def params(limit_mb):
    return pltpu.CompilerParams(vmem_limit_bytes=limit_mb * 1024 * 1024)


def fill_tables(coord_ref, rand_ref, place_ref, nat_ref, heads, span):
    per_span = span // BLOCK

    def one(b, carry):
        own = b // per_span
        kz = (own // 8) ^ coord_ref[0]
        kx = (own // 4 % 2) ^ coord_ref[1]
        ky = (own // 2 % 2) ^ coord_ref[2]
        kc = (own % 2) ^ coord_ref[3]
        odd = kz % 2
        one, two = jnp.where(odd == 0, kx, ky), jnp.where(odd == 0, ky, kx)
        spot = ((((odd * 2 + kc) * 2 + two) * 2 + one) * 2 + kz // 2) * per_span + b % per_span
        place_ref[b] = spot
        nat_ref[spot] = b
        return carry

    lax.fori_loop(0, place_ref.shape[0], one, 0)


def natural_block(coord_ref, jl, per_span):
    kz = (jl // per_span % 2 * 2 + jl // (per_span * 2) % 2) ^ coord_ref[0]
    kc = jl // (per_span * 4) % 2 ^ coord_ref[3]
    ky = jl // (per_span * 8) ^ coord_ref[2]
    return (((kz * 2 + coord_ref[1]) * 2 + ky) * 2 + kc) * per_span + jl % per_span


def edge_of(coord_ref, blocks, per_span):
    last = coord_ref[1]
    kz = (last * 3) ^ coord_ref[0]
    ky = last ^ coord_ref[2]
    kc = last ^ coord_ref[3]
    return ((ky * 2 + kc) * 4 + kz % 2 * 2 + kz // 2) * per_span + last * (per_span - 1)


def picks_of(coord_ref, rand_ref, jl, h, heads, per_span, blocks_all):
    b = natural_block(coord_ref, jl, per_span)
    inner = (b > 0) & (b < blocks_all - 1)
    ids, rows = [], []
    for u in range(3):
        key = b + u - 1
        ids.append(jnp.clip(key, 0, blocks_all - 1))
        rows.append(jnp.where(inner & (key >= 1) & (key <= blocks_all - 2), key, blocks_all))
    for key in (0, blocks_all - 1):
        ids.append(key)
        rows.append(jnp.where(inner, key, blocks_all))
    for u in range(3):
        key = rand_ref[(b * heads + h) * 3 + u]
        ids.append(key)
        rows.append(jnp.where(inner, key, blocks_all))
    return ids, rows


def mask_of(mask_ref, rows, left):
    pairs = []
    for u in range(0, len(rows), 2):
        a, b = mask_ref[pl.ds(rows[u], 1), :], mask_ref[pl.ds(rows[u + 1], 1), :]
        pairs.append(jnp.where(left, a, b))
    return jnp.concatenate(pairs, axis=1)


def blocks_of(kv_ref, place_ref, ids, cols):
    return jnp.concatenate(
        [kv_ref[pl.ds(pl.multiple_of(place_ref[b] * BLOCK, BLOCK), BLOCK), cols] for b in ids], axis=0
    )


def query_pieces(pair):
    out = []
    for ky in range(2):
        for kc in range(2):
            at = (ky * 2 + kc) * 2 * pair
            out.append((at, kc * 2 + ky, 0))
            out.append((at + pair, 4 + kc * 2, ky * pair))
    return out


def project_and_attend_kernel(heads, hd, span, n_orders, coord_ref, rand_ref, *refs):
    x_from = refs[:8]
    w_from, (b_kv_ref, b_q_ref, mask_ref) = refs[8:10], refs[10:13]
    refs = refs[13 + n_orders :]
    outs, refs = refs[:5], refs[5:]
    x_refs, (w_kv_ref, w_q_ref), o_refs = refs[:8], refs[8:10], refs[10:12]
    lse_ref, kv_ref, q_ref, s_ref, place_ref, nat_ref, in_sems, out_sems = refs[12:]
    arriving = [
        pltpu.make_async_copy(a, b, in_sems.at[i])
        for i, (a, b) in enumerate(zip((*w_from, *x_from), (w_kv_ref, w_q_ref, *x_refs)))
    ]
    for copy in arriving:
        copy.start()
    leaving = []

    def leave(src, dst):
        leaving.append(pltpu.make_async_copy(src, dst, out_sems.at[len(leaving)]))
        leaving[-1].start()

    near = o_refs[0].shape[0] // BLOCK
    wide = 2 * hd
    piece, pair = 4 * span, 2 * span
    per_span = span // BLOCK
    blocks = q_ref.shape[0] // BLOCK
    blocks_all = kv_ref.shape[0] // BLOCK
    chunks = kv_ref.shape[0] // CHUNK
    lanes = lax.broadcasted_iota(jnp.int32, (BLOCK, 128), 1)
    left = lax.broadcasted_iota(jnp.int32, (1, 128), 1) < BLOCK
    fill_tables(coord_ref, rand_ref, place_ref, nat_ref, heads, span)

    arriving[0].wait()
    arriving[1].wait()
    for n, x_ref in enumerate(x_refs):
        arriving[2 + n].wait()
        of = slice(n * piece, (n + 1) * piece)
        kv_ref[of, :] = (dot_nn(x_ref[...], w_kv_ref[...]) + b_kv_ref[...]).astype(bf16)
        leave(kv_ref.at[of], outs[3].at[of])
    for at, n, src in query_pieces(pair):
        x = x_refs[n][src : src + pair, :]
        q_ref[at : at + pair, :] = (dot_nn(x, w_q_ref[...]) + b_q_ref[...]).astype(bf16) * bf16(hd**-0.5)
    leave(q_ref, outs[4])

    def finish(jl, accs, tops, totals):
        lse_tile = jnp.zeros((BLOCK, 128), f32)
        for h in range(heads):
            lse_tile = jnp.where(lanes == h, tops[h] + jnp.log(totals[h]), lse_tile)
        lse_ref[pl.ds(pl.multiple_of(jl * BLOCK, BLOCK), BLOCK), :] = lse_tile
        return jnp.concatenate([accs[h][:, hd:] * (1.0 / totals[h]) for h in range(heads)], axis=1).astype(bf16)

    def put(o_ref, jl, value):
        o_ref[pl.ds(pl.multiple_of(jl * BLOCK, BLOCK), BLOCK), :] = value

    unroll = 4

    def some(half, it, carry):
        items = [(half * near + it * unroll + u, h) for u in range(unroll) for h in range(heads)]
        scores, kvs = [], []
        for jl, h in items:
            rows = pl.ds(pl.multiple_of(jl * BLOCK, BLOCK), BLOCK)
            cols = slice(h * wide, (h + 1) * wide)
            ids, mask_rows = picks_of(coord_ref, rand_ref, jl, h, heads, per_span, blocks_all)
            kvg = blocks_of(kv_ref, place_ref, ids, cols)
            scores.append(dot_nt(q_ref[rows, cols], kvg) + mask_of(mask_ref, mask_rows, left))
            kvs.append(kvg)
        lows, tops, totals = [], [], []
        for s in scores:
            top = jnp.max(s, axis=1, keepdims=True)
            p = jnp.exp(s - top)
            totals.append(jnp.sum(p, axis=1, keepdims=True))
            tops.append(top)
            lows.append(p.astype(bf16))
        accs = [dot_nn(p, kvg) for p, kvg in zip(lows, kvs)]
        for u in range(unroll):
            of = slice(u * heads, (u + 1) * heads)
            jl = it * unroll + u
            put(o_refs[half], jl, finish(half * near + jl, accs[of], tops[of], totals[of]))
        return carry

    for half in range(2):
        lax.fori_loop(0, near // unroll, functools.partial(some, half), 0)

    edge = edge_of(coord_ref, blocks, per_span)
    rows = pl.ds(pl.multiple_of(edge * BLOCK, BLOCK), BLOCK)
    head_cols = [slice(h * wide, (h + 1) * wide) for h in range(heads)]
    qs = [q_ref[rows, cols] for cols in head_cols]

    def score(c, tops):
        parts = [pl.ds(pl.multiple_of((c * 2 + i) * CHUNK, CHUNK), CHUNK) for i in range(2)]
        masks = [
            mask_of(mask_ref, [nat_ref[(c * 2 + i) * PICKS + u] for u in range(PICKS)], left) for i in range(2)
        ]
        ss = [
            [dot_nt(qs[h], kv_ref[parts[i], head_cols[h]]) + masks[i] for h in range(heads)] for i in range(2)
        ]
        for i in range(2):
            for h in range(heads):
                s_ref[h, :, parts[i]] = ss[i][h]
        return tuple(jnp.maximum(tops[h], jnp.maximum(ss[0][h], ss[1][h])) for h in range(heads))

    tops = lax.fori_loop(0, chunks // 2, score, tuple(jnp.full((BLOCK, CHUNK), -3e38, f32) for _ in range(heads)))
    tops = [jnp.max(t, axis=1, keepdims=True) for t in tops]

    def out(c, carry):
        accs, sums = carry
        parts = [pl.ds(pl.multiple_of((c * 2 + i) * CHUNK, CHUNK), CHUNK) for i in range(2)]
        ps = [[jnp.exp(s_ref[h, :, part] - tops[h]) for h in range(heads)] for part in parts]
        adds = [
            [dot_nn(ps[i][h].astype(bf16), kv_ref[parts[i], head_cols[h]]) for h in range(heads)] for i in range(2)
        ]
        accs = tuple(accs[h] + (adds[0][h] + adds[1][h]) for h in range(heads))
        sums = tuple(sums[h] + (ps[0][h] + ps[1][h]) for h in range(heads))
        return accs, sums

    accs, sums = lax.fori_loop(
        0,
        chunks // 2,
        out,
        (
            tuple(jnp.zeros((BLOCK, wide), f32) for _ in range(heads)),
            tuple(jnp.zeros((BLOCK, CHUNK), f32) for _ in range(heads)),
        ),
    )
    value = finish(edge, accs, tops, [jnp.sum(t, axis=1, keepdims=True) for t in sums])

    @pl.when(edge < near)
    def _():
        put(o_refs[0], edge, value)

    @pl.when(edge >= near)
    def _():
        put(o_refs[1], edge - near, value)

    for src, dst in zip((*o_refs, lse_ref), outs):
        leave(src, dst)
    for copy in leaving:
        copy.wait()


def project_and_attend(heads, hd, span, coords, rand, xs, w_kv, w_q, b_kv, b_q, mask, orders):
    keys = 8 * xs[0].shape[0]
    rows = keys // 2
    cols = heads * 2 * hd
    return pl.pallas_call(
        functools.partial(project_and_attend_kernel, heads, hd, span, len(orders)),
        out_shape=(
            jax.ShapeDtypeStruct((rows // 2, heads * hd), bf16),
            jax.ShapeDtypeStruct((rows // 2, heads * hd), bf16),
            jax.ShapeDtypeStruct((rows, 128), f32),
            jax.ShapeDtypeStruct((keys, cols), bf16),
            jax.ShapeDtypeStruct((rows, cols), bf16),
        ),
        in_specs=[SMEM_SPEC] * 2 + [ANY_SPEC] * 10 + [VMEM_SPEC] * 3 + [ANY_SPEC] * len(orders),
        out_specs=(ANY_SPEC,) * 5,
        scratch_shapes=[pltpu.VMEM(a.shape, bf16) for a in (*xs, w_kv, w_q)]
        + [pltpu.VMEM((rows // 2, heads * hd), bf16)] * 2
        + [
            pltpu.VMEM((rows, 128), f32),
            pltpu.VMEM((keys, cols), bf16),
            pltpu.VMEM((rows, cols), bf16),
            pltpu.VMEM((heads, BLOCK, keys), f32),
            pltpu.SMEM((keys // BLOCK,), jnp.int32),
            pltpu.SMEM((keys // BLOCK,), jnp.int32),
            pltpu.SemaphoreType.DMA((10,)),
            pltpu.SemaphoreType.DMA((12,)),
        ],
        compiler_params=params(60),
        cost_estimate=pl.CostEstimate(
            flops=40 << 30, bytes_accessed=16 << 20, transcendentals=rows * heads * CHUNK
        ),
        name="project_and_attend",
    )(coords, rand, *xs, w_kv, w_q, b_kv, b_q, mask, *orders)


def attend_back_kernel(heads, hd, span, n_orders, coord_ref, rand_ref, q_from, *refs):
    do_parts, o_parts, (kv_from, lse_from, w_kv_from, w_q_from, mask_ref) = refs[:4], refs[4:6], refs[6:11]
    refs = refs[11 + n_orders :]
    dq_out, dkv_out, near_out, far_out, acc_ref, do_ref, o_ref, place_ref, nat_ref = refs[:9]
    q_ref, kv_ref, lse_ref, w_kv_ref, w_q_ref, dq_ref, dkv_ref, dx_ref, in_sems, out_sems = refs[9:]
    own = do_parts[0].shape[0]
    pairs = [(q_from, q_ref), (kv_from, kv_ref), (lse_from, lse_ref)]
    for k, ref in enumerate(do_parts):
        pairs.append((ref.at[0] if len(ref.shape) == 3 else ref, do_ref.at[k * own : (k + 1) * own]))
    for k, ref in enumerate(o_parts):
        pairs.append((ref, o_ref.at[k * 2 * own : (k + 1) * 2 * own]))
    pairs += [(w_kv_from, w_kv_ref), (w_q_from, w_q_ref)]
    arriving = [pltpu.make_async_copy(a, b, in_sems.at[i]) for i, (a, b) in enumerate(pairs)]
    for copy in arriving:
        copy.start()
    wide = 2 * hd
    piece = 4 * span
    per_span = span // BLOCK
    scale = hd**-0.5
    blocks = q_ref.shape[0] // BLOCK
    blocks_all = kv_ref.shape[0] // BLOCK
    chunks = kv_ref.shape[0] // CHUNK
    head_cols = [slice(h * wide, (h + 1) * wide) for h in range(heads)]
    nil = jnp.zeros((BLOCK, hd), bf16)
    left = lax.broadcasted_iota(jnp.int32, (1, 128), 1) < BLOCK
    fill_tables(coord_ref, rand_ref, place_ref, nat_ref, heads, span)

    def clear(c, carry):
        part = pl.ds(pl.multiple_of(c * CHUNK, CHUNK), CHUNK)
        acc_ref[part, :] = jnp.zeros((CHUNK, heads * wide), f32)
        return carry

    lax.fori_loop(0, chunks, clear, 0)
    for copy in arriving[:-2]:
        copy.wait()

    def of_rows(rows):
        d_o = do_ref[rows, :]
        prod = d_o.astype(f32) * o_ref[rows, :].astype(f32)
        lse = lse_ref[rows, :]
        boths, dots, lses = [], [], []
        for h in range(heads):
            low = jnp.concatenate([nil, d_o[:, h * hd : (h + 1) * hd]], axis=1)
            boths.append(jnp.concatenate([q_ref[rows, head_cols[h]], low], axis=0))
            dots.append(jnp.sum(prod[:, h * hd : (h + 1) * hd], axis=1, keepdims=True))
            lses.append(lse[:, h : h + 1])
        return boths, dots, lses

    unroll = 4

    def some(it, carry):
        items, boths, dots, lses = [], [], [], []
        for u in range(unroll):
            jl = it * unroll + u
            rows = pl.ds(pl.multiple_of(jl * BLOCK, BLOCK), BLOCK)
            b, d, e = of_rows(rows)
            boths, dots, lses = boths + b, dots + d, lses + e
            items += [(jl, h) for h in range(heads)]
        kvs, prods, picks, masks = [], [], [], []
        for i, (jl, h) in enumerate(items):
            ids, mask_rows = picks_of(coord_ref, rand_ref, jl, h, heads, per_span, blocks_all)
            kvg = blocks_of(kv_ref, place_ref, ids, head_cols[h])
            prods.append(dot_nt(boths[i], kvg))
            masks.append(mask_of(mask_ref, mask_rows, left))
            kvs.append(kvg)
            picks.append(ids)
        dss, lows = [], []
        for i, (jl, h) in enumerate(items):
            p = jnp.exp(prods[i][:BLOCK] + masks[i] - lses[i])
            dss.append((p * (prods[i][BLOCK:] - dots[i])).astype(bf16))
            lows.append(p.astype(bf16))
        dqs = [dot_nn(ds, kvg)[:, :hd] for ds, kvg in zip(dss, kvs)]
        dkvs = [dot_tn(jnp.concatenate([ds, p], axis=0), both) for ds, p, both in zip(dss, lows, boths)]
        for i, (jl, h) in enumerate(items):
            for u in range(PICKS):
                place = pl.ds(pl.multiple_of(place_ref[picks[i][u]] * BLOCK, BLOCK), BLOCK)
                acc_ref[place, head_cols[h]] += dkvs[i][u * BLOCK : (u + 1) * BLOCK]
        for u in range(unroll):
            rows = pl.ds(pl.multiple_of((it * unroll + u) * BLOCK, BLOCK), BLOCK)
            dq_ref[rows, :] = (jnp.concatenate(dqs[u * heads : (u + 1) * heads], axis=1) * scale).astype(bf16)
        return carry

    lax.fori_loop(0, blocks // unroll, some, 0)

    rows = pl.ds(pl.multiple_of(edge_of(coord_ref, blocks, per_span) * BLOCK, BLOCK), BLOCK)
    boths, dots, lses = of_rows(rows)

    def edge(c, dqs):
        items = [(i, h) for i in range(2) for h in range(heads)]
        parts = [pl.ds(pl.multiple_of((c * 2 + i) * CHUNK, CHUNK), CHUNK) for i in range(2)]
        masks = [
            mask_of(mask_ref, [nat_ref[(c * 2 + i) * PICKS + u] for u in range(PICKS)], left) for i in range(2)
        ]
        kvs = [kv_ref[parts[i], head_cols[h]] for i, h in items]
        prods = [dot_nt(boths[h], kvg) for (i, h), kvg in zip(items, kvs)]
        dss, lows = [], []
        for (i, h), prod in zip(items, prods):
            p = jnp.exp(prod[:BLOCK] + masks[i] - lses[h])
            dss.append((p * (prod[BLOCK:] - dots[h])).astype(bf16))
            lows.append(p.astype(bf16))
        adds = [dot_nn(ds, kvg) for ds, kvg in zip(dss, kvs)]
        dkvs = [dot_tn(jnp.concatenate([ds, p], axis=0), boths[h]) for (i, h), ds, p in zip(items, dss, lows)]
        for (i, h), dkv in zip(items, dkvs):
            acc_ref[parts[i], head_cols[h]] += dkv
        return tuple(dqs[h] + (adds[h] + adds[heads + h]) for h in range(heads))

    dqs = lax.fori_loop(0, chunks // 2, edge, tuple(jnp.zeros((BLOCK, wide), f32) for _ in range(heads)))
    dq_ref[rows, :] = (jnp.concatenate([dq[:, :hd] for dq in dqs], axis=1) * scale).astype(bf16)

    pair = 2 * span
    mine = {(n, src): at for at, n, src in query_pieces(pair)}
    leaving = [pltpu.make_async_copy(dq_ref, dq_out, out_sems.at[0])]
    leaving[0].start()
    arriving[-2].wait()
    arriving[-1].wait()
    moves = []
    for i, n in enumerate((2, 3, 6, 7, 0, 1, 4, 5)):
        kc = n // 2 % 2
        to = n % 2 * piece
        of = slice(n * piece, (n + 1) * piece)
        slot = i % 2
        if i >= 2:
            for copy in moves[i - 2]:
                copy.wait()
        dkv = acc_ref[of, :].astype(bf16)
        dkv_ref[slot] = dkv
        dx = dot_nt(dkv, w_kv_ref[...])
        for src in (0, pair):
            part = dx[src : src + pair]
            if (n, src) in mine:
                at = mine[n, src]
                part = part + dot_nt(dq_ref[at : at + pair, :], w_q_ref[...])
            dx_ref[slot, src : src + pair, :] = part.astype(bf16)
        dx_out = (far_out if kc else near_out).at[n // 4, to : to + piece]
        moves.append(
            [
                pltpu.make_async_copy(dkv_ref.at[slot], dkv_out.at[of], out_sems.at[1 + 2 * i]),
                pltpu.make_async_copy(dx_ref.at[slot], dx_out, out_sems.at[2 + 2 * i]),
            ]
        )
        for copy in moves[-1]:
            copy.start()
    for copy in (*leaving, *moves[-2], *moves[-1]):
        copy.wait()


def attend_back(heads, hd, span, coords, rand, q, d_os, os, kv, mask, lse, w_kv, w_q, orders):
    rows, keys = q.shape[0], kv.shape[0]
    width = w_kv.shape[0]
    piece = 4 * span
    return pl.pallas_call(
        functools.partial(attend_back_kernel, heads, hd, span, len(orders)),
        out_shape=(
            jax.ShapeDtypeStruct((rows, heads * hd), bf16),
            jax.ShapeDtypeStruct((keys, heads * 2 * hd), bf16),
        )
        + (jax.ShapeDtypeStruct((2, 2 * piece, width), bf16),) * 2,
        in_specs=[SMEM_SPEC] * 2 + [ANY_SPEC] * 11 + [VMEM_SPEC] + [ANY_SPEC] * len(orders),
        out_specs=(ANY_SPEC,) * 4,
        scratch_shapes=[
            pltpu.VMEM((keys, heads * 2 * hd), f32),
            pltpu.VMEM((rows, heads * hd), bf16),
            pltpu.VMEM((rows, heads * hd), bf16),
            pltpu.SMEM((keys // BLOCK,), jnp.int32),
            pltpu.SMEM((keys // BLOCK,), jnp.int32),
            pltpu.VMEM(q.shape, bf16),
            pltpu.VMEM(kv.shape, bf16),
            pltpu.VMEM(lse.shape, f32),
            pltpu.VMEM(w_kv.shape, bf16),
            pltpu.VMEM(w_q.shape, bf16),
            pltpu.VMEM((rows, heads * hd), bf16),
            pltpu.VMEM((2, piece, heads * 2 * hd), bf16),
            pltpu.VMEM((2, piece, width), bf16),
            pltpu.SemaphoreType.DMA((11,)),
            pltpu.SemaphoreType.DMA((17,)),
        ],
        compiler_params=params(60),
        cost_estimate=pl.CostEstimate(
            flops=60 << 30, bytes_accessed=24 << 20, transcendentals=rows * heads * CHUNK
        ),
        name="attend_back",
    )(coords, rand, q, *d_os, *os, kv, lse, w_kv, w_q, mask, *orders)


def split_low(value):
    top = value.astype(bf16)
    return jnp.concatenate([top, (value - top.astype(f32)).astype(bf16)], axis=0)


def joined(low):
    return low[:8].astype(f32) + low[8:16].astype(f32)


def qkv_grad_kernel(span, spot_ref, coord_ref, dq_ref, dkv_ref, keep_ref, got_ref, small_ref, *refs):
    x_refs, (keep_out, send_out, held_ref) = refs[:8], refs[-3:]
    piece = 4 * span
    n_kv = dkv_ref.shape[1]
    n_q = dq_ref.shape[1]
    rows, width = held_ref.shape[1], x_refs[0].shape[1]
    acc = jnp.zeros((n_kv, width), f32)
    acc_q = jnp.zeros((n_q, width), f32)
    for n, x_ref in enumerate(x_refs):
        acc = acc + dot_tn(dkv_ref[n * piece : (n + 1) * piece, :], x_ref[...])
    pair = 2 * span
    for at, n, src in query_pieces(pair):
        acc_q = acc_q + dot_tn(dq_ref[at : at + pair, :], x_refs[n][src : src + pair, :])
    held_ref[...] = jnp.zeros_like(held_ref)
    both = jnp.concatenate([acc, acc_q], axis=0)
    octets = [both[o * rows : (o + 1) * rows] for o in range(6)]
    w_out = keep_ref[4].astype(f32) + got_ref[4 * rows : 5 * rows, :].astype(f32)
    octets += [w_out[:, :width], w_out[:, width:]]
    sums = jnp.concatenate(
        [
            jnp.sum(dq_ref[...].astype(f32), axis=0, keepdims=True),
            jnp.sum(dkv_ref[...].astype(f32), axis=0, keepdims=True),
            jnp.zeros((1, 1024 - n_q - n_kv), f32),
        ],
        axis=1,
    )
    sums = jnp.concatenate([sums[:, i * 128 : (i + 1) * 128] for i in range(8)], axis=0)

    others = joined(got_ref[5 * rows :, :width])
    own = joined(split_low(small_ref[...]))
    small = own + others
    held = split_low(own + pltpu.roll(others, 7, 0))
    unit = lax.broadcasted_iota(jnp.int32, (width, width), 0)
    octet = unit // rows
    zq = (octet // 2 % 2 + octet % 2 * 2) ^ coord_ref[0]
    own_unit = (zq * 2 + (octet // 4 ^ coord_ref[1])) * rows + unit % rows
    turn = jnp.where(own_unit == lax.broadcasted_iota(jnp.int32, (width, width), 1), 1.0, 0.0).astype(bf16)
    b_in = joined(dot_nn(held, turn))[6:7]

    def lanes_down(row):
        parts = [row[:, i * 128 : (i + 1) * 128] for i in range(width // 128)]
        return jnp.concatenate(parts + [jnp.zeros((8 - width // 128, 128), f32)], axis=0)

    vectors = [lanes_down(small[i : i + 1]) for i in range(6)] + [lanes_down(b_in), sums]
    for o in range(8):
        spot = spot_ref[o]
        held_ref[spot, :, :width] = octets[o].astype(bf16)
        held_ref[spot, :16, width:] = split_low(vectors[o])
    keep_out[...] = held_ref[0:4]
    send_out[...] = held_ref[4:8]


def qkv_grad(span, spots, coords, dq, dkv, keep, got, small, xs, orders):
    width = xs[0].shape[1]
    rows = (dq.shape[1] + dkv.shape[1]) // 6
    return pl.pallas_call(
        functools.partial(qkv_grad_kernel, span),
        out_shape=(jax.ShapeDtypeStruct((4, rows, width + 128), bf16),) * 2,
        in_specs=[SMEM_SPEC] * 2 + [VMEM_SPEC] * 13 + [ANY_SPEC] * len(orders),
        out_specs=(VMEM_SPEC,) * 2,
        scratch_shapes=[pltpu.VMEM((8, rows, width + 128), bf16)],
        compiler_params=params(60),
        cost_estimate=pl.CostEstimate(
            flops=14 << 30, bytes_accessed=12 << 20, transcendentals=0
        ),
        name="qkv_grad",
    )(spots, coords, dq, dkv, keep, got, small, *xs, *orders)


def across_sum_kernel(a_ref, b_ref, c_ref, d_ref, out_ref):
    out_ref[...] = sum(r[...].astype(f32) for r in (a_ref, b_ref, c_ref, d_ref)).astype(bf16)


def across_sum(parts):
    return pl.pallas_call(
        across_sum_kernel,
        out_shape=jax.ShapeDtypeStruct(parts[0].shape, bf16),
        in_specs=[VMEM_SPEC] * 4,
        out_specs=VMEM_SPEC,
        compiler_params=params(60),
        cost_estimate=pl.CostEstimate(flops=1 << 24, bytes_accessed=1 << 20, transcendentals=0),
        name="across_sum",
    )(*parts)


def wide_sum_kernel(order_ref, keep_ref, y_ref, x_ref, *refs):
    out_ref = refs[-1]
    rows = keep_ref.shape[1]
    for k in range(4):
        of = slice(k * rows, (k + 1) * rows)
        out_ref[order_ref[k]] = (keep_ref[k].astype(f32) + y_ref[of, :].astype(f32) + x_ref[k].astype(f32)).astype(bf16)


def wide_sum(order, keep, y_got, x_got, orders):
    _, rows, cols = keep.shape
    four = pl.BlockSpec((4, rows, cols), lambda i: (0, 0, 0))
    return pl.pallas_call(
        wide_sum_kernel,
        grid=(1,),
        in_specs=[SMEM_SPEC, four, pl.BlockSpec((4 * rows, cols), lambda i: (0, 0)), four] + [ANY_SPEC] * len(orders),
        out_specs=four,
        out_shape=jax.ShapeDtypeStruct((4, rows, cols), bf16),
        compiler_params=params(60),
        cost_estimate=pl.CostEstimate(flops=4 << 30, bytes_accessed=6 << 20, transcendentals=0),
        name="wide_sum",
    )(order, keep, y_got, x_got, *orders)


def low_sum(out_ref, at, refs):
    rows, cols = out_ref.shape[1:]
    thin = cols - 128
    out_ref[at, :, :thin] = sum(ref[k, :, :thin].astype(f32) for ref, k in refs).astype(bf16)
    out_ref[at, :, thin:] = jnp.zeros((rows, 128), bf16)
    out_ref[at, :16, thin:] = split_low(sum(joined(ref[k, :16, thin:]) for ref, k in refs))


def tail_sum_kernel(tail_ref, got_ref, *refs):
    keep_ref, send_ref = refs[-2:]
    for k in range(4):
        low_sum(keep_ref if k < 2 else send_ref, k % 2, [(tail_ref, k), (got_ref, k)])


def tail_sum(tail, got, orders):
    _, rows, cols = tail.shape
    return pl.pallas_call(
        tail_sum_kernel,
        out_shape=(jax.ShapeDtypeStruct((2, rows, cols), bf16),) * 2,
        in_specs=[VMEM_SPEC] * 2 + [ANY_SPEC] * len(orders),
        out_specs=(VMEM_SPEC,) * 2,
        compiler_params=params(60),
        cost_estimate=pl.CostEstimate(flops=1 << 28, bytes_accessed=2 << 20, transcendentals=0),
        name="tail_sum",
    )(tail, got, *orders)


def tail_mid_kernel(keep_ref, got_ref, own_ref, send_ref):
    low_sum(own_ref, 0, [(keep_ref, 0), (got_ref, 0)])
    low_sum(send_ref, 0, [(keep_ref, 1), (got_ref, 1)])


def tail_mid(keep, got):
    _, rows, cols = keep.shape
    return pl.pallas_call(
        tail_mid_kernel,
        out_shape=(jax.ShapeDtypeStruct((1, rows, cols), bf16),) * 2,
        in_specs=[VMEM_SPEC] * 2,
        out_specs=(VMEM_SPEC,) * 2,
        compiler_params=params(60),
        cost_estimate=pl.CostEstimate(flops=1 << 28, bytes_accessed=2 << 20, transcendentals=0),
        name="tail_mid",
    )(keep, got)


def wide_end_kernel(wide_ref, across_ref, *refs):
    refs[-1][...] = (wide_ref[...].astype(f32) + across_ref[...].astype(f32)).astype(bf16)


def wide_end(wide, across, orders):
    return pl.pallas_call(
        wide_end_kernel,
        out_shape=jax.ShapeDtypeStruct(wide.shape, bf16),
        in_specs=[VMEM_SPEC] * 2 + [ANY_SPEC] * len(orders),
        out_specs=VMEM_SPEC,
        compiler_params=params(60),
        cost_estimate=pl.CostEstimate(flops=1 << 28, bytes_accessed=3 << 20, transcendentals=0),
        name="wide_end",
    )(wide, across, *orders)


def tail_end_kernel(own_ref, got_ref, *refs):
    low_sum(refs[-1], 0, [(own_ref, 0), (got_ref, 0)])


def tail_end(own, got, orders):
    return pl.pallas_call(
        tail_end_kernel,
        out_shape=jax.ShapeDtypeStruct(own.shape, bf16),
        in_specs=[VMEM_SPEC] * 2 + [ANY_SPEC] * len(orders),
        out_specs=VMEM_SPEC,
        compiler_params=params(60),
        cost_estimate=pl.CostEstimate(flops=1 << 28, bytes_accessed=3 << 20, transcendentals=0),
        name="tail_end",
    )(own, got, *orders)


def wide_place_kernel(spot_ref, *refs):
    ins, (in_ref, back_ref, held_ref) = refs[:8], refs[-3:]
    rows, width = ins[0].shape[0], back_ref.shape[1]
    for n in range(8):
        to = pl.ds(pl.multiple_of(spot_ref[n] * rows, 16), rows)
        held_ref[to, :] = ins[n][:, :width].astype(f32)
        back_ref[to, :] = ins[n][:, width:].astype(f32)
    in_ref[...] = held_ref[...].T


def wide_place(spots, parts, orders):
    rows, cols = parts[0].shape
    width = cols // 2
    return pl.pallas_call(
        wide_place_kernel,
        out_shape=(jax.ShapeDtypeStruct((width, 8 * rows), f32), jax.ShapeDtypeStruct((8 * rows, width), f32)),
        in_specs=[SMEM_SPEC] + [VMEM_SPEC] * 8 + [ANY_SPEC] * len(orders),
        out_specs=(VMEM_SPEC,) * 2,
        scratch_shapes=[pltpu.VMEM((8 * rows, width), f32)],
        compiler_params=params(60),
        cost_estimate=pl.CostEstimate(flops=1 << 28, bytes_accessed=3 << 20, transcendentals=0),
        name="wide_place",
    )(spots, *parts, *orders)


def tail_place_kernel(n_qkv, heads, spot_ref, *refs):
    ins, (qkv_ref, w_out_ref, small_ref, held_ref) = refs[:8], refs[-4:]
    rows = ins[0].shape[1]
    cols = held_ref.shape[1]
    for n in range(8):
        spot = spot_ref[n]
        held_ref[pl.ds(pl.multiple_of(spot * rows, 16), rows), :] = ins[n][0, :, :cols].astype(f32)
        small_ref[spot] = joined(ins[n][0, :16, cols:])
    w_out_ref[...] = held_ref[n_qkv:, :]
    hd = n_qkv // 3 // heads
    parts = []
    for h in range(heads):
        q_at, kv_at = 2 * heads * hd + h * hd, 2 * h * hd
        parts += [held_ref[q_at : q_at + hd, :], held_ref[kv_at : kv_at + 2 * hd, :]]
    qkv_ref[...] = jnp.concatenate(parts, axis=0).T


def tail_place(spots, parts, n_qkv, heads, orders):
    _, rows, cols = parts[0].shape
    width = cols - 128
    return pl.pallas_call(
        functools.partial(tail_place_kernel, n_qkv, heads),
        out_shape=(
            jax.ShapeDtypeStruct((width, n_qkv), f32),
            jax.ShapeDtypeStruct((8 * rows - n_qkv, width), f32),
            jax.ShapeDtypeStruct((8, 8, 128), f32),
        ),
        in_specs=[SMEM_SPEC] + [VMEM_SPEC] * 8 + [ANY_SPEC] * len(orders),
        out_specs=(VMEM_SPEC,) * 3,
        scratch_shapes=[pltpu.VMEM((8 * rows, width), f32)],
        compiler_params=params(60),
        cost_estimate=pl.CostEstimate(flops=1 << 28, bytes_accessed=3 << 20, transcendentals=0),
        name="tail_place",
    )(spots, *parts, *orders)


def split_kernel(n_orders, coord_ref, rows_ref, *refs):
    value = rows_ref[...].astype(f32)
    pieces = [value[:, s, :] for s in range(4)]
    z = coord_ref[0]
    for k, out in enumerate(refs[n_orders:]):
        low = jnp.where((z ^ k) % 2 == 0, pieces[0], pieces[1])
        high = jnp.where((z ^ k) % 2 == 0, pieces[2], pieces[3])
        out[...] = jnp.where((z ^ k) // 2 == 0, low, high).astype(bf16)


def split(coords, rows, orders=()):
    span, seqs, width = rows.shape
    return pl.pallas_call(
        functools.partial(split_kernel, len(orders)),
        out_shape=(jax.ShapeDtypeStruct((span, width), bf16),) * seqs,
        in_specs=[SMEM_SPEC, VMEM_SPEC] + [ANY_SPEC] * len(orders),
        out_specs=(VMEM_SPEC,) * seqs,
        compiler_params=params(32),
        cost_estimate=pl.CostEstimate(flops=1 << 20, bytes_accessed=1 << 20, transcendentals=0),
        name="split",
    )(coords, rows, *orders)


def qkv_weights_kernel(n_orders, w_ref, b_ref, *refs):
    kv_ref, q_pad_ref, q_ref, b_kv_ref, b_q_ref = refs[n_orders:]
    width, heads, _, hd = w_ref.shape
    wide = 2 * hd
    value = w_ref[...].astype(f32)
    nil = jnp.zeros((width, hd), f32)
    qs = []
    for h in range(heads):
        q, k, v = [value[:, h, c, :] for c in range(3)]
        cols = slice(h * wide, (h + 1) * wide)
        kv_ref[:, cols] = jnp.concatenate([k, v], axis=1).astype(bf16)
        q_pad_ref[:, cols] = jnp.concatenate([q, nil], axis=1).astype(bf16)
        b_kv_ref[:, cols] = jnp.concatenate([nil[:1], b_ref[h, 1:2, :]], axis=1)
        b_q_ref[:, cols] = jnp.concatenate([b_ref[h, 0:1, :], nil[:1]], axis=1)
        qs.append(q)
    q_ref[...] = jnp.concatenate(qs, axis=1).astype(bf16)


def qkv_weights(w_qkv, bias_qv, orders):
    width, heads, _, hd = w_qkv.shape
    cols = heads * 2 * hd
    return pl.pallas_call(
        functools.partial(qkv_weights_kernel, len(orders)),
        out_shape=(
            jax.ShapeDtypeStruct((width, cols), bf16),
            jax.ShapeDtypeStruct((width, cols), bf16),
            jax.ShapeDtypeStruct((width, heads * hd), bf16),
            jax.ShapeDtypeStruct((1, cols), f32),
            jax.ShapeDtypeStruct((1, cols), f32),
        ),
        in_specs=[VMEM_SPEC] * 2 + [ANY_SPEC] * len(orders),
        out_specs=(VMEM_SPEC,) * 5,
        compiler_params=params(40),
        cost_estimate=pl.CostEstimate(flops=1 << 20, bytes_accessed=1 << 20, transcendentals=0),
        name="qkv_weights",
    )(w_qkv, bias_qv, *orders)


def pack_kernel(n_orders, order_ref, up_ref, down_ref, w_out_ref, bias_ref, *refs):
    pack_ref, first_ref, out_ref, up_rows_ref = refs[n_orders:]
    width = up_ref.shape[0]
    eighth = down_ref.shape[0] // 8
    half = w_out_ref.shape[0] // 2
    for i in range(0, down_ref.shape[0], 256):
        up_rows_ref[i : i + 256, :] = up_ref[:, i : i + 256].astype(f32).T.astype(bf16)
    for ref in (pack_ref, out_ref):
        ref[:half, :width] = w_out_ref[:half, :]
        ref[:half, width:] = w_out_ref[half:, :]
        ref[half : half + 16, :width] = bias_ref[...]
        ref[half : half + 16, width:] = jnp.zeros((16, width), bf16)
    for n in range(8):
        src = pl.ds(pl.multiple_of(order_ref[n] * eighth, 16), eighth)
        for ref, at in ((pack_ref, half + 16), (first_ref, 0))[: 2 if n < 4 else 1]:
            to = slice(at + n * eighth, at + (n + 1) * eighth)
            ref[to, :width] = up_rows_ref[src, :]
            ref[to, width:] = down_ref[src, :]


def pack(order, up, down, w_out, bias, orders):
    hidden, width = down.shape
    rows = w_out.shape[0] // 2 + 16
    return pl.pallas_call(
        functools.partial(pack_kernel, len(orders)),
        out_shape=(
            jax.ShapeDtypeStruct((rows + hidden, 2 * width), bf16),
            jax.ShapeDtypeStruct((hidden // 2, 2 * width), bf16),
            jax.ShapeDtypeStruct((rows, 2 * width), bf16),
        ),
        in_specs=[SMEM_SPEC] + [VMEM_SPEC] * 4 + [ANY_SPEC] * len(orders),
        out_specs=(VMEM_SPEC,) * 3,
        scratch_shapes=[pltpu.VMEM((hidden, width), bf16)],
        compiler_params=params(32),
        cost_estimate=pl.CostEstimate(flops=1 << 20, bytes_accessed=1 << 20, transcendentals=0),
        name="pack",
    )(order, up, down, w_out, bias, *orders)


def rows_kernel(width, n_out, tile_rows, *refs):
    attn_refs, pack_refs = refs[:4], refs[4 : 4 + len(tile_rows)]
    refs = refs[4 + len(tile_rows) :]
    tok_refs, dres_refs, vec_ref = refs[:2], refs[2:6], refs[6]
    result_refs = refs[7:11]
    done_ref, hid_ref, dpre_ref, ylow_ref, dffn_ref, dbr_ref = refs[11:17]
    dattn_refs = refs[17:20]
    small_ref, bin_ref = refs[20:22]
    slope_ref = refs[22]
    bias_out, gain_one, bias_one, down_bias, gain_two, bias_two = [vec_ref[i : i + 1, :] for i in range(6)]
    step = pl.program_id(0)
    half = n_out // 2
    tiles, wos, biases = [], [], []
    for ref, (first, whole) in zip(pack_refs, tile_rows):
        if whole:
            wos.append(jnp.concatenate([ref[:half, :width], ref[:half, width:]], axis=0))
            biases.append(ref[half : half + 1, :width].astype(f32))
        left = ref.shape[0] - first
        if left == 0:
            continue
        size = min(left, width // 2)
        tiles += [ref.at[first + i * size : first + (i + 1) * size] for i in range(left // size)]
    up_bias = jnp.concatenate(biases, axis=1)

    def by_step(ones, twos):
        pairs = [jnp.where(step == 0, a[...].astype(f32), b[...].astype(f32)) for a, b in zip(ones, twos)]
        return pairs[0] if len(pairs) == 1 else jnp.concatenate(pairs, axis=0)

    @pl.when(pl.program_id(0) == 0)
    def _():
        small_ref[...] = jnp.zeros_like(small_ref)
        bin_ref[...] = jnp.zeros_like(bin_ref)

    branch = bias_out
    for k in range(4):
        branch = branch + dot_nn(attn_refs[k][...], wos[k])
    y_one, normed_one, inv_one = norm_fwd(by_step(tok_refs[:1], tok_refs[1:]) + branch, gain_one, bias_one)
    y_low = y_one.astype(bf16)
    ylow_ref[...] = y_low
    ffn = down_bias
    at = 0
    spans = []
    for tile in tiles:
        spans.append(slice(at, at + tile.shape[0]))
        at += tile.shape[0]
    for cols, tile in zip(spans, tiles):
        v = dot_nt(y_low, tile[:, :width]) + up_bias[:, cols]
        sq = v * v
        th = jnp.tanh(0.7978845608028654 * v * (1.0 + 0.044715 * sq))
        half = 0.5 * (1.0 + th)
        slope_ref[:, cols] = half + 0.5 * v * (1.0 - th * th) * (
            0.7978845608028654 * (1.0 + 3.0 * 0.044715 * sq)
        )
        hid = (v * half).astype(bf16)
        hid_ref[:, cols] = hid
        ffn = ffn + dot_nn(hid, tile[:, width:])
    result, normed_two, inv_two = norm_fwd(y_one + ffn, gain_two, bias_two)
    for s in range(2):

        @pl.when(step == s)
        def _(s=s):
            for k in range(2):
                ref = result_refs[s + 2 * k]
                ref[...] = result[k * ref.shape[0] : (k + 1) * ref.shape[0]].astype(bf16)

    d_two, g_gain_two, g_bias_two = norm_back(by_step(dres_refs[::2], dres_refs[1::2]), normed_two, inv_two, gain_two)
    d_ffn = d_two.astype(bf16)
    dffn_ref[...] = d_ffn
    g_bias_back = jnp.sum(d_ffn.astype(f32), axis=0)
    d_y = d_two
    for cols, tile in zip(spans, tiles):
        d_pre = (dot_nt(d_ffn, tile[:, width:]) * slope_ref[:, cols]).astype(bf16)
        dpre_ref[:, cols] = d_pre
        bin_ref[:, cols] += jnp.sum(d_pre.astype(f32), axis=0, keepdims=True)
        d_y = d_y + dot_nn(d_pre, tile[:, :width])
    d_one, g_gain_one, g_bias_one = norm_back(d_y, normed_one, inv_one, gain_one)
    done_ref[...] = d_one
    d_branch = d_one.astype(bf16)
    dbr_ref[...] = d_branch
    g_bias_out = jnp.sum(d_branch.astype(f32), axis=0)
    for k in range(4):
        d_attn = dot_nt(d_branch, wos[k]).astype(bf16)
        if k < 2:
            dattn_refs[k][...] = d_attn
        else:
            dattn_refs[2][k - 2] = d_attn
    sums = [g_bias_out, g_gain_one, g_bias_one, g_bias_back, g_gain_two, g_bias_two]
    for i, one in enumerate(sums):
        small_ref[i : i + 1, :] += one[None, :]


def rows_work(attns, packs, first_rows, toks, d_res, vecs):
    span, width = d_res[0].shape
    rows = 4 * span
    cols = attns[0].shape[1]
    hidden = sum(a.shape[0] - n for a, (n, _) in zip(packs, first_rows))
    tile = rows // 2

    def by_rows(n):
        return pl.BlockSpec((tile, n), lambda i: (i, 0))

    def whole(a):
        return pl.BlockSpec(a.shape, lambda i, nd=a.ndim: (0,) * nd, pipeline_mode=pl.Buffered(1))

    def fixed(shape):
        return pl.BlockSpec(shape, lambda i: (0, 0))

    low = functools.partial(jax.ShapeDtypeStruct, dtype=bf16)
    return pl.pallas_call(
        functools.partial(rows_kernel, width, cols, first_rows),
        grid=(rows // tile,),
        out_shape=(low((span, width)),) * 4
        + (
            jax.ShapeDtypeStruct((rows, width), f32),
            low((rows, hidden)),
            low((rows, hidden)),
            low((rows, width)),
            low((rows, width)),
            low((rows, width)),
            low((rows, cols)),
            low((rows, cols)),
            low((2, rows, cols)),
            jax.ShapeDtypeStruct((8, width), f32),
            jax.ShapeDtypeStruct((1, hidden), f32),
        ),
        in_specs=[by_rows(cols)] * 4 + [whole(a) for a in (*packs, *toks, *d_res, vecs)],
        out_specs=(fixed((span, width)),) * 4
        + (
            by_rows(width),
            by_rows(hidden),
            by_rows(hidden),
            by_rows(width),
            by_rows(width),
            by_rows(width),
            by_rows(cols),
            by_rows(cols),
            pl.BlockSpec((2, tile, cols), lambda i: (0, i, 0)),
            fixed((8, width)),
            fixed((1, hidden)),
        ),
        scratch_shapes=[pltpu.VMEM((tile, hidden), f32)],
        compiler_params=params(60),
        cost_estimate=pl.CostEstimate(flops=50 << 30, bytes_accessed=30 << 20, transcendentals=rows * hidden),
        name="rows_work",
    )(*attns, *packs, *toks, *d_res, vecs)


def small_rows(kc, small_ref, bin_ref):
    width = small_ref.shape[1]
    ends = [bin_ref[:, (ky * 2 + kc) * width : (ky * 2 + kc + 1) * width] for ky in range(2)]
    return jnp.concatenate([small_ref[:6, :]] + ends, axis=0)


def rows_grad_kernel(kc, n_orders, *refs):
    *sources, small_ref, bin_ref = refs[:9]
    refs = refs[9:]
    got_from = refs[0] if kc == 0 else None
    refs = refs[(1 if kc == 0 else 0) + n_orders :]
    n_outs = 1 if kc else 8
    outs, (ylow_ref, dpre_ref, hid_ref, dffn_ref, dbr_ref, attn0_ref, attn1_ref, held_ref, got_ref, low_ref) = (
        refs[:n_outs],
        refs[n_outs : n_outs + 10],
    )
    in_sems, got_sems, out_sems = refs[n_outs + 10 :]
    width = ylow_ref.shape[1]
    rows = ylow_ref.shape[0]
    part = width // 2
    eighth = held_ref.shape[1]

    def cols_of(n):
        at = ((n // 2) * 4 + kc * 2 + n % 2) * part
        return slice(at, at + part)

    pairs = [(sources[0], ylow_ref), (sources[3], dffn_ref)]
    for n in range(4):
        pairs.append((sources[1].at[:, cols_of(n)], dpre_ref.at[n]))
        pairs.append((sources[2].at[:, cols_of(n)], hid_ref.at[n]))
    pairs += [(sources[4], dbr_ref)]
    pairs += [(source.at[0:rows], ref) for source, ref in zip(sources[5:], (attn0_ref, attn1_ref))]
    arriving = [pltpu.make_async_copy(a, b, in_sems.at[i]) for i, (a, b) in enumerate(pairs)]
    gots = []
    if kc == 0:
        gots = [
            pltpu.make_async_copy(got_from.at[4 * n : 4 * n + 4], got_ref.at[4 * n : 4 * n + 4], got_sems.at[n])
            for n in range(5)
        ]
    for i, copy in enumerate(arriving):
        copy.start()
        if gots and i in (3, 5, 7, 9):
            gots[(i - 3) // 2].start()
    if gots:
        gots[4].start()
    arriving[0].wait()
    arriving[1].wait()
    leaving = []

    def leave(src, dst):
        leaving.append(pltpu.make_async_copy(src, dst, out_sems.at[len(leaving)]))
        leaving[-1].start()

    def put(at, k, lanes, value):
        if gots:
            value = value + got_ref[at + k, :, lanes].astype(f32)
        held_ref[at + k, :, lanes] = value.astype(bf16)

    left, right = slice(0, width), slice(width, 2 * width)
    for n in range(4):
        arriving[2 + 2 * n].wait()
        arriving[3 + 2 * n].wait()
        g_in = dot_tn(dpre_ref[n], ylow_ref[...])
        g_back = dot_tn(hid_ref[n], dffn_ref[...])
        if gots:
            gots[n].wait()
        for k in range(4):
            put(4 * n, k, left, g_in[k * eighth : (k + 1) * eighth])
            put(4 * n, k, right, g_back[k * eighth : (k + 1) * eighth])
        if kc:
            leave(held_ref.at[4 * n : 4 * n + 4], outs[0].at[4 * n : 4 * n + 4])
        elif n < 2:
            leave(held_ref.at[4 * n : 4 * n + 4], outs[2 * n].at[0:4])
        elif n == 2:
            for k in range(4):
                leave(held_ref.at[8 + k], outs[1].at[k * eighth : (k + 1) * eighth])
        else:
            for k in range(4):
                leave(held_ref.at[12 + k], outs[3 + k])
    for copy in arriving[10:]:
        copy.wait()
    if gots:
        gots[4].wait()
    for ky, attn_ref in enumerate((attn0_ref, attn1_ref)):
        g_out = dot_tn(attn_ref[...], dbr_ref[...])
        put(16, ky, left, g_out[:eighth])
        put(16, ky, right, g_out[eighth:])
    low_ref[...] = jnp.zeros_like(low_ref)
    if kc:
        low_ref[:16, :width] = split_low(small_rows(1, small_ref, bin_ref))
        leave(held_ref.at[16:18], outs[0].at[16:18])
        leave(low_ref, outs[0].at[18])
        leave(low_ref, outs[0].at[19])
    else:
        sums = joined(split_low(small_rows(0, small_ref, bin_ref))) + joined(got_ref[18, :16, :width])
        outs[7][...] = sums
        low_ref[:16, :width] = split_low(sums)
        leave(held_ref.at[16], outs[0].at[4])
        leave(held_ref.at[17], outs[1].at[4 * eighth : 5 * eighth])
        leave(low_ref.at[0:16], outs[1].at[5 * eighth : 5 * eighth + 16])
    for copy in leaving:
        copy.wait()


def rows_grad(kc, y_low, d_pre, hidden, d_ffn, d_branch, attn0, attn1, small, bin_sum, got=None, orders=()):
    rows, width = y_low.shape
    part = hidden.shape[1] // 8
    eighth = part // 4
    octet = (eighth, 2 * width)
    low = functools.partial(jax.ShapeDtypeStruct, dtype=bf16)
    if kc == 1:
        out_shape = (low((20,) + octet),)
        out_specs = (ANY_SPEC,)
    else:
        out_shape = (low((5,) + octet), low((5 * eighth + 16, 2 * width)), low((4,) + octet)) + (low(octet),) * 4
        out_shape += (jax.ShapeDtypeStruct((8, width), f32),)
        out_specs = (ANY_SPEC,) * 7 + (VMEM_SPEC,)
    extra = () if got is None else (got,)
    out = pl.pallas_call(
        functools.partial(rows_grad_kernel, kc, len(orders)),
        out_shape=out_shape,
        in_specs=[ANY_SPEC] * 7 + [VMEM_SPEC] * 2 + [ANY_SPEC] * (len(extra) + len(orders)),
        out_specs=out_specs,
        scratch_shapes=[
            pltpu.VMEM((rows, width), bf16),
            pltpu.VMEM((4, rows, part), bf16),
            pltpu.VMEM((4, rows, part), bf16),
            pltpu.VMEM((rows, width), bf16),
            pltpu.VMEM((rows, width), bf16),
            pltpu.VMEM((rows, attn0.shape[1]), bf16),
            pltpu.VMEM((rows, attn1.shape[1]), bf16),
            pltpu.VMEM((18,) + octet, bf16),
            pltpu.VMEM((20,) + octet, bf16),
            pltpu.VMEM(octet, bf16),
            pltpu.SemaphoreType.DMA((13,)),
            pltpu.SemaphoreType.DMA((5,)),
            pltpu.SemaphoreType.DMA((16,)),
        ],
        compiler_params=params(60),
        cost_estimate=pl.CostEstimate(flops=8 << 30, bytes_accessed=16 << 20, transcendentals=0),
        name="far_grad" if kc else "near_grad",
    )(y_low, d_pre, hidden, d_ffn, d_branch, attn0, attn1, small, bin_sum, *extra, *orders)
    return out[0] if kc else out


def row_sum_one_kernel(n_orders, near_from, got_from, *refs):
    outs, (near_ref, got_ref, in_sems, out_sems) = refs[n_orders : n_orders + 2], refs[n_orders + 2 :]
    rows = near_ref.shape[1]
    far = pl.ds(rows, rows)
    arriving, leaving = [], []
    for i in range(2):
        for j, (src, dst) in enumerate(((near_from, near_ref), (got_from, got_ref))):
            arriving.append(pltpu.make_async_copy(src.at[i, far], dst.at[i], in_sems.at[i, j]))
            arriving[-1].start()
    for i in range(2):
        arriving[2 * i].wait()
        arriving[2 * i + 1].wait()
        near_ref[i] = (near_ref[i].astype(f32) + got_ref[i].astype(f32)).astype(bf16)
        leaving.append(pltpu.make_async_copy(near_ref.at[i], outs[i], out_sems.at[i]))
        leaving[-1].start()
    for copy in leaving:
        copy.wait()


def row_sum_one(near, got, orders):
    _, rows, width = near.shape
    half = (2, rows // 2, width)
    return pl.pallas_call(
        functools.partial(row_sum_one_kernel, len(orders)),
        out_shape=(jax.ShapeDtypeStruct(half[1:], bf16),) * 2,
        in_specs=[ANY_SPEC] * (2 + len(orders)),
        out_specs=(ANY_SPEC,) * 2,
        scratch_shapes=[
            pltpu.VMEM(half, bf16),
            pltpu.VMEM(half, bf16),
            pltpu.SemaphoreType.DMA((2, 2)),
            pltpu.SemaphoreType.DMA((2,)),
        ],
        compiler_params=params(60),
        cost_estimate=pl.CostEstimate(flops=1 << 28, bytes_accessed=6 << 20, transcendentals=0),
        name="row_sum_one",
    )(near, got, *orders)


def row_sum_two_kernel(n_orders, near_from, got_from, even_from, odd_from, *refs):
    outs, (near_ref, got_ref, more_ref, in_sems, out_sems) = refs[n_orders : n_orders + 2], refs[n_orders + 2 :]
    rows = near_ref.shape[1]
    part = pl.ds(rows, rows)
    arriving, leaving = [], []
    for i, more_from in enumerate((even_from, odd_from)):
        pairs = (
            (near_from.at[i, part], near_ref.at[i]),
            (got_from.at[i, part], got_ref.at[i]),
            (more_from.at[part], more_ref.at[i]),
        )
        for j, (src, dst) in enumerate(pairs):
            arriving.append(pltpu.make_async_copy(src, dst, in_sems.at[i, j]))
            arriving[-1].start()
    for i in range(2):
        for copy in arriving[3 * i : 3 * i + 3]:
            copy.wait()
        near_ref[i] = (near_ref[i].astype(f32) + got_ref[i].astype(f32) + more_ref[i].astype(f32)).astype(bf16)
        leaving.append(pltpu.make_async_copy(near_ref.at[i], outs[i], out_sems.at[i]))
        leaving[-1].start()
    for copy in leaving:
        copy.wait()


def row_sum_two(near, got, even, odd, orders):
    quarter, width = near.shape[1] // 4, near.shape[2]
    two = pltpu.VMEM((2, quarter, width), bf16)
    return pl.pallas_call(
        functools.partial(row_sum_two_kernel, len(orders)),
        out_shape=(jax.ShapeDtypeStruct((quarter, width), bf16),) * 2,
        in_specs=[ANY_SPEC] * (4 + len(orders)),
        out_specs=(ANY_SPEC,) * 2,
        scratch_shapes=[two, two, two, pltpu.SemaphoreType.DMA((2, 3)), pltpu.SemaphoreType.DMA((2,))],
        compiler_params=params(60),
        cost_estimate=pl.CostEstimate(flops=1 << 28, bytes_accessed=4 << 20, transcendentals=0),
        name="row_sum_two",
    )(near, got, even, odd, *orders)


def row_sum_three_kernel(n_orders, near_from, got_from, even_from, odd_from, even_got, odd_got, done_from, *refs):
    refs = refs[n_orders:]
    outs, (near_ref, got_ref, one_ref, two_ref, done_ref, in_sems, out_sems) = refs[:4], refs[4:]
    rows = near_ref.shape[1]
    part = pl.ds(0, rows)
    arriving, leaving = [], []
    for i, (one, two) in enumerate(((even_from, even_got), (odd_from, odd_got))):
        pairs = (
            (near_from.at[i, part], near_ref.at[i]),
            (got_from.at[i, part], got_ref.at[i]),
            (one.at[part], one_ref.at[i]),
            (two, two_ref.at[i]),
            (done_from.at[pl.ds(i * rows, rows)], done_ref.at[i]),
        )
        for j, (src, dst) in enumerate(pairs):
            arriving.append(pltpu.make_async_copy(src, dst, in_sems.at[i, j]))
            arriving[-1].start()
    for i in range(2):
        for copy in arriving[5 * i : 5 * i + 5]:
            copy.wait()
        total = near_ref[i].astype(f32) + got_ref[i].astype(f32) + one_ref[i].astype(f32) + two_ref[i].astype(f32)
        near_ref[i] = (total + done_ref[i]).astype(bf16)
        for k in range(2):
            src = near_ref.at[i, pl.ds(k * (rows // 2), rows // 2)]
            leaving.append(pltpu.make_async_copy(src, outs[i + 2 * k], out_sems.at[i, k]))
            leaving[-1].start()
    for copy in leaving:
        copy.wait()


def row_sum_three(near, got, even, odd, even_got, odd_got, d_one, orders):
    quarter, width = near.shape[1] // 4, near.shape[2]
    two = pltpu.VMEM((2, quarter, width), bf16)
    return pl.pallas_call(
        functools.partial(row_sum_three_kernel, len(orders)),
        out_shape=(jax.ShapeDtypeStruct((quarter // 2, width), bf16),) * 4,
        in_specs=[ANY_SPEC] * (7 + len(orders)),
        out_specs=(ANY_SPEC,) * 4,
        scratch_shapes=[two, two, two, two, pltpu.VMEM((2, quarter, width), f32)]
        + [pltpu.SemaphoreType.DMA((2, 5)), pltpu.SemaphoreType.DMA((2, 2))],
        compiler_params=params(60),
        cost_estimate=pl.CostEstimate(flops=1 << 28, bytes_accessed=4 << 20, transcendentals=0),
        name="row_sum_three",
    )(near, got, even, odd, even_got, odd_got, d_one, *orders)


def plane_layer(
    tokens,
    w_qkv,
    bias_qv,
    w_out,
    bias_out,
    gain_one,
    bias_one,
    up_weight,
    up_bias_vector,
    down_weight,
    down_bias_vector,
    gain_two,
    bias_two,
    d_out,
    key_mask,
    rand_idx,
):
    z = lax.axis_index("sq")
    px = lax.axis_index("part")
    hy = lax.axis_index("hy")
    hc = lax.axis_index("hc")
    head = hy * 2 + hc
    span, seqs, width = tokens.shape
    heads, hd = w_qkv.shape[1], w_qkv.shape[3]
    n_o, n_kv = heads * hd, heads * 2 * hd
    hidden_dev = up_weight.shape[1]
    eighth = hidden_dev // 8
    length = key_mask.shape[1]
    blocks_all = length // BLOCK
    rows = seqs * span
    coords = jnp.stack([z, px, hy, hc]).astype(jnp.int32)
    octet = jnp.arange(8)

    def turn_octets(value):
        shape = value.shape
        value = flipped(value.reshape((2, 2, 2) + shape[1:]), z // 2, 0)
        return flipped(flipped(value, z % 2, 1), px, 2).reshape(shape)

    held_zd = octet // 2 % 2 + octet % 2 * 2
    held_order = ((held_zd ^ z) * 2 + ((octet // 4) ^ px)).astype(jnp.int32)
    bias_row = jnp.moveaxis(turn_octets(up_bias_vector.reshape(8, eighth)).reshape(2, 2, 2, eighth), (0, 2), (2, 0))
    bias_row = jnp.pad(bias_row.reshape(1, hidden_dev), ((0, 15), (0, 0)))
    n_wo = n_o // 2 + 16
    wf, wf_first, wo = pack(held_order, up_weight, down_weight, w_out.reshape(n_o, width), bias_row, [])
    wf_y = swap(wf_first, "hy", name="weight")
    wf_c = swap(wf, "hc", name="weight")

    raw = split(coords, tokens, [wf])
    tok = [raw[0]] + [swap(raw[k], "sq", k, name="tok") for k in range(1, 4)]
    w_kv, w_q_pad, w_q, b_kv, b_q = qkv_weights(w_qkv, bias_qv, raw)
    dres_raw = split(coords, d_out, raw)
    dres = [dres_raw[0]] + [swap(dres_raw[k], "sq", k, name="dres") for k in range(1, 4)]
    odd = after(jnp.concatenate([tok[1], tok[3]], axis=0), *tok, w_kv, wf_y, wf_c, *dres_raw)
    even = after(jnp.concatenate([tok[0], tok[2]], axis=0), *tok, w_kv, wf_y, wf_c, *dres_raw)
    even_x = swap(even, "part", name="tok")
    odd_y = swap(odd, "hy", name="tok")
    wo_y = swap(after(wo, odd), "hy", name="weight")
    even_near = after(jnp.concatenate([even, even_x], axis=0), odd_y, wo_y)
    odd_near = after(jnp.concatenate([odd, odd_y], axis=0), even_x)
    even_far = swap(even_near, "hy", name="tok")
    odd_far = swap(odd_near, "part", name="tok")
    mask_seq = lax.dynamic_index_in_dim(key_mask, z, 0, keepdims=False).reshape(blocks_all, BLOCK)
    mask = jnp.where(mask_seq == 1, 0.0, MASK_FILL).astype(f32)
    mask = jnp.pad(jnp.concatenate([mask, mask], axis=1), ((0, 8), (0, 0)), constant_values=MASK_FILL)
    rand = lax.dynamic_slice(rand_idx, (z, 0, head * heads, 0), (1, blocks_all, heads, 3)).reshape(-1)
    even_far = after(even_far, mask, rand, *dres[1:])
    xs = [even_near, even_far, swap(even_near, "hc", name="tok"), swap(even_far, "hc", name="tok")]
    xs += [odd_near, odd_far, swap(odd_near, "hc", name="tok"), swap(odd_far, "hc", name="tok")]
    vecs = jnp.stack([bias_out, gain_one, bias_one, down_bias_vector, gain_two, bias_two])
    vecs = jnp.pad(vecs, ((0, 2), (0, 0)))

    wf_yc = swap(wf_y, "hc", name="weight")
    wf_x = swap(wf_y, "part", name="weight")
    wo_yc = swap(wo_y, "hc", name="weight")

    o_near, o_far, lse, kv, q = project_and_attend(
        heads, hd, span, coords, rand, xs, w_kv, w_q_pad, b_kv, b_q, mask, []
    )
    attn_y = swap(o_far, "hy", name="attn")
    attn_c = swap(o_near[rows:], "hc", name="attn")
    attn_yc = swap(attn_y[rows:], "hc", name="attn")
    wf_x = after(wf_x, attn_c)
    wf_xc = swap(wf_x, "hc", name="weight")

    packs = [wf, wf_c, wo_y, wf_y, wf_x, wo_yc, wf_yc, wf_xc]
    first_rows = tuple((n, n > 0) for n in (n_wo, n_wo, n_wo, 0, 0, n_wo, 0, 0))
    out = rows_work([o_near, attn_c, attn_y, attn_yc], packs, first_rows, [even, odd], dres, vecs)
    result, (d_one, hidden, d_pre, y_low, d_ffn, d_branch, d_00, d_01, d_far, small, bin_sum) = out[:4], out[4:]

    d_y = swap(d_far, "hy", name="dattn")
    d_c = swap(d_01, "hc", name="dattn")
    d_yc = swap(d_y[1], "hc", name="dattn")

    other = rows_grad(1, y_low, d_pre, hidden, d_ffn, d_branch, attn_c, attn_yc, small, bin_sum)
    wide_got = swap(other, "hc", name="wide")
    res = [result[0]] + [swap(result[k], "sq", k, name="result") for k in range(1, 4)]
    keep, to_y, to_x, *across, small = rows_grad(
        0, y_low, d_pre, hidden, d_ffn, d_branch, o_near, attn_y, small, bin_sum, wide_got, [d_y, d_c]
    )
    y_got = swap(to_y, "hy", name="wide")
    x_got = swap(to_x, "part", name="wide")
    across_got = [swap(across[p], "sq", k, name="wide") for p, k in ((2, 1), (1, 2), (3, 3))]

    dq, dkv, dx, dx_far = attend_back(
        heads,
        hd,
        span,
        coords,
        rand,
        q,
        [d_00, d_c, d_y, d_yc],
        [o_near, o_far],
        kv,
        mask,
        lse,
        w_kv,
        w_q,
        [to_y, to_x, *across, *res[1:]],
    )
    dx_far = after(dx_far, y_got, x_got, *across_got)

    dx_got = swap(dx_far, "hc", name="dtok")
    octets = octet[:4]
    beyond = across_sum([across[0]] + across_got)
    wide = wide_sum(((octets // 2 + octets % 2 * 2) ^ z).astype(jnp.int32), keep, y_got, x_got, [beyond])
    beyond = swap_both(beyond, "across")
    zq, xq = octet // 2, octet % 2
    zd = zq ^ z
    spots = ((xq ^ px) * 4 + (zd % 2) * 2 + zd // 2).astype(jnp.int32)
    tail, tail_got = qkv_grad(span, spots, coords, dq, dkv, keep, y_got, small, xs, [wide])
    wide = lax.psum_scatter(wide, "sq", scatter_dimension=0, tiled=True)[0]
    tail_got = swap(tail_got, "part", name="tail")
    sent = row_sum_one(dx, dx_got, [tail])
    even_got, odd_got = swap(sent[0], "hy", name="dtok"), swap(sent[1], "part", name="dtok")
    keep, send = tail_sum(tail, tail_got, [*sent])
    wide = wide_end(wide, beyond, [*sent, keep])
    wide_two = swap(wide, "sq", 2, name="wide")
    wide = [wide, swap(wide, "sq", 1, name="wide")]
    own, send = tail_mid(keep, swap(send, "sq", 1, name="tail"))
    back_spots = (((octet % 4) ^ z) * 2 + ((octet // 4) ^ px)).astype(jnp.int32)
    sent_two = row_sum_two(dx, dx_got, even_got, odd_got, [send])
    wide[1], wide_two = after(wide[1], send), after(wide_two, send)
    wide += [wide_two, swap(wide_two, "sq", 1, name="wide")]
    wide += [swap(a, "part", name="wide") for a in wide]
    own = tail_end(own, swap(send, "sq", 2, name="tail"), [*sent_two])
    even_got2, odd_got2 = swap(sent_two[0], "part", name="dtok"), swap(sent_two[1], "hy", name="dtok")
    back_sent = row_sum_three(dx, dx_got, even_got, odd_got, even_got2, odd_got2, d_one, [own])
    back = [back_sent[0]] + [swap(back_sent[k], "sq", k, name="dtok") for k in range(1, 4)]

    beyond = swap(own, "sq", 2, name="tail")
    thin_held = [own, swap(own, "sq", 1, name="tail"), beyond, swap(beyond, "sq", 1, name="tail")]
    thin_held += [swap(a, "part", name="tail") for a in thin_held]
    grad_w_in, grad_w_back = wide_place(back_spots, wide, [*back_sent])
    thin, grad_w_out, small = tail_place(
        back_spots, thin_held, n_o + n_kv, heads, [grad_w_in, grad_w_back]
    )
    grad_w_out = grad_w_out.reshape(heads, hd, width)
    grad_w_qkv = thin.reshape(width, heads, 3, hd)
    small = small.reshape(8, 1024)
    grad_bias_qv = jnp.stack(
        [small[7, :n_o].reshape(heads, hd), small[7, n_o : n_o + n_kv].reshape(heads, 2, hd)[:, 1]], axis=1
    )
    small = small[:, :width]
    return (
        jnp.transpose(relative(jnp.stack(res), z), (1, 0, 2)),
        jnp.transpose(relative(jnp.stack(back), z), (1, 0, 2)),
        grad_w_qkv,
        grad_bias_qv,
        grad_w_out,
        small[0],
        small[1],
        small[2],
        grad_w_in,
        small[6],
        grad_w_back,
        small[3],
        small[4],
        small[5],
    )


def solution(mesh):
    seq_size, head_size = mesh.shape["seq"], mesh.shape["head"]

    def run(*args):
        seqs = args[0].shape[1]
        fine = Mesh(
            np.asarray(mesh.devices).reshape(seqs, seq_size // seqs, head_size // 2, 2),
            ("sq", "part", "hy", "hc"),
        )
        rows = P(("sq", "part", "hy", "hc"), None, None)
        span = args[0].shape[0] // (seq_size * head_size)
        fits = seqs == 4 and seq_size == 8 and head_size == 4 and span % BLOCK == 0
        layer = plane_layer if fits else general_layer
        placed = (
            rows,
            P(None, HEAD, None, None),
            P(HEAD, None, None),
            P(HEAD, None, None),
            P(),
            P(),
            P(),
            P(None, HEAD),
            P(HEAD),
            P(HEAD, None),
            P(),
            P(),
            P(),
            rows,
            P(),
            P(),
        )
        return jax.shard_map(
            layer,
            mesh=fine,
            in_specs=placed,
            out_specs=(
                rows,
                rows,
                P(None, HEAD, None, None),
                P(HEAD, None, None),
                P(HEAD, None, None),
                P(),
                P(),
                P(),
                P(None, HEAD),
                P(HEAD),
                P(HEAD, None),
                P(),
                P(),
                P(),
            ),
            check_vma=False,
        )(*args)

    return run
```

```python
import functools

import jax
import jax.numpy as jnp
import numpy as np
from jax import lax
from jax.experimental import pallas as pl
from jax.experimental.pallas import tpu as pltpu
from jax.sharding import Mesh
from jax.sharding import PartitionSpec as P

BLOCK = 64
PICKS = 8
CHUNK = 512
NORM_EPS = 1e-12
MASK_FILL = -1000000000.0

f32 = jnp.float32
bf16 = jnp.bfloat16

PLANE = ("part", "hy", "hc")
HEAD = ("hy", "hc")
SEQ = ("sq", "part")


def norm_fwd(resid, gain, shift):
    row_mean = jnp.mean(resid, axis=-1, keepdims=True)
    centred = resid - row_mean
    inv_std = lax.rsqrt(jnp.mean(centred * centred, axis=-1, keepdims=True) + NORM_EPS)
    normed = centred * inv_std
    return (normed * gain + shift, normed, inv_std)


def norm_back(upstream, normed, inv_std, gain):
    d_normed = upstream * gain
    d_resid = inv_std * (
        d_normed
        - jnp.mean(d_normed, axis=-1, keepdims=True)
        - normed * jnp.mean(d_normed * normed, axis=-1, keepdims=True)
    )
    return (d_resid, jnp.sum(upstream * normed, axis=0), jnp.sum(upstream, axis=0))


def tanh_gelu(values):
    return jax.nn.gelu(values, approximate=True)


def gelu_back(preactivation_values, upstream):
    return jax.vjp(tanh_gelu, preactivation_values)[1](upstream)[0]


def dot_nt(a, b):
    return lax.dot_general(a, b, (((1,), (1,)), ((), ())), preferred_element_type=f32)


def dot_nn(a, b):
    return lax.dot_general(a, b, (((1,), (0,)), ((), ())), preferred_element_type=f32)


def dot_tn(a, b):
    return lax.dot_general(a, b, (((0,), (0,)), ((), ())), preferred_element_type=f32)


def gathered(kv_ref, table_ref, base, cols):
    return jnp.concatenate(
        [
            kv_ref[pl.ds(pl.multiple_of(table_ref[base + u] * BLOCK, BLOCK), BLOCK), cols]
            for u in range(PICKS)
        ],
        axis=0,
    )


def lane_pick(values, lane):
    lanes = lax.broadcasted_iota(jnp.int32, values.shape, 1)
    return jnp.sum(jnp.where(lanes == lane, values, 0.0), axis=1, keepdims=True)


def attn_fwd_kernel(heads, hd, table_ref, edge_ref, q_ref, kv_ref, bias_ref, mask_ref, o_ref, lse_ref, s_ref):
    wide = 2 * hd
    blocks = q_ref.shape[0] // BLOCK
    chunks = kv_ref.shape[0] // CHUNK
    lanes = lax.broadcasted_iota(jnp.int32, (BLOCK, 128), 1)

    def one(jl, carry):
        rows = pl.ds(pl.multiple_of(jl * BLOCK, BLOCK), BLOCK)
        outs = []
        lse_tile = jnp.zeros((BLOCK, 128), f32)
        for h in range(heads):
            cols = slice(h * wide, (h + 1) * wide)
            kvg = gathered(kv_ref, table_ref, (jl * heads + h) * PICKS, cols)
            s = dot_nt(q_ref[rows, cols], kvg) + bias_ref[jl, h : h + 1, :]
            top = jnp.max(s, axis=1, keepdims=True)
            p = jnp.exp(s - top)
            total = jnp.sum(p, axis=1, keepdims=True)
            low = (p * (1.0 / total)).astype(bf16)
            outs.append(dot_nn(low, kvg)[:, hd:])
            lse_tile = jnp.where(lanes == h, top + jnp.log(total), lse_tile)
        o_ref[rows, :] = jnp.concatenate(outs, axis=1).astype(bf16)
        lse_ref[rows, :] = lse_tile
        return carry

    lax.fori_loop(0, blocks, one, 0)

    def edge(jl):
        rows = slice(jl * BLOCK, (jl + 1) * BLOCK)
        outs = []
        lse_tile = jnp.zeros((BLOCK, 128), f32)
        for h in range(heads):
            cols = slice(h * wide, (h + 1) * wide)
            q = q_ref[rows, cols]

            def score(c, top):
                part = pl.ds(pl.multiple_of(c * CHUNK, CHUNK), CHUNK)
                s = dot_nt(q, kv_ref[part, cols]) + mask_ref[:, part]
                s_ref[:, part] = s
                return jnp.maximum(top, jnp.max(s, axis=1, keepdims=True))

            top = lax.fori_loop(0, chunks, score, jnp.full((BLOCK, 1), -3e38, f32))

            def add(c, total):
                part = pl.ds(pl.multiple_of(c * CHUNK, CHUNK), CHUNK)
                return total + jnp.sum(jnp.exp(s_ref[:, part] - top), axis=1, keepdims=True)

            total = lax.fori_loop(0, chunks, add, jnp.zeros((BLOCK, 1), f32))
            inv = 1.0 / total

            def out(c, acc):
                part = pl.ds(pl.multiple_of(c * CHUNK, CHUNK), CHUNK)
                low = (jnp.exp(s_ref[:, part] - top) * inv).astype(bf16)
                return acc + dot_nn(low, kv_ref[part, cols])

            acc = lax.fori_loop(0, chunks, out, jnp.zeros((BLOCK, wide), f32))
            outs.append(acc[:, hd:])
            lse_tile = jnp.where(lanes == h, top + jnp.log(total), lse_tile)
        o_ref[rows, :] = jnp.concatenate(outs, axis=1).astype(bf16)
        lse_ref[rows, :] = lse_tile

    @pl.when(edge_ref[0] == 1)
    def _():
        edge(0)

    @pl.when(edge_ref[1] == 1)
    def _():
        edge(blocks - 1)


def attn_bwd_kernel(
    heads, hd, scale, table_ref, edge_ref, qd_ref, kv_ref, bias_ref, mask_ref, lse_ref, dq_ref, dkv_ref, acc_ref, p_ref, dp_ref
):
    wide = 2 * hd
    blocks = qd_ref.shape[0] // BLOCK
    chunks = kv_ref.shape[0] // CHUNK
    left = lax.broadcasted_iota(jnp.int32, (BLOCK, wide), 1) < hd
    nil = jnp.zeros((BLOCK, wide), bf16)

    def clear(c, carry):
        part = pl.ds(pl.multiple_of(c * CHUNK, CHUNK), CHUNK)
        acc_ref[part, :] = jnp.zeros((CHUNK, heads * wide), f32)
        return carry

    lax.fori_loop(0, chunks, clear, 0)

    def stacked(qd):
        return jnp.concatenate([jnp.where(left, qd, nil), jnp.where(left, nil, qd)], axis=0)

    def one(jl, carry):
        rows = pl.ds(pl.multiple_of(jl * BLOCK, BLOCK), BLOCK)
        lse_tile = lse_ref[rows, :]
        outs = []
        for h in range(heads):
            cols = slice(h * wide, (h + 1) * wide)
            base = (jl * heads + h) * PICKS
            kvg = gathered(kv_ref, table_ref, base, cols)
            both = stacked(qd_ref[rows, cols])
            prod = dot_nt(both, kvg)
            p = jnp.exp(prod[:BLOCK] + bias_ref[jl, h : h + 1, :] - lane_pick(lse_tile, h))
            dp = prod[BLOCK:]
            dot_row = jnp.sum(p * dp, axis=1, keepdims=True)
            ds = (p * (dp - dot_row)).astype(bf16)
            outs.append(dot_nn(ds, kvg)[:, :hd])
            dkv = dot_tn(jnp.concatenate([ds, p.astype(bf16)], axis=0), both)
            for u in range(PICKS):
                place = pl.ds(pl.multiple_of(table_ref[base + u] * BLOCK, BLOCK), BLOCK)
                acc_ref[place, cols] += dkv[u * BLOCK : (u + 1) * BLOCK]
        dq_ref[rows, :] = (jnp.concatenate(outs, axis=1) * scale).astype(bf16)
        return carry

    lax.fori_loop(edge_ref[0], blocks - edge_ref[1], one, 0)

    def edge(jl):
        rows = slice(jl * BLOCK, (jl + 1) * BLOCK)
        lse_tile = lse_ref[rows, :]
        outs = []
        for h in range(heads):
            cols = slice(h * wide, (h + 1) * wide)
            both = stacked(qd_ref[rows, cols])
            lse = lane_pick(lse_tile, h)

            def first(c, total):
                part = pl.ds(pl.multiple_of(c * CHUNK, CHUNK), CHUNK)
                prod = dot_nt(both, kv_ref[part, cols])
                p = jnp.exp(prod[:BLOCK] + mask_ref[:, part] - lse)
                dp = prod[BLOCK:]
                p_ref[:, part] = p
                dp_ref[:, part] = dp
                return total + jnp.sum(p * dp, axis=1, keepdims=True)

            dot_row = lax.fori_loop(0, chunks, first, jnp.zeros((BLOCK, 1), f32))

            def second(c, dq):
                part = pl.ds(pl.multiple_of(c * CHUNK, CHUNK), CHUNK)
                p = p_ref[:, part]
                ds = (p * (dp_ref[:, part] - dot_row)).astype(bf16)
                acc_ref[part, cols] += dot_tn(jnp.concatenate([ds, p.astype(bf16)], axis=0), both)
                return dq + dot_nn(ds, kv_ref[part, cols])

            dq = lax.fori_loop(0, chunks, second, jnp.zeros((BLOCK, wide), f32))
            outs.append(dq[:, :hd])
        dq_ref[rows, :] = (jnp.concatenate(outs, axis=1) * scale).astype(bf16)

    @pl.when(edge_ref[0] == 1)
    def _():
        edge(0)

    @pl.when(edge_ref[1] == 1)
    def _():
        edge(blocks - 1)

    def put(c, carry):
        part = pl.ds(pl.multiple_of(c * CHUNK, CHUNK), CHUNK)
        dkv_ref[part, :] = acc_ref[part, :].astype(bf16)
        return carry

    lax.fori_loop(0, chunks, put, 0)


SMEM_SPEC = pl.BlockSpec(memory_space=pltpu.SMEM)
VMEM_SPEC = pl.BlockSpec(memory_space=pltpu.VMEM)
VMEM_LIMIT = 48 * 1024 * 1024


def attn_forward(heads, hd, table, edges, q, kv, bias, mask):
    rows, keys = q.shape[0], kv.shape[0]
    return pl.pallas_call(
        functools.partial(attn_fwd_kernel, heads, hd),
        out_shape=(
            jax.ShapeDtypeStruct((rows, heads * hd), bf16),
            jax.ShapeDtypeStruct((rows, 128), f32),
        ),
        in_specs=[SMEM_SPEC] * 2 + [VMEM_SPEC] * 4,
        out_specs=(VMEM_SPEC, VMEM_SPEC),
        scratch_shapes=[pltpu.VMEM((BLOCK, keys), f32)],
        compiler_params=pltpu.CompilerParams(vmem_limit_bytes=VMEM_LIMIT),
        cost_estimate=pl.CostEstimate(
            flops=4 * rows * heads * CHUNK * 2 * hd, bytes_accessed=8 << 20, transcendentals=rows * heads * CHUNK
        ),
        name="attn_forward",
    )(table, edges, q, kv, bias, mask)


def attn_backward(heads, hd, scale, table, edges, qd, kv, bias, mask, lse):
    rows, keys = qd.shape[0], kv.shape[0]
    return pl.pallas_call(
        functools.partial(attn_bwd_kernel, heads, hd, scale),
        out_shape=(
            jax.ShapeDtypeStruct((rows, heads * hd), bf16),
            jax.ShapeDtypeStruct((keys, heads * 2 * hd), bf16),
        ),
        in_specs=[SMEM_SPEC] * 2 + [VMEM_SPEC] * 5,
        out_specs=(VMEM_SPEC, VMEM_SPEC),
        scratch_shapes=[
            pltpu.VMEM((keys, heads * 2 * hd), f32),
            pltpu.VMEM((BLOCK, keys), f32),
            pltpu.VMEM((BLOCK, keys), f32),
        ],
        compiler_params=pltpu.CompilerParams(vmem_limit_bytes=VMEM_LIMIT),
        cost_estimate=pl.CostEstimate(
            flops=10 * rows * heads * CHUNK * 2 * hd, bytes_accessed=12 << 20, transcendentals=rows * heads * CHUNK
        ),
        name="attn_backward",
    )(table, edges, qd, kv, bias, mask, lse)


def general_layer(
    tokens,
    w_qkv,
    bias_qv,
    w_out,
    bias_out,
    gain_one,
    bias_one,
    up_weight,
    up_bias_vector,
    down_weight,
    down_bias_vector,
    gain_two,
    bias_two,
    d_out,
    key_mask,
    rand_idx,
):
    sq = lax.axis_index("sq")
    part = lax.axis_index("part")
    head = lax.axis_index(HEAD)
    parts = lax.axis_size("part")
    groups = lax.axis_size(HEAD)
    span, seqs, width = tokens.shape
    heads, hd = w_qkv.shape[1], w_qkv.shape[3]
    scale = hd ** (-0.5)
    length = key_mask.shape[1]
    blocks_all = length // BLOCK
    per_chunk = groups * span // BLOCK
    mine = seqs * per_chunk

    tok = lax.all_to_all(jnp.transpose(tokens, (1, 0, 2)), "sq", 0, 0, tiled=True)
    x_all = lax.all_gather(tok, PLANE, axis=0, tiled=False)
    d_res = lax.all_to_all(jnp.transpose(d_out, (1, 0, 2)), "sq", 0, 0, tiled=True)

    w_out_full = lax.all_gather(w_out.reshape(heads * hd, width), HEAD, axis=0, tiled=False)
    up_full = lax.all_gather(up_weight, HEAD, axis=0, tiled=False)
    down_full = lax.all_gather(down_weight, HEAD, axis=0, tiled=False)
    up_bias_full = lax.all_gather(up_bias_vector.astype(f32), HEAD, axis=0, tiled=False)

    chunk_ids = jnp.arange(seqs) * parts + part
    block_ids = (chunk_ids[:, None] * per_chunk + jnp.arange(per_chunk)[None, :]).reshape(mine)
    rand_seq = lax.dynamic_index_in_dim(rand_idx, sq, 0, keepdims=False)
    rand_head = lax.dynamic_slice_in_dim(rand_seq, head * heads, heads, 1)
    chosen = jnp.take(rand_head, block_ids, axis=0)
    window = block_ids[:, None] + jnp.arange(-1, 2)[None, :]
    window_ok = (window >= 1) & (window <= blocks_all - 2)
    fixed_ids = jnp.concatenate(
        [
            jnp.clip(window, 0, blocks_all - 1),
            jnp.broadcast_to(jnp.array([0, blocks_all - 1], jnp.int32), (mine, 2)),
        ],
        axis=1,
    )
    fixed_ok = jnp.concatenate([window_ok, jnp.ones((mine, 2), bool)], axis=1)
    table = jnp.concatenate(
        [jnp.broadcast_to(fixed_ids[:, None, :], (mine, heads, 5)), chosen], axis=2
    )
    table_ok = jnp.concatenate(
        [
            jnp.broadcast_to(fixed_ok[:, None, :], (mine, heads, 5)),
            jnp.ones((mine, heads, PICKS - 5), bool),
        ],
        axis=2,
    )
    mask_seq = lax.dynamic_index_in_dim(key_mask, sq, 0, keepdims=False)
    mask_blocks = (mask_seq == 1).reshape(blocks_all, BLOCK).astype(bf16)
    onehot = (table[..., None] == jnp.arange(blocks_all)).astype(bf16) * table_ok[..., None].astype(bf16)
    allowed = jnp.einsum("jhub,bk->jhuk", onehot, mask_blocks, preferred_element_type=f32)
    bias_rows = ((1.0 - allowed) * MASK_FILL).reshape(mine, heads, PICKS * BLOCK)
    mask_row = jnp.where(mask_seq == 1, 0.0, MASK_FILL).astype(f32).reshape(1, length)
    edges = jnp.stack([part == 0, part == parts - 1]).astype(jnp.int32)
    table = table.reshape(-1).astype(jnp.int32)

    w_kv = w_qkv[:, :, 1:].reshape(width, heads * 2 * hd)
    bias_kv = jnp.stack([jnp.zeros((heads, hd), f32), bias_qv[:, 1]], axis=1).reshape(heads * 2 * hd)
    w_q = w_qkv[:, :, 0].reshape(width, heads * hd)
    bias_q = bias_qv[:, 0].reshape(heads * hd)
    x_rows = x_all.reshape(parts, groups, seqs, span, width)
    x_mine = lax.dynamic_index_in_dim(x_rows, part, 0, keepdims=False)
    kv_rows = (jnp.einsum("pgzsd,dc->pgzsc", x_rows, w_kv, preferred_element_type=f32) + bias_kv).astype(bf16)
    kv = jnp.transpose(kv_rows, (2, 0, 1, 3, 4)).reshape(length, heads * 2 * hd)
    q_rows = (jnp.einsum("gzsd,dc->gzsc", x_mine, w_q, preferred_element_type=f32) + bias_q).astype(bf16)
    q_low = jnp.transpose(q_rows, (1, 0, 2, 3)).reshape(mine * BLOCK, heads, hd) * bf16(scale)
    q_pad = jnp.concatenate([q_low, jnp.zeros_like(q_low)], axis=-1).reshape(mine * BLOCK, heads * 2 * hd)

    attn_mine, lse = attn_forward(heads, hd, table, edges, q_pad, kv, bias_rows, mask_row)
    attn_send = jnp.transpose(attn_mine.reshape(seqs, groups, span, heads * hd), (1, 0, 2, 3))
    attn = lax.all_to_all(attn_send, HEAD, 0, 0, tiled=True).reshape(groups, seqs * span, heads * hd)

    rows = seqs * span
    tok_rows = tok.reshape(rows, width)
    branch = jnp.einsum("grc,gcd->rd", attn, w_out_full, preferred_element_type=f32) + bias_out
    y_one, normed_one, inv_one = norm_fwd(tok_rows.astype(f32) + branch, gain_one, bias_one)
    y_low = y_one.astype(bf16)
    pre = jnp.einsum("rd,gdf->grf", y_low, up_full, preferred_element_type=f32) + up_bias_full[:, None, :]
    hidden = tanh_gelu(pre).astype(bf16)
    ffn = jnp.einsum("grf,gfd->rd", hidden, down_full, preferred_element_type=f32) + down_bias_vector
    result, normed_two, inv_two = norm_fwd(y_one + ffn, gain_two, bias_two)
    result = lax.all_to_all(result.astype(bf16).reshape(seqs, span, width), "sq", 0, 0, tiled=True)
    d_two, grad_gain_two, grad_bias_two = norm_back(
        d_res.reshape(rows, width).astype(f32), normed_two, inv_two, gain_two
    )
    d_ffn = d_two.astype(bf16)
    grad_bias_back = jnp.sum(d_ffn.astype(f32), axis=0)
    d_hidden = jnp.einsum("rd,gfd->grf", d_ffn, down_full, preferred_element_type=f32)
    d_pre = gelu_back(pre, d_hidden).astype(bf16)
    d_y_ffn = jnp.einsum("grf,gdf->rd", d_pre, up_full, preferred_element_type=f32)
    grad_w_in = jnp.einsum("rd,grf->gdf", y_low, d_pre, preferred_element_type=f32).astype(bf16)
    grad_bias_in = jnp.sum(d_pre.astype(f32), axis=1)
    grad_w_back = jnp.einsum("grf,rd->gfd", hidden, d_ffn, preferred_element_type=f32).astype(bf16)
    d_one, grad_gain_one, grad_bias_one = norm_back(d_two + d_y_ffn, normed_one, inv_one, gain_one)
    d_branch = d_one.astype(bf16)
    grad_bias_out = jnp.sum(d_branch.astype(f32), axis=0)
    d_attn = jnp.einsum("rd,gcd->grc", d_branch, w_out_full, preferred_element_type=f32).astype(bf16)
    grad_w_out = jnp.einsum("grc,rd->gcd", attn, d_branch, preferred_element_type=f32).astype(bf16)

    d_attn_mine = lax.all_to_all(d_attn.reshape(groups, seqs, span, heads * hd), HEAD, 0, 0, tiled=True)
    d_attn_nat = jnp.transpose(d_attn_mine, (1, 0, 2, 3)).reshape(mine * BLOCK, heads, hd)
    qd = jnp.concatenate([q_low, d_attn_nat], axis=-1).reshape(mine * BLOCK, heads * 2 * hd)

    wide_part = jnp.concatenate([grad_w_in, grad_w_back, grad_w_out], axis=1)
    wide_sum = lax.psum_scatter(wide_part, HEAD, scatter_dimension=0, tiled=True)[0]
    wide_sum = lax.psum(wide_sum, SEQ)

    dq, dkv = attn_backward(heads, hd, scale, table, edges, qd, kv, bias_rows, mask_row, lse)
    dkv_rows = jnp.transpose(
        dkv.reshape(seqs, parts, groups, span, heads * 2 * hd), (1, 2, 0, 3, 4)
    )
    dq_rows = jnp.transpose(dq.reshape(seqs, groups, span, heads * hd), (1, 0, 2, 3))
    dq_all = lax.dynamic_update_index_in_dim(
        jnp.zeros((parts, groups, seqs, span, heads * hd), bf16), dq_rows, part, 0
    )
    d_x = jnp.einsum("pgzsc,dc->pgzsd", dkv_rows, w_kv, preferred_element_type=f32) + jnp.einsum(
        "pgzsc,dc->pgzsd", dq_all, w_q, preferred_element_type=f32
    )
    d_x = lax.psum_scatter(
        d_x.astype(bf16).reshape(parts * groups, seqs, span, width), PLANE, scatter_dimension=0, tiled=True
    )
    d_tok = (d_one + d_x.reshape(rows, width).astype(f32)).astype(bf16)
    d_tok = lax.all_to_all(d_tok.reshape(seqs, span, width), "sq", 0, 0, tiled=True)

    grad_kv = jnp.einsum("pgzsd,pgzsc->dc", x_rows, dkv_rows, preferred_element_type=f32)
    grad_q = jnp.einsum("gzsd,gzsc->dc", x_mine, dq_rows, preferred_element_type=f32)
    grad_w_qkv = jnp.concatenate(
        [grad_q.reshape(width, heads, 1, hd), grad_kv.reshape(width, heads, 2, hd)], axis=2
    )
    bias_q_sum = jnp.sum(dq_rows.astype(f32), axis=(0, 1, 2)).reshape(heads, 1, hd)
    bias_v_sum = jnp.sum(dkv_rows.astype(f32), axis=(0, 1, 2, 3)).reshape(heads, 2, hd)[:, 1:]
    grad_bias_qv = jnp.concatenate([bias_q_sum, bias_v_sum], axis=1)
    grad_w_qkv = lax.psum(grad_w_qkv.astype(bf16), SEQ).astype(f32)

    small = jnp.stack(
        [grad_bias_out, grad_gain_one, grad_bias_one, grad_bias_back, grad_gain_two, grad_bias_two]
    )
    all_bias_in = grad_bias_in
    bias_qv_all = lax.dynamic_update_index_in_dim(
        jnp.zeros((groups, heads * 2 * hd), f32), grad_bias_qv.reshape(-1), head, 0
    )
    packed = jnp.concatenate([small.reshape(-1), all_bias_in.reshape(-1), bias_qv_all.reshape(-1)])
    packed = lax.psum(packed, ("sq", "part", "hy", "hc"))
    n_small = 6 * width
    small = packed[:n_small].reshape(6, width)
    n_in = n_small + all_bias_in.size
    hidden_dev = up_weight.shape[1]
    grad_bias_in = lax.dynamic_slice_in_dim(packed[n_small:n_in], head * hidden_dev, hidden_dev, 0)
    grad_bias_qv = lax.dynamic_slice_in_dim(
        packed[n_in:], head * heads * 2 * hd, heads * 2 * hd, 0
    ).reshape(heads, 2, hd)

    wide_sum = wide_sum.astype(f32)
    grad_w_in = wide_sum[:width]
    grad_w_back = wide_sum[width : width + hidden_dev]
    grad_w_out = wide_sum[width + hidden_dev :].reshape(heads, hd, width)
    return (
        jnp.transpose(result, (1, 0, 2)),
        jnp.transpose(d_tok, (1, 0, 2)),
        grad_w_qkv,
        grad_bias_qv,
        grad_w_out,
        small[0],
        small[1],
        small[2],
        grad_w_in,
        grad_bias_in,
        grad_w_back,
        small[3],
        small[4],
        small[5],
    )


def swap(value, axis, step=1, name="swap"):
    size = lax.axis_size(axis)
    with jax.named_scope(name + "_" + axis + str(step)):
        return lax.ppermute(value, axis, [(i, i ^ step) for i in range(size)])


def flipped(value, bit, axis):
    return jnp.where(bit == 1, jnp.flip(value, axis), value)


def relative(value, place):
    shape = value.shape
    value = value.reshape((2, 2) + shape[1:])
    value = flipped(flipped(value, place // 2, 0), place % 2, 1)
    return value.reshape(shape)


def swap_both(value, name):
    order = [(i, i ^ 3) for i in range(4)]
    with jax.named_scope(name + "_both"):
        return lax.ppermute(value, ("part", "hy"), order)


ANY_SPEC = pl.BlockSpec(memory_space=pl.ANY)


def after(value, *orders):
    return pl.pallas_call(
        lambda *refs: None,
        out_shape=jax.ShapeDtypeStruct(value.shape, value.dtype),
        in_specs=[ANY_SPEC] * (1 + len(orders)),
        out_specs=ANY_SPEC,
        input_output_aliases={0: 0},
        name="after",
    )(value, *orders)


def params(limit_mb):
    return pltpu.CompilerParams(vmem_limit_bytes=limit_mb * 1024 * 1024)


def fill_tables(coord_ref, rand_ref, place_ref, nat_ref, heads, span):
    per_span = span // BLOCK

    def one(b, carry):
        own = b // per_span
        kz = (own // 8) ^ coord_ref[0]
        kx = (own // 4 % 2) ^ coord_ref[1]
        ky = (own // 2 % 2) ^ coord_ref[2]
        kc = (own % 2) ^ coord_ref[3]
        odd = kz % 2
        one, two = jnp.where(odd == 0, kx, ky), jnp.where(odd == 0, ky, kx)
        spot = ((((odd * 2 + kc) * 2 + two) * 2 + one) * 2 + kz // 2) * per_span + b % per_span
        place_ref[b] = spot
        nat_ref[spot] = b
        return carry

    lax.fori_loop(0, place_ref.shape[0], one, 0)


def natural_block(coord_ref, jl, per_span):
    kz = (jl // per_span % 2 * 2 + jl // (per_span * 2) % 2) ^ coord_ref[0]
    kc = jl // (per_span * 4) % 2 ^ coord_ref[3]
    ky = jl // (per_span * 8) ^ coord_ref[2]
    return (((kz * 2 + coord_ref[1]) * 2 + ky) * 2 + kc) * per_span + jl % per_span


def edge_of(coord_ref, blocks, per_span):
    last = coord_ref[1]
    kz = (last * 3) ^ coord_ref[0]
    ky = last ^ coord_ref[2]
    kc = last ^ coord_ref[3]
    return ((ky * 2 + kc) * 4 + kz % 2 * 2 + kz // 2) * per_span + last * (per_span - 1)


def picks_of(coord_ref, rand_ref, jl, h, heads, per_span, blocks_all):
    b = natural_block(coord_ref, jl, per_span)
    inner = (b > 0) & (b < blocks_all - 1)
    ids, rows = [], []
    for u in range(3):
        key = b + u - 1
        ids.append(jnp.clip(key, 0, blocks_all - 1))
        rows.append(jnp.where(inner & (key >= 1) & (key <= blocks_all - 2), key, blocks_all))
    for key in (0, blocks_all - 1):
        ids.append(key)
        rows.append(jnp.where(inner, key, blocks_all))
    for u in range(3):
        key = rand_ref[(b * heads + h) * 3 + u]
        ids.append(key)
        rows.append(jnp.where(inner, key, blocks_all))
    return ids, rows


def mask_of(mask_ref, rows, left):
    pairs = []
    for u in range(0, len(rows), 2):
        a, b = mask_ref[pl.ds(rows[u], 1), :], mask_ref[pl.ds(rows[u + 1], 1), :]
        pairs.append(jnp.where(left, a, b))
    return jnp.concatenate(pairs, axis=1)


def blocks_of(kv_ref, place_ref, ids, cols):
    return jnp.concatenate(
        [kv_ref[pl.ds(pl.multiple_of(place_ref[b] * BLOCK, BLOCK), BLOCK), cols] for b in ids], axis=0
    )


def query_pieces(pair):
    out = []
    for ky in range(2):
        for kc in range(2):
            at = (ky * 2 + kc) * 2 * pair
            out.append((at, kc * 2 + ky, 0))
            out.append((at + pair, 4 + kc * 2, ky * pair))
    return out


def project_and_attend_kernel(heads, hd, span, n_orders, coord_ref, rand_ref, *refs):
    x_from = refs[:8]
    w_from, (b_kv_ref, b_q_ref, mask_ref) = refs[8:10], refs[10:13]
    refs = refs[13 + n_orders :]
    outs, refs = refs[:5], refs[5:]
    x_refs, (w_kv_ref, w_q_ref), o_refs = refs[:8], refs[8:10], refs[10:12]
    lse_ref, kv_ref, q_ref, s_ref, place_ref, nat_ref, in_sems, out_sems = refs[12:]
    arriving = [
        pltpu.make_async_copy(a, b, in_sems.at[i])
        for i, (a, b) in enumerate(zip((*w_from, *x_from), (w_kv_ref, w_q_ref, *x_refs)))
    ]
    for copy in arriving:
        copy.start()
    leaving = []

    def leave(src, dst):
        leaving.append(pltpu.make_async_copy(src, dst, out_sems.at[len(leaving)]))
        leaving[-1].start()

    near = o_refs[0].shape[0] // BLOCK
    wide = 2 * hd
    piece, pair = 4 * span, 2 * span
    per_span = span // BLOCK
    blocks = q_ref.shape[0] // BLOCK
    blocks_all = kv_ref.shape[0] // BLOCK
    chunks = kv_ref.shape[0] // CHUNK
    lanes = lax.broadcasted_iota(jnp.int32, (BLOCK, 128), 1)
    left = lax.broadcasted_iota(jnp.int32, (1, 128), 1) < BLOCK
    fill_tables(coord_ref, rand_ref, place_ref, nat_ref, heads, span)

    arriving[0].wait()
    arriving[1].wait()
    for n, x_ref in enumerate(x_refs):
        arriving[2 + n].wait()
        of = slice(n * piece, (n + 1) * piece)
        kv_ref[of, :] = (dot_nn(x_ref[...], w_kv_ref[...]) + b_kv_ref[...]).astype(bf16)
        leave(kv_ref.at[of], outs[3].at[of])
    for at, n, src in query_pieces(pair):
        x = x_refs[n][src : src + pair, :]
        q_ref[at : at + pair, :] = (dot_nn(x, w_q_ref[...]) + b_q_ref[...]).astype(bf16) * bf16(hd**-0.5)
    leave(q_ref, outs[4])

    def finish(jl, accs, tops, totals):
        lse_tile = jnp.zeros((BLOCK, 128), f32)
        for h in range(heads):
            lse_tile = jnp.where(lanes == h, tops[h] + jnp.log(totals[h]), lse_tile)
        lse_ref[pl.ds(pl.multiple_of(jl * BLOCK, BLOCK), BLOCK), :] = lse_tile
        return jnp.concatenate([accs[h][:, hd:] * (1.0 / totals[h]) for h in range(heads)], axis=1).astype(bf16)

    def put(o_ref, jl, value):
        o_ref[pl.ds(pl.multiple_of(jl * BLOCK, BLOCK), BLOCK), :] = value

    unroll = 4

    def some(half, it, carry):
        items = [(half * near + it * unroll + u, h) for u in range(unroll) for h in range(heads)]
        scores, kvs = [], []
        for jl, h in items:
            rows = pl.ds(pl.multiple_of(jl * BLOCK, BLOCK), BLOCK)
            cols = slice(h * wide, (h + 1) * wide)
            ids, mask_rows = picks_of(coord_ref, rand_ref, jl, h, heads, per_span, blocks_all)
            kvg = blocks_of(kv_ref, place_ref, ids, cols)
            scores.append(dot_nt(q_ref[rows, cols], kvg) + mask_of(mask_ref, mask_rows, left))
            kvs.append(kvg)
        lows, tops, totals = [], [], []
        for s in scores:
            top = jnp.max(s, axis=1, keepdims=True)
            p = jnp.exp(s - top)
            totals.append(jnp.sum(p, axis=1, keepdims=True))
            tops.append(top)
            lows.append(p.astype(bf16))
        accs = [dot_nn(p, kvg) for p, kvg in zip(lows, kvs)]
        for u in range(unroll):
            of = slice(u * heads, (u + 1) * heads)
            jl = it * unroll + u
            put(o_refs[half], jl, finish(half * near + jl, accs[of], tops[of], totals[of]))
        return carry

    for half in range(2):
        lax.fori_loop(0, near // unroll, functools.partial(some, half), 0)

    edge = edge_of(coord_ref, blocks, per_span)
    rows = pl.ds(pl.multiple_of(edge * BLOCK, BLOCK), BLOCK)
    head_cols = [slice(h * wide, (h + 1) * wide) for h in range(heads)]
    qs = [q_ref[rows, cols] for cols in head_cols]

    def score(c, tops):
        parts = [pl.ds(pl.multiple_of((c * 2 + i) * CHUNK, CHUNK), CHUNK) for i in range(2)]
        masks = [
            mask_of(mask_ref, [nat_ref[(c * 2 + i) * PICKS + u] for u in range(PICKS)], left) for i in range(2)
        ]
        ss = [
            [dot_nt(qs[h], kv_ref[parts[i], head_cols[h]]) + masks[i] for h in range(heads)] for i in range(2)
        ]
        for i in range(2):
            for h in range(heads):
                s_ref[h, :, parts[i]] = ss[i][h]
        return tuple(jnp.maximum(tops[h], jnp.maximum(ss[0][h], ss[1][h])) for h in range(heads))

    tops = lax.fori_loop(0, chunks // 2, score, tuple(jnp.full((BLOCK, CHUNK), -3e38, f32) for _ in range(heads)))
    tops = [jnp.max(t, axis=1, keepdims=True) for t in tops]

    def out(c, carry):
        accs, sums = carry
        parts = [pl.ds(pl.multiple_of((c * 2 + i) * CHUNK, CHUNK), CHUNK) for i in range(2)]
        ps = [[jnp.exp(s_ref[h, :, part] - tops[h]) for h in range(heads)] for part in parts]
        adds = [
            [dot_nn(ps[i][h].astype(bf16), kv_ref[parts[i], head_cols[h]]) for h in range(heads)] for i in range(2)
        ]
        accs = tuple(accs[h] + (adds[0][h] + adds[1][h]) for h in range(heads))
        sums = tuple(sums[h] + (ps[0][h] + ps[1][h]) for h in range(heads))
        return accs, sums

    accs, sums = lax.fori_loop(
        0,
        chunks // 2,
        out,
        (
            tuple(jnp.zeros((BLOCK, wide), f32) for _ in range(heads)),
            tuple(jnp.zeros((BLOCK, CHUNK), f32) for _ in range(heads)),
        ),
    )
    value = finish(edge, accs, tops, [jnp.sum(t, axis=1, keepdims=True) for t in sums])

    @pl.when(edge < near)
    def _():
        put(o_refs[0], edge, value)

    @pl.when(edge >= near)
    def _():
        put(o_refs[1], edge - near, value)

    for src, dst in zip((*o_refs, lse_ref), outs):
        leave(src, dst)
    for copy in leaving:
        copy.wait()


def project_and_attend(heads, hd, span, coords, rand, xs, w_kv, w_q, b_kv, b_q, mask, orders):
    keys = 8 * xs[0].shape[0]
    rows = keys // 2
    cols = heads * 2 * hd
    return pl.pallas_call(
        functools.partial(project_and_attend_kernel, heads, hd, span, len(orders)),
        out_shape=(
            jax.ShapeDtypeStruct((rows // 2, heads * hd), bf16),
            jax.ShapeDtypeStruct((rows // 2, heads * hd), bf16),
            jax.ShapeDtypeStruct((rows, 128), f32),
            jax.ShapeDtypeStruct((keys, cols), bf16),
            jax.ShapeDtypeStruct((rows, cols), bf16),
        ),
        in_specs=[SMEM_SPEC] * 2 + [ANY_SPEC] * 10 + [VMEM_SPEC] * 3 + [ANY_SPEC] * len(orders),
        out_specs=(ANY_SPEC,) * 5,
        scratch_shapes=[pltpu.VMEM(a.shape, bf16) for a in (*xs, w_kv, w_q)]
        + [pltpu.VMEM((rows // 2, heads * hd), bf16)] * 2
        + [
            pltpu.VMEM((rows, 128), f32),
            pltpu.VMEM((keys, cols), bf16),
            pltpu.VMEM((rows, cols), bf16),
            pltpu.VMEM((heads, BLOCK, keys), f32),
            pltpu.SMEM((keys // BLOCK,), jnp.int32),
            pltpu.SMEM((keys // BLOCK,), jnp.int32),
            pltpu.SemaphoreType.DMA((10,)),
            pltpu.SemaphoreType.DMA((12,)),
        ],
        compiler_params=params(60),
        cost_estimate=pl.CostEstimate(
            flops=40 << 30, bytes_accessed=16 << 20, transcendentals=rows * heads * CHUNK
        ),
        name="project_and_attend",
    )(coords, rand, *xs, w_kv, w_q, b_kv, b_q, mask, *orders)


def attend_back_kernel(heads, hd, span, n_orders, coord_ref, rand_ref, q_from, *refs):
    do_parts, o_parts, (kv_from, lse_from, w_kv_from, w_q_from, mask_ref) = refs[:4], refs[4:6], refs[6:11]
    refs = refs[11 + n_orders :]
    dq_out, dkv_out, near_out, far_out, acc_ref, do_ref, o_ref, place_ref, nat_ref = refs[:9]
    q_ref, kv_ref, lse_ref, w_kv_ref, w_q_ref, dq_ref, dkv_ref, dx_ref, in_sems, out_sems = refs[9:]
    own = do_parts[0].shape[0]
    pairs = [(q_from, q_ref), (kv_from, kv_ref), (lse_from, lse_ref)]
    for k, ref in enumerate(do_parts):
        pairs.append((ref.at[0] if len(ref.shape) == 3 else ref, do_ref.at[k * own : (k + 1) * own]))
    for k, ref in enumerate(o_parts):
        pairs.append((ref, o_ref.at[k * 2 * own : (k + 1) * 2 * own]))
    pairs += [(w_kv_from, w_kv_ref), (w_q_from, w_q_ref)]
    arriving = [pltpu.make_async_copy(a, b, in_sems.at[i]) for i, (a, b) in enumerate(pairs)]
    for copy in arriving:
        copy.start()
    wide = 2 * hd
    piece = 4 * span
    per_span = span // BLOCK
    scale = hd**-0.5
    blocks = q_ref.shape[0] // BLOCK
    blocks_all = kv_ref.shape[0] // BLOCK
    chunks = kv_ref.shape[0] // CHUNK
    head_cols = [slice(h * wide, (h + 1) * wide) for h in range(heads)]
    nil = jnp.zeros((BLOCK, hd), bf16)
    left = lax.broadcasted_iota(jnp.int32, (1, 128), 1) < BLOCK
    fill_tables(coord_ref, rand_ref, place_ref, nat_ref, heads, span)

    def clear(c, carry):
        part = pl.ds(pl.multiple_of(c * CHUNK, CHUNK), CHUNK)
        acc_ref[part, :] = jnp.zeros((CHUNK, heads * wide), f32)
        return carry

    lax.fori_loop(0, chunks, clear, 0)
    for copy in arriving[:-2]:
        copy.wait()

    def of_rows(rows):
        d_o = do_ref[rows, :]
        prod = d_o.astype(f32) * o_ref[rows, :].astype(f32)
        lse = lse_ref[rows, :]
        boths, dots, lses = [], [], []
        for h in range(heads):
            low = jnp.concatenate([nil, d_o[:, h * hd : (h + 1) * hd]], axis=1)
            boths.append(jnp.concatenate([q_ref[rows, head_cols[h]], low], axis=0))
            dots.append(jnp.sum(prod[:, h * hd : (h + 1) * hd], axis=1, keepdims=True))
            lses.append(lse[:, h : h + 1])
        return boths, dots, lses

    unroll = 4

    def some(it, carry):
        items, boths, dots, lses = [], [], [], []
        for u in range(unroll):
            jl = it * unroll + u
            rows = pl.ds(pl.multiple_of(jl * BLOCK, BLOCK), BLOCK)
            b, d, e = of_rows(rows)
            boths, dots, lses = boths + b, dots + d, lses + e
            items += [(jl, h) for h in range(heads)]
        kvs, prods, picks, masks = [], [], [], []
        for i, (jl, h) in enumerate(items):
            ids, mask_rows = picks_of(coord_ref, rand_ref, jl, h, heads, per_span, blocks_all)
            kvg = blocks_of(kv_ref, place_ref, ids, head_cols[h])
            prods.append(dot_nt(boths[i], kvg))
            masks.append(mask_of(mask_ref, mask_rows, left))
            kvs.append(kvg)
            picks.append(ids)
        dss, lows = [], []
        for i, (jl, h) in enumerate(items):
            p = jnp.exp(prods[i][:BLOCK] + masks[i] - lses[i])
            dss.append((p * (prods[i][BLOCK:] - dots[i])).astype(bf16))
            lows.append(p.astype(bf16))
        dqs = [dot_nn(ds, kvg)[:, :hd] for ds, kvg in zip(dss, kvs)]
        dkvs = [dot_tn(jnp.concatenate([ds, p], axis=0), both) for ds, p, both in zip(dss, lows, boths)]
        for i, (jl, h) in enumerate(items):
            for u in range(PICKS):
                place = pl.ds(pl.multiple_of(place_ref[picks[i][u]] * BLOCK, BLOCK), BLOCK)
                acc_ref[place, head_cols[h]] += dkvs[i][u * BLOCK : (u + 1) * BLOCK]
        for u in range(unroll):
            rows = pl.ds(pl.multiple_of((it * unroll + u) * BLOCK, BLOCK), BLOCK)
            dq_ref[rows, :] = (jnp.concatenate(dqs[u * heads : (u + 1) * heads], axis=1) * scale).astype(bf16)
        return carry

    lax.fori_loop(0, blocks // unroll, some, 0)

    rows = pl.ds(pl.multiple_of(edge_of(coord_ref, blocks, per_span) * BLOCK, BLOCK), BLOCK)
    boths, dots, lses = of_rows(rows)

    def edge(c, dqs):
        items = [(i, h) for i in range(2) for h in range(heads)]
        parts = [pl.ds(pl.multiple_of((c * 2 + i) * CHUNK, CHUNK), CHUNK) for i in range(2)]
        masks = [
            mask_of(mask_ref, [nat_ref[(c * 2 + i) * PICKS + u] for u in range(PICKS)], left) for i in range(2)
        ]
        kvs = [kv_ref[parts[i], head_cols[h]] for i, h in items]
        prods = [dot_nt(boths[h], kvg) for (i, h), kvg in zip(items, kvs)]
        dss, lows = [], []
        for (i, h), prod in zip(items, prods):
            p = jnp.exp(prod[:BLOCK] + masks[i] - lses[h])
            dss.append((p * (prod[BLOCK:] - dots[h])).astype(bf16))
            lows.append(p.astype(bf16))
        adds = [dot_nn(ds, kvg) for ds, kvg in zip(dss, kvs)]
        dkvs = [dot_tn(jnp.concatenate([ds, p], axis=0), boths[h]) for (i, h), ds, p in zip(items, dss, lows)]
        for (i, h), dkv in zip(items, dkvs):
            acc_ref[parts[i], head_cols[h]] += dkv
        return tuple(dqs[h] + (adds[h] + adds[heads + h]) for h in range(heads))

    dqs = lax.fori_loop(0, chunks // 2, edge, tuple(jnp.zeros((BLOCK, wide), f32) for _ in range(heads)))
    dq_ref[rows, :] = (jnp.concatenate([dq[:, :hd] for dq in dqs], axis=1) * scale).astype(bf16)

    pair = 2 * span
    mine = {(n, src): at for at, n, src in query_pieces(pair)}
    leaving = [pltpu.make_async_copy(dq_ref, dq_out, out_sems.at[0])]
    leaving[0].start()
    arriving[-2].wait()
    arriving[-1].wait()
    moves = []
    for i, n in enumerate((2, 3, 6, 7, 0, 1, 4, 5)):
        kc = n // 2 % 2
        to = n % 2 * piece
        of = slice(n * piece, (n + 1) * piece)
        slot = i % 2
        if i >= 2:
            for copy in moves[i - 2]:
                copy.wait()
        dkv = acc_ref[of, :].astype(bf16)
        dkv_ref[slot] = dkv
        dx = dot_nt(dkv, w_kv_ref[...])
        for src in (0, pair):
            part = dx[src : src + pair]
            if (n, src) in mine:
                at = mine[n, src]
                part = part + dot_nt(dq_ref[at : at + pair, :], w_q_ref[...])
            dx_ref[slot, src : src + pair, :] = part.astype(bf16)
        dx_out = (far_out if kc else near_out).at[n // 4, to : to + piece]
        moves.append(
            [
                pltpu.make_async_copy(dkv_ref.at[slot], dkv_out.at[of], out_sems.at[1 + 2 * i]),
                pltpu.make_async_copy(dx_ref.at[slot], dx_out, out_sems.at[2 + 2 * i]),
            ]
        )
        for copy in moves[-1]:
            copy.start()
    for copy in (*leaving, *moves[-2], *moves[-1]):
        copy.wait()


def attend_back(heads, hd, span, coords, rand, q, d_os, os, kv, mask, lse, w_kv, w_q, orders):
    rows, keys = q.shape[0], kv.shape[0]
    width = w_kv.shape[0]
    piece = 4 * span
    return pl.pallas_call(
        functools.partial(attend_back_kernel, heads, hd, span, len(orders)),
        out_shape=(
            jax.ShapeDtypeStruct((rows, heads * hd), bf16),
            jax.ShapeDtypeStruct((keys, heads * 2 * hd), bf16),
        )
        + (jax.ShapeDtypeStruct((2, 2 * piece, width), bf16),) * 2,
        in_specs=[SMEM_SPEC] * 2 + [ANY_SPEC] * 11 + [VMEM_SPEC] + [ANY_SPEC] * len(orders),
        out_specs=(ANY_SPEC,) * 4,
        scratch_shapes=[
            pltpu.VMEM((keys, heads * 2 * hd), f32),
            pltpu.VMEM((rows, heads * hd), bf16),
            pltpu.VMEM((rows, heads * hd), bf16),
            pltpu.SMEM((keys // BLOCK,), jnp.int32),
            pltpu.SMEM((keys // BLOCK,), jnp.int32),
            pltpu.VMEM(q.shape, bf16),
            pltpu.VMEM(kv.shape, bf16),
            pltpu.VMEM(lse.shape, f32),
            pltpu.VMEM(w_kv.shape, bf16),
            pltpu.VMEM(w_q.shape, bf16),
            pltpu.VMEM((rows, heads * hd), bf16),
            pltpu.VMEM((2, piece, heads * 2 * hd), bf16),
            pltpu.VMEM((2, piece, width), bf16),
            pltpu.SemaphoreType.DMA((11,)),
            pltpu.SemaphoreType.DMA((17,)),
        ],
        compiler_params=params(60),
        cost_estimate=pl.CostEstimate(
            flops=60 << 30, bytes_accessed=24 << 20, transcendentals=rows * heads * CHUNK
        ),
        name="attend_back",
    )(coords, rand, q, *d_os, *os, kv, lse, w_kv, w_q, mask, *orders)


def split_low(value):
    top = value.astype(bf16)
    return jnp.concatenate([top, (value - top.astype(f32)).astype(bf16)], axis=0)


def joined(low):
    return low[:8].astype(f32) + low[8:16].astype(f32)


def qkv_grad_kernel(span, spot_ref, coord_ref, dq_ref, dkv_ref, keep_ref, got_ref, small_ref, *refs):
    x_refs, (keep_out, send_out, held_ref) = refs[:8], refs[-3:]
    piece = 4 * span
    n_kv = dkv_ref.shape[1]
    n_q = dq_ref.shape[1]
    rows, width = held_ref.shape[1], x_refs[0].shape[1]
    acc = jnp.zeros((n_kv, width), f32)
    acc_q = jnp.zeros((n_q, width), f32)
    for n, x_ref in enumerate(x_refs):
        acc = acc + dot_tn(dkv_ref[n * piece : (n + 1) * piece, :], x_ref[...])
    pair = 2 * span
    for at, n, src in query_pieces(pair):
        acc_q = acc_q + dot_tn(dq_ref[at : at + pair, :], x_refs[n][src : src + pair, :])
    held_ref[...] = jnp.zeros_like(held_ref)
    both = jnp.concatenate([acc, acc_q], axis=0)
    octets = [both[o * rows : (o + 1) * rows] for o in range(6)]
    w_out = keep_ref[4].astype(f32) + got_ref[4 * rows : 5 * rows, :].astype(f32)
    octets += [w_out[:, :width], w_out[:, width:]]
    sums = jnp.concatenate(
        [
            jnp.sum(dq_ref[...].astype(f32), axis=0, keepdims=True),
            jnp.sum(dkv_ref[...].astype(f32), axis=0, keepdims=True),
            jnp.zeros((1, 1024 - n_q - n_kv), f32),
        ],
        axis=1,
    )
    sums = jnp.concatenate([sums[:, i * 128 : (i + 1) * 128] for i in range(8)], axis=0)

    others = joined(got_ref[5 * rows :, :width])
    own = joined(split_low(small_ref[...]))
    small = own + others
    held = split_low(own + pltpu.roll(others, 7, 0))
    unit = lax.broadcasted_iota(jnp.int32, (width, width), 0)
    octet = unit // rows
    zq = (octet // 2 % 2 + octet % 2 * 2) ^ coord_ref[0]
    own_unit = (zq * 2 + (octet // 4 ^ coord_ref[1])) * rows + unit % rows
    turn = jnp.where(own_unit == lax.broadcasted_iota(jnp.int32, (width, width), 1), 1.0, 0.0).astype(bf16)
    b_in = joined(dot_nn(held, turn))[6:7]

    def lanes_down(row):
        parts = [row[:, i * 128 : (i + 1) * 128] for i in range(width // 128)]
        return jnp.concatenate(parts + [jnp.zeros((8 - width // 128, 128), f32)], axis=0)

    vectors = [lanes_down(small[i : i + 1]) for i in range(6)] + [lanes_down(b_in), sums]
    for o in range(8):
        spot = spot_ref[o]
        held_ref[spot, :, :width] = octets[o].astype(bf16)
        held_ref[spot, :16, width:] = split_low(vectors[o])
    keep_out[...] = held_ref[0:4]
    send_out[...] = held_ref[4:8]


def qkv_grad(span, spots, coords, dq, dkv, keep, got, small, xs, orders):
    width = xs[0].shape[1]
    rows = (dq.shape[1] + dkv.shape[1]) // 6
    return pl.pallas_call(
        functools.partial(qkv_grad_kernel, span),
        out_shape=(jax.ShapeDtypeStruct((4, rows, width + 128), bf16),) * 2,
        in_specs=[SMEM_SPEC] * 2 + [VMEM_SPEC] * 13 + [ANY_SPEC] * len(orders),
        out_specs=(VMEM_SPEC,) * 2,
        scratch_shapes=[pltpu.VMEM((8, rows, width + 128), bf16)],
        compiler_params=params(60),
        cost_estimate=pl.CostEstimate(
            flops=14 << 30, bytes_accessed=12 << 20, transcendentals=0
        ),
        name="qkv_grad",
    )(spots, coords, dq, dkv, keep, got, small, *xs, *orders)


def across_sum_kernel(a_ref, b_ref, c_ref, d_ref, out_ref):
    out_ref[...] = sum(r[...].astype(f32) for r in (a_ref, b_ref, c_ref, d_ref)).astype(bf16)


def across_sum(parts):
    return pl.pallas_call(
        across_sum_kernel,
        out_shape=jax.ShapeDtypeStruct(parts[0].shape, bf16),
        in_specs=[VMEM_SPEC] * 4,
        out_specs=VMEM_SPEC,
        compiler_params=params(60),
        cost_estimate=pl.CostEstimate(flops=1 << 24, bytes_accessed=1 << 20, transcendentals=0),
        name="across_sum",
    )(*parts)


def wide_sum_kernel(order_ref, keep_ref, y_ref, x_ref, *refs):
    out_ref = refs[-1]
    rows = keep_ref.shape[1]
    for k in range(4):
        of = slice(k * rows, (k + 1) * rows)
        out_ref[order_ref[k]] = (keep_ref[k].astype(f32) + y_ref[of, :].astype(f32) + x_ref[k].astype(f32)).astype(bf16)


def wide_sum(order, keep, y_got, x_got, orders):
    _, rows, cols = keep.shape
    four = pl.BlockSpec((4, rows, cols), lambda i: (0, 0, 0))
    return pl.pallas_call(
        wide_sum_kernel,
        grid=(1,),
        in_specs=[SMEM_SPEC, four, pl.BlockSpec((4 * rows, cols), lambda i: (0, 0)), four] + [ANY_SPEC] * len(orders),
        out_specs=four,
        out_shape=jax.ShapeDtypeStruct((4, rows, cols), bf16),
        compiler_params=params(60),
        cost_estimate=pl.CostEstimate(flops=4 << 30, bytes_accessed=6 << 20, transcendentals=0),
        name="wide_sum",
    )(order, keep, y_got, x_got, *orders)


def low_sum(out_ref, at, refs):
    rows, cols = out_ref.shape[1:]
    thin = cols - 128
    out_ref[at, :, :thin] = sum(ref[k, :, :thin].astype(f32) for ref, k in refs).astype(bf16)
    out_ref[at, :, thin:] = jnp.zeros((rows, 128), bf16)
    out_ref[at, :16, thin:] = split_low(sum(joined(ref[k, :16, thin:]) for ref, k in refs))


def tail_sum_kernel(tail_ref, got_ref, *refs):
    keep_ref, send_ref = refs[-2:]
    for k in range(4):
        low_sum(keep_ref if k < 2 else send_ref, k % 2, [(tail_ref, k), (got_ref, k)])


def tail_sum(tail, got, orders):
    _, rows, cols = tail.shape
    return pl.pallas_call(
        tail_sum_kernel,
        out_shape=(jax.ShapeDtypeStruct((2, rows, cols), bf16),) * 2,
        in_specs=[VMEM_SPEC] * 2 + [ANY_SPEC] * len(orders),
        out_specs=(VMEM_SPEC,) * 2,
        compiler_params=params(60),
        cost_estimate=pl.CostEstimate(flops=1 << 28, bytes_accessed=2 << 20, transcendentals=0),
        name="tail_sum",
    )(tail, got, *orders)


def tail_mid_kernel(keep_ref, got_ref, own_ref, send_ref):
    low_sum(own_ref, 0, [(keep_ref, 0), (got_ref, 0)])
    low_sum(send_ref, 0, [(keep_ref, 1), (got_ref, 1)])


def tail_mid(keep, got):
    _, rows, cols = keep.shape
    return pl.pallas_call(
        tail_mid_kernel,
        out_shape=(jax.ShapeDtypeStruct((1, rows, cols), bf16),) * 2,
        in_specs=[VMEM_SPEC] * 2,
        out_specs=(VMEM_SPEC,) * 2,
        compiler_params=params(60),
        cost_estimate=pl.CostEstimate(flops=1 << 28, bytes_accessed=2 << 20, transcendentals=0),
        name="tail_mid",
    )(keep, got)


def wide_end_kernel(wide_ref, across_ref, *refs):
    refs[-1][...] = (wide_ref[...].astype(f32) + across_ref[...].astype(f32)).astype(bf16)


def wide_end(wide, across, orders):
    return pl.pallas_call(
        wide_end_kernel,
        out_shape=jax.ShapeDtypeStruct(wide.shape, bf16),
        in_specs=[VMEM_SPEC] * 2 + [ANY_SPEC] * len(orders),
        out_specs=VMEM_SPEC,
        compiler_params=params(60),
        cost_estimate=pl.CostEstimate(flops=1 << 28, bytes_accessed=3 << 20, transcendentals=0),
        name="wide_end",
    )(wide, across, *orders)


def tail_end_kernel(own_ref, got_ref, *refs):
    low_sum(refs[-1], 0, [(own_ref, 0), (got_ref, 0)])


def tail_end(own, got, orders):
    return pl.pallas_call(
        tail_end_kernel,
        out_shape=jax.ShapeDtypeStruct(own.shape, bf16),
        in_specs=[VMEM_SPEC] * 2 + [ANY_SPEC] * len(orders),
        out_specs=VMEM_SPEC,
        compiler_params=params(60),
        cost_estimate=pl.CostEstimate(flops=1 << 28, bytes_accessed=3 << 20, transcendentals=0),
        name="tail_end",
    )(own, got, *orders)


def wide_place_kernel(spot_ref, *refs):
    ins, (in_ref, back_ref, held_ref) = refs[:8], refs[-3:]
    rows, width = ins[0].shape[0], back_ref.shape[1]
    for n in range(8):
        to = pl.ds(pl.multiple_of(spot_ref[n] * rows, 16), rows)
        held_ref[to, :] = ins[n][:, :width].astype(f32)
        back_ref[to, :] = ins[n][:, width:].astype(f32)
    in_ref[...] = held_ref[...].T


def wide_place(spots, parts, orders):
    rows, cols = parts[0].shape
    width = cols // 2
    return pl.pallas_call(
        wide_place_kernel,
        out_shape=(jax.ShapeDtypeStruct((width, 8 * rows), f32), jax.ShapeDtypeStruct((8 * rows, width), f32)),
        in_specs=[SMEM_SPEC] + [VMEM_SPEC] * 8 + [ANY_SPEC] * len(orders),
        out_specs=(VMEM_SPEC,) * 2,
        scratch_shapes=[pltpu.VMEM((8 * rows, width), f32)],
        compiler_params=params(60),
        cost_estimate=pl.CostEstimate(flops=1 << 28, bytes_accessed=3 << 20, transcendentals=0),
        name="wide_place",
    )(spots, *parts, *orders)


def tail_place_kernel(n_qkv, heads, spot_ref, *refs):
    ins, (qkv_ref, w_out_ref, small_ref, held_ref) = refs[:8], refs[-4:]
    rows = ins[0].shape[1]
    cols = held_ref.shape[1]
    for n in range(8):
        spot = spot_ref[n]
        held_ref[pl.ds(pl.multiple_of(spot * rows, 16), rows), :] = ins[n][0, :, :cols].astype(f32)
        small_ref[spot] = joined(ins[n][0, :16, cols:])
    w_out_ref[...] = held_ref[n_qkv:, :]
    hd = n_qkv // 3 // heads
    parts = []
    for h in range(heads):
        q_at, kv_at = 2 * heads * hd + h * hd, 2 * h * hd
        parts += [held_ref[q_at : q_at + hd, :], held_ref[kv_at : kv_at + 2 * hd, :]]
    qkv_ref[...] = jnp.concatenate(parts, axis=0).T


def tail_place(spots, parts, n_qkv, heads, orders):
    _, rows, cols = parts[0].shape
    width = cols - 128
    return pl.pallas_call(
        functools.partial(tail_place_kernel, n_qkv, heads),
        out_shape=(
            jax.ShapeDtypeStruct((width, n_qkv), f32),
            jax.ShapeDtypeStruct((8 * rows - n_qkv, width), f32),
            jax.ShapeDtypeStruct((8, 8, 128), f32),
        ),
        in_specs=[SMEM_SPEC] + [VMEM_SPEC] * 8 + [ANY_SPEC] * len(orders),
        out_specs=(VMEM_SPEC,) * 3,
        scratch_shapes=[pltpu.VMEM((8 * rows, width), f32)],
        compiler_params=params(60),
        cost_estimate=pl.CostEstimate(flops=1 << 28, bytes_accessed=3 << 20, transcendentals=0),
        name="tail_place",
    )(spots, *parts, *orders)


def split_kernel(n_orders, coord_ref, rows_ref, *refs):
    value = rows_ref[...].astype(f32)
    pieces = [value[:, s, :] for s in range(4)]
    z = coord_ref[0]
    for k, out in enumerate(refs[n_orders:]):
        low = jnp.where((z ^ k) % 2 == 0, pieces[0], pieces[1])
        high = jnp.where((z ^ k) % 2 == 0, pieces[2], pieces[3])
        out[...] = jnp.where((z ^ k) // 2 == 0, low, high).astype(bf16)


def split(coords, rows, orders=()):
    span, seqs, width = rows.shape
    return pl.pallas_call(
        functools.partial(split_kernel, len(orders)),
        out_shape=(jax.ShapeDtypeStruct((span, width), bf16),) * seqs,
        in_specs=[SMEM_SPEC, VMEM_SPEC] + [ANY_SPEC] * len(orders),
        out_specs=(VMEM_SPEC,) * seqs,
        compiler_params=params(32),
        cost_estimate=pl.CostEstimate(flops=1 << 20, bytes_accessed=1 << 20, transcendentals=0),
        name="split",
    )(coords, rows, *orders)


def qkv_weights_kernel(n_orders, w_ref, b_ref, *refs):
    kv_ref, q_pad_ref, q_ref, b_kv_ref, b_q_ref = refs[n_orders:]
    width, heads, _, hd = w_ref.shape
    wide = 2 * hd
    value = w_ref[...].astype(f32)
    nil = jnp.zeros((width, hd), f32)
    qs = []
    for h in range(heads):
        q, k, v = [value[:, h, c, :] for c in range(3)]
        cols = slice(h * wide, (h + 1) * wide)
        kv_ref[:, cols] = jnp.concatenate([k, v], axis=1).astype(bf16)
        q_pad_ref[:, cols] = jnp.concatenate([q, nil], axis=1).astype(bf16)
        b_kv_ref[:, cols] = jnp.concatenate([nil[:1], b_ref[h, 1:2, :]], axis=1)
        b_q_ref[:, cols] = jnp.concatenate([b_ref[h, 0:1, :], nil[:1]], axis=1)
        qs.append(q)
    q_ref[...] = jnp.concatenate(qs, axis=1).astype(bf16)


def qkv_weights(w_qkv, bias_qv, orders):
    width, heads, _, hd = w_qkv.shape
    cols = heads * 2 * hd
    return pl.pallas_call(
        functools.partial(qkv_weights_kernel, len(orders)),
        out_shape=(
            jax.ShapeDtypeStruct((width, cols), bf16),
            jax.ShapeDtypeStruct((width, cols), bf16),
            jax.ShapeDtypeStruct((width, heads * hd), bf16),
            jax.ShapeDtypeStruct((1, cols), f32),
            jax.ShapeDtypeStruct((1, cols), f32),
        ),
        in_specs=[VMEM_SPEC] * 2 + [ANY_SPEC] * len(orders),
        out_specs=(VMEM_SPEC,) * 5,
        compiler_params=params(40),
        cost_estimate=pl.CostEstimate(flops=1 << 20, bytes_accessed=1 << 20, transcendentals=0),
        name="qkv_weights",
    )(w_qkv, bias_qv, *orders)


def pack_kernel(n_orders, order_ref, up_ref, down_ref, w_out_ref, bias_ref, *refs):
    pack_ref, first_ref, out_ref, up_rows_ref = refs[n_orders:]
    width = up_ref.shape[0]
    eighth = down_ref.shape[0] // 8
    half = w_out_ref.shape[0] // 2
    for i in range(0, down_ref.shape[0], 256):
        up_rows_ref[i : i + 256, :] = up_ref[:, i : i + 256].astype(f32).T.astype(bf16)
    for ref in (pack_ref, out_ref):
        ref[:half, :width] = w_out_ref[:half, :]
        ref[:half, width:] = w_out_ref[half:, :]
        ref[half : half + 16, :width] = bias_ref[...]
        ref[half : half + 16, width:] = jnp.zeros((16, width), bf16)
    for n in range(8):
        src = pl.ds(pl.multiple_of(order_ref[n] * eighth, 16), eighth)
        for ref, at in ((pack_ref, half + 16), (first_ref, 0))[: 2 if n < 4 else 1]:
            to = slice(at + n * eighth, at + (n + 1) * eighth)
            ref[to, :width] = up_rows_ref[src, :]
            ref[to, width:] = down_ref[src, :]


def pack(order, up, down, w_out, bias, orders):
    hidden, width = down.shape
    rows = w_out.shape[0] // 2 + 16
    return pl.pallas_call(
        functools.partial(pack_kernel, len(orders)),
        out_shape=(
            jax.ShapeDtypeStruct((rows + hidden, 2 * width), bf16),
            jax.ShapeDtypeStruct((hidden // 2, 2 * width), bf16),
            jax.ShapeDtypeStruct((rows, 2 * width), bf16),
        ),
        in_specs=[SMEM_SPEC] + [VMEM_SPEC] * 4 + [ANY_SPEC] * len(orders),
        out_specs=(VMEM_SPEC,) * 3,
        scratch_shapes=[pltpu.VMEM((hidden, width), bf16)],
        compiler_params=params(32),
        cost_estimate=pl.CostEstimate(flops=1 << 20, bytes_accessed=1 << 20, transcendentals=0),
        name="pack",
    )(order, up, down, w_out, bias, *orders)


def rows_kernel(width, n_out, tile_rows, *refs):
    attn_refs, pack_refs = refs[:4], refs[4 : 4 + len(tile_rows)]
    refs = refs[4 + len(tile_rows) :]
    tok_refs, dres_refs, vec_ref = refs[:2], refs[2:6], refs[6]
    result_refs = refs[7:11]
    done_ref, hid_ref, dpre_ref, ylow_ref, dffn_ref, dbr_ref = refs[11:17]
    dattn_refs = refs[17:20]
    small_ref, bin_ref = refs[20:22]
    slope_ref = refs[22]
    bias_out, gain_one, bias_one, down_bias, gain_two, bias_two = [vec_ref[i : i + 1, :] for i in range(6)]
    step = pl.program_id(0)
    half = n_out // 2
    tiles, wos, biases = [], [], []
    for ref, (first, whole) in zip(pack_refs, tile_rows):
        if whole:
            wos.append(jnp.concatenate([ref[:half, :width], ref[:half, width:]], axis=0))
            biases.append(ref[half : half + 1, :width].astype(f32))
        left = ref.shape[0] - first
        if left == 0:
            continue
        size = min(left, width // 2)
        tiles += [ref.at[first + i * size : first + (i + 1) * size] for i in range(left // size)]
    up_bias = jnp.concatenate(biases, axis=1)

    def by_step(ones, twos):
        pairs = [jnp.where(step == 0, a[...].astype(f32), b[...].astype(f32)) for a, b in zip(ones, twos)]
        return pairs[0] if len(pairs) == 1 else jnp.concatenate(pairs, axis=0)

    @pl.when(pl.program_id(0) == 0)
    def _():
        small_ref[...] = jnp.zeros_like(small_ref)
        bin_ref[...] = jnp.zeros_like(bin_ref)

    branch = bias_out
    for k in range(4):
        branch = branch + dot_nn(attn_refs[k][...], wos[k])
    y_one, normed_one, inv_one = norm_fwd(by_step(tok_refs[:1], tok_refs[1:]) + branch, gain_one, bias_one)
    y_low = y_one.astype(bf16)
    ylow_ref[...] = y_low
    ffn = down_bias
    at = 0
    spans = []
    for tile in tiles:
        spans.append(slice(at, at + tile.shape[0]))
        at += tile.shape[0]
    for cols, tile in zip(spans, tiles):
        v = dot_nt(y_low, tile[:, :width]) + up_bias[:, cols]
        sq = v * v
        th = jnp.tanh(0.7978845608028654 * v * (1.0 + 0.044715 * sq))
        half = 0.5 * (1.0 + th)
        slope_ref[:, cols] = half + 0.5 * v * (1.0 - th * th) * (
            0.7978845608028654 * (1.0 + 3.0 * 0.044715 * sq)
        )
        hid = (v * half).astype(bf16)
        hid_ref[:, cols] = hid
        ffn = ffn + dot_nn(hid, tile[:, width:])
    result, normed_two, inv_two = norm_fwd(y_one + ffn, gain_two, bias_two)
    for s in range(2):

        @pl.when(step == s)
        def _(s=s):
            for k in range(2):
                ref = result_refs[s + 2 * k]
                ref[...] = result[k * ref.shape[0] : (k + 1) * ref.shape[0]].astype(bf16)

    d_two, g_gain_two, g_bias_two = norm_back(by_step(dres_refs[::2], dres_refs[1::2]), normed_two, inv_two, gain_two)
    d_ffn = d_two.astype(bf16)
    dffn_ref[...] = d_ffn
    g_bias_back = jnp.sum(d_ffn.astype(f32), axis=0)
    d_y = d_two
    for cols, tile in zip(spans, tiles):
        d_pre = (dot_nt(d_ffn, tile[:, width:]) * slope_ref[:, cols]).astype(bf16)
        dpre_ref[:, cols] = d_pre
        bin_ref[:, cols] += jnp.sum(d_pre.astype(f32), axis=0, keepdims=True)
        d_y = d_y + dot_nn(d_pre, tile[:, :width])
    d_one, g_gain_one, g_bias_one = norm_back(d_y, normed_one, inv_one, gain_one)
    done_ref[...] = d_one
    d_branch = d_one.astype(bf16)
    dbr_ref[...] = d_branch
    g_bias_out = jnp.sum(d_branch.astype(f32), axis=0)
    for k in range(4):
        d_attn = dot_nt(d_branch, wos[k]).astype(bf16)
        if k < 2:
            dattn_refs[k][...] = d_attn
        else:
            dattn_refs[2][k - 2] = d_attn
    sums = [g_bias_out, g_gain_one, g_bias_one, g_bias_back, g_gain_two, g_bias_two]
    for i, one in enumerate(sums):
        small_ref[i : i + 1, :] += one[None, :]


def rows_work(attns, packs, first_rows, toks, d_res, vecs):
    span, width = d_res[0].shape
    rows = 4 * span
    cols = attns[0].shape[1]
    hidden = sum(a.shape[0] - n for a, (n, _) in zip(packs, first_rows))
    tile = rows // 2

    def by_rows(n):
        return pl.BlockSpec((tile, n), lambda i: (i, 0))

    def whole(a):
        return pl.BlockSpec(a.shape, lambda i, nd=a.ndim: (0,) * nd, pipeline_mode=pl.Buffered(1))

    def fixed(shape):
        return pl.BlockSpec(shape, lambda i: (0, 0))

    low = functools.partial(jax.ShapeDtypeStruct, dtype=bf16)
    return pl.pallas_call(
        functools.partial(rows_kernel, width, cols, first_rows),
        grid=(rows // tile,),
        out_shape=(low((span, width)),) * 4
        + (
            jax.ShapeDtypeStruct((rows, width), f32),
            low((rows, hidden)),
            low((rows, hidden)),
            low((rows, width)),
            low((rows, width)),
            low((rows, width)),
            low((rows, cols)),
            low((rows, cols)),
            low((2, rows, cols)),
            jax.ShapeDtypeStruct((8, width), f32),
            jax.ShapeDtypeStruct((1, hidden), f32),
        ),
        in_specs=[by_rows(cols)] * 4 + [whole(a) for a in (*packs, *toks, *d_res, vecs)],
        out_specs=(fixed((span, width)),) * 4
        + (
            by_rows(width),
            by_rows(hidden),
            by_rows(hidden),
            by_rows(width),
            by_rows(width),
            by_rows(width),
            by_rows(cols),
            by_rows(cols),
            pl.BlockSpec((2, tile, cols), lambda i: (0, i, 0)),
            fixed((8, width)),
            fixed((1, hidden)),
        ),
        scratch_shapes=[pltpu.VMEM((tile, hidden), f32)],
        compiler_params=params(60),
        cost_estimate=pl.CostEstimate(flops=50 << 30, bytes_accessed=30 << 20, transcendentals=rows * hidden),
        name="rows_work",
    )(*attns, *packs, *toks, *d_res, vecs)


def small_rows(kc, small_ref, bin_ref):
    width = small_ref.shape[1]
    ends = [bin_ref[:, (ky * 2 + kc) * width : (ky * 2 + kc + 1) * width] for ky in range(2)]
    return jnp.concatenate([small_ref[:6, :]] + ends, axis=0)


def rows_grad_kernel(kc, n_orders, *refs):
    *sources, small_ref, bin_ref = refs[:9]
    refs = refs[9:]
    got_from = refs[0] if kc == 0 else None
    refs = refs[(1 if kc == 0 else 0) + n_orders :]
    n_outs = 1 if kc else 8
    outs, (ylow_ref, dpre_ref, hid_ref, dffn_ref, dbr_ref, attn0_ref, attn1_ref, held_ref, got_ref, low_ref) = (
        refs[:n_outs],
        refs[n_outs : n_outs + 10],
    )
    in_sems, got_sems, out_sems = refs[n_outs + 10 :]
    width = ylow_ref.shape[1]
    rows = ylow_ref.shape[0]
    part = width // 2
    eighth = held_ref.shape[1]

    def cols_of(n):
        at = ((n // 2) * 4 + kc * 2 + n % 2) * part
        return slice(at, at + part)

    pairs = [(sources[0], ylow_ref), (sources[3], dffn_ref)]
    for n in range(4):
        pairs.append((sources[1].at[:, cols_of(n)], dpre_ref.at[n]))
        pairs.append((sources[2].at[:, cols_of(n)], hid_ref.at[n]))
    pairs += [(sources[4], dbr_ref)]
    pairs += [(source.at[0:rows], ref) for source, ref in zip(sources[5:], (attn0_ref, attn1_ref))]
    arriving = [pltpu.make_async_copy(a, b, in_sems.at[i]) for i, (a, b) in enumerate(pairs)]
    gots = []
    if kc == 0:
        gots = [
            pltpu.make_async_copy(got_from.at[4 * n : 4 * n + 4], got_ref.at[4 * n : 4 * n + 4], got_sems.at[n])
            for n in range(5)
        ]
    for i, copy in enumerate(arriving):
        copy.start()
        if gots and i in (3, 5, 7, 9):
            gots[(i - 3) // 2].start()
    if gots:
        gots[4].start()
    arriving[0].wait()
    arriving[1].wait()
    leaving = []

    def leave(src, dst):
        leaving.append(pltpu.make_async_copy(src, dst, out_sems.at[len(leaving)]))
        leaving[-1].start()

    def put(at, k, lanes, value):
        if gots:
            value = value + got_ref[at + k, :, lanes].astype(f32)
        held_ref[at + k, :, lanes] = value.astype(bf16)

    left, right = slice(0, width), slice(width, 2 * width)
    for n in range(4):
        arriving[2 + 2 * n].wait()
        arriving[3 + 2 * n].wait()
        g_in = dot_tn(dpre_ref[n], ylow_ref[...])
        g_back = dot_tn(hid_ref[n], dffn_ref[...])
        if gots:
            gots[n].wait()
        for k in range(4):
            put(4 * n, k, left, g_in[k * eighth : (k + 1) * eighth])
            put(4 * n, k, right, g_back[k * eighth : (k + 1) * eighth])
        if kc:
            leave(held_ref.at[4 * n : 4 * n + 4], outs[0].at[4 * n : 4 * n + 4])
        elif n < 2:
            leave(held_ref.at[4 * n : 4 * n + 4], outs[2 * n].at[0:4])
        elif n == 2:
            for k in range(4):
                leave(held_ref.at[8 + k], outs[1].at[k * eighth : (k + 1) * eighth])
        else:
            for k in range(4):
                leave(held_ref.at[12 + k], outs[3 + k])
    for copy in arriving[10:]:
        copy.wait()
    if gots:
        gots[4].wait()
    for ky, attn_ref in enumerate((attn0_ref, attn1_ref)):
        g_out = dot_tn(attn_ref[...], dbr_ref[...])
        put(16, ky, left, g_out[:eighth])
        put(16, ky, right, g_out[eighth:])
    low_ref[...] = jnp.zeros_like(low_ref)
    if kc:
        low_ref[:16, :width] = split_low(small_rows(1, small_ref, bin_ref))
        leave(held_ref.at[16:18], outs[0].at[16:18])
        leave(low_ref, outs[0].at[18])
        leave(low_ref, outs[0].at[19])
    else:
        sums = joined(split_low(small_rows(0, small_ref, bin_ref))) + joined(got_ref[18, :16, :width])
        outs[7][...] = sums
        low_ref[:16, :width] = split_low(sums)
        leave(held_ref.at[16], outs[0].at[4])
        leave(held_ref.at[17], outs[1].at[4 * eighth : 5 * eighth])
        leave(low_ref.at[0:16], outs[1].at[5 * eighth : 5 * eighth + 16])
    for copy in leaving:
        copy.wait()


def rows_grad(kc, y_low, d_pre, hidden, d_ffn, d_branch, attn0, attn1, small, bin_sum, got=None, orders=()):
    rows, width = y_low.shape
    part = hidden.shape[1] // 8
    eighth = part // 4
    octet = (eighth, 2 * width)
    low = functools.partial(jax.ShapeDtypeStruct, dtype=bf16)
    if kc == 1:
        out_shape = (low((20,) + octet),)
        out_specs = (ANY_SPEC,)
    else:
        out_shape = (low((5,) + octet), low((5 * eighth + 16, 2 * width)), low((4,) + octet)) + (low(octet),) * 4
        out_shape += (jax.ShapeDtypeStruct((8, width), f32),)
        out_specs = (ANY_SPEC,) * 7 + (VMEM_SPEC,)
    extra = () if got is None else (got,)
    out = pl.pallas_call(
        functools.partial(rows_grad_kernel, kc, len(orders)),
        out_shape=out_shape,
        in_specs=[ANY_SPEC] * 7 + [VMEM_SPEC] * 2 + [ANY_SPEC] * (len(extra) + len(orders)),
        out_specs=out_specs,
        scratch_shapes=[
            pltpu.VMEM((rows, width), bf16),
            pltpu.VMEM((4, rows, part), bf16),
            pltpu.VMEM((4, rows, part), bf16),
            pltpu.VMEM((rows, width), bf16),
            pltpu.VMEM((rows, width), bf16),
            pltpu.VMEM((rows, attn0.shape[1]), bf16),
            pltpu.VMEM((rows, attn1.shape[1]), bf16),
            pltpu.VMEM((18,) + octet, bf16),
            pltpu.VMEM((20,) + octet, bf16),
            pltpu.VMEM(octet, bf16),
            pltpu.SemaphoreType.DMA((13,)),
            pltpu.SemaphoreType.DMA((5,)),
            pltpu.SemaphoreType.DMA((16,)),
        ],
        compiler_params=params(60),
        cost_estimate=pl.CostEstimate(flops=8 << 30, bytes_accessed=16 << 20, transcendentals=0),
        name="far_grad" if kc else "near_grad",
    )(y_low, d_pre, hidden, d_ffn, d_branch, attn0, attn1, small, bin_sum, *extra, *orders)
    return out[0] if kc else out


def row_sum_one_kernel(n_orders, near_from, got_from, *refs):
    outs, (near_ref, got_ref, in_sems, out_sems) = refs[n_orders : n_orders + 2], refs[n_orders + 2 :]
    rows = near_ref.shape[1]
    far = pl.ds(rows, rows)
    arriving, leaving = [], []
    for i in range(2):
        for j, (src, dst) in enumerate(((near_from, near_ref), (got_from, got_ref))):
            arriving.append(pltpu.make_async_copy(src.at[i, far], dst.at[i], in_sems.at[i, j]))
            arriving[-1].start()
    for i in range(2):
        arriving[2 * i].wait()
        arriving[2 * i + 1].wait()
        near_ref[i] = (near_ref[i].astype(f32) + got_ref[i].astype(f32)).astype(bf16)
        leaving.append(pltpu.make_async_copy(near_ref.at[i], outs[i], out_sems.at[i]))
        leaving[-1].start()
    for copy in leaving:
        copy.wait()


def row_sum_one(near, got, orders):
    _, rows, width = near.shape
    half = (2, rows // 2, width)
    return pl.pallas_call(
        functools.partial(row_sum_one_kernel, len(orders)),
        out_shape=(jax.ShapeDtypeStruct(half[1:], bf16),) * 2,
        in_specs=[ANY_SPEC] * (2 + len(orders)),
        out_specs=(ANY_SPEC,) * 2,
        scratch_shapes=[
            pltpu.VMEM(half, bf16),
            pltpu.VMEM(half, bf16),
            pltpu.SemaphoreType.DMA((2, 2)),
            pltpu.SemaphoreType.DMA((2,)),
        ],
        compiler_params=params(60),
        cost_estimate=pl.CostEstimate(flops=1 << 28, bytes_accessed=6 << 20, transcendentals=0),
        name="row_sum_one",
    )(near, got, *orders)


def row_sum_two_kernel(n_orders, near_from, got_from, even_from, odd_from, *refs):
    outs, (near_ref, got_ref, more_ref, in_sems, out_sems) = refs[n_orders : n_orders + 2], refs[n_orders + 2 :]
    rows = near_ref.shape[1]
    part = pl.ds(rows, rows)
    arriving, leaving = [], []
    for i, more_from in enumerate((even_from, odd_from)):
        pairs = (
            (near_from.at[i, part], near_ref.at[i]),
            (got_from.at[i, part], got_ref.at[i]),
            (more_from.at[part], more_ref.at[i]),
        )
        for j, (src, dst) in enumerate(pairs):
            arriving.append(pltpu.make_async_copy(src, dst, in_sems.at[i, j]))
            arriving[-1].start()
    for i in range(2):
        for copy in arriving[3 * i : 3 * i + 3]:
            copy.wait()
        near_ref[i] = (near_ref[i].astype(f32) + got_ref[i].astype(f32) + more_ref[i].astype(f32)).astype(bf16)
        leaving.append(pltpu.make_async_copy(near_ref.at[i], outs[i], out_sems.at[i]))
        leaving[-1].start()
    for copy in leaving:
        copy.wait()


def row_sum_two(near, got, even, odd, orders):
    quarter, width = near.shape[1] // 4, near.shape[2]
    two = pltpu.VMEM((2, quarter, width), bf16)
    return pl.pallas_call(
        functools.partial(row_sum_two_kernel, len(orders)),
        out_shape=(jax.ShapeDtypeStruct((quarter, width), bf16),) * 2,
        in_specs=[ANY_SPEC] * (4 + len(orders)),
        out_specs=(ANY_SPEC,) * 2,
        scratch_shapes=[two, two, two, pltpu.SemaphoreType.DMA((2, 3)), pltpu.SemaphoreType.DMA((2,))],
        compiler_params=params(60),
        cost_estimate=pl.CostEstimate(flops=1 << 28, bytes_accessed=4 << 20, transcendentals=0),
        name="row_sum_two",
    )(near, got, even, odd, *orders)


def row_sum_three_kernel(n_orders, near_from, got_from, even_from, odd_from, even_got, odd_got, done_from, *refs):
    refs = refs[n_orders:]
    outs, (near_ref, got_ref, one_ref, two_ref, done_ref, in_sems, out_sems) = refs[:4], refs[4:]
    rows = near_ref.shape[1]
    part = pl.ds(0, rows)
    arriving, leaving = [], []
    for i, (one, two) in enumerate(((even_from, even_got), (odd_from, odd_got))):
        pairs = (
            (near_from.at[i, part], near_ref.at[i]),
            (got_from.at[i, part], got_ref.at[i]),
            (one.at[part], one_ref.at[i]),
            (two, two_ref.at[i]),
            (done_from.at[pl.ds(i * rows, rows)], done_ref.at[i]),
        )
        for j, (src, dst) in enumerate(pairs):
            arriving.append(pltpu.make_async_copy(src, dst, in_sems.at[i, j]))
            arriving[-1].start()
    for i in range(2):
        for copy in arriving[5 * i : 5 * i + 5]:
            copy.wait()
        total = near_ref[i].astype(f32) + got_ref[i].astype(f32) + one_ref[i].astype(f32) + two_ref[i].astype(f32)
        near_ref[i] = (total + done_ref[i]).astype(bf16)
        for k in range(2):
            src = near_ref.at[i, pl.ds(k * (rows // 2), rows // 2)]
            leaving.append(pltpu.make_async_copy(src, outs[i + 2 * k], out_sems.at[i, k]))
            leaving[-1].start()
    for copy in leaving:
        copy.wait()


def row_sum_three(near, got, even, odd, even_got, odd_got, d_one, orders):
    quarter, width = near.shape[1] // 4, near.shape[2]
    two = pltpu.VMEM((2, quarter, width), bf16)
    return pl.pallas_call(
        functools.partial(row_sum_three_kernel, len(orders)),
        out_shape=(jax.ShapeDtypeStruct((quarter // 2, width), bf16),) * 4,
        in_specs=[ANY_SPEC] * (7 + len(orders)),
        out_specs=(ANY_SPEC,) * 4,
        scratch_shapes=[two, two, two, two, pltpu.VMEM((2, quarter, width), f32)]
        + [pltpu.SemaphoreType.DMA((2, 5)), pltpu.SemaphoreType.DMA((2, 2))],
        compiler_params=params(60),
        cost_estimate=pl.CostEstimate(flops=1 << 28, bytes_accessed=4 << 20, transcendentals=0),
        name="row_sum_three",
    )(near, got, even, odd, even_got, odd_got, d_one, *orders)


def plane_layer(
    tokens,
    w_qkv,
    bias_qv,
    w_out,
    bias_out,
    gain_one,
    bias_one,
    up_weight,
    up_bias_vector,
    down_weight,
    down_bias_vector,
    gain_two,
    bias_two,
    d_out,
    key_mask,
    rand_idx,
):
    z = lax.axis_index("sq")
    px = lax.axis_index("part")
    hy = lax.axis_index("hy")
    hc = lax.axis_index("hc")
    head = hy * 2 + hc
    span, seqs, width = tokens.shape
    heads, hd = w_qkv.shape[1], w_qkv.shape[3]
    n_o, n_kv = heads * hd, heads * 2 * hd
    hidden_dev = up_weight.shape[1]
    eighth = hidden_dev // 8
    length = key_mask.shape[1]
    blocks_all = length // BLOCK
    rows = seqs * span
    coords = jnp.stack([z, px, hy, hc]).astype(jnp.int32)
    octet = jnp.arange(8)

    def turn_octets(value):
        shape = value.shape
        value = flipped(value.reshape((2, 2, 2) + shape[1:]), z // 2, 0)
        return flipped(flipped(value, z % 2, 1), px, 2).reshape(shape)

    held_zd = octet // 2 % 2 + octet % 2 * 2
    held_order = ((held_zd ^ z) * 2 + ((octet // 4) ^ px)).astype(jnp.int32)
    bias_row = jnp.moveaxis(turn_octets(up_bias_vector.reshape(8, eighth)).reshape(2, 2, 2, eighth), (0, 2), (2, 0))
    bias_row = jnp.pad(bias_row.reshape(1, hidden_dev), ((0, 15), (0, 0)))
    n_wo = n_o // 2 + 16
    wf, wf_first, wo = pack(held_order, up_weight, down_weight, w_out.reshape(n_o, width), bias_row, [])
    wf_y = swap(wf_first, "hy", name="weight")
    wf_c = swap(wf, "hc", name="weight")

    raw = split(coords, tokens, [wf])
    tok = [raw[0]] + [swap(raw[k], "sq", k, name="tok") for k in range(1, 4)]
    w_kv, w_q_pad, w_q, b_kv, b_q = qkv_weights(w_qkv, bias_qv, raw)
    dres_raw = split(coords, d_out, raw)
    dres = [dres_raw[0]] + [swap(dres_raw[k], "sq", k, name="dres") for k in range(1, 4)]
    odd = after(jnp.concatenate([tok[1], tok[3]], axis=0), *tok, w_kv, wf_y, wf_c, *dres_raw)
    even = after(jnp.concatenate([tok[0], tok[2]], axis=0), *tok, w_kv, wf_y, wf_c, *dres_raw)
    even_x = swap(even, "part", name="tok")
    odd_y = swap(odd, "hy", name="tok")
    wo_y = swap(after(wo, odd), "hy", name="weight")
    even_near = after(jnp.concatenate([even, even_x], axis=0), odd_y, wo_y)
    odd_near = after(jnp.concatenate([odd, odd_y], axis=0), even_x)
    even_far = swap(even_near, "hy", name="tok")
    odd_far = swap(odd_near, "part", name="tok")
    mask_seq = lax.dynamic_index_in_dim(key_mask, z, 0, keepdims=False).reshape(blocks_all, BLOCK)
    mask = jnp.where(mask_seq == 1, 0.0, MASK_FILL).astype(f32)
    mask = jnp.pad(jnp.concatenate([mask, mask], axis=1), ((0, 8), (0, 0)), constant_values=MASK_FILL)
    rand = lax.dynamic_slice(rand_idx, (z, 0, head * heads, 0), (1, blocks_all, heads, 3)).reshape(-1)
    even_far = after(even_far, mask, rand, *dres[1:])
    xs = [even_near, even_far, swap(even_near, "hc", name="tok"), swap(even_far, "hc", name="tok")]
    xs += [odd_near, odd_far, swap(odd_near, "hc", name="tok"), swap(odd_far, "hc", name="tok")]
    vecs = jnp.stack([bias_out, gain_one, bias_one, down_bias_vector, gain_two, bias_two])
    vecs = jnp.pad(vecs, ((0, 2), (0, 0)))

    wf_yc = swap(wf_y, "hc", name="weight")
    wf_x = swap(wf_y, "part", name="weight")
    wo_yc = swap(wo_y, "hc", name="weight")

    o_near, o_far, lse, kv, q = project_and_attend(
        heads, hd, span, coords, rand, xs, w_kv, w_q_pad, b_kv, b_q, mask, []
    )
    attn_y = swap(o_far, "hy", name="attn")
    attn_c = swap(o_near[rows:], "hc", name="attn")
    attn_yc = swap(attn_y[rows:], "hc", name="attn")
    wf_x = after(wf_x, attn_c)
    wf_xc = swap(wf_x, "hc", name="weight")

    packs = [wf, wf_c, wo_y, wf_y, wf_x, wo_yc, wf_yc, wf_xc]
    first_rows = tuple((n, n > 0) for n in (n_wo, n_wo, n_wo, 0, 0, n_wo, 0, 0))
    out = rows_work([o_near, attn_c, attn_y, attn_yc], packs, first_rows, [even, odd], dres, vecs)
    result, (d_one, hidden, d_pre, y_low, d_ffn, d_branch, d_00, d_01, d_far, small, bin_sum) = out[:4], out[4:]

    d_y = swap(d_far, "hy", name="dattn")
    d_c = swap(d_01, "hc", name="dattn")
    d_yc = swap(d_y[1], "hc", name="dattn")

    other = rows_grad(1, y_low, d_pre, hidden, d_ffn, d_branch, attn_c, attn_yc, small, bin_sum)
    wide_got = swap(other, "hc", name="wide")
    res = [result[0]] + [swap(result[k], "sq", k, name="result") for k in range(1, 4)]
    keep, to_y, to_x, *across, small = rows_grad(
        0, y_low, d_pre, hidden, d_ffn, d_branch, o_near, attn_y, small, bin_sum, wide_got, [d_y, d_c]
    )
    y_got = swap(to_y, "hy", name="wide")
    x_got = swap(to_x, "part", name="wide")
    across_got = [swap(across[p], "sq", k, name="wide") for p, k in ((2, 1), (1, 2), (3, 3))]

    dq, dkv, dx, dx_far = attend_back(
        heads,
        hd,
        span,
        coords,
        rand,
        q,
        [d_00, d_c, d_y, d_yc],
        [o_near, o_far],
        kv,
        mask,
        lse,
        w_kv,
        w_q,
        [to_y, to_x, *across, *res[1:]],
    )
    dx_far = after(dx_far, y_got, x_got, *across_got)

    dx_got = swap(dx_far, "hc", name="dtok")
    octets = octet[:4]
    beyond = across_sum([across[0]] + across_got)
    wide = wide_sum(((octets // 2 + octets % 2 * 2) ^ z).astype(jnp.int32), keep, y_got, x_got, [beyond])
    beyond = swap_both(beyond, "across")
    zq, xq = octet // 2, octet % 2
    zd = zq ^ z
    spots = ((xq ^ px) * 4 + (zd % 2) * 2 + zd // 2).astype(jnp.int32)
    tail, tail_got = qkv_grad(span, spots, coords, dq, dkv, keep, y_got, small, xs, [wide])
    wide = lax.psum_scatter(wide, "sq", scatter_dimension=0, tiled=True)[0]
    tail_got = swap(tail_got, "part", name="tail")
    sent = row_sum_one(dx, dx_got, [tail])
    even_got, odd_got = swap(sent[0], "hy", name="dtok"), swap(sent[1], "part", name="dtok")
    keep, send = tail_sum(tail, tail_got, [*sent])
    wide = wide_end(wide, beyond, [*sent, keep])
    wide_two = swap(wide, "sq", 2, name="wide")
    wide = [wide, swap(wide, "sq", 1, name="wide")]
    own, send = tail_mid(keep, swap(send, "sq", 1, name="tail"))
    back_spots = (((octet % 4) ^ z) * 2 + ((octet // 4) ^ px)).astype(jnp.int32)
    sent_two = row_sum_two(dx, dx_got, even_got, odd_got, [send])
    wide[1], wide_two = after(wide[1], send), after(wide_two, send)
    wide += [wide_two, swap(wide_two, "sq", 1, name="wide")]
    wide += [swap(a, "part", name="wide") for a in wide]
    own = tail_end(own, swap(send, "sq", 2, name="tail"), [*sent_two])
    even_got2, odd_got2 = swap(sent_two[0], "part", name="dtok"), swap(sent_two[1], "hy", name="dtok")
    back_sent = row_sum_three(dx, dx_got, even_got, odd_got, even_got2, odd_got2, d_one, [])
    back = [back_sent[0]] + [swap(back_sent[k], "sq", k, name="dtok") for k in range(1, 4)]

    beyond = swap(own, "sq", 2, name="tail")
    thin_held = [own, swap(own, "sq", 1, name="tail"), beyond, swap(beyond, "sq", 1, name="tail")]
    thin_held += [swap(a, "part", name="tail") for a in thin_held]
    grad_w_in, grad_w_back = wide_place(back_spots, wide, [*back_sent])
    thin, grad_w_out, small = tail_place(
        back_spots, thin_held, n_o + n_kv, heads, [grad_w_in, grad_w_back]
    )
    grad_w_out = grad_w_out.reshape(heads, hd, width)
    grad_w_qkv = thin.reshape(width, heads, 3, hd)
    small = small.reshape(8, 1024)
    grad_bias_qv = jnp.stack(
        [small[7, :n_o].reshape(heads, hd), small[7, n_o : n_o + n_kv].reshape(heads, 2, hd)[:, 1]], axis=1
    )
    small = small[:, :width]
    return (
        jnp.transpose(relative(jnp.stack(res), z), (1, 0, 2)),
        jnp.transpose(relative(jnp.stack(back), z), (1, 0, 2)),
        grad_w_qkv,
        grad_bias_qv,
        grad_w_out,
        small[0],
        small[1],
        small[2],
        grad_w_in,
        small[6],
        grad_w_back,
        small[3],
        small[4],
        small[5],
    )


def solution(mesh):
    seq_size, head_size = mesh.shape["seq"], mesh.shape["head"]

    def run(*args):
        seqs = args[0].shape[1]
        fine = Mesh(
            np.asarray(mesh.devices).reshape(seqs, seq_size // seqs, head_size // 2, 2),
            ("sq", "part", "hy", "hc"),
        )
        rows = P(("sq", "part", "hy", "hc"), None, None)
        span = args[0].shape[0] // (seq_size * head_size)
        fits = seqs == 4 and seq_size == 8 and head_size == 4 and span % BLOCK == 0
        layer = plane_layer if fits else general_layer
        placed = (
            rows,
            P(None, HEAD, None, None),
            P(HEAD, None, None),
            P(HEAD, None, None),
            P(),
            P(),
            P(),
            P(None, HEAD),
            P(HEAD),
            P(HEAD, None),
            P(),
            P(),
            P(),
            rows,
            P(),
            P(),
        )
        return jax.shard_map(
            layer,
            mesh=fine,
            in_specs=placed,
            out_specs=(
                rows,
                rows,
                P(None, HEAD, None, None),
                P(HEAD, None, None),
                P(HEAD, None, None),
                P(),
                P(),
                P(),
                P(None, HEAD),
                P(HEAD),
                P(HEAD, None),
                P(),
                P(),
                P(),
            ),
            check_vma=False,
        )(*args)

    return run
```
